32 devices in a mesh: gr: 4 (over x, core), ty: 2 (over y), tx: 4 (over z).
Axes of the slice: x: 2, y: 2, z: 4, core: 2. Of those that a mesh axis runs over, the one named last changes fastest.
Arguments:
- encoder_out: bfloat16 [32, 32, 32, 768], P('gr', 'ty', 'tx'), may hold values from -6 to 6
- code_ids: int32 [32, 32, 32], P('gr', 'ty', 'tx'), may hold values from 0 to 50264, as said below
- segments: int32 [32, 32, 32], P('gr', 'ty', 'tx'), may hold values from 0 to 2, as said below
- embed_table: bfloat16 [50272, 768], P(('ty', 'tx')), may hold values from -6 to 6
- recon_grad: bfloat16 [32, 32, 32, 768], P('gr', 'ty', 'tx'), may hold values from -6 to 6
- qkv_weight: bfloat16 [768, 2304], replicated, may hold values from -0.21875 to 0.21875
- query_bias: bfloat16 [768], replicated, may hold values from -3 to 3
- value_bias: bfloat16 [768], replicated, may hold values from -3 to 3
- out_weight: bfloat16 [768, 768], replicated, may hold values from -2.5 to 2.5
- out_bias: bfloat16 [768], replicated, may hold values from -3 to 3
- first_gain: bfloat16 [768], replicated, may hold values from 0.25 to 1.75
- first_shift: bfloat16 [768], replicated, may hold values from -1.75 to 1.75
- second_gain: bfloat16 [768], replicated, may hold values from 0.25 to 1.75
- second_shift: bfloat16 [768], replicated, may hold values from -1.75 to 1.75
- up_weight: bfloat16 [768, 3072], replicated, may hold values from -0.21875 to 0.21875
- up_bias: bfloat16 [3072], replicated, may hold values from -3 to 3
- down_weight: bfloat16 [3072, 768], replicated, may hold values from -0.109375 to 0.109375
- down_bias: bfloat16 [768], replicated, may hold values from -3 to 3
- pixel_weight: bfloat16 [768, 9, 768], replicated, may hold values from -0.078125 to 0.078125
- pixel_bias: bfloat16 [768], replicated, may hold values from -3 to 3
Outputs:
- recon: bfloat16 [32, 32, 32, 768], P('gr', 'ty', 'tx')
- input_grad: bfloat16 [32, 32, 32, 768], P('gr', 'ty', 'tx')
- qkv_weight_grad: float32 [768, 2304], P(('ty', 'tx'))
- query_bias_grad: float32 [768], P(('ty', 'tx'))
- value_bias_grad: float32 [768], P(('ty', 'tx'))
- out_weight_grad: float32 [768, 768], P(('ty', 'tx'))
- out_bias_grad: float32 [768], P(('ty', 'tx'))
- first_gain_grad: float32 [768], P(('ty', 'tx'))
- first_shift_grad: float32 [768], P(('ty', 'tx'))
- second_gain_grad: float32 [768], P(('ty', 'tx'))
- second_shift_grad: float32 [768], P(('ty', 'tx'))
- up_weight_grad: float32 [768, 3072], P(('ty', 'tx'))
- up_bias_grad: float32 [3072], P(('ty', 'tx'))
- down_weight_grad: float32 [3072, 768], P(('ty', 'tx'))
- down_bias_grad: float32 [768], P(('ty', 'tx'))
- pixel_weight_grad: float32 [768, 9, 768], P(('ty', 'tx'))
- pixel_bias_grad: float32 [768], P(('ty', 'tx'))
The draws below stay inside these ranges and needn't reach their ends.
Inputs may be any that keep to these rules, and one draw needn't show every extreme that they name: `code_ids`: cut the stored table into 8 consecutive shares of 6284 rows, numbered as the devices of ty+tx with ty first; ids are below 50265. The ids of one device's 1024 patches fall at most 192 times into one share, and in each index of gr one share receives exactly 192 from every device. `segments`: each image is a rectangle of patches; a grid holds one to three images. Among the 8 grids of each index of gr, one is a single image.
All inputs are finite; a program needn't handle non-finite values.
Results may differ from the reference program's by a relative error of at most 0.02.
Values may be sent and summed in bfloat16 or wider, within the bound.
A program may use at most 384 MiB of HBM per device.

```python
import jax
import jax.numpy as jnp
from jax import lax

D = 768
HEADS = 12
HEAD_DIM = 64
FF = 3072
PIX = 768
V = 50265
GH = 32
GW = 32
GD = 8
GRIDS = 32
TH = 16
TW = 8
OWNERS = 8
VP = 50272
VD = 6284
ROWS = 1024
CAP = 192


def draw_code_ids(key, part):
    base_key = jax.random.fold_in(key, 5)
    score_key, holder_key, order_key, entry_key = jax.random.split(base_key, 4)
    groups = GRIDS // GD
    device_count = groups * OWNERS
    slot_total = OWNERS * CAP
    slot_index = jnp.arange(slot_total, dtype=jnp.int32)
    scores = jax.random.randint(score_key, (device_count, slot_total), 0, 1 << 18) * slot_total + slot_index[None, :]
    busiest = jnp.repeat(jax.random.randint(holder_key, (groups, 1), 0, OWNERS), OWNERS, axis=0)
    scores = jnp.where(slot_index[None, :] // CAP == busiest, -1, scores)
    picked = jnp.argsort(scores, axis=1, stable=True)[:, :ROWS]
    holders = picked // CAP
    mixing = jax.random.randint(order_key, (device_count, ROWS), 0, 1 << 18) * ROWS + jnp.arange(ROWS, dtype=jnp.int32)[None, :]
    holders = jnp.take_along_axis(holders, jnp.argsort(mixing, axis=1, stable=True), axis=1)
    limits = jnp.minimum(VD, V - holders * VD).astype(jnp.int32)
    entries = holders * VD + jax.random.randint(entry_key, (device_count, ROWS), 0, limits)
    tiles_down = GH // TH
    tiles_across = GW // TW
    entries = entries.reshape(groups, tiles_down, tiles_across, GD, TH, TW).transpose(0, 3, 1, 4, 2, 5)
    return entries.reshape(GRIDS, GH, GW).astype(jnp.int32)


def draw_segments(key, part):
    base_key = jax.random.fold_in(key, 9)
    column_key, row_key, whole_key = jax.random.split(base_key, 3)
    cut_column = jax.random.randint(column_key, (GRIDS, 1, 1), 1, GW)
    cut_row = jax.random.randint(row_key, (GRIDS, 1, 1), 1, GH)
    chosen = jnp.repeat(jax.random.randint(whole_key, (GRIDS // GD,), 0, GD), GD)
    row_index = jnp.arange(GH, dtype=jnp.int32)[None, :, None]
    column_index = jnp.arange(GW, dtype=jnp.int32)[None, None, :]
    labels = jnp.where(column_index < cut_column, 0, jnp.where(row_index < cut_row, 1, 2))
    single = jnp.arange(GRIDS, dtype=jnp.int32) % GD == chosen
    return jnp.where(single[:, None, None], 0, labels).astype(jnp.int32)


def block_levels(rng, shape, cuts, smallest, high):
    loudness = 1.0
    for position, shards_of in cuts:
        steps = jax.random.uniform(jax.random.fold_in(jax.random.fold_in(rng, 6), position), (shards_of,), jnp.float32, smallest / len(cuts), high / len(cuts))
        loudness = loudness * jnp.repeat(jnp.exp(steps), shape[position] // shards_of).reshape((-1,) + (1,) * (len(shape) - 1 - position))
    return loudness


def gaussian(key, shape, width, limit, cuts=(), kind=jnp.bfloat16):
    values = jax.random.normal(key, shape, jnp.float32) * width
    if len(cuts) > 0:
        values = block_levels(key, shape, cuts, -0.22, 0.18) * values
    return jnp.clip(values, min=-limit, max=limit).astype(kind)


def setup_inputs(seed: int = 0) -> dict:
    key_list = jax.random.split(jax.random.key(seed), 21)
    encoder_out = gaussian(key_list[0], (GRIDS, GH, GW, D), 1.0, 6.0, ((0, 4), (1, 2), (2, 4)))
    code_ids = draw_code_ids(jax.random.fold_in(key_list[20], 71), 0)
    segments = draw_segments(jax.random.fold_in(key_list[20], 71), 0)
    embed_table = gaussian(key_list[3], (VP, D), 1.0, 6.0, ((0, 8),))
    recon_grad = gaussian(key_list[4], (GRIDS, GH, GW, PIX), 1.0, 6.0, ((0, 4), (1, 2), (2, 4)))
    qkv_weight = gaussian(key_list[5], (D, 3 * D), D ** -0.5, 0.21875)
    query_bias = gaussian(key_list[6], (D,), 0.5, 3.0)
    value_bias = gaussian(key_list[7], (D,), 0.5, 3.0)
    out_weight = gaussian(key_list[8], (D, D), (max(D // 128, 1)) ** -0.5, 2.5)
    out_bias = gaussian(key_list[9], (D,), 0.5, 3.0)
    first_gain = jnp.clip(1.0 + 0.15 * jax.random.normal(key_list[10], (D,), jnp.float32), 0.25, 1.75).astype(jnp.bfloat16)
    first_shift = gaussian(key_list[11], (D,), 0.3, 1.75)
    second_gain = jnp.clip(1.0 + 0.15 * jax.random.normal(key_list[12], (D,), jnp.float32), 0.25, 1.75).astype(jnp.bfloat16)
    second_shift = gaussian(key_list[13], (D,), 0.3, 1.75)
    up_weight = gaussian(key_list[14], (D, FF), D ** -0.5, 0.21875)
    up_bias = gaussian(key_list[15], (FF,), 0.5, 3.0)
    down_weight = gaussian(key_list[16], (FF, D), FF ** -0.5, 0.109375)
    down_bias = gaussian(key_list[17], (D,), 0.5, 3.0)
    pixel_weight = gaussian(key_list[18], (D, 9, PIX), (9 * D) ** -0.5, 0.078125)
    pixel_bias = gaussian(key_list[19], (PIX,), 0.5, 3.0)
    return dict(encoder_out=encoder_out, code_ids=code_ids, segments=segments, embed_table=embed_table, recon_grad=recon_grad, qkv_weight=qkv_weight, query_bias=query_bias, value_bias=value_bias, out_weight=out_weight, out_bias=out_bias, first_gain=first_gain, first_shift=first_shift, second_gain=second_gain, second_shift=second_shift, up_weight=up_weight, up_bias=up_bias, down_weight=down_weight, down_bias=down_bias, pixel_weight=pixel_weight, pixel_bias=pixel_bias)


@jax.custom_vjp
def low(v):
    return lax.optimization_barrier(v.astype(jnp.bfloat16)).astype(jnp.float32)

@jax.custom_vjp
def low_back(v):
    return v

def low_keep(v):
    return (low(v), None)

def low_pass(kept, grad):
    return (grad,)

def back_keep(v):
    return (v, None)

def back_low(kept, grad):
    return (low(grad),)
low.defvjp(low_keep, low_pass)
low_back.defvjp(back_keep, back_low)
epsilon = 1e-06
commit_weight = 0.25
highest = lax.Precision.HIGHEST

def layer_norm(values, gain, shift):
    center = values - lax.optimization_barrier(jnp.mean(values, axis=-1, keepdims=True))
    spread = lax.optimization_barrier(jnp.mean(center * center, axis=-1, keepdims=True))
    return center * lax.rsqrt(spread + epsilon) * gain + shift

def grid_attention(bundle):
    queries, key_rows, values, segment_marks = bundle
    tokens, features = queries.shape
    query_heads = queries.reshape(tokens, HEADS, HEAD_DIM)
    key_heads = key_rows.reshape(tokens, HEADS, HEAD_DIM)
    value_heads = values.reshape(tokens, HEADS, HEAD_DIM)
    scores = jnp.einsum('qhd,khd->hqk', query_heads, key_heads, precision=highest) * float(HEAD_DIM) ** (-0.5)
    same_image = (segment_marks[:, None] == segment_marks[None, :])[None]
    scores = low_back(jnp.where(same_image, scores, -1000000000.0))
    probability = low(jax.nn.softmax(scores, axis=-1))
    attended = jnp.einsum('hqk,khd->qhd', probability, value_heads, precision=highest)
    return attended.reshape(tokens, features)

def pixel_head(features_low, segment_marks, pixel_weight, pixel_bias):
    grid_rows = features_low.shape[1]
    grid_cols = features_low.shape[2]
    padded = jnp.pad(features_low, ((0, 0), (1, 1), (1, 1), (0, 0)))
    marks_pad = jnp.pad(segment_marks, ((0, 0), (1, 1), (1, 1)), constant_values=-1)
    tap_list = []
    for vertical in range(3):
        for lateral in range(3):
            inside = marks_pad[:, vertical:vertical + grid_rows, lateral:lateral + grid_cols] == segment_marks
            tap_list.append(jnp.where(inside[..., None], padded[:, vertical:vertical + grid_rows, lateral:lateral + grid_cols], 0.0))
    stacked = jnp.stack(tap_list, axis=3)
    return jnp.einsum('nhwkd,dkp->nhwp', stacked, pixel_weight, precision=highest) + pixel_bias

def layer_forward(params, start_rows, segment_marks):
    qkv_weight, query_bias, value_bias, out_weight, out_bias, first_gain, first_shift, second_gain, second_shift, up_weight, up_bias, down_weight, down_bias, pixel_weight, pixel_bias = params
    grid_count = start_rows.shape[0]
    features = start_rows.shape[-1]
    flat_rows = start_rows.reshape(grid_count, GH * GW, features)
    normed = low(layer_norm(flat_rows, first_gain, first_shift))
    projected = jnp.einsum('gtd,de->gte', normed, qkv_weight, precision=highest)
    queries = low(low_back(projected[..., :features] + query_bias))
    key_rows = low(low_back(projected[..., features:2 * features]))
    values = low(low_back(projected[..., 2 * features:] + value_bias))
    marks_flat = segment_marks.reshape(grid_count, GH * GW)
    attended = lax.map(jax.checkpoint(grid_attention), (queries, key_rows, values, marks_flat))
    attended = low(low_back(attended))
    branch = low_back(jnp.einsum('gtd,de->gte', attended, out_weight, precision=highest) + out_bias)
    middle = flat_rows + branch
    normed_two = low(layer_norm(middle, second_gain, second_shift))
    hidden_pre = low_back(jnp.einsum('gtd,df->gtf', normed_two, up_weight, precision=highest) + up_bias)
    hidden_act = low(jax.nn.gelu(hidden_pre, approximate=False))
    lower_rows = low_back(jnp.einsum('gtf,fd->gtd', hidden_act, down_weight, precision=highest) + down_bias)
    output_rows = middle + lower_rows
    features_low = low(output_rows).reshape(grid_count, GH, GW, features)
    return pixel_head(features_low, segment_marks, pixel_weight, pixel_bias)

def reference(encoder_out, code_ids, segments, embed_table, recon_grad, qkv_weight, query_bias, value_bias, out_weight, out_bias, first_gain, first_shift, second_gain, second_shift, up_weight, up_bias, down_weight, down_bias, pixel_weight, pixel_bias):
    params = tuple((weight.astype(jnp.float32) for weight in (qkv_weight, query_bias, value_bias, out_weight, out_bias, first_gain, first_shift, second_gain, second_shift, up_weight, up_bias, down_weight, down_bias, pixel_weight, pixel_bias)))
    group_size = 2
    block_count = GRIDS // group_size

    def regroup(array):
        return array.reshape((block_count, group_size) + array.shape[1:])

    def one_block(carried, bundle):
        inputs_block, ids_block, marks_block, cotangent = bundle
        inputs_block = inputs_block.astype(jnp.float32)
        codes_block = jnp.take(embed_table, ids_block, axis=0).astype(jnp.float32)
        shift_block = codes_block - inputs_block

        def objective(weights, entry):
            recon_block = layer_forward(weights, entry + shift_block, marks_block)
            distance = entry - codes_block
            return (recon_block, commit_weight * jnp.sum(distance * distance))
        (recon_block, commit_loss), pullback = jax.vjp(objective, params, inputs_block)
        weight_grads, entry_grad = pullback((cotangent.astype(jnp.float32), jnp.float32(1.0) + 0.0 * commit_loss))
        carried = jax.tree.map(lambda running, addend: running + addend, carried, weight_grads)
        return (carried, (recon_block.astype(jnp.bfloat16), entry_grad.astype(jnp.bfloat16)))
    initial = tuple((jnp.zeros(weight.shape, jnp.float32) for weight in params))
    summed, (recon_blocks, input_blocks) = lax.scan(one_block, initial, (regroup(encoder_out), regroup(code_ids), regroup(segments), regroup(recon_grad)))
    recon = recon_blocks.reshape((GRIDS, GH, GW, PIX))
    input_grad = input_blocks.reshape((GRIDS, GH, GW, D))
    return (recon, input_grad, summed[0], summed[1], summed[2], summed[3], summed[4], summed[5], summed[6], summed[7], summed[8], summed[9], summed[10], summed[11], summed[12], summed[13], summed[14])
```

```python
from functools import partial

import jax
import jax.numpy as jnp
from jax import lax
from jax.experimental import pallas as pl
from jax.experimental.pallas import tpu as pltpu
from jax.sharding import PartitionSpec as P

HEADS = 12
HEAD_DIM = 64


epsilon = 1e-06
commit_weight = 0.25


def with_halo(block, sides, width):
    for axis, dim in sides:
        count = lax.axis_size(axis)
        forward = [(i, i + 1) for i in range(count - 1)]
        backward = [(target, source) for source, target in forward]
        low = lax.ppermute(
            lax.slice_in_dim(block, block.shape[dim] - width, None, axis=dim), axis, forward
        )
        high = lax.ppermute(lax.slice_in_dim(block, 0, width, axis=dim), axis, backward)
        block = jnp.concatenate([low, block, high], axis=dim)
    return block


def layer_norm(values, gain, shift):
    center = values - jnp.mean(values, axis=-1, keepdims=True)
    spread = jnp.mean(center * center, axis=-1, keepdims=True)
    return center * lax.rsqrt(spread + epsilon) * gain + shift


def exact_gelu(values):
    return jax.nn.gelu(values, approximate=False)


def matmul(left_side, right_side):
    return jnp.dot(left_side, right_side, preferred_element_type=jnp.float32)


def left_product(left_side, right_side):
    return lax.dot_general(
        left_side, right_side, (((0,), (0,)), ((), ())), preferred_element_type=jnp.float32
    )


def right_product(left_side, right_side):
    return lax.dot_general(
        left_side, right_side, (((1,), (1,)), ((), ())), preferred_element_type=jnp.float32
    )


def pad_side(array, axis_index):
    widths = [(0, 0)] * array.ndim
    widths[axis_index] = (1, 1)
    return jnp.pad(array, widths)


def blocked(array, block_size):
    return array.reshape((array.shape[0] // block_size, block_size) + array.shape[1:])


def unblock(array):
    return array.reshape((-1,) + array.shape[2:])


def head_scores(queries, key_rows, marks_query, marks_key, head_count, score_scale):
    grid_count, query_rows, features = queries.shape
    query_heads = queries.reshape(grid_count, query_rows, head_count, features // head_count)
    key_heads = key_rows.reshape(grid_count, key_rows.shape[1], head_count, features // head_count)
    scores = (
        jnp.einsum("bqhd,bkhd->bhqk", query_heads, key_heads, preferred_element_type=jnp.float32)
        * score_scale
    )
    same_image = (marks_query[:, :, None] == marks_key[:, None, :])[:, None]
    return jnp.where(same_image, scores, -1000000000.0)


def attend_block(bundle, head_count, score_scale):
    queries, key_rows, values, marks_query, marks_key = bundle
    grid_count, query_rows, features = queries.shape
    scores = head_scores(queries, key_rows, marks_query, marks_key, head_count, score_scale)
    running_max = jnp.max(scores, axis=-1, keepdims=True)
    exponent = jnp.exp(scores - running_max)
    denominator = jnp.sum(exponent, axis=-1, keepdims=True)
    probability = (exponent / denominator).astype(jnp.bfloat16)
    value_heads = values.reshape(grid_count, values.shape[1], head_count, features // head_count)
    attended = jnp.einsum(
        "bhqk,bkhd->bqhd", probability, value_heads, preferred_element_type=jnp.float32
    )
    return (
        attended.reshape(grid_count, query_rows, features).astype(jnp.bfloat16),
        running_max + jnp.log(denominator),
    )


def attend_back(bundle, head_count, score_scale):
    queries, key_rows, values, marks_query, marks_key, log_total, out_grad = bundle
    grid_count, query_rows, features = queries.shape
    head_size = features // head_count
    scores = head_scores(queries, key_rows, marks_query, marks_key, head_count, score_scale)
    probability = jnp.exp(scores - log_total)
    query_heads = queries.reshape(grid_count, query_rows, head_count, head_size)
    key_heads = key_rows.reshape(grid_count, key_rows.shape[1], head_count, head_size)
    value_heads = values.reshape(grid_count, values.shape[1], head_count, head_size)
    grad_heads = out_grad.reshape(grid_count, query_rows, head_count, head_size)
    prob_grad = jnp.einsum(
        "bqhd,bkhd->bhqk", grad_heads, value_heads, preferred_element_type=jnp.float32
    )
    inner_sum = jnp.sum(probability * prob_grad, axis=-1, keepdims=True)
    score_grad = (probability * (prob_grad - inner_sum)).astype(jnp.bfloat16)
    query_grad = (
        jnp.einsum("bhqk,bkhd->bqhd", score_grad, key_heads, preferred_element_type=jnp.float32)
        * score_scale
    )
    key_grad = (
        jnp.einsum("bhqk,bqhd->bkhd", score_grad, query_heads, preferred_element_type=jnp.float32)
        * score_scale
    )
    value_grad = jnp.einsum(
        "bhqk,bqhd->bkhd",
        probability.astype(jnp.bfloat16),
        grad_heads,
        preferred_element_type=jnp.float32,
    )
    key_count = key_rows.shape[1]
    return (
        query_grad.reshape(grid_count, query_rows, features).astype(jnp.bfloat16),
        key_grad.reshape(grid_count, key_count, features),
        value_grad.reshape(grid_count, key_count, features),
    )


def on_device_bands(
    encoder_out,
    code_ids,
    segments,
    embed_table,
    recon_grad,
    qkv_weight,
    query_bias,
    value_bias,
    out_weight,
    out_bias,
    first_gain,
    first_shift,
    second_gain,
    second_shift,
    up_weight,
    up_bias,
    down_weight,
    down_bias,
    pixel_weight,
    pixel_bias,
):
    features = encoder_out.shape[-1]
    head_count = HEADS
    score_scale = float(HEAD_DIM) ** (-0.5)
    holder_count = lax.axis_size(("ty", "tx"))
    share_rows = embed_table.shape[0]
    flat_ids = code_ids.reshape(-1)
    row_count = flat_ids.shape[0]
    slot_count = 3 * row_count // (2 * holder_count)
    holder = flat_ids // share_rows
    offsets = flat_ids - holder * share_rows
    belongs = (holder[:, None] == jnp.arange(holder_count, dtype=jnp.int32)[None, :]).astype(
        jnp.int32
    )
    slot_rank = jnp.sum((jnp.cumsum(belongs, axis=0) - 1) * belongs, axis=1)
    slot_index = holder * slot_count + slot_rank
    requests = jnp.zeros((holder_count * slot_count,), jnp.int32).at[slot_index].set(offsets)
    requests = requests.reshape(holder_count, slot_count)
    fetched = jnp.take(
        embed_table,
        lax.all_to_all(requests, ("ty", "tx"), split_axis=0, concat_axis=0, tiled=True),
        axis=0,
    )
    returned = lax.all_to_all(fetched, ("ty", "tx"), split_axis=0, concat_axis=0, tiled=True)
    codes = returned.reshape(holder_count * slot_count, features)[slot_index].reshape(
        encoder_out.shape
    )
    marks_tile = (segments + 1).astype(jnp.bfloat16)
    arrived = (
        lax.all_to_all(encoder_out, "tx", split_axis=0, concat_axis=2, tiled=True),
        lax.all_to_all(codes, "tx", split_axis=0, concat_axis=2, tiled=True),
        lax.all_to_all(recon_grad, "tx", split_axis=0, concat_axis=2, tiled=True),
        lax.all_to_all(marks_tile, "tx", split_axis=0, concat_axis=2, tiled=True),
    )
    inputs_band, codes_band, cotangent_band, marks_band = arrived
    grid_count, band_rows, band_cols = marks_band.shape
    tokens = band_rows * band_cols
    all_rows = grid_count * tokens
    block_size = max(1, 512 // tokens)
    while grid_count % block_size:
        block_size -= 1
    start_rows = codes_band.reshape(all_rows, features).astype(jnp.float32)
    marks_query = marks_band.reshape(grid_count, tokens)
    normed, first_pull = jax.vjp(
        layer_norm, start_rows, first_gain.astype(jnp.float32), first_shift.astype(jnp.float32)
    )
    normed_low = normed.astype(jnp.bfloat16)
    projected = matmul(normed_low, qkv_weight)
    queries = (
        (projected[:, :features] + query_bias.astype(jnp.float32))
        .astype(jnp.bfloat16)
        .reshape(grid_count, tokens, features)
    )
    key_rows = (
        projected[:, features : 2 * features]
        .astype(jnp.bfloat16)
        .reshape(grid_count, tokens, features)
    )
    values = (
        (projected[:, 2 * features :] + value_bias.astype(jnp.float32))
        .astype(jnp.bfloat16)
        .reshape(grid_count, tokens, features)
    )
    bundle = (key_rows, values, marks_query)
    keys_all = lax.all_gather(bundle[0], "ty", axis=1, tiled=True)
    values_all = lax.all_gather(bundle[1], "ty", axis=1, tiled=True)
    marks_key = lax.all_gather(bundle[2], "ty", axis=1, tiled=True)
    attended_blocks, log_total = lax.map(
        partial(attend_block, head_count=head_count, score_scale=score_scale),
        (
            blocked(queries, block_size),
            blocked(keys_all, block_size),
            blocked(values_all, block_size),
            blocked(marks_query, block_size),
            blocked(marks_key, block_size),
        ),
    )
    attended = unblock(attended_blocks).reshape(all_rows, features)
    branch = matmul(attended, out_weight) + out_bias.astype(jnp.float32)
    middle = start_rows + branch
    normed_two, second_pull = jax.vjp(
        layer_norm, middle, second_gain.astype(jnp.float32), second_shift.astype(jnp.float32)
    )
    normed_two_low = normed_two.astype(jnp.bfloat16)
    hidden_pre = matmul(normed_two_low, up_weight) + up_bias.astype(jnp.float32)
    hidden_act, gelu_pull = jax.vjp(exact_gelu, hidden_pre)
    hidden_low = hidden_act.astype(jnp.bfloat16)
    output_rows = middle + (matmul(hidden_low, down_weight) + down_bias.astype(jnp.float32))
    features_low = output_rows.astype(jnp.bfloat16).reshape(
        grid_count, band_rows, band_cols, features
    )
    bundle = (features_low, marks_band, cotangent_band)
    grown = (
        with_halo(bundle[0], (("ty", 1),), 1),
        with_halo(bundle[1], (("ty", 1),), 1),
        with_halo(bundle[2], (("ty", 1),), 1),
    )
    features_pad, marks_pad, cotangent_pad = tuple((pad_side(member, 2) for member in grown))
    ahead_list = []
    behind_list = []
    for vertical in range(3):
        for lateral in range(3):
            inside = (
                marks_pad[:, vertical : vertical + band_rows, lateral : lateral + band_cols]
                == marks_band
            )
            ahead_list.append(
                jnp.where(
                    inside[..., None],
                    features_pad[:, vertical : vertical + band_rows, lateral : lateral + band_cols],
                    0,
                )
            )
            mirror_row = 2 - vertical
            mirror_col = 2 - lateral
            facing = (
                marks_pad[
                    :, mirror_row : mirror_row + band_rows, mirror_col : mirror_col + band_cols
                ]
                == marks_band
            )
            behind_list.append(
                jnp.where(
                    facing[..., None],
                    cotangent_pad[
                        :, mirror_row : mirror_row + band_rows, mirror_col : mirror_col + band_cols
                    ],
                    0,
                )
            )
    ahead = jnp.stack(ahead_list, axis=3)
    behind = jnp.stack(behind_list, axis=3)
    recon_band = jnp.einsum(
        "nhwkd,dkp->nhwp", ahead, pixel_weight, preferred_element_type=jnp.float32
    ) + pixel_bias.astype(jnp.float32)
    pixel_weight_grad = jnp.einsum(
        "nhwkd,nhwp->dkp", ahead, cotangent_band, preferred_element_type=jnp.float32
    )
    pixel_bias_grad = jnp.sum(cotangent_band.astype(jnp.float32), axis=(0, 1, 2))
    final_grad = jnp.einsum(
        "nhwkp,dkp->nhwd", behind, pixel_weight, preferred_element_type=jnp.float32
    ).reshape(all_rows, features)
    lower_grad = final_grad.astype(jnp.bfloat16)
    down_weight_grad = left_product(hidden_low, lower_grad)
    down_bias_grad = jnp.sum(lower_grad.astype(jnp.float32), axis=0)
    pre_grad = gelu_pull(right_product(lower_grad, down_weight))[0].astype(jnp.bfloat16)
    up_weight_grad = left_product(normed_two_low, pre_grad)
    up_bias_grad = jnp.sum(pre_grad.astype(jnp.float32), axis=0)
    middle_part, second_gain_grad, second_shift_grad = second_pull(
        right_product(pre_grad, up_weight)
    )
    middle_grad = final_grad + middle_part
    branch_grad = middle_grad.astype(jnp.bfloat16)
    out_weight_grad = left_product(attended, branch_grad)
    out_bias_grad = jnp.sum(branch_grad.astype(jnp.float32), axis=0)
    attended_grad = (
        right_product(branch_grad, out_weight)
        .astype(jnp.bfloat16)
        .reshape(grid_count, tokens, features)
    )
    query_blocks, key_blocks, value_blocks = lax.map(
        partial(attend_back, head_count=head_count, score_scale=score_scale),
        (
            blocked(queries, block_size),
            blocked(keys_all, block_size),
            blocked(values_all, block_size),
            blocked(marks_query, block_size),
            blocked(marks_key, block_size),
            log_total,
            blocked(attended_grad, block_size),
        ),
    )
    query_grad = unblock(query_blocks)
    bundle = (unblock(key_blocks), unblock(value_blocks))
    key_sum = lax.psum_scatter(
        bundle[0].astype(jnp.bfloat16), "ty", scatter_dimension=1, tiled=True
    )
    value_sum = lax.psum_scatter(
        bundle[1].astype(jnp.bfloat16), "ty", scatter_dimension=1, tiled=True
    )
    projected_grad = jnp.concatenate([query_grad, key_sum, value_sum], axis=-1).reshape(
        all_rows, 3 * features
    )
    qkv_weight_grad = left_product(normed_low, projected_grad)
    query_bias_grad = jnp.sum(query_grad.astype(jnp.float32), axis=(0, 1))
    value_bias_grad = jnp.sum(value_sum.astype(jnp.float32), axis=(0, 1))
    start_part, first_gain_grad, first_shift_grad = first_pull(
        right_product(projected_grad, qkv_weight)
    )
    start_grad = middle_grad + start_part
    inputs_rows = inputs_band.reshape(all_rows, features).astype(jnp.float32)
    input_band = (start_grad + 2.0 * commit_weight * (inputs_rows - start_rows)).astype(
        jnp.bfloat16
    )
    bundle = (
        recon_band.astype(jnp.bfloat16),
        input_band.reshape(grid_count, band_rows, band_cols, features),
    )
    recon_tiles = lax.all_to_all(bundle[0], "tx", split_axis=2, concat_axis=0, tiled=True)
    input_tiles = lax.all_to_all(bundle[1], "tx", split_axis=2, concat_axis=0, tiled=True)
    local_grads = (
        qkv_weight_grad,
        query_bias_grad,
        value_bias_grad,
        out_weight_grad,
        out_bias_grad,
        first_gain_grad,
        first_shift_grad,
        second_gain_grad,
        second_shift_grad,
        up_weight_grad,
        up_bias_grad,
        down_weight_grad,
        down_bias_grad,
        pixel_weight_grad,
        pixel_bias_grad,
    )
    tile_shares = (
        lax.psum_scatter(
            local_grads[0].astype(jnp.bfloat16), ("ty", "tx"), scatter_dimension=0, tiled=True
        ).astype(jnp.float32),
        lax.psum_scatter(
            local_grads[1].astype(jnp.bfloat16), ("ty", "tx"), scatter_dimension=0, tiled=True
        ).astype(jnp.float32),
        lax.psum_scatter(
            local_grads[2].astype(jnp.bfloat16), ("ty", "tx"), scatter_dimension=0, tiled=True
        ).astype(jnp.float32),
        lax.psum_scatter(
            local_grads[3].astype(jnp.bfloat16), ("ty", "tx"), scatter_dimension=0, tiled=True
        ).astype(jnp.float32),
        lax.psum_scatter(
            local_grads[4].astype(jnp.bfloat16), ("ty", "tx"), scatter_dimension=0, tiled=True
        ).astype(jnp.float32),
        lax.psum_scatter(
            local_grads[5].astype(jnp.bfloat16), ("ty", "tx"), scatter_dimension=0, tiled=True
        ).astype(jnp.float32),
        lax.psum_scatter(
            local_grads[6].astype(jnp.bfloat16), ("ty", "tx"), scatter_dimension=0, tiled=True
        ).astype(jnp.float32),
        lax.psum_scatter(
            local_grads[7].astype(jnp.bfloat16), ("ty", "tx"), scatter_dimension=0, tiled=True
        ).astype(jnp.float32),
        lax.psum_scatter(
            local_grads[8].astype(jnp.bfloat16), ("ty", "tx"), scatter_dimension=0, tiled=True
        ).astype(jnp.float32),
        lax.psum_scatter(
            local_grads[9].astype(jnp.bfloat16), ("ty", "tx"), scatter_dimension=0, tiled=True
        ).astype(jnp.float32),
        lax.psum_scatter(
            local_grads[10].astype(jnp.bfloat16), ("ty", "tx"), scatter_dimension=0, tiled=True
        ).astype(jnp.float32),
        lax.psum_scatter(
            local_grads[11].astype(jnp.bfloat16), ("ty", "tx"), scatter_dimension=0, tiled=True
        ).astype(jnp.float32),
        lax.psum_scatter(
            local_grads[12].astype(jnp.bfloat16), ("ty", "tx"), scatter_dimension=0, tiled=True
        ).astype(jnp.float32),
        lax.psum_scatter(
            local_grads[13].astype(jnp.bfloat16), ("ty", "tx"), scatter_dimension=0, tiled=True
        ).astype(jnp.float32),
        lax.psum_scatter(
            local_grads[14].astype(jnp.bfloat16), ("ty", "tx"), scatter_dimension=0, tiled=True
        ).astype(jnp.float32),
    )
    summed = (
        lax.psum(tile_shares[0].astype(jnp.bfloat16), "gr").astype(jnp.float32),
        lax.psum(tile_shares[1].astype(jnp.bfloat16), "gr").astype(jnp.float32),
        lax.psum(tile_shares[2].astype(jnp.bfloat16), "gr").astype(jnp.float32),
        lax.psum(tile_shares[3].astype(jnp.bfloat16), "gr").astype(jnp.float32),
        lax.psum(tile_shares[4].astype(jnp.bfloat16), "gr").astype(jnp.float32),
        lax.psum(tile_shares[5].astype(jnp.bfloat16), "gr").astype(jnp.float32),
        lax.psum(tile_shares[6].astype(jnp.bfloat16), "gr").astype(jnp.float32),
        lax.psum(tile_shares[7].astype(jnp.bfloat16), "gr").astype(jnp.float32),
        lax.psum(tile_shares[8].astype(jnp.bfloat16), "gr").astype(jnp.float32),
        lax.psum(tile_shares[9].astype(jnp.bfloat16), "gr").astype(jnp.float32),
        lax.psum(tile_shares[10].astype(jnp.bfloat16), "gr").astype(jnp.float32),
        lax.psum(tile_shares[11].astype(jnp.bfloat16), "gr").astype(jnp.float32),
        lax.psum(tile_shares[12].astype(jnp.bfloat16), "gr").astype(jnp.float32),
        lax.psum(tile_shares[13].astype(jnp.bfloat16), "gr").astype(jnp.float32),
        lax.psum(tile_shares[14].astype(jnp.bfloat16), "gr").astype(jnp.float32),
    )
    return (
        recon_tiles,
        input_tiles,
        summed[0],
        summed[1],
        summed[2],
        summed[3],
        summed[4],
        summed[5],
        summed[6],
        summed[7],
        summed[8],
        summed[9],
        summed[10],
        summed[11],
        summed[12],
        summed[13],
        summed[14],
    )


far = float(2.0**30)


def nt(left_side, right_side):
    return lax.dot_general(
        left_side, right_side, (((1,), (1,)), ((), ())), preferred_element_type=jnp.float32
    )


def nn(left_side, right_side):
    return lax.dot_general(
        left_side, right_side, (((1,), (0,)), ((), ())), preferred_element_type=jnp.float32
    )


def mark_columns(marks):
    lane = lax.broadcasted_iota(jnp.int32, (1, 128), 1) % 64
    hot = marks[:, None] == lane
    query_side = jnp.where(hot, 1.0, 0.0)
    key_side = jnp.where((lane < 3) & ~hot, -far, 0.0)
    return query_side.astype(jnp.bfloat16), key_side.astype(jnp.bfloat16)


def attend_kernel(q_ref, k_ref, v_ref, qa_ref, ka_ref, o_ref, col_ref):
    lane = lax.broadcasted_iota(jnp.int32, (1, 128), 1)
    low = lane < 64
    local = lane % 64
    one = jnp.ones((), jnp.bfloat16)
    queries, key_rows, values = q_ref[...], k_ref[...], v_ref[...]
    query_marks, key_marks = qa_ref[...], ka_ref[...]
    outs = []
    logs = []
    for head in range(2):
        own = low if head == 0 else ~low
        scores = nt(jnp.where(own, queries, query_marks), jnp.where(own, key_rows, key_marks))
        top = jnp.max(scores, axis=1, keepdims=True)
        weights = jnp.exp(scores - top).astype(jnp.bfloat16)
        sums = nn(weights, jnp.where(own, values, one))
        outs.append(sums / pltpu.roll(sums, 64, 1))
        logs.append(top + jnp.log(sums))
    o_ref[...] = jnp.where(low, outs[0], outs[1]).astype(jnp.bfloat16)
    minus = -jnp.where(low, logs[1], logs[0])
    first = minus.astype(jnp.bfloat16).astype(jnp.float32)
    second = (minus - first).astype(jnp.bfloat16).astype(jnp.float32)
    third = minus - first - second
    columns = jnp.where(
        local == 3,
        first,
        jnp.where(local == 4, second, jnp.where(local == 5, third, query_marks.astype(jnp.float32))),
    )
    col_ref[...] = columns.astype(jnp.bfloat16)


def attend(queries, key_rows, values, query_marks, key_marks):
    tokens, features = queries.shape
    pair = pl.BlockSpec((tokens, 128), lambda i: (0, i))
    shared = pl.BlockSpec((tokens, 128), lambda i: (0, 0))
    shape = jax.ShapeDtypeStruct((tokens, features), jnp.bfloat16)
    return pl.pallas_call(
        attend_kernel,
        grid=(features // 128,),
        in_specs=[pair, pair, pair, shared, shared],
        out_specs=[pair, pair],
        out_shape=[shape, shape],
        compiler_params=pltpu.CompilerParams(vmem_limit_bytes=48 * 2**20),
        cost_estimate=pl.CostEstimate(
            flops=16 * tokens * tokens * features,
            bytes_accessed=10 * tokens * features,
            transcendentals=tokens * tokens * features // 64,
        ),
        name="attend",
    )(queries, key_rows, values, query_marks, key_marks)


def attend_back_kernel(
    q_ref, k_ref, v_ref, col_ref, ka_ref, o_ref, g_ref, dq_ref, dk_ref, dv_ref, k_sum, v_sum, *, step
):
    lane = lax.broadcasted_iota(jnp.int32, (1, 128), 1)
    low = lane < 64
    local = lane % 64
    zero = jnp.zeros((), jnp.bfloat16)
    one = jnp.ones((), jnp.bfloat16)
    key_rows, values = k_ref[...], v_ref[...]
    tokens = key_rows.shape[0]
    key_columns = jnp.where((local >= 3) & (local < 6), one, ka_ref[...])
    value_columns = jnp.where(local < 2, one, zero)
    keys_of = [jnp.where(low, key_rows, key_columns), jnp.where(low, key_columns, key_rows)]
    values_of = [jnp.where(low, values, value_columns), jnp.where(low, value_columns, values)]
    keys_across = key_rows.T
    upper = lax.broadcasted_iota(jnp.int32, (128, 1), 0) < 64
    k_sum[...] = jnp.zeros_like(k_sum)
    v_sum[...] = jnp.zeros_like(v_sum)

    def one_block(i, _):
        rows = pl.ds(pl.multiple_of(i * step, step), step)
        queries, columns = q_ref[rows, :], col_ref[rows, :]
        grad, out = g_ref[rows, :], o_ref[rows, :]
        both = grad.astype(jnp.float32) * out.astype(jnp.float32)
        of_low = -jnp.sum(jnp.where(low, both, 0.0), axis=1, keepdims=True)
        of_high = -jnp.sum(jnp.where(low, 0.0, both), axis=1, keepdims=True)
        inner = jnp.where(low, of_high, of_low)
        first = inner.astype(jnp.bfloat16).astype(jnp.float32)
        grad_columns = jnp.where(
            local == 0, first, jnp.where(local == 1, inner - first, 0.0)
        ).astype(jnp.bfloat16)
        query_parts, key_parts, value_parts = [], [], []
        for head in range(2):
            own = low if head == 0 else ~low
            weights = jnp.exp(nt(keys_of[head], jnp.where(own, queries, columns)))
            change = nt(values_of[head], jnp.where(own, grad, grad_columns))
            score_grad = (weights * change).astype(jnp.bfloat16)
            value_parts.append(nn(weights.astype(jnp.bfloat16), grad))
            key_parts.append(nn(score_grad, queries))
            query_parts.append(nn(keys_across, score_grad))
        k_sum[...] += jnp.where(low, key_parts[0], key_parts[1])
        v_sum[...] += jnp.where(low, value_parts[0], value_parts[1])
        query_grad = jnp.where(upper, query_parts[0], query_parts[1]).T
        dq_ref[rows, :] = (query_grad * HEAD_DIM**-0.5).astype(jnp.bfloat16)
        return 0

    lax.fori_loop(0, tokens // step, one_block, 0)
    dk_ref[...] = k_sum[...].astype(jnp.bfloat16)
    dv_ref[...] = v_sum[...].astype(jnp.bfloat16)


def attend_back_grid(queries, key_rows, values, columns, key_marks, out, grad):
    tokens, features = queries.shape
    pair = pl.BlockSpec((tokens, 128), lambda i: (0, i))
    shared = pl.BlockSpec((tokens, 128), lambda i: (0, 0))
    shape = jax.ShapeDtypeStruct((tokens, features), jnp.bfloat16)
    return pl.pallas_call(
        partial(attend_back_kernel, step=min(512, tokens)),
        grid=(features // 128,),
        in_specs=[pair, pair, pair, pair, shared, pair, pair],
        out_specs=[pair, pair, pair],
        out_shape=[shape, shape, shape],
        scratch_shapes=[pltpu.VMEM((tokens, 128), jnp.float32)] * 2,
        compiler_params=pltpu.CompilerParams(vmem_limit_bytes=48 * 2**20),
        cost_estimate=pl.CostEstimate(
            flops=24 * tokens * tokens * features,
            bytes_accessed=18 * tokens * features,
            transcendentals=tokens * tokens * features // 64,
        ),
        name="attend_back",
    )(queries, key_rows, values, columns, key_marks, out, grad)


def fetch_codes(code_ids, embed_table):
    features = embed_table.shape[1]
    holder_count = lax.axis_size(("ty", "tx"))
    share_rows = embed_table.shape[0]
    flat_ids = code_ids.reshape(-1)
    row_count = flat_ids.shape[0]
    slot_count = 3 * row_count // (2 * holder_count)
    starts = jnp.arange(1, holder_count, dtype=jnp.int32) * share_rows
    holder = jnp.sum((flat_ids[:, None] >= starts[None, :]).astype(jnp.int32), axis=1)
    offsets = flat_ids - holder * share_rows
    belongs = holder[:, None] == jnp.arange(holder_count, dtype=jnp.int32)[None, :]
    place = jnp.arange(row_count, dtype=jnp.int32)
    before = (place[:, None] > place[None, :]).astype(jnp.bfloat16)
    ranks = matmul(before, belongs.astype(jnp.bfloat16))
    slot_rank = jnp.sum(jnp.where(belongs, ranks, 0.0), axis=1).astype(jnp.int32)
    slot_index = holder * slot_count + slot_rank
    requests = jnp.zeros((holder_count * slot_count,), jnp.int32)
    requests = requests.at[slot_index].set(offsets, mode="promise_in_bounds", unique_indices=True)
    requests = requests.reshape(holder_count, slot_count)
    asked = lax.all_to_all(requests, ("ty", "tx"), split_axis=0, concat_axis=0, tiled=True)
    fetched = embed_table.at[asked.reshape(-1)].get(mode="promise_in_bounds")
    fetched = fetched.reshape(holder_count, slot_count, features)
    returned = lax.all_to_all(fetched, ("ty", "tx"), split_axis=0, concat_axis=0, tiled=True)
    returned = returned.reshape(holder_count * slot_count, features)
    return returned.at[slot_index].get(mode="promise_in_bounds")


def to_grid(tiles):
    down, across = lax.axis_size("ty"), lax.axis_size("tx")
    parts = lax.all_to_all(tiles, ("ty", "tx"), split_axis=0, concat_axis=0, tiled=True)
    parts = parts.reshape((down, across) + tiles.shape[1:])
    parts = jnp.moveaxis(parts, 1, 2)
    return parts.reshape((down * tiles.shape[1], across * tiles.shape[2]) + tiles.shape[3:])


def to_tiles(grid):
    down, across = lax.axis_size("ty"), lax.axis_size("tx")
    rows, cols = grid.shape[0] // down, grid.shape[1] // across
    parts = grid.reshape((down, rows, across, cols) + grid.shape[2:])
    parts = jnp.moveaxis(parts, 2, 1).reshape((down * across, rows, cols) + grid.shape[2:])
    return lax.all_to_all(parts, ("ty", "tx"), split_axis=0, concat_axis=0, tiled=True)


def neighbours(rows_grid, marks_grid, direction):
    height, width = marks_grid.shape
    padded = jnp.pad(rows_grid, ((1, 1), (1, 1), (0, 0)))
    marks_pad = jnp.pad(marks_grid, ((1, 1), (1, 1)), constant_values=-1)
    taps = []
    for vertical in range(3):
        for lateral in range(3):
            down = vertical if direction > 0 else 2 - vertical
            right = lateral if direction > 0 else 2 - lateral
            inside = marks_pad[down : down + height, right : right + width] == marks_grid
            rows = padded[down : down + height, right : right + width]
            taps.append(jnp.where(inside[..., None], rows, 0).reshape(height * width, -1))
    return jnp.concatenate(taps, axis=1)


def gelu_parts(values):
    spread = jnp.exp(-0.5 * values * values)
    upto = 0.5 * (1.0 + lax.erf(values * 0.7071067811865476))
    return values * upto, upto + values * spread * 0.3989422804014327


def sum_shares(grad):
    shares = lax.psum_scatter(
        grad.astype(jnp.bfloat16), ("ty", "tx", "gr"), scatter_dimension=0, tiled=True
    )
    return lax.all_gather(shares, "gr", axis=0, tiled=True).astype(jnp.float32)


def on_device_grids(
    encoder_out,
    code_ids,
    segments,
    embed_table,
    recon_grad,
    qkv_weight,
    query_bias,
    value_bias,
    out_weight,
    out_bias,
    first_gain,
    first_shift,
    second_gain,
    second_shift,
    up_weight,
    up_bias,
    down_weight,
    down_bias,
    pixel_weight,
    pixel_bias,
):
    features = encoder_out.shape[-1]
    wide = jnp.float32
    marks_grid = to_grid(segments)
    cotangent_grid = to_grid(recon_grad)
    height, width = marks_grid.shape
    tokens = height * width
    codes_tile = fetch_codes(code_ids, embed_table).reshape(encoder_out.shape)
    start_rows = to_grid(codes_tile).reshape(tokens, features).astype(wide)
    query_marks, key_marks = mark_columns(marks_grid.reshape(tokens))

    cotangent = cotangent_grid.reshape(tokens, features)
    behind = neighbours(cotangent_grid, marks_grid, -1)
    pixel_flat = pixel_weight.reshape(features, 9 * features)
    final_grad = right_product(behind, pixel_flat)
    lower_grad = final_grad.astype(jnp.bfloat16)
    pixel_bias_grad = jnp.sum(cotangent.astype(wide), axis=0)
    down_bias_grad = jnp.sum(lower_grad.astype(wide), axis=0)
    hidden_grad = right_product(lower_grad, down_weight)

    normed, first_pull = jax.vjp(
        layer_norm, start_rows, first_gain.astype(wide), first_shift.astype(wide)
    )
    normed_low = normed.astype(jnp.bfloat16)
    projected = matmul(normed_low, qkv_weight)
    scale = HEAD_DIM**-0.5
    queries = (projected[:, :features] + query_bias.astype(wide)).astype(jnp.bfloat16)
    queries = queries * jnp.asarray(scale, jnp.bfloat16)
    key_rows = projected[:, features : 2 * features].astype(jnp.bfloat16)
    values = (projected[:, 2 * features :] + value_bias.astype(wide)).astype(jnp.bfloat16)
    attended, columns = attend(queries, key_rows, values, query_marks, key_marks)
    middle = start_rows + (matmul(attended, out_weight) + out_bias.astype(wide))
    normed_two, second_pull = jax.vjp(
        layer_norm, middle, second_gain.astype(wide), second_shift.astype(wide)
    )
    normed_two_low = normed_two.astype(jnp.bfloat16)
    hidden_pre = matmul(normed_two_low, up_weight) + up_bias.astype(wide)
    hidden_act, slope = gelu_parts(hidden_pre)
    hidden_low = hidden_act.astype(jnp.bfloat16)
    pre_grad = (hidden_grad * slope).astype(jnp.bfloat16)
    output_rows = middle + (matmul(hidden_low, down_weight) + down_bias.astype(wide))
    features_low = output_rows.astype(jnp.bfloat16)

    pixel_weight_grad = left_product(features_low, behind)
    down_weight_grad = left_product(hidden_low, lower_grad)
    up_weight_grad = left_product(normed_two_low, pre_grad)
    up_bias_grad = jnp.sum(pre_grad.astype(wide), axis=0)

    ahead = neighbours(features_low.reshape(height, width, features), marks_grid, 1)
    pixel_rows = jnp.swapaxes(pixel_weight, 0, 1).reshape(9 * features, features)
    recon_grid = (matmul(ahead, pixel_rows) + pixel_bias.astype(wide)).astype(jnp.bfloat16)
    recon_tiles = to_tiles(recon_grid.reshape(height, width, features))

    middle_part, second_gain_grad, second_shift_grad = second_pull(
        right_product(pre_grad, up_weight)
    )
    middle_grad = final_grad + middle_part
    branch_grad = middle_grad.astype(jnp.bfloat16)
    out_weight_grad = left_product(attended, branch_grad)
    out_bias_grad = jnp.sum(branch_grad.astype(wide), axis=0)
    attended_grad = right_product(branch_grad, out_weight).astype(jnp.bfloat16)
    query_grad, key_grad, value_grad = attend_back_grid(
        queries, key_rows, values, columns, key_marks, attended, attended_grad
    )
    projected_grad = jnp.concatenate([query_grad, key_grad, value_grad], axis=1)
    qkv_weight_grad = left_product(normed_low, projected_grad)
    query_bias_grad = jnp.sum(query_grad.astype(wide), axis=0)
    value_bias_grad = jnp.sum(value_grad.astype(wide), axis=0)
    start_part, first_gain_grad, first_shift_grad = first_pull(
        right_product(projected_grad, qkv_weight)
    )
    start_grad = middle_grad + start_part
    share = (start_grad - 2.0 * commit_weight * start_rows).astype(jnp.bfloat16)
    share_tiles = to_tiles(share.reshape(height, width, features))
    input_tiles = (
        share_tiles.astype(wide) + 2.0 * commit_weight * encoder_out.astype(wide)
    ).astype(jnp.bfloat16)

    vectors = [
        query_bias_grad,
        value_bias_grad,
        out_bias_grad,
        first_gain_grad,
        first_shift_grad,
        second_gain_grad,
        second_shift_grad,
        up_bias_grad,
        down_bias_grad,
        pixel_bias_grad,
    ]
    shards = lax.axis_size(("ty", "tx"))
    packed = jnp.concatenate([v.reshape(shards, -1) for v in vectors], axis=1).reshape(-1)
    packed = sum_shares(packed)
    sums = []
    at = 0
    for vector in vectors:
        size = vector.shape[0] // shards
        sums.append(packed[at : at + size])
        at += size
    (query_bias_sum, value_bias_sum, out_bias_sum, first_gain_sum, first_shift_sum) = sums[:5]
    (second_gain_sum, second_shift_sum, up_bias_sum, down_bias_sum, pixel_bias_sum) = sums[5:]
    return (
        recon_tiles,
        input_tiles,
        sum_shares(qkv_weight_grad),
        query_bias_sum,
        value_bias_sum,
        sum_shares(out_weight_grad),
        out_bias_sum,
        first_gain_sum,
        first_shift_sum,
        second_gain_sum,
        second_shift_sum,
        sum_shares(up_weight_grad),
        up_bias_sum,
        sum_shares(down_weight_grad),
        down_bias_sum,
        sum_shares(pixel_weight_grad).reshape(-1, 9, features),
        pixel_bias_sum,
    )


def solution(mesh):
    in_specs = (
        P("gr", "ty", "tx", None),
        P("gr", "ty", "tx"),
        P("gr", "ty", "tx"),
        P(("ty", "tx"), None),
        P("gr", "ty", "tx", None),
        P(),
        P(),
        P(),
        P(),
        P(),
        P(),
        P(),
        P(),
        P(),
        P(),
        P(),
        P(),
        P(),
        P(),
        P(),
    )
    out_specs = (
        P("gr", "ty", "tx", None),
        P("gr", "ty", "tx", None),
        P(("ty", "tx"), None),
        P(("ty", "tx")),
        P(("ty", "tx")),
        P(("ty", "tx"), None),
        P(("ty", "tx")),
        P(("ty", "tx")),
        P(("ty", "tx")),
        P(("ty", "tx")),
        P(("ty", "tx")),
        P(("ty", "tx"), None),
        P(("ty", "tx")),
        P(("ty", "tx"), None),
        P(("ty", "tx")),
        P(("ty", "tx"), None, None),
        P(("ty", "tx")),
    )
    def on_device(encoder_out, *rest):
        members = mesh.shape["ty"] * mesh.shape["tx"]
        whole_grids = encoder_out.shape[0] == members
        body = on_device_grids if whole_grids else on_device_bands
        return body(encoder_out, *rest)

    return jax.shard_map(
        on_device, mesh=mesh, in_specs=in_specs, out_specs=out_specs, check_vma=False
    )
```

```python
from functools import partial

import jax
import jax.numpy as jnp
from jax import lax
from jax.experimental import pallas as pl
from jax.experimental.pallas import tpu as pltpu
from jax.sharding import PartitionSpec as P

HEADS = 12
HEAD_DIM = 64


epsilon = 1e-06
commit_weight = 0.25


def with_halo(block, sides, width):
    for axis, dim in sides:
        count = lax.axis_size(axis)
        forward = [(i, i + 1) for i in range(count - 1)]
        backward = [(target, source) for source, target in forward]
        low = lax.ppermute(
            lax.slice_in_dim(block, block.shape[dim] - width, None, axis=dim), axis, forward
        )
        high = lax.ppermute(lax.slice_in_dim(block, 0, width, axis=dim), axis, backward)
        block = jnp.concatenate([low, block, high], axis=dim)
    return block


def layer_norm(values, gain, shift):
    center = values - jnp.mean(values, axis=-1, keepdims=True)
    spread = jnp.mean(center * center, axis=-1, keepdims=True)
    return center * lax.rsqrt(spread + epsilon) * gain + shift


def exact_gelu(values):
    return jax.nn.gelu(values, approximate=False)


def matmul(left_side, right_side):
    return jnp.dot(left_side, right_side, preferred_element_type=jnp.float32)


def left_product(left_side, right_side):
    return lax.dot_general(
        left_side, right_side, (((0,), (0,)), ((), ())), preferred_element_type=jnp.float32
    )


def right_product(left_side, right_side):
    return lax.dot_general(
        left_side, right_side, (((1,), (1,)), ((), ())), preferred_element_type=jnp.float32
    )


def pad_side(array, axis_index):
    widths = [(0, 0)] * array.ndim
    widths[axis_index] = (1, 1)
    return jnp.pad(array, widths)


def blocked(array, block_size):
    return array.reshape((array.shape[0] // block_size, block_size) + array.shape[1:])


def unblock(array):
    return array.reshape((-1,) + array.shape[2:])


def head_scores(queries, key_rows, marks_query, marks_key, head_count, score_scale):
    grid_count, query_rows, features = queries.shape
    query_heads = queries.reshape(grid_count, query_rows, head_count, features // head_count)
    key_heads = key_rows.reshape(grid_count, key_rows.shape[1], head_count, features // head_count)
    scores = (
        jnp.einsum("bqhd,bkhd->bhqk", query_heads, key_heads, preferred_element_type=jnp.float32)
        * score_scale
    )
    same_image = (marks_query[:, :, None] == marks_key[:, None, :])[:, None]
    return jnp.where(same_image, scores, -1000000000.0)


def attend_block(bundle, head_count, score_scale):
    queries, key_rows, values, marks_query, marks_key = bundle
    grid_count, query_rows, features = queries.shape
    scores = head_scores(queries, key_rows, marks_query, marks_key, head_count, score_scale)
    running_max = jnp.max(scores, axis=-1, keepdims=True)
    exponent = jnp.exp(scores - running_max)
    denominator = jnp.sum(exponent, axis=-1, keepdims=True)
    probability = (exponent / denominator).astype(jnp.bfloat16)
    value_heads = values.reshape(grid_count, values.shape[1], head_count, features // head_count)
    attended = jnp.einsum(
        "bhqk,bkhd->bqhd", probability, value_heads, preferred_element_type=jnp.float32
    )
    return (
        attended.reshape(grid_count, query_rows, features).astype(jnp.bfloat16),
        running_max + jnp.log(denominator),
    )


def attend_back(bundle, head_count, score_scale):
    queries, key_rows, values, marks_query, marks_key, log_total, out_grad = bundle
    grid_count, query_rows, features = queries.shape
    head_size = features // head_count
    scores = head_scores(queries, key_rows, marks_query, marks_key, head_count, score_scale)
    probability = jnp.exp(scores - log_total)
    query_heads = queries.reshape(grid_count, query_rows, head_count, head_size)
    key_heads = key_rows.reshape(grid_count, key_rows.shape[1], head_count, head_size)
    value_heads = values.reshape(grid_count, values.shape[1], head_count, head_size)
    grad_heads = out_grad.reshape(grid_count, query_rows, head_count, head_size)
    prob_grad = jnp.einsum(
        "bqhd,bkhd->bhqk", grad_heads, value_heads, preferred_element_type=jnp.float32
    )
    inner_sum = jnp.sum(probability * prob_grad, axis=-1, keepdims=True)
    score_grad = (probability * (prob_grad - inner_sum)).astype(jnp.bfloat16)
    query_grad = (
        jnp.einsum("bhqk,bkhd->bqhd", score_grad, key_heads, preferred_element_type=jnp.float32)
        * score_scale
    )
    key_grad = (
        jnp.einsum("bhqk,bqhd->bkhd", score_grad, query_heads, preferred_element_type=jnp.float32)
        * score_scale
    )
    value_grad = jnp.einsum(
        "bhqk,bqhd->bkhd",
        probability.astype(jnp.bfloat16),
        grad_heads,
        preferred_element_type=jnp.float32,
    )
    key_count = key_rows.shape[1]
    return (
        query_grad.reshape(grid_count, query_rows, features).astype(jnp.bfloat16),
        key_grad.reshape(grid_count, key_count, features),
        value_grad.reshape(grid_count, key_count, features),
    )


def on_device_bands(
    encoder_out,
    code_ids,
    segments,
    embed_table,
    recon_grad,
    qkv_weight,
    query_bias,
    value_bias,
    out_weight,
    out_bias,
    first_gain,
    first_shift,
    second_gain,
    second_shift,
    up_weight,
    up_bias,
    down_weight,
    down_bias,
    pixel_weight,
    pixel_bias,
):
    features = encoder_out.shape[-1]
    head_count = HEADS
    score_scale = float(HEAD_DIM) ** (-0.5)
    holder_count = lax.axis_size(("ty", "tx"))
    share_rows = embed_table.shape[0]
    flat_ids = code_ids.reshape(-1)
    row_count = flat_ids.shape[0]
    slot_count = 3 * row_count // (2 * holder_count)
    holder = flat_ids // share_rows
    offsets = flat_ids - holder * share_rows
    belongs = (holder[:, None] == jnp.arange(holder_count, dtype=jnp.int32)[None, :]).astype(
        jnp.int32
    )
    slot_rank = jnp.sum((jnp.cumsum(belongs, axis=0) - 1) * belongs, axis=1)
    slot_index = holder * slot_count + slot_rank
    requests = jnp.zeros((holder_count * slot_count,), jnp.int32).at[slot_index].set(offsets)
    requests = requests.reshape(holder_count, slot_count)
    fetched = jnp.take(
        embed_table,
        lax.all_to_all(requests, ("ty", "tx"), split_axis=0, concat_axis=0, tiled=True),
        axis=0,
    )
    returned = lax.all_to_all(fetched, ("ty", "tx"), split_axis=0, concat_axis=0, tiled=True)
    codes = returned.reshape(holder_count * slot_count, features)[slot_index].reshape(
        encoder_out.shape
    )
    marks_tile = (segments + 1).astype(jnp.bfloat16)
    arrived = (
        lax.all_to_all(encoder_out, "tx", split_axis=0, concat_axis=2, tiled=True),
        lax.all_to_all(codes, "tx", split_axis=0, concat_axis=2, tiled=True),
        lax.all_to_all(recon_grad, "tx", split_axis=0, concat_axis=2, tiled=True),
        lax.all_to_all(marks_tile, "tx", split_axis=0, concat_axis=2, tiled=True),
    )
    inputs_band, codes_band, cotangent_band, marks_band = arrived
    grid_count, band_rows, band_cols = marks_band.shape
    tokens = band_rows * band_cols
    all_rows = grid_count * tokens
    block_size = max(1, 512 // tokens)
    while grid_count % block_size:
        block_size -= 1
    start_rows = codes_band.reshape(all_rows, features).astype(jnp.float32)
    marks_query = marks_band.reshape(grid_count, tokens)
    normed, first_pull = jax.vjp(
        layer_norm, start_rows, first_gain.astype(jnp.float32), first_shift.astype(jnp.float32)
    )
    normed_low = normed.astype(jnp.bfloat16)
    projected = matmul(normed_low, qkv_weight)
    queries = (
        (projected[:, :features] + query_bias.astype(jnp.float32))
        .astype(jnp.bfloat16)
        .reshape(grid_count, tokens, features)
    )
    key_rows = (
        projected[:, features : 2 * features]
        .astype(jnp.bfloat16)
        .reshape(grid_count, tokens, features)
    )
    values = (
        (projected[:, 2 * features :] + value_bias.astype(jnp.float32))
        .astype(jnp.bfloat16)
        .reshape(grid_count, tokens, features)
    )
    bundle = (key_rows, values, marks_query)
    keys_all = lax.all_gather(bundle[0], "ty", axis=1, tiled=True)
    values_all = lax.all_gather(bundle[1], "ty", axis=1, tiled=True)
    marks_key = lax.all_gather(bundle[2], "ty", axis=1, tiled=True)
    attended_blocks, log_total = lax.map(
        partial(attend_block, head_count=head_count, score_scale=score_scale),
        (
            blocked(queries, block_size),
            blocked(keys_all, block_size),
            blocked(values_all, block_size),
            blocked(marks_query, block_size),
            blocked(marks_key, block_size),
        ),
    )
    attended = unblock(attended_blocks).reshape(all_rows, features)
    branch = matmul(attended, out_weight) + out_bias.astype(jnp.float32)
    middle = start_rows + branch
    normed_two, second_pull = jax.vjp(
        layer_norm, middle, second_gain.astype(jnp.float32), second_shift.astype(jnp.float32)
    )
    normed_two_low = normed_two.astype(jnp.bfloat16)
    hidden_pre = matmul(normed_two_low, up_weight) + up_bias.astype(jnp.float32)
    hidden_act, gelu_pull = jax.vjp(exact_gelu, hidden_pre)
    hidden_low = hidden_act.astype(jnp.bfloat16)
    output_rows = middle + (matmul(hidden_low, down_weight) + down_bias.astype(jnp.float32))
    features_low = output_rows.astype(jnp.bfloat16).reshape(
        grid_count, band_rows, band_cols, features
    )
    bundle = (features_low, marks_band, cotangent_band)
    grown = (
        with_halo(bundle[0], (("ty", 1),), 1),
        with_halo(bundle[1], (("ty", 1),), 1),
        with_halo(bundle[2], (("ty", 1),), 1),
    )
    features_pad, marks_pad, cotangent_pad = tuple((pad_side(member, 2) for member in grown))
    ahead_list = []
    behind_list = []
    for vertical in range(3):
        for lateral in range(3):
            inside = (
                marks_pad[:, vertical : vertical + band_rows, lateral : lateral + band_cols]
                == marks_band
            )
            ahead_list.append(
                jnp.where(
                    inside[..., None],
                    features_pad[:, vertical : vertical + band_rows, lateral : lateral + band_cols],
                    0,
                )
            )
            mirror_row = 2 - vertical
            mirror_col = 2 - lateral
            facing = (
                marks_pad[
                    :, mirror_row : mirror_row + band_rows, mirror_col : mirror_col + band_cols
                ]
                == marks_band
            )
            behind_list.append(
                jnp.where(
                    facing[..., None],
                    cotangent_pad[
                        :, mirror_row : mirror_row + band_rows, mirror_col : mirror_col + band_cols
                    ],
                    0,
                )
            )
    ahead = jnp.stack(ahead_list, axis=3)
    behind = jnp.stack(behind_list, axis=3)
    recon_band = jnp.einsum(
        "nhwkd,dkp->nhwp", ahead, pixel_weight, preferred_element_type=jnp.float32
    ) + pixel_bias.astype(jnp.float32)
    pixel_weight_grad = jnp.einsum(
        "nhwkd,nhwp->dkp", ahead, cotangent_band, preferred_element_type=jnp.float32
    )
    pixel_bias_grad = jnp.sum(cotangent_band.astype(jnp.float32), axis=(0, 1, 2))
    final_grad = jnp.einsum(
        "nhwkp,dkp->nhwd", behind, pixel_weight, preferred_element_type=jnp.float32
    ).reshape(all_rows, features)
    lower_grad = final_grad.astype(jnp.bfloat16)
    down_weight_grad = left_product(hidden_low, lower_grad)
    down_bias_grad = jnp.sum(lower_grad.astype(jnp.float32), axis=0)
    pre_grad = gelu_pull(right_product(lower_grad, down_weight))[0].astype(jnp.bfloat16)
    up_weight_grad = left_product(normed_two_low, pre_grad)
    up_bias_grad = jnp.sum(pre_grad.astype(jnp.float32), axis=0)
    middle_part, second_gain_grad, second_shift_grad = second_pull(
        right_product(pre_grad, up_weight)
    )
    middle_grad = final_grad + middle_part
    branch_grad = middle_grad.astype(jnp.bfloat16)
    out_weight_grad = left_product(attended, branch_grad)
    out_bias_grad = jnp.sum(branch_grad.astype(jnp.float32), axis=0)
    attended_grad = (
        right_product(branch_grad, out_weight)
        .astype(jnp.bfloat16)
        .reshape(grid_count, tokens, features)
    )
    query_blocks, key_blocks, value_blocks = lax.map(
        partial(attend_back, head_count=head_count, score_scale=score_scale),
        (
            blocked(queries, block_size),
            blocked(keys_all, block_size),
            blocked(values_all, block_size),
            blocked(marks_query, block_size),
            blocked(marks_key, block_size),
            log_total,
            blocked(attended_grad, block_size),
        ),
    )
    query_grad = unblock(query_blocks)
    bundle = (unblock(key_blocks), unblock(value_blocks))
    key_sum = lax.psum_scatter(
        bundle[0].astype(jnp.bfloat16), "ty", scatter_dimension=1, tiled=True
    )
    value_sum = lax.psum_scatter(
        bundle[1].astype(jnp.bfloat16), "ty", scatter_dimension=1, tiled=True
    )
    projected_grad = jnp.concatenate([query_grad, key_sum, value_sum], axis=-1).reshape(
        all_rows, 3 * features
    )
    qkv_weight_grad = left_product(normed_low, projected_grad)
    query_bias_grad = jnp.sum(query_grad.astype(jnp.float32), axis=(0, 1))
    value_bias_grad = jnp.sum(value_sum.astype(jnp.float32), axis=(0, 1))
    start_part, first_gain_grad, first_shift_grad = first_pull(
        right_product(projected_grad, qkv_weight)
    )
    start_grad = middle_grad + start_part
    inputs_rows = inputs_band.reshape(all_rows, features).astype(jnp.float32)
    input_band = (start_grad + 2.0 * commit_weight * (inputs_rows - start_rows)).astype(
        jnp.bfloat16
    )
    bundle = (
        recon_band.astype(jnp.bfloat16),
        input_band.reshape(grid_count, band_rows, band_cols, features),
    )
    recon_tiles = lax.all_to_all(bundle[0], "tx", split_axis=2, concat_axis=0, tiled=True)
    input_tiles = lax.all_to_all(bundle[1], "tx", split_axis=2, concat_axis=0, tiled=True)
    local_grads = (
        qkv_weight_grad,
        query_bias_grad,
        value_bias_grad,
        out_weight_grad,
        out_bias_grad,
        first_gain_grad,
        first_shift_grad,
        second_gain_grad,
        second_shift_grad,
        up_weight_grad,
        up_bias_grad,
        down_weight_grad,
        down_bias_grad,
        pixel_weight_grad,
        pixel_bias_grad,
    )
    tile_shares = (
        lax.psum_scatter(
            local_grads[0].astype(jnp.bfloat16), ("ty", "tx"), scatter_dimension=0, tiled=True
        ).astype(jnp.float32),
        lax.psum_scatter(
            local_grads[1].astype(jnp.bfloat16), ("ty", "tx"), scatter_dimension=0, tiled=True
        ).astype(jnp.float32),
        lax.psum_scatter(
            local_grads[2].astype(jnp.bfloat16), ("ty", "tx"), scatter_dimension=0, tiled=True
        ).astype(jnp.float32),
        lax.psum_scatter(
            local_grads[3].astype(jnp.bfloat16), ("ty", "tx"), scatter_dimension=0, tiled=True
        ).astype(jnp.float32),
        lax.psum_scatter(
            local_grads[4].astype(jnp.bfloat16), ("ty", "tx"), scatter_dimension=0, tiled=True
        ).astype(jnp.float32),
        lax.psum_scatter(
            local_grads[5].astype(jnp.bfloat16), ("ty", "tx"), scatter_dimension=0, tiled=True
        ).astype(jnp.float32),
        lax.psum_scatter(
            local_grads[6].astype(jnp.bfloat16), ("ty", "tx"), scatter_dimension=0, tiled=True
        ).astype(jnp.float32),
        lax.psum_scatter(
            local_grads[7].astype(jnp.bfloat16), ("ty", "tx"), scatter_dimension=0, tiled=True
        ).astype(jnp.float32),
        lax.psum_scatter(
            local_grads[8].astype(jnp.bfloat16), ("ty", "tx"), scatter_dimension=0, tiled=True
        ).astype(jnp.float32),
        lax.psum_scatter(
            local_grads[9].astype(jnp.bfloat16), ("ty", "tx"), scatter_dimension=0, tiled=True
        ).astype(jnp.float32),
        lax.psum_scatter(
            local_grads[10].astype(jnp.bfloat16), ("ty", "tx"), scatter_dimension=0, tiled=True
        ).astype(jnp.float32),
        lax.psum_scatter(
            local_grads[11].astype(jnp.bfloat16), ("ty", "tx"), scatter_dimension=0, tiled=True
        ).astype(jnp.float32),
        lax.psum_scatter(
            local_grads[12].astype(jnp.bfloat16), ("ty", "tx"), scatter_dimension=0, tiled=True
        ).astype(jnp.float32),
        lax.psum_scatter(
            local_grads[13].astype(jnp.bfloat16), ("ty", "tx"), scatter_dimension=0, tiled=True
        ).astype(jnp.float32),
        lax.psum_scatter(
            local_grads[14].astype(jnp.bfloat16), ("ty", "tx"), scatter_dimension=0, tiled=True
        ).astype(jnp.float32),
    )
    summed = (
        lax.psum(tile_shares[0].astype(jnp.bfloat16), "gr").astype(jnp.float32),
        lax.psum(tile_shares[1].astype(jnp.bfloat16), "gr").astype(jnp.float32),
        lax.psum(tile_shares[2].astype(jnp.bfloat16), "gr").astype(jnp.float32),
        lax.psum(tile_shares[3].astype(jnp.bfloat16), "gr").astype(jnp.float32),
        lax.psum(tile_shares[4].astype(jnp.bfloat16), "gr").astype(jnp.float32),
        lax.psum(tile_shares[5].astype(jnp.bfloat16), "gr").astype(jnp.float32),
        lax.psum(tile_shares[6].astype(jnp.bfloat16), "gr").astype(jnp.float32),
        lax.psum(tile_shares[7].astype(jnp.bfloat16), "gr").astype(jnp.float32),
        lax.psum(tile_shares[8].astype(jnp.bfloat16), "gr").astype(jnp.float32),
        lax.psum(tile_shares[9].astype(jnp.bfloat16), "gr").astype(jnp.float32),
        lax.psum(tile_shares[10].astype(jnp.bfloat16), "gr").astype(jnp.float32),
        lax.psum(tile_shares[11].astype(jnp.bfloat16), "gr").astype(jnp.float32),
        lax.psum(tile_shares[12].astype(jnp.bfloat16), "gr").astype(jnp.float32),
        lax.psum(tile_shares[13].astype(jnp.bfloat16), "gr").astype(jnp.float32),
        lax.psum(tile_shares[14].astype(jnp.bfloat16), "gr").astype(jnp.float32),
    )
    return (
        recon_tiles,
        input_tiles,
        summed[0],
        summed[1],
        summed[2],
        summed[3],
        summed[4],
        summed[5],
        summed[6],
        summed[7],
        summed[8],
        summed[9],
        summed[10],
        summed[11],
        summed[12],
        summed[13],
        summed[14],
    )


far = float(2.0**30)


def nt(left_side, right_side):
    return lax.dot_general(
        left_side, right_side, (((1,), (1,)), ((), ())), preferred_element_type=jnp.float32
    )


def nn(left_side, right_side):
    return lax.dot_general(
        left_side, right_side, (((1,), (0,)), ((), ())), preferred_element_type=jnp.float32
    )


def mark_columns(marks):
    lane = lax.broadcasted_iota(jnp.int32, (1, 128), 1) % 64
    hot = marks[:, None] == lane
    query_side = jnp.where(hot, 1.0, 0.0)
    key_side = jnp.where((lane < 3) & ~hot, -far, 0.0)
    return query_side.astype(jnp.bfloat16), key_side.astype(jnp.bfloat16)


def attend_kernel(q_ref, k_ref, v_ref, qa_ref, ka_ref, o_ref, col_ref):
    lane = lax.broadcasted_iota(jnp.int32, (1, 128), 1)
    low = lane < 64
    local = lane % 64
    one = jnp.ones((), jnp.bfloat16)
    queries, key_rows, values = q_ref[...], k_ref[...], v_ref[...]
    query_marks, key_marks = qa_ref[...], ka_ref[...]
    outs = []
    logs = []
    for head in range(2):
        own = low if head == 0 else ~low
        scores = nt(jnp.where(own, queries, query_marks), jnp.where(own, key_rows, key_marks))
        top = jnp.max(scores, axis=1, keepdims=True)
        weights = jnp.exp(scores - top).astype(jnp.bfloat16)
        sums = nn(weights, jnp.where(own, values, one))
        outs.append(sums / pltpu.roll(sums, 64, 1))
        logs.append(top + jnp.log(sums))
    o_ref[...] = jnp.where(low, outs[0], outs[1]).astype(jnp.bfloat16)
    minus = -jnp.where(low, logs[1], logs[0])
    first = minus.astype(jnp.bfloat16).astype(jnp.float32)
    second = (minus - first).astype(jnp.bfloat16).astype(jnp.float32)
    third = minus - first - second
    columns = jnp.where(
        local == 3,
        first,
        jnp.where(local == 4, second, jnp.where(local == 5, third, query_marks.astype(jnp.float32))),
    )
    col_ref[...] = columns.astype(jnp.bfloat16)


def attend(queries, key_rows, values, query_marks, key_marks):
    tokens, features = queries.shape
    pair = pl.BlockSpec((tokens, 128), lambda i: (0, i))
    shared = pl.BlockSpec((tokens, 128), lambda i: (0, 0))
    shape = jax.ShapeDtypeStruct((tokens, features), jnp.bfloat16)
    return pl.pallas_call(
        attend_kernel,
        grid=(features // 128,),
        in_specs=[pair, pair, pair, shared, shared],
        out_specs=[pair, pair],
        out_shape=[shape, shape],
        compiler_params=pltpu.CompilerParams(vmem_limit_bytes=48 * 2**20),
        cost_estimate=pl.CostEstimate(
            flops=16 * tokens * tokens * features,
            bytes_accessed=10 * tokens * features,
            transcendentals=tokens * tokens * features // 64,
        ),
        name="attend",
    )(queries, key_rows, values, query_marks, key_marks)


def attend_back_kernel(
    q_ref, k_ref, v_ref, col_ref, ka_ref, o_ref, g_ref, dq_ref, dk_ref, dv_ref, k_sum, v_sum, *, step
):
    lane = lax.broadcasted_iota(jnp.int32, (1, 128), 1)
    low = lane < 64
    local = lane % 64
    zero = jnp.zeros((), jnp.bfloat16)
    one = jnp.ones((), jnp.bfloat16)
    key_rows, values = k_ref[...], v_ref[...]
    tokens = key_rows.shape[0]
    key_columns = jnp.where((local >= 3) & (local < 6), one, ka_ref[...])
    value_columns = jnp.where(local < 2, one, zero)
    keys_of = [jnp.where(low, key_rows, key_columns), jnp.where(low, key_columns, key_rows)]
    values_of = [jnp.where(low, values, value_columns), jnp.where(low, value_columns, values)]
    keys_across = key_rows.T
    upper = lax.broadcasted_iota(jnp.int32, (128, 1), 0) < 64
    k_sum[...] = jnp.zeros_like(k_sum)
    v_sum[...] = jnp.zeros_like(v_sum)

    def one_block(i, _):
        rows = pl.ds(pl.multiple_of(i * step, step), step)
        queries, columns = q_ref[rows, :], col_ref[rows, :]
        grad, out = g_ref[rows, :], o_ref[rows, :]
        both = grad.astype(jnp.float32) * out.astype(jnp.float32)
        of_low = -jnp.sum(jnp.where(low, both, 0.0), axis=1, keepdims=True)
        of_high = -jnp.sum(jnp.where(low, 0.0, both), axis=1, keepdims=True)
        inner = jnp.where(low, of_high, of_low)
        first = inner.astype(jnp.bfloat16).astype(jnp.float32)
        grad_columns = jnp.where(
            local == 0, first, jnp.where(local == 1, inner - first, 0.0)
        ).astype(jnp.bfloat16)
        query_parts, key_parts, value_parts = [], [], []
        for head in range(2):
            own = low if head == 0 else ~low
            weights = jnp.exp(nt(keys_of[head], jnp.where(own, queries, columns)))
            change = nt(values_of[head], jnp.where(own, grad, grad_columns))
            score_grad = (weights * change).astype(jnp.bfloat16)
            value_parts.append(nn(weights.astype(jnp.bfloat16), grad))
            key_parts.append(nn(score_grad, queries))
            query_parts.append(nn(keys_across, score_grad))
        k_sum[...] += jnp.where(low, key_parts[0], key_parts[1])
        v_sum[...] += jnp.where(low, value_parts[0], value_parts[1])
        query_grad = jnp.where(upper, query_parts[0], query_parts[1]).T
        dq_ref[rows, :] = (query_grad * HEAD_DIM**-0.5).astype(jnp.bfloat16)
        return 0

    lax.fori_loop(0, tokens // step, one_block, 0)
    dk_ref[...] = k_sum[...].astype(jnp.bfloat16)
    dv_ref[...] = v_sum[...].astype(jnp.bfloat16)


def attend_back_grid(queries, key_rows, values, columns, key_marks, out, grad):
    tokens, features = queries.shape
    pair = pl.BlockSpec((tokens, 128), lambda i: (0, i))
    shared = pl.BlockSpec((tokens, 128), lambda i: (0, 0))
    shape = jax.ShapeDtypeStruct((tokens, features), jnp.bfloat16)
    return pl.pallas_call(
        partial(attend_back_kernel, step=min(512, tokens)),
        grid=(features // 128,),
        in_specs=[pair, pair, pair, pair, shared, pair, pair],
        out_specs=[pair, pair, pair],
        out_shape=[shape, shape, shape],
        scratch_shapes=[pltpu.VMEM((tokens, 128), jnp.float32)] * 2,
        compiler_params=pltpu.CompilerParams(vmem_limit_bytes=48 * 2**20),
        cost_estimate=pl.CostEstimate(
            flops=24 * tokens * tokens * features,
            bytes_accessed=18 * tokens * features,
            transcendentals=tokens * tokens * features // 64,
        ),
        name="attend_back",
    )(queries, key_rows, values, columns, key_marks, out, grad)


def fetch_codes(code_ids, embed_table, first):
    features = embed_table.shape[1]
    holder_count = lax.axis_size(("ty", "tx"))
    share_rows = embed_table.shape[0]
    flat_ids = code_ids.reshape(-1)
    row_count = flat_ids.shape[0]
    slot_count = 3 * row_count // (2 * holder_count)
    starts = jnp.arange(1, holder_count, dtype=jnp.int32) * share_rows
    holder = jnp.sum((flat_ids[:, None] >= starts[None, :]).astype(jnp.int32), axis=1)
    offsets = flat_ids - holder * share_rows
    belongs = holder[:, None] == jnp.arange(holder_count, dtype=jnp.int32)[None, :]
    place = jnp.arange(row_count, dtype=jnp.int32)
    before = (place[:, None] > place[None, :]).astype(jnp.bfloat16)
    ranks = matmul(before, belongs.astype(jnp.bfloat16))
    slot_rank = jnp.sum(jnp.where(belongs, ranks, 0.0), axis=1).astype(jnp.int32)
    slot_index = holder * slot_count + slot_rank
    requests = jnp.zeros((holder_count * slot_count,), jnp.int32)
    requests = requests.at[slot_index].set(offsets, mode="promise_in_bounds", unique_indices=True)
    requests = requests.reshape(holder_count, slot_count)
    asked = lax.all_to_all(requests, ("ty", "tx"), split_axis=0, concat_axis=0, tiled=True)
    fetched = embed_table.at[asked.reshape(-1)].get(mode="promise_in_bounds")
    fetched, _ = lax.optimization_barrier((fetched, first))
    fetched = fetched.reshape(holder_count, slot_count, features)
    returned = lax.all_to_all(fetched, ("ty", "tx"), split_axis=0, concat_axis=0, tiled=True)
    returned = returned.reshape(holder_count * slot_count, features)
    return returned.at[slot_index].get(mode="promise_in_bounds")


def to_grid(tiles):
    down, across = lax.axis_size("ty"), lax.axis_size("tx")
    parts = lax.all_to_all(tiles, ("ty", "tx"), split_axis=0, concat_axis=0, tiled=True)
    parts = parts.reshape((down, across) + tiles.shape[1:])
    parts = jnp.moveaxis(parts, 1, 2)
    return parts.reshape((down * tiles.shape[1], across * tiles.shape[2]) + tiles.shape[3:])


def to_tiles(grid):
    down, across = lax.axis_size("ty"), lax.axis_size("tx")
    rows, cols = grid.shape[0] // down, grid.shape[1] // across
    parts = grid.reshape((down, rows, across, cols) + grid.shape[2:])
    parts = jnp.moveaxis(parts, 2, 1).reshape((down * across, rows, cols) + grid.shape[2:])
    return lax.all_to_all(parts, ("ty", "tx"), split_axis=0, concat_axis=0, tiled=True)


def conv_kernel(rows_ref, mask_ref, weight_ref, bias_ref, *refs, width, sign):
    if sign > 0:
        out_ref, shifted, total = refs
    else:
        out_ref, low_ref, taps_ref, shifted, total = refs
    tap = pl.program_id(0)
    tokens, features = rows_ref.shape

    @pl.when(tap == 0)
    def _():
        total[...] = jnp.zeros_like(total)
        rows = rows_ref[...]
        for j in range(3):
            moved = rows
            if j != 1:
                moved = pltpu.roll(rows.astype(jnp.float32), (1 - j) % tokens, 0)
            shifted[j, 0:width, :] = jnp.zeros((width, features), jnp.bfloat16)
            shifted[j, width + tokens :, :] = jnp.zeros((width, features), jnp.bfloat16)
            shifted[j, width : width + tokens, :] = moved.astype(jnp.bfloat16)

    down, right = tap // 3, tap % 3
    if sign < 0:
        down, right = 2 - down, 2 - right
    step = tokens // 4
    for i in range(4):
        rows = slice(i * step, (i + 1) * step)
        first = pl.multiple_of(down * width + i * step, width)
        mask = jnp.concatenate([mask_ref[0, rows, :]] * (features // 128), axis=1)
        taken = shifted[right, pl.ds(first, step), :] * mask
        if sign < 0:
            taps_ref[rows, :] = taken
            total[rows, :] += nt(taken, weight_ref[0])
        else:
            total[rows, :] += nn(taken, weight_ref[0])

    @pl.when(tap == 8)
    def _():
        if sign > 0:
            out_ref[...] = (total[...] + bias_ref[...].astype(jnp.float32)).astype(jnp.bfloat16)
        else:
            out_ref[...] = total[...]
            low_ref[...] = total[...].astype(jnp.bfloat16)


def conv(rows, masks, weight, bias, width, sign):
    tokens, features = rows.shape

    def whole(shape):
        return pl.BlockSpec(shape, lambda k: (0, 0))

    low = jax.ShapeDtypeStruct((tokens, features), jnp.bfloat16)
    out_shape, out_specs = low, whole((tokens, features))
    if sign < 0:
        taps = jax.ShapeDtypeStruct((tokens, 9 * features), jnp.bfloat16)
        out_shape = [jax.ShapeDtypeStruct((tokens, features), jnp.float32), low, taps]
        out_specs = [out_specs, out_specs, pl.BlockSpec((tokens, features), lambda k: (0, k))]
    tap_of = (lambda k: (k, 0, 0)) if sign > 0 else (lambda k: (8 - k, 0, 0))
    return pl.pallas_call(
        partial(conv_kernel, width=width, sign=sign),
        grid=(9,),
        in_specs=[
            whole((tokens, features)),
            pl.BlockSpec((1, tokens, 128), tap_of),
            pl.BlockSpec((1, features, features), lambda k: (k, 0, 0)),
            whole((1, features)),
        ],
        out_specs=out_specs,
        out_shape=out_shape,
        scratch_shapes=[
            pltpu.VMEM((3, tokens + 2 * width, features), jnp.bfloat16),
            pltpu.VMEM((tokens, features), jnp.float32),
        ],
        compiler_params=pltpu.CompilerParams(vmem_limit_bytes=48 * 2**20),
        cost_estimate=pl.CostEstimate(
            flops=18 * tokens * features * features,
            bytes_accessed=18 * features * features + 4 * tokens * features,
            transcendentals=0,
        ),
        name="conv",
    )(rows, masks, weight, bias)


def tap_masks(marks_grid):
    height, width = marks_grid.shape
    padded = jnp.pad(marks_grid, ((1, 1), (1, 1)), constant_values=-1)
    masks = jnp.stack(
        [
            (padded[a : a + height, b : b + width] == marks_grid).reshape(height * width)
            for a in range(3)
            for b in range(3)
        ]
    ).astype(jnp.bfloat16)
    return jnp.broadcast_to(masks[:, :, None], (9, height * width, 128))


def gelu_parts(values):
    spread = jnp.exp(-0.5 * values * values)
    upto = 0.5 * (1.0 + lax.erf(values * 0.7071067811865476))
    return values * upto, upto + values * spread * 0.3989422804014327


def sum_kernel(*refs, layout, count, lead):
    ins = refs[: max(item[0] for item in layout) + 1]
    out = refs[len(ins)]
    (own, got0, got1, got2, got3, got4, whole) = refs[len(ins) + 1 : len(ins) + 8]
    (own_sem, s0, r0, s1, r1, s2, r2, s3, r3, s4, r4, s5, r5, s6, r6, out_sem) = refs[len(ins) + 8 :]
    gr, ty, tx = lax.axis_index("gr"), lax.axis_index("ty"), lax.axis_index("tx")
    x, core, half, par = gr // 2, gr % 2, tx // 2, tx % 2
    mate = (2 * x + 1 - core, ty, tx)
    over_x = (2 * (1 - x) + core, ty, tx)
    over_y = (gr, 1 - ty, tx)
    near = (gr, ty, half * 2 + (1 - par))
    away = (gr, ty, (1 - half) * 2 + par)
    barrier = pltpu.get_barrier_semaphore()
    for device in (mate, over_x, over_y, near, away):
        pl.semaphore_signal(barrier, inc=1, device_id=device, device_id_type=pl.DeviceIdType.MESH)
    pl.semaphore_wait(barrier, 5)
    width = own.shape[-1]
    own_columns = pl.ds(pl.multiple_of(core * width, 128), width)

    def part(block, which):
        source, prefix, column = layout[block]
        columns = pl.ds(pl.multiple_of(column + which * width, 128), width)
        if prefix is None:
            return ins[source].at[:, :, :, :, :, columns]
        return ins[source].at[:, :, :, prefix, :, :, columns]

    def put(source, target, sent, received, device):
        return pltpu.make_async_remote_copy(
            src_ref=source,
            dst_ref=target,
            send_sem=sent,
            recv_sem=received,
            device_id=device,
            device_id_type=pl.DeviceIdType.MESH,
        )

    for block in range(2 * count):
        put(part(block, 1 - core), got0.at[block], s0.at[block], r0.at[block], mate).start()
        pltpu.make_async_copy(part(block, core), own.at[block], own_sem.at[block]).start()

    def level0(b):
        return put(got0.at[b], got0.at[b], s0.at[b], r0.at[b], mate)

    def level1x(c):
        return put(own.at[2 * c, :, :, :, 1 - x], got1.at[c, 0], s1.at[c, 0], r1.at[c, 0], over_x)

    def level1y(c):
        return put(own.at[2 * c + 1, 1 - ty], got1.at[c, 1], s1.at[c, 1], r1.at[c, 1], over_y)

    def level2y(c):
        return put(got1.at[c, 0, 1 - ty], got2.at[c, 0], s2.at[c, 0], r2.at[c, 0], over_y)

    def level2x(c):
        return put(got1.at[c, 1, :, :, 1 - x], got2.at[c, 1], s2.at[c, 1], r2.at[c, 1], over_x)

    def level3(c):
        return put(got2.at[c, :, :, 1 - par], got3.at[c], s3.at[c], r3.at[c], near)

    def level4(c):
        return put(got3.at[c, :, 1 - half], got4.at[c], s4.at[c], r4.at[c], away)

    def level5(c):
        place = whole.at[pl.ds(2 * c, 2), x, :, own_columns]
        return put(place, place, s5.at[c], r5.at[c], over_x)

    def level6(c):
        place = whole.at[pl.ds(2 * c, 2), :, :, own_columns]
        return put(place, place, s6.at[c], r6.at[c], mate)

    def stage1(c):
        for b in (2 * c, 2 * c + 1):
            level0(b).wait_recv()
            pltpu.make_async_copy(own.at[b], own.at[b], own_sem.at[b]).wait()

            def add(i, _):
                y, h, p = i // 4, (i // 2) % 2, i % 2
                own[b, y, h, p] = own[b, y, h, p] + got0[b, y, h, p]
                return 0

            lax.fori_loop(0, 8, add, 0)
        level1x(c).start()
        level1y(c).start()

    def stage2(c):
        level1x(c).wait_recv()
        got1[c, 0] = got1[c, 0] + own[2 * c, :, :, :, x]
        level2y(c).start()
        level1y(c).wait_recv()
        got1[c, 1] = got1[c, 1] + own[2 * c + 1, ty]
        level2x(c).start()

    def stage3(c):
        level2y(c).wait_recv()
        level2x(c).wait_recv()
        got2[c, 0] = got2[c, 0] + got1[c, 0, ty]
        got2[c, 1] = got2[c, 1] + got1[c, 1, :, :, x]
        level3(c).start()

    def stage4(c):
        level3(c).wait_recv()
        got3[c] = got3[c] + got2[c, :, :, par]
        level4(c).start()

    def stage5(c):
        level4(c).wait_recv()
        whole[pl.ds(2 * c, 2), x, :, own_columns] = got4[c] + got3[c, :, half]
        level5(c).start()

    def stage6(c):
        level5(c).wait_recv()
        level6(c).start()

    stages = (stage1, stage2, stage3, stage4, stage5, stage6)

    def turn(t, _):
        for stage, behind in zip(stages, lead):
            c = t - behind
            pl.when((c >= 0) & (c < count))(partial(stage, c))
        return 0

    lax.fori_loop(0, count + lead[-1], turn, 0)

    def finish(c, _):
        level6(c).wait_recv()
        level0(2 * c).wait_send()
        level0(2 * c + 1).wait_send()
        for level in (level1x, level1y, level2x, level2y, level3, level4, level5, level6):
            level(c).wait_send()
        return 0

    lax.fori_loop(0, count, finish, 0)
    done = pltpu.make_async_copy(whole, out, out_sem)
    done.start()
    done.wait()


def sum_blocks(ins, layout, collective_id):
    blocks = len(layout)
    count = blocks // 2
    rows, width = ins[0].shape[-2], 384
    dma = pltpu.SemaphoreType.DMA
    half_block = pltpu.VMEM((blocks, 2, 2, 2, 2, rows, width), jnp.bfloat16)
    return pl.pallas_call(
        partial(sum_kernel, layout=layout, count=count, lead=(0, 2, 4, 6, 8, 10)),
        in_specs=[pl.BlockSpec(memory_space=pl.ANY)] * len(ins),
        out_specs=pl.BlockSpec(memory_space=pl.ANY),
        out_shape=jax.ShapeDtypeStruct((blocks, 2, rows, 2 * width), jnp.bfloat16),
        scratch_shapes=[
            half_block,
            half_block,
            pltpu.VMEM((count, 2, 2, 2, 2, rows, width), jnp.bfloat16),
            pltpu.VMEM((count, 2, 2, 2, rows, width), jnp.bfloat16),
            pltpu.VMEM((count, 2, 2, rows, width), jnp.bfloat16),
            pltpu.VMEM((count, 2, rows, width), jnp.bfloat16),
            pltpu.VMEM((blocks, 2, rows, 2 * width), jnp.bfloat16),
        ]
        + [dma((blocks,))] * 3
        + [dma((count, 2))] * 4
        + [dma((count,))] * 8
        + [dma],
        compiler_params=pltpu.CompilerParams(
            collective_id=collective_id, has_side_effects=True, vmem_limit_bytes=56 * 2**20
        ),
        name="sum_blocks",
    )(*ins)


def on_device_grids(
    encoder_out,
    code_ids,
    segments,
    embed_table,
    recon_grad,
    qkv_weight,
    query_bias,
    value_bias,
    out_weight,
    out_bias,
    first_gain,
    first_shift,
    second_gain,
    second_shift,
    up_weight,
    up_bias,
    down_weight,
    down_bias,
    pixel_weight,
    pixel_bias,
):
    features = encoder_out.shape[-1]
    wide = jnp.float32
    marks_grid = to_grid(segments)
    cotangent_grid = to_grid(recon_grad)
    height, width = marks_grid.shape
    tokens = height * width
    codes_tile = fetch_codes(code_ids, embed_table, cotangent_grid).reshape(encoder_out.shape)
    start_rows = to_grid(codes_tile).reshape(tokens, features).astype(wide)
    query_marks, key_marks = mark_columns(marks_grid.reshape(tokens))

    masks = tap_masks(marks_grid)
    cotangent = cotangent_grid.reshape(tokens, features)
    pixel_taps = jnp.swapaxes(pixel_weight, 0, 1)
    final_grad, lower_grad, behind = conv(
        cotangent, masks, pixel_taps, pixel_bias.reshape(1, features), width, -1
    )
    pixel_bias_grad = jnp.sum(cotangent.astype(wide), axis=0)
    down_bias_grad = jnp.sum(lower_grad.astype(wide), axis=0)
    hidden_grad = right_product(lower_grad, down_weight)

    normed, first_pull = jax.vjp(
        layer_norm, start_rows, first_gain.astype(wide), first_shift.astype(wide)
    )
    normed_low = normed.astype(jnp.bfloat16)
    projected = matmul(normed_low, qkv_weight)
    scale = HEAD_DIM**-0.5
    queries = (projected[:, :features] + query_bias.astype(wide)).astype(jnp.bfloat16)
    queries = queries * jnp.asarray(scale, jnp.bfloat16)
    key_rows = projected[:, features : 2 * features].astype(jnp.bfloat16)
    values = (projected[:, 2 * features :] + value_bias.astype(wide)).astype(jnp.bfloat16)
    attended, columns = attend(queries, key_rows, values, query_marks, key_marks)
    middle = start_rows + (matmul(attended, out_weight) + out_bias.astype(wide))
    normed_two, second_pull = jax.vjp(
        layer_norm, middle, second_gain.astype(wide), second_shift.astype(wide)
    )
    normed_two_low = normed_two.astype(jnp.bfloat16)
    hidden_pre = matmul(normed_two_low, up_weight) + up_bias.astype(wide)
    hidden_act, slope = gelu_parts(hidden_pre)
    hidden_low = hidden_act.astype(jnp.bfloat16)
    pre_grad = (hidden_grad * slope).astype(jnp.bfloat16)
    output_rows = middle + (matmul(hidden_low, down_weight) + down_bias.astype(wide))
    features_low = output_rows.astype(jnp.bfloat16)

    recon_rows = conv(features_low, masks, pixel_taps, pixel_bias.reshape(1, features), width, 1)
    recon_tiles = to_tiles(recon_rows.reshape(height, width, features))

    pixel_weight_grad = left_product(features_low, behind)
    down_weight_grad = left_product(hidden_low, lower_grad)
    up_weight_grad = left_product(normed_two_low, pre_grad)
    up_bias_grad = jnp.sum(pre_grad.astype(wide), axis=0)

    middle_part, second_gain_grad, second_shift_grad = second_pull(
        right_product(pre_grad, up_weight)
    )
    middle_grad = final_grad + middle_part
    branch_grad = middle_grad.astype(jnp.bfloat16)
    out_weight_grad = left_product(attended, branch_grad)
    out_bias_grad = jnp.sum(branch_grad.astype(wide), axis=0)
    attended_grad = right_product(branch_grad, out_weight).astype(jnp.bfloat16)
    query_grad, key_grad, value_grad = attend_back_grid(
        queries, key_rows, values, columns, key_marks, attended, attended_grad
    )
    projected_grad = jnp.concatenate([query_grad, key_grad, value_grad], axis=1)
    qkv_weight_grad = left_product(normed_low, projected_grad)
    query_bias_grad = jnp.sum(query_grad.astype(wide), axis=0)
    value_bias_grad = jnp.sum(value_grad.astype(wide), axis=0)
    start_part, first_gain_grad, first_shift_grad = first_pull(
        right_product(projected_grad, qkv_weight)
    )
    start_grad = middle_grad + start_part
    share = (start_grad - 2.0 * commit_weight * start_rows).astype(jnp.bfloat16)
    share_tiles = to_tiles(share.reshape(height, width, features))
    input_tiles = (
        share_tiles.astype(wide) + 2.0 * commit_weight * encoder_out.astype(wide)
    ).astype(jnp.bfloat16)

    vectors = [
        query_bias_grad,
        value_bias_grad,
        out_bias_grad,
        first_gain_grad,
        first_shift_grad,
        second_gain_grad,
        second_shift_grad,
        up_bias_grad,
        down_bias_grad,
        pixel_bias_grad,
    ]
    shards = lax.axis_size(("ty", "tx"))
    rows = features // shards
    packed = jnp.concatenate([v.reshape(shards, -1) for v in vectors], axis=1)
    packed = jnp.pad(packed, ((0, 0), (0, rows * features - packed.shape[1])))
    spread = (2, 2, 2)

    def cut(grad):
        split = spread + ((grad.shape[0] // features,) if grad.shape[0] > features else ())
        return grad.astype(jnp.bfloat16).reshape(split + (2, rows // 2, grad.shape[1]))

    ins = [
        cut(pixel_weight_grad),
        cut(up_weight_grad),
        cut(down_weight_grad),
        cut(out_weight_grad),
        cut(qkv_weight_grad),
        cut(packed.reshape(features, features)),
    ]
    layout = [(0, None, features * k) for k in range(9)]
    layout += [(1, None, features * k) for k in range(4)]
    layout += [(2, k, 0) for k in range(4)]
    layout += [(3, None, 0)]
    layout += [(4, None, features * k) for k in range(3)]
    layout += [(5, None, 0)]
    summed = sum_blocks(ins, layout, 1).reshape(len(layout), rows, features).astype(wide)
    packed = summed[21].reshape(-1)
    sums = []
    at = 0
    for vector in vectors:
        size = vector.shape[0] // shards
        sums.append(packed[at : at + size])
        at += size
    (query_bias_sum, value_bias_sum, out_bias_sum, first_gain_sum, first_shift_sum) = sums[:5]
    (second_gain_sum, second_shift_sum, up_bias_sum, down_bias_sum, pixel_bias_sum) = sums[5:]
    return (
        recon_tiles,
        input_tiles,
        jnp.swapaxes(summed[18:21], 0, 1).reshape(rows, 3 * features),
        query_bias_sum,
        value_bias_sum,
        summed[17],
        out_bias_sum,
        first_gain_sum,
        first_shift_sum,
        second_gain_sum,
        second_shift_sum,
        jnp.swapaxes(summed[9:13], 0, 1).reshape(rows, 4 * features),
        up_bias_sum,
        summed[13:17].reshape(4 * rows, features),
        down_bias_sum,
        jnp.swapaxes(summed[0:9], 0, 1),
        pixel_bias_sum,
    )


def solution(mesh):
    in_specs = (
        P("gr", "ty", "tx", None),
        P("gr", "ty", "tx"),
        P("gr", "ty", "tx"),
        P(("ty", "tx"), None),
        P("gr", "ty", "tx", None),
        P(),
        P(),
        P(),
        P(),
        P(),
        P(),
        P(),
        P(),
        P(),
        P(),
        P(),
        P(),
        P(),
        P(),
        P(),
    )
    out_specs = (
        P("gr", "ty", "tx", None),
        P("gr", "ty", "tx", None),
        P(("ty", "tx"), None),
        P(("ty", "tx")),
        P(("ty", "tx")),
        P(("ty", "tx"), None),
        P(("ty", "tx")),
        P(("ty", "tx")),
        P(("ty", "tx")),
        P(("ty", "tx")),
        P(("ty", "tx")),
        P(("ty", "tx"), None),
        P(("ty", "tx")),
        P(("ty", "tx"), None),
        P(("ty", "tx")),
        P(("ty", "tx"), None, None),
        P(("ty", "tx")),
    )
    def on_device(encoder_out, *rest):
        members = mesh.shape["ty"] * mesh.shape["tx"]
        whole_grids = encoder_out.shape[0] == members and tuple(mesh.devices.shape) == (4, 2, 4)
        body = on_device_grids if whole_grids else on_device_bands
        return body(encoder_out, *rest)

    return jax.shard_map(
        on_device, mesh=mesh, in_specs=in_specs, out_specs=out_specs, check_vma=False
    )
```

```python
from functools import partial

import jax
import jax.numpy as jnp
from jax import lax
from jax.experimental import pallas as pl
from jax.experimental.pallas import tpu as pltpu
from jax.sharding import PartitionSpec as P

HEADS = 12
HEAD_DIM = 64


epsilon = 1e-06
commit_weight = 0.25


def with_halo(block, sides, width):
    for axis, dim in sides:
        count = lax.axis_size(axis)
        forward = [(i, i + 1) for i in range(count - 1)]
        backward = [(target, source) for source, target in forward]
        low = lax.ppermute(
            lax.slice_in_dim(block, block.shape[dim] - width, None, axis=dim), axis, forward
        )
        high = lax.ppermute(lax.slice_in_dim(block, 0, width, axis=dim), axis, backward)
        block = jnp.concatenate([low, block, high], axis=dim)
    return block


def layer_norm(values, gain, shift):
    center = values - jnp.mean(values, axis=-1, keepdims=True)
    spread = jnp.mean(center * center, axis=-1, keepdims=True)
    return center * lax.rsqrt(spread + epsilon) * gain + shift


def exact_gelu(values):
    return jax.nn.gelu(values, approximate=False)


def matmul(left_side, right_side):
    return jnp.dot(left_side, right_side, preferred_element_type=jnp.float32)


def left_product(left_side, right_side):
    return lax.dot_general(
        left_side, right_side, (((0,), (0,)), ((), ())), preferred_element_type=jnp.float32
    )


def right_product(left_side, right_side):
    return lax.dot_general(
        left_side, right_side, (((1,), (1,)), ((), ())), preferred_element_type=jnp.float32
    )


def pad_side(array, axis_index):
    widths = [(0, 0)] * array.ndim
    widths[axis_index] = (1, 1)
    return jnp.pad(array, widths)


def blocked(array, block_size):
    return array.reshape((array.shape[0] // block_size, block_size) + array.shape[1:])


def unblock(array):
    return array.reshape((-1,) + array.shape[2:])


def head_scores(queries, key_rows, marks_query, marks_key, head_count, score_scale):
    grid_count, query_rows, features = queries.shape
    query_heads = queries.reshape(grid_count, query_rows, head_count, features // head_count)
    key_heads = key_rows.reshape(grid_count, key_rows.shape[1], head_count, features // head_count)
    scores = (
        jnp.einsum("bqhd,bkhd->bhqk", query_heads, key_heads, preferred_element_type=jnp.float32)
        * score_scale
    )
    same_image = (marks_query[:, :, None] == marks_key[:, None, :])[:, None]
    return jnp.where(same_image, scores, -1000000000.0)


def attend_block(bundle, head_count, score_scale):
    queries, key_rows, values, marks_query, marks_key = bundle
    grid_count, query_rows, features = queries.shape
    scores = head_scores(queries, key_rows, marks_query, marks_key, head_count, score_scale)
    running_max = jnp.max(scores, axis=-1, keepdims=True)
    exponent = jnp.exp(scores - running_max)
    denominator = jnp.sum(exponent, axis=-1, keepdims=True)
    probability = (exponent / denominator).astype(jnp.bfloat16)
    value_heads = values.reshape(grid_count, values.shape[1], head_count, features // head_count)
    attended = jnp.einsum(
        "bhqk,bkhd->bqhd", probability, value_heads, preferred_element_type=jnp.float32
    )
    return (
        attended.reshape(grid_count, query_rows, features).astype(jnp.bfloat16),
        running_max + jnp.log(denominator),
    )


def attend_back(bundle, head_count, score_scale):
    queries, key_rows, values, marks_query, marks_key, log_total, out_grad = bundle
    grid_count, query_rows, features = queries.shape
    head_size = features // head_count
    scores = head_scores(queries, key_rows, marks_query, marks_key, head_count, score_scale)
    probability = jnp.exp(scores - log_total)
    query_heads = queries.reshape(grid_count, query_rows, head_count, head_size)
    key_heads = key_rows.reshape(grid_count, key_rows.shape[1], head_count, head_size)
    value_heads = values.reshape(grid_count, values.shape[1], head_count, head_size)
    grad_heads = out_grad.reshape(grid_count, query_rows, head_count, head_size)
    prob_grad = jnp.einsum(
        "bqhd,bkhd->bhqk", grad_heads, value_heads, preferred_element_type=jnp.float32
    )
    inner_sum = jnp.sum(probability * prob_grad, axis=-1, keepdims=True)
    score_grad = (probability * (prob_grad - inner_sum)).astype(jnp.bfloat16)
    query_grad = (
        jnp.einsum("bhqk,bkhd->bqhd", score_grad, key_heads, preferred_element_type=jnp.float32)
        * score_scale
    )
    key_grad = (
        jnp.einsum("bhqk,bqhd->bkhd", score_grad, query_heads, preferred_element_type=jnp.float32)
        * score_scale
    )
    value_grad = jnp.einsum(
        "bhqk,bqhd->bkhd",
        probability.astype(jnp.bfloat16),
        grad_heads,
        preferred_element_type=jnp.float32,
    )
    key_count = key_rows.shape[1]
    return (
        query_grad.reshape(grid_count, query_rows, features).astype(jnp.bfloat16),
        key_grad.reshape(grid_count, key_count, features),
        value_grad.reshape(grid_count, key_count, features),
    )


def on_device_bands(
    encoder_out,
    code_ids,
    segments,
    embed_table,
    recon_grad,
    qkv_weight,
    query_bias,
    value_bias,
    out_weight,
    out_bias,
    first_gain,
    first_shift,
    second_gain,
    second_shift,
    up_weight,
    up_bias,
    down_weight,
    down_bias,
    pixel_weight,
    pixel_bias,
):
    features = encoder_out.shape[-1]
    head_count = HEADS
    score_scale = float(HEAD_DIM) ** (-0.5)
    holder_count = lax.axis_size(("ty", "tx"))
    share_rows = embed_table.shape[0]
    flat_ids = code_ids.reshape(-1)
    row_count = flat_ids.shape[0]
    slot_count = 3 * row_count // (2 * holder_count)
    holder = flat_ids // share_rows
    offsets = flat_ids - holder * share_rows
    belongs = (holder[:, None] == jnp.arange(holder_count, dtype=jnp.int32)[None, :]).astype(
        jnp.int32
    )
    slot_rank = jnp.sum((jnp.cumsum(belongs, axis=0) - 1) * belongs, axis=1)
    slot_index = holder * slot_count + slot_rank
    requests = jnp.zeros((holder_count * slot_count,), jnp.int32).at[slot_index].set(offsets)
    requests = requests.reshape(holder_count, slot_count)
    fetched = jnp.take(
        embed_table,
        lax.all_to_all(requests, ("ty", "tx"), split_axis=0, concat_axis=0, tiled=True),
        axis=0,
    )
    returned = lax.all_to_all(fetched, ("ty", "tx"), split_axis=0, concat_axis=0, tiled=True)
    codes = returned.reshape(holder_count * slot_count, features)[slot_index].reshape(
        encoder_out.shape
    )
    marks_tile = (segments + 1).astype(jnp.bfloat16)
    arrived = (
        lax.all_to_all(encoder_out, "tx", split_axis=0, concat_axis=2, tiled=True),
        lax.all_to_all(codes, "tx", split_axis=0, concat_axis=2, tiled=True),
        lax.all_to_all(recon_grad, "tx", split_axis=0, concat_axis=2, tiled=True),
        lax.all_to_all(marks_tile, "tx", split_axis=0, concat_axis=2, tiled=True),
    )
    inputs_band, codes_band, cotangent_band, marks_band = arrived
    grid_count, band_rows, band_cols = marks_band.shape
    tokens = band_rows * band_cols
    all_rows = grid_count * tokens
    block_size = max(1, 512 // tokens)
    while grid_count % block_size:
        block_size -= 1
    start_rows = codes_band.reshape(all_rows, features).astype(jnp.float32)
    marks_query = marks_band.reshape(grid_count, tokens)
    normed, first_pull = jax.vjp(
        layer_norm, start_rows, first_gain.astype(jnp.float32), first_shift.astype(jnp.float32)
    )
    normed_low = normed.astype(jnp.bfloat16)
    projected = matmul(normed_low, qkv_weight)
    queries = (
        (projected[:, :features] + query_bias.astype(jnp.float32))
        .astype(jnp.bfloat16)
        .reshape(grid_count, tokens, features)
    )
    key_rows = (
        projected[:, features : 2 * features]
        .astype(jnp.bfloat16)
        .reshape(grid_count, tokens, features)
    )
    values = (
        (projected[:, 2 * features :] + value_bias.astype(jnp.float32))
        .astype(jnp.bfloat16)
        .reshape(grid_count, tokens, features)
    )
    bundle = (key_rows, values, marks_query)
    keys_all = lax.all_gather(bundle[0], "ty", axis=1, tiled=True)
    values_all = lax.all_gather(bundle[1], "ty", axis=1, tiled=True)
    marks_key = lax.all_gather(bundle[2], "ty", axis=1, tiled=True)
    attended_blocks, log_total = lax.map(
        partial(attend_block, head_count=head_count, score_scale=score_scale),
        (
            blocked(queries, block_size),
            blocked(keys_all, block_size),
            blocked(values_all, block_size),
            blocked(marks_query, block_size),
            blocked(marks_key, block_size),
        ),
    )
    attended = unblock(attended_blocks).reshape(all_rows, features)
    branch = matmul(attended, out_weight) + out_bias.astype(jnp.float32)
    middle = start_rows + branch
    normed_two, second_pull = jax.vjp(
        layer_norm, middle, second_gain.astype(jnp.float32), second_shift.astype(jnp.float32)
    )
    normed_two_low = normed_two.astype(jnp.bfloat16)
    hidden_pre = matmul(normed_two_low, up_weight) + up_bias.astype(jnp.float32)
    hidden_act, gelu_pull = jax.vjp(exact_gelu, hidden_pre)
    hidden_low = hidden_act.astype(jnp.bfloat16)
    output_rows = middle + (matmul(hidden_low, down_weight) + down_bias.astype(jnp.float32))
    features_low = output_rows.astype(jnp.bfloat16).reshape(
        grid_count, band_rows, band_cols, features
    )
    bundle = (features_low, marks_band, cotangent_band)
    grown = (
        with_halo(bundle[0], (("ty", 1),), 1),
        with_halo(bundle[1], (("ty", 1),), 1),
        with_halo(bundle[2], (("ty", 1),), 1),
    )
    features_pad, marks_pad, cotangent_pad = tuple((pad_side(member, 2) for member in grown))
    ahead_list = []
    behind_list = []
    for vertical in range(3):
        for lateral in range(3):
            inside = (
                marks_pad[:, vertical : vertical + band_rows, lateral : lateral + band_cols]
                == marks_band
            )
            ahead_list.append(
                jnp.where(
                    inside[..., None],
                    features_pad[:, vertical : vertical + band_rows, lateral : lateral + band_cols],
                    0,
                )
            )
            mirror_row = 2 - vertical
            mirror_col = 2 - lateral
            facing = (
                marks_pad[
                    :, mirror_row : mirror_row + band_rows, mirror_col : mirror_col + band_cols
                ]
                == marks_band
            )
            behind_list.append(
                jnp.where(
                    facing[..., None],
                    cotangent_pad[
                        :, mirror_row : mirror_row + band_rows, mirror_col : mirror_col + band_cols
                    ],
                    0,
                )
            )
    ahead = jnp.stack(ahead_list, axis=3)
    behind = jnp.stack(behind_list, axis=3)
    recon_band = jnp.einsum(
        "nhwkd,dkp->nhwp", ahead, pixel_weight, preferred_element_type=jnp.float32
    ) + pixel_bias.astype(jnp.float32)
    pixel_weight_grad = jnp.einsum(
        "nhwkd,nhwp->dkp", ahead, cotangent_band, preferred_element_type=jnp.float32
    )
    pixel_bias_grad = jnp.sum(cotangent_band.astype(jnp.float32), axis=(0, 1, 2))
    final_grad = jnp.einsum(
        "nhwkp,dkp->nhwd", behind, pixel_weight, preferred_element_type=jnp.float32
    ).reshape(all_rows, features)
    lower_grad = final_grad.astype(jnp.bfloat16)
    down_weight_grad = left_product(hidden_low, lower_grad)
    down_bias_grad = jnp.sum(lower_grad.astype(jnp.float32), axis=0)
    pre_grad = gelu_pull(right_product(lower_grad, down_weight))[0].astype(jnp.bfloat16)
    up_weight_grad = left_product(normed_two_low, pre_grad)
    up_bias_grad = jnp.sum(pre_grad.astype(jnp.float32), axis=0)
    middle_part, second_gain_grad, second_shift_grad = second_pull(
        right_product(pre_grad, up_weight)
    )
    middle_grad = final_grad + middle_part
    branch_grad = middle_grad.astype(jnp.bfloat16)
    out_weight_grad = left_product(attended, branch_grad)
    out_bias_grad = jnp.sum(branch_grad.astype(jnp.float32), axis=0)
    attended_grad = (
        right_product(branch_grad, out_weight)
        .astype(jnp.bfloat16)
        .reshape(grid_count, tokens, features)
    )
    query_blocks, key_blocks, value_blocks = lax.map(
        partial(attend_back, head_count=head_count, score_scale=score_scale),
        (
            blocked(queries, block_size),
            blocked(keys_all, block_size),
            blocked(values_all, block_size),
            blocked(marks_query, block_size),
            blocked(marks_key, block_size),
            log_total,
            blocked(attended_grad, block_size),
        ),
    )
    query_grad = unblock(query_blocks)
    bundle = (unblock(key_blocks), unblock(value_blocks))
    key_sum = lax.psum_scatter(
        bundle[0].astype(jnp.bfloat16), "ty", scatter_dimension=1, tiled=True
    )
    value_sum = lax.psum_scatter(
        bundle[1].astype(jnp.bfloat16), "ty", scatter_dimension=1, tiled=True
    )
    projected_grad = jnp.concatenate([query_grad, key_sum, value_sum], axis=-1).reshape(
        all_rows, 3 * features
    )
    qkv_weight_grad = left_product(normed_low, projected_grad)
    query_bias_grad = jnp.sum(query_grad.astype(jnp.float32), axis=(0, 1))
    value_bias_grad = jnp.sum(value_sum.astype(jnp.float32), axis=(0, 1))
    start_part, first_gain_grad, first_shift_grad = first_pull(
        right_product(projected_grad, qkv_weight)
    )
    start_grad = middle_grad + start_part
    inputs_rows = inputs_band.reshape(all_rows, features).astype(jnp.float32)
    input_band = (start_grad + 2.0 * commit_weight * (inputs_rows - start_rows)).astype(
        jnp.bfloat16
    )
    bundle = (
        recon_band.astype(jnp.bfloat16),
        input_band.reshape(grid_count, band_rows, band_cols, features),
    )
    recon_tiles = lax.all_to_all(bundle[0], "tx", split_axis=2, concat_axis=0, tiled=True)
    input_tiles = lax.all_to_all(bundle[1], "tx", split_axis=2, concat_axis=0, tiled=True)
    local_grads = (
        qkv_weight_grad,
        query_bias_grad,
        value_bias_grad,
        out_weight_grad,
        out_bias_grad,
        first_gain_grad,
        first_shift_grad,
        second_gain_grad,
        second_shift_grad,
        up_weight_grad,
        up_bias_grad,
        down_weight_grad,
        down_bias_grad,
        pixel_weight_grad,
        pixel_bias_grad,
    )
    tile_shares = (
        lax.psum_scatter(
            local_grads[0].astype(jnp.bfloat16), ("ty", "tx"), scatter_dimension=0, tiled=True
        ).astype(jnp.float32),
        lax.psum_scatter(
            local_grads[1].astype(jnp.bfloat16), ("ty", "tx"), scatter_dimension=0, tiled=True
        ).astype(jnp.float32),
        lax.psum_scatter(
            local_grads[2].astype(jnp.bfloat16), ("ty", "tx"), scatter_dimension=0, tiled=True
        ).astype(jnp.float32),
        lax.psum_scatter(
            local_grads[3].astype(jnp.bfloat16), ("ty", "tx"), scatter_dimension=0, tiled=True
        ).astype(jnp.float32),
        lax.psum_scatter(
            local_grads[4].astype(jnp.bfloat16), ("ty", "tx"), scatter_dimension=0, tiled=True
        ).astype(jnp.float32),
        lax.psum_scatter(
            local_grads[5].astype(jnp.bfloat16), ("ty", "tx"), scatter_dimension=0, tiled=True
        ).astype(jnp.float32),
        lax.psum_scatter(
            local_grads[6].astype(jnp.bfloat16), ("ty", "tx"), scatter_dimension=0, tiled=True
        ).astype(jnp.float32),
        lax.psum_scatter(
            local_grads[7].astype(jnp.bfloat16), ("ty", "tx"), scatter_dimension=0, tiled=True
        ).astype(jnp.float32),
        lax.psum_scatter(
            local_grads[8].astype(jnp.bfloat16), ("ty", "tx"), scatter_dimension=0, tiled=True
        ).astype(jnp.float32),
        lax.psum_scatter(
            local_grads[9].astype(jnp.bfloat16), ("ty", "tx"), scatter_dimension=0, tiled=True
        ).astype(jnp.float32),
        lax.psum_scatter(
            local_grads[10].astype(jnp.bfloat16), ("ty", "tx"), scatter_dimension=0, tiled=True
        ).astype(jnp.float32),
        lax.psum_scatter(
            local_grads[11].astype(jnp.bfloat16), ("ty", "tx"), scatter_dimension=0, tiled=True
        ).astype(jnp.float32),
        lax.psum_scatter(
            local_grads[12].astype(jnp.bfloat16), ("ty", "tx"), scatter_dimension=0, tiled=True
        ).astype(jnp.float32),
        lax.psum_scatter(
            local_grads[13].astype(jnp.bfloat16), ("ty", "tx"), scatter_dimension=0, tiled=True
        ).astype(jnp.float32),
        lax.psum_scatter(
            local_grads[14].astype(jnp.bfloat16), ("ty", "tx"), scatter_dimension=0, tiled=True
        ).astype(jnp.float32),
    )
    summed = (
        lax.psum(tile_shares[0].astype(jnp.bfloat16), "gr").astype(jnp.float32),
        lax.psum(tile_shares[1].astype(jnp.bfloat16), "gr").astype(jnp.float32),
        lax.psum(tile_shares[2].astype(jnp.bfloat16), "gr").astype(jnp.float32),
        lax.psum(tile_shares[3].astype(jnp.bfloat16), "gr").astype(jnp.float32),
        lax.psum(tile_shares[4].astype(jnp.bfloat16), "gr").astype(jnp.float32),
        lax.psum(tile_shares[5].astype(jnp.bfloat16), "gr").astype(jnp.float32),
        lax.psum(tile_shares[6].astype(jnp.bfloat16), "gr").astype(jnp.float32),
        lax.psum(tile_shares[7].astype(jnp.bfloat16), "gr").astype(jnp.float32),
        lax.psum(tile_shares[8].astype(jnp.bfloat16), "gr").astype(jnp.float32),
        lax.psum(tile_shares[9].astype(jnp.bfloat16), "gr").astype(jnp.float32),
        lax.psum(tile_shares[10].astype(jnp.bfloat16), "gr").astype(jnp.float32),
        lax.psum(tile_shares[11].astype(jnp.bfloat16), "gr").astype(jnp.float32),
        lax.psum(tile_shares[12].astype(jnp.bfloat16), "gr").astype(jnp.float32),
        lax.psum(tile_shares[13].astype(jnp.bfloat16), "gr").astype(jnp.float32),
        lax.psum(tile_shares[14].astype(jnp.bfloat16), "gr").astype(jnp.float32),
    )
    return (
        recon_tiles,
        input_tiles,
        summed[0],
        summed[1],
        summed[2],
        summed[3],
        summed[4],
        summed[5],
        summed[6],
        summed[7],
        summed[8],
        summed[9],
        summed[10],
        summed[11],
        summed[12],
        summed[13],
        summed[14],
    )


far = float(2.0**30)


def nt(left_side, right_side):
    return lax.dot_general(
        left_side, right_side, (((1,), (1,)), ((), ())), preferred_element_type=jnp.float32
    )


def nn(left_side, right_side):
    return lax.dot_general(
        left_side, right_side, (((1,), (0,)), ((), ())), preferred_element_type=jnp.float32
    )


def attend_kernel(q_ref, k_ref, v_ref, qa_ref, ka_ref, o_ref, col_ref):
    lane = lax.broadcasted_iota(jnp.int32, (1, 128), 1)
    low = lane < 64
    local = lane % 64
    one = jnp.ones((), jnp.bfloat16)
    queries, key_rows, values = q_ref[...], k_ref[...], v_ref[...]
    query_marks, key_marks = qa_ref[...], ka_ref[...]
    outs = []
    logs = []
    for head in range(2):
        own = low if head == 0 else ~low
        scores = nt(jnp.where(own, queries, query_marks), jnp.where(own, key_rows, key_marks))
        top = jnp.max(scores, axis=1, keepdims=True)
        weights = jnp.exp(scores - top).astype(jnp.bfloat16)
        sums = nn(weights, jnp.where(own, values, one))
        outs.append(sums / pltpu.roll(sums, 64, 1))
        logs.append(top + jnp.log(sums))
    o_ref[...] = jnp.where(low, outs[0], outs[1]).astype(jnp.bfloat16)
    minus = -jnp.where(low, logs[1], logs[0])
    first = minus.astype(jnp.bfloat16).astype(jnp.float32)
    second = (minus - first).astype(jnp.bfloat16).astype(jnp.float32)
    third = minus - first - second
    columns = jnp.where(
        local == 3,
        first,
        jnp.where(local == 4, second, jnp.where(local == 5, third, query_marks.astype(jnp.float32))),
    )
    col_ref[...] = columns.astype(jnp.bfloat16)


def attend(queries, key_rows, values, query_marks, key_marks):
    tokens, features = queries.shape
    pair = pl.BlockSpec((tokens, 128), lambda i: (0, i))
    shared = pl.BlockSpec((tokens, 128), lambda i: (0, 0))
    shape = jax.ShapeDtypeStruct((tokens, features), jnp.bfloat16)
    return pl.pallas_call(
        attend_kernel,
        grid=(features // 128,),
        in_specs=[pair, pair, pair, shared, shared],
        out_specs=[pair, pair],
        out_shape=[shape, shape],
        compiler_params=pltpu.CompilerParams(vmem_limit_bytes=48 * 2**20),
        cost_estimate=pl.CostEstimate(
            flops=16 * tokens * tokens * features,
            bytes_accessed=10 * tokens * features,
            transcendentals=tokens * tokens * features // 64,
        ),
        name="attend",
    )(queries, key_rows, values, query_marks, key_marks)


def attend_back_kernel(
    q_ref, k_ref, v_ref, col_ref, ka_ref, o_ref, g_ref, dq_ref, dk_ref, dv_ref, k_sum, v_sum, *, step
):
    lane = lax.broadcasted_iota(jnp.int32, (1, 128), 1)
    low = lane < 64
    local = lane % 64
    zero = jnp.zeros((), jnp.bfloat16)
    one = jnp.ones((), jnp.bfloat16)
    key_rows, values = k_ref[...], v_ref[...]
    tokens = key_rows.shape[0]
    key_columns = jnp.where((local >= 3) & (local < 6), one, ka_ref[...])
    value_columns = jnp.where(local < 2, one, zero)
    keys_of = [jnp.where(low, key_rows, key_columns), jnp.where(low, key_columns, key_rows)]
    values_of = [jnp.where(low, values, value_columns), jnp.where(low, value_columns, values)]
    keys_across = key_rows.T
    upper = lax.broadcasted_iota(jnp.int32, (128, 1), 0) < 64
    k_sum[...] = jnp.zeros_like(k_sum)
    v_sum[...] = jnp.zeros_like(v_sum)

    def one_block(i, _):
        rows = pl.ds(pl.multiple_of(i * step, step), step)
        queries, columns = q_ref[rows, :], col_ref[rows, :]
        grad, out = g_ref[rows, :], o_ref[rows, :]
        both = grad.astype(jnp.float32) * out.astype(jnp.float32)
        of_low = -jnp.sum(jnp.where(low, both, 0.0), axis=1, keepdims=True)
        of_high = -jnp.sum(jnp.where(low, 0.0, both), axis=1, keepdims=True)
        inner = jnp.where(low, of_high, of_low)
        first = inner.astype(jnp.bfloat16).astype(jnp.float32)
        grad_columns = jnp.where(
            local == 0, first, jnp.where(local == 1, inner - first, 0.0)
        ).astype(jnp.bfloat16)
        query_parts, key_parts, value_parts = [], [], []
        for head in range(2):
            own = low if head == 0 else ~low
            weights = jnp.exp(nt(keys_of[head], jnp.where(own, queries, columns)))
            change = nt(values_of[head], jnp.where(own, grad, grad_columns))
            score_grad = (weights * change).astype(jnp.bfloat16)
            value_parts.append(nn(weights.astype(jnp.bfloat16), grad))
            key_parts.append(nn(score_grad, queries))
            query_parts.append(nn(keys_across, score_grad))
        k_sum[...] += jnp.where(low, key_parts[0], key_parts[1])
        v_sum[...] += jnp.where(low, value_parts[0], value_parts[1])
        query_grad = jnp.where(upper, query_parts[0], query_parts[1]).T
        dq_ref[rows, :] = (query_grad * HEAD_DIM**-0.5).astype(jnp.bfloat16)
        return 0

    lax.fori_loop(0, tokens // step, one_block, 0)
    dk_ref[...] = k_sum[...].astype(jnp.bfloat16)
    dv_ref[...] = v_sum[...].astype(jnp.bfloat16)


def attend_back_grid(queries, key_rows, values, columns, key_marks, out, grad):
    tokens, features = queries.shape
    pair = pl.BlockSpec((tokens, 128), lambda i: (0, i))
    shared = pl.BlockSpec((tokens, 128), lambda i: (0, 0))
    shape = jax.ShapeDtypeStruct((tokens, features), jnp.bfloat16)
    return pl.pallas_call(
        partial(attend_back_kernel, step=min(512, tokens)),
        grid=(features // 128,),
        in_specs=[pair, pair, pair, pair, shared, pair, pair],
        out_specs=[pair, pair, pair],
        out_shape=[shape, shape, shape],
        scratch_shapes=[pltpu.VMEM((tokens, 128), jnp.float32)] * 2,
        compiler_params=pltpu.CompilerParams(vmem_limit_bytes=48 * 2**20),
        cost_estimate=pl.CostEstimate(
            flops=24 * tokens * tokens * features,
            bytes_accessed=18 * tokens * features,
            transcendentals=tokens * tokens * features // 64,
        ),
        name="attend_back",
    )(queries, key_rows, values, columns, key_marks, out, grad)


def fetch_codes(code_ids, embed_table):
    features = embed_table.shape[1]
    holder_count = lax.axis_size(("ty", "tx"))
    share_rows = embed_table.shape[0]
    flat_ids = code_ids.reshape(-1)
    row_count = flat_ids.shape[0]
    slot_count = 3 * row_count // (2 * holder_count)
    starts = jnp.arange(1, holder_count, dtype=jnp.int32) * share_rows
    holder = jnp.sum((flat_ids[:, None] >= starts[None, :]).astype(jnp.int32), axis=1)
    offsets = flat_ids - holder * share_rows
    belongs = holder[:, None] == jnp.arange(holder_count, dtype=jnp.int32)[None, :]
    place = jnp.arange(row_count, dtype=jnp.int32)
    before = (place[:, None] > place[None, :]).astype(jnp.bfloat16)
    ranks = matmul(before, belongs.astype(jnp.bfloat16))
    slot_rank = jnp.sum(jnp.where(belongs, ranks, 0.0), axis=1).astype(jnp.int32)
    slot_index = holder * slot_count + slot_rank
    requests = jnp.zeros((holder_count * slot_count,), jnp.int32)
    requests = requests.at[slot_index].set(offsets, mode="promise_in_bounds", unique_indices=True)
    requests = requests.reshape(holder_count, slot_count)
    asked = lax.all_to_all(requests, ("ty", "tx"), split_axis=0, concat_axis=0, tiled=True)
    fetched = embed_table.at[asked.reshape(-1)].get(mode="promise_in_bounds")
    return slot_index, fetched.reshape(holder_count, slot_count, features)


def to_grid(tiles):
    down, across = lax.axis_size("ty"), lax.axis_size("tx")
    parts = lax.all_to_all(tiles, ("ty", "tx"), split_axis=0, concat_axis=0, tiled=True)
    parts = parts.reshape((down, across) + tiles.shape[1:])
    parts = jnp.moveaxis(parts, 1, 2)
    return parts.reshape((down * tiles.shape[1], across * tiles.shape[2]) + tiles.shape[3:])


def to_tiles(grid):
    down, across = lax.axis_size("ty"), lax.axis_size("tx")
    rows, cols = grid.shape[0] // down, grid.shape[1] // across
    parts = grid.reshape((down, rows, across, cols) + grid.shape[2:])
    parts = jnp.moveaxis(parts, 2, 1).reshape((down * across, rows, cols) + grid.shape[2:])
    return lax.all_to_all(parts, ("ty", "tx"), split_axis=0, concat_axis=0, tiled=True)


def conv_kernel(rows_ref, mask_ref, weight_ref, bias_ref, *refs, width, sign):
    if sign > 0:
        out_ref, shifted, total = refs
    else:
        out_ref, low_ref, taps_ref, shifted, total = refs
    tap = pl.program_id(0)
    tokens, features = rows_ref.shape

    @pl.when(tap == 0)
    def _():
        total[...] = jnp.zeros_like(total)
        rows = rows_ref[...]
        for j in range(3):
            moved = rows
            if j != 1:
                moved = pltpu.roll(rows.astype(jnp.float32), (1 - j) % tokens, 0)
            shifted[j, 0:width, :] = jnp.zeros((width, features), jnp.bfloat16)
            shifted[j, width + tokens :, :] = jnp.zeros((width, features), jnp.bfloat16)
            shifted[j, width : width + tokens, :] = moved.astype(jnp.bfloat16)

    down, right = tap // 3, tap % 3
    if sign < 0:
        down, right = 2 - down, 2 - right
    step = tokens // 4
    for i in range(4):
        rows = slice(i * step, (i + 1) * step)
        first = pl.multiple_of(down * width + i * step, width)
        same = mask_ref[right, pl.ds(first, step), :] == mask_ref[1, width + i * step : width + (i + 1) * step, :]
        mask = jnp.where(same, 1.0, 0.0).astype(jnp.bfloat16)
        mask = jnp.concatenate([mask] * (features // 128), axis=1)
        taken = shifted[right, pl.ds(first, step), :] * mask
        if sign < 0:
            taps_ref[rows, :] = taken
            total[rows, :] += nt(taken, weight_ref[0])
        else:
            total[rows, :] += nn(taken, weight_ref[0])

    @pl.when(tap == 8)
    def _():
        if sign > 0:
            out_ref[...] = (total[...] + bias_ref[...].astype(jnp.float32)).astype(jnp.bfloat16)
        else:
            out_ref[...] = total[...]
            low_ref[...] = total[...].astype(jnp.bfloat16)


def conv(rows, masks, weight, bias, width, sign):
    tokens, features = rows.shape

    def whole(shape):
        return pl.BlockSpec(shape, lambda k: (0, 0))

    low = jax.ShapeDtypeStruct((tokens, features), jnp.bfloat16)
    out_shape, out_specs = low, whole((tokens, features))
    if sign < 0:
        taps = jax.ShapeDtypeStruct((tokens, 9 * features), jnp.bfloat16)
        out_shape = [jax.ShapeDtypeStruct((tokens, features), jnp.float32), low, taps]
        out_specs = [out_specs, out_specs, pl.BlockSpec((tokens, features), lambda k: (0, k))]
    return pl.pallas_call(
        partial(conv_kernel, width=width, sign=sign),
        grid=(9,),
        in_specs=[
            whole((tokens, features)),
            pl.BlockSpec(masks.shape, lambda k: (0, 0, 0)),
            pl.BlockSpec((1, features, features), lambda k: (k, 0, 0)),
            whole((1, features)),
        ],
        out_specs=out_specs,
        out_shape=out_shape,
        scratch_shapes=[
            pltpu.VMEM((3, tokens + 2 * width, features), jnp.bfloat16),
            pltpu.VMEM((tokens, features), jnp.float32),
        ],
        compiler_params=pltpu.CompilerParams(vmem_limit_bytes=48 * 2**20),
        cost_estimate=pl.CostEstimate(
            flops=18 * tokens * features * features,
            bytes_accessed=18 * features * features + 4 * tokens * features,
            transcendentals=0,
        ),
        name="conv",
    )(rows, masks, weight, bias)


def marks_kernel(parts_ref, moved_ref, query_ref, key_ref, *, down, across, rows, cols):
    width = across * cols
    tokens = down * rows * width
    turned = parts_ref[...].astype(jnp.float32).T
    nowhere = jnp.full((width, 128), -1.0, jnp.float32)
    for j in range(3):
        moved_ref[j, 0:width, :] = nowhere
        moved_ref[j, width + tokens :, :] = nowhere
    for part in range(down * across):
        spread = jnp.broadcast_to(turned[:, part : part + 1], (rows * cols, 128))
        for r in range(rows):
            first = ((part // across) * rows + r) * width + (part % across) * cols + width
            moved_ref[1, first : first + cols, :] = spread[r * cols : (r + 1) * cols]
    marks = moved_ref[1, width : width + tokens, :]
    column = lax.broadcasted_iota(jnp.int32, (tokens, 128), 0) % width
    left = jnp.where(column == 0, -1.0, pltpu.roll(marks, 1, 0))
    right = jnp.where(column == width - 1, -1.0, pltpu.roll(marks, tokens - 1, 0))
    moved_ref[0, width : width + tokens, :] = left
    moved_ref[2, width : width + tokens, :] = right
    lane = lax.broadcasted_iota(jnp.int32, (tokens, 128), 1) % 64
    hot = marks == lane.astype(jnp.float32)
    query_ref[...] = jnp.where(hot, 1.0, 0.0).astype(jnp.bfloat16)
    key_ref[...] = jnp.where((lane < 3) & ~hot, -far, 0.0).astype(jnp.bfloat16)


def spread_marks(parts, down, across, rows, cols):
    tokens = down * across * rows * cols
    low = jax.ShapeDtypeStruct((tokens, 128), jnp.bfloat16)
    return pl.pallas_call(
        partial(marks_kernel, down=down, across=across, rows=rows, cols=cols),
        out_shape=[
            jax.ShapeDtypeStruct((3, tokens + 2 * across * cols, 128), jnp.float32),
            low,
            low,
        ],
        compiler_params=pltpu.CompilerParams(vmem_limit_bytes=48 * 2**20),
        name="spread_marks",
    )(parts)


def normalize(values):
    center = values - jnp.mean(values, axis=-1, keepdims=True)
    scale = lax.rsqrt(jnp.mean(center * center, axis=-1, keepdims=True) + epsilon)
    return center * scale, scale


def norm_back(grad, gain, unit, scale):
    scaled = grad * gain
    mean = jnp.mean(scaled, axis=-1, keepdims=True)
    along = jnp.mean(scaled * unit, axis=-1, keepdims=True)
    return scale * (scaled - mean - unit * along)


def row(ref):
    return ref[...].astype(jnp.float32)


def add_rows(ref, values):
    ref[...] += jnp.sum(values, axis=0, keepdims=True)


def enter_kernel(
    codes_ref, gain_ref, shift_ref, weight_ref, qb_ref, vb_ref, normed_ref, q_ref, k_ref, v_ref
):
    features = codes_ref.shape[1]
    unit, _ = normalize(row(codes_ref))
    normed = (unit * row(gain_ref) + row(shift_ref)).astype(jnp.bfloat16)
    normed_ref[...] = normed
    queries = nn(normed, weight_ref[:, 0:features]) + row(qb_ref)
    q_ref[...] = queries.astype(jnp.bfloat16) * jnp.asarray(HEAD_DIM**-0.5, jnp.bfloat16)
    k_ref[...] = nn(normed, weight_ref[:, features : 2 * features]).astype(jnp.bfloat16)
    values = nn(normed, weight_ref[:, 2 * features :]) + row(vb_ref)
    v_ref[...] = values.astype(jnp.bfloat16)


def held(shape):
    return pl.BlockSpec(shape, lambda i: (0,) * len(shape), pipeline_mode=pl.Buffered(1))


def by_rows(step, columns):
    return pl.BlockSpec((step, columns), lambda i: (i, 0))


def enter(codes, gain, shift, weight, query_bias, value_bias, step=256):
    tokens, features = codes.shape
    block = by_rows(step, features)
    vector = held((1, features))
    return pl.pallas_call(
        enter_kernel,
        grid=(tokens // step,),
        in_specs=[block, vector, vector, held(weight.shape), vector, vector],
        out_specs=[block] * 4,
        out_shape=[jax.ShapeDtypeStruct((tokens, features), jnp.bfloat16)] * 4,
        compiler_params=pltpu.CompilerParams(vmem_limit_bytes=48 * 2**20),
        cost_estimate=pl.CostEstimate(
            flops=6 * tokens * features * features,
            bytes_accessed=6 * features * features + 10 * tokens * features,
            transcendentals=0,
        ),
        name="enter",
    )(codes, gain, shift, weight, query_bias, value_bias)


def gelu_parts(values):
    spread = jnp.exp(-0.5 * values * values)
    t = 1.0 / (1.0 + (0.3275911 * 0.5**0.5) * jnp.abs(values))
    series = 0.5 * 1.061405429
    for factor in (-1.453152027, 1.421413741, -0.284496736, 0.254829592):
        series = series * t + 0.5 * factor
    tail = series * t * spread
    upto = jnp.where(values < 0.0, tail, 1.0 - tail)
    return values * upto, upto + values * spread * 0.3989422804014327


def middle_kernel(
    codes_ref,
    attended_ref,
    final_ref,
    hidden_grad_ref,
    out_weight_ref,
    up_ref,
    down_ref,
    out_bias_ref,
    gain_ref,
    shift_ref,
    up_bias_ref,
    down_bias_ref,
    features_ref,
    normed_ref,
    hidden_ref,
    pre_ref,
    middle_grad_ref,
    branch_ref,
    attended_grad_ref,
    out_bias_sum,
    gain_sum,
    shift_sum,
    up_bias_sum,
):
    @pl.when(pl.program_id(0) == 0)
    def _():
        for ref in (out_bias_sum, gain_sum, shift_sum, up_bias_sum):
            ref[...] = jnp.zeros_like(ref)

    features = codes_ref.shape[1]
    middle = row(codes_ref) + (nn(attended_ref[...], out_weight_ref[...]) + row(out_bias_ref))
    unit, scale = normalize(middle)
    normed = (unit * row(gain_ref) + row(shift_ref)).astype(jnp.bfloat16)
    normed_ref[...] = normed
    total = middle + row(down_bias_ref)
    grad = jnp.zeros_like(middle)
    for first in range(0, up_ref.shape[1], features):
        columns = slice(first, first + features)
        weight = up_ref[:, columns]
        hidden_pre = nn(normed, weight) + up_bias_ref[:, columns].astype(jnp.float32)
        act, slope = gelu_parts(hidden_pre)
        hidden = act.astype(jnp.bfloat16)
        hidden_ref[:, columns] = hidden
        pre = (hidden_grad_ref[:, columns].astype(jnp.float32) * slope).astype(jnp.bfloat16)
        pre_ref[:, columns] = pre
        up_bias_sum[:, columns] += jnp.sum(pre.astype(jnp.float32), axis=0, keepdims=True)
        total = total + nn(hidden, down_ref[columns, :])
        grad = grad + nt(pre, weight)
    features_ref[...] = total.astype(jnp.bfloat16)
    add_rows(gain_sum, grad * unit)
    add_rows(shift_sum, grad)
    middle_grad = final_ref[...] + norm_back(grad, row(gain_ref), unit, scale)
    middle_grad_ref[...] = middle_grad
    branch = middle_grad.astype(jnp.bfloat16)
    branch_ref[...] = branch
    add_rows(out_bias_sum, branch.astype(jnp.float32))
    attended_grad_ref[...] = nt(branch, out_weight_ref[...]).astype(jnp.bfloat16)


def middle_block(
    codes,
    attended,
    final_grad,
    hidden_grad,
    out_weight,
    up_weight,
    down_weight,
    out_bias,
    gain,
    shift,
    up_bias,
    down_bias,
    step=256,
):
    tokens, features = codes.shape
    wide = up_weight.shape[1]
    block = by_rows(step, features)
    broad = by_rows(step, wide)
    vector = held((1, features))

    def like(columns, dtype=jnp.bfloat16, rows=tokens):
        return jax.ShapeDtypeStruct((rows, columns), dtype)

    def total(columns):
        return pl.BlockSpec((1, columns), lambda i: (0, 0))

    return pl.pallas_call(
        middle_kernel,
        grid=(tokens // step,),
        in_specs=[
            block,
            block,
            block,
            broad,
            held(out_weight.shape),
            held(up_weight.shape),
            held(down_weight.shape),
            vector,
            vector,
            vector,
            held((1, wide)),
            vector,
        ],
        out_specs=[block, block, broad, broad, block, block, block]
        + [total(features)] * 3
        + [total(wide)],
        out_shape=[
            like(features),
            like(features),
            like(wide),
            like(wide),
            like(features, jnp.float32),
            like(features),
            like(features),
        ]
        + [like(features, jnp.float32, 1)] * 3
        + [like(wide, jnp.float32, 1)],
        compiler_params=pltpu.CompilerParams(vmem_limit_bytes=56 * 2**20),
        cost_estimate=pl.CostEstimate(
            flops=2 * tokens * features * (2 * features + 3 * wide),
            bytes_accessed=4 * features * wide + 6 * tokens * wide + 16 * tokens * features,
            transcendentals=2 * tokens * wide,
        ),
        name="middle",
    )(
        codes,
        attended,
        final_grad,
        hidden_grad,
        out_weight,
        up_weight,
        down_weight,
        out_bias,
        gain,
        shift,
        up_bias,
        down_bias,
    )


def leave_kernel(
    codes_ref,
    middle_grad_ref,
    dq_ref,
    dk_ref,
    dv_ref,
    weight_ref,
    gain_ref,
    share_ref,
    gain_sum,
    shift_sum,
    query_sum,
    value_sum,
):
    @pl.when(pl.program_id(0) == 0)
    def _():
        for ref in (gain_sum, shift_sum, query_sum, value_sum):
            ref[...] = jnp.zeros_like(ref)

    features = codes_ref.shape[1]
    grad = nt(dq_ref[...], weight_ref[:, 0:features])
    grad = grad + nt(dk_ref[...], weight_ref[:, features : 2 * features])
    grad = grad + nt(dv_ref[...], weight_ref[:, 2 * features :])
    start = row(codes_ref)
    unit, scale = normalize(start)
    add_rows(gain_sum, grad * unit)
    add_rows(shift_sum, grad)
    add_rows(query_sum, row(dq_ref))
    add_rows(value_sum, row(dv_ref))
    start_grad = middle_grad_ref[...] + norm_back(grad, row(gain_ref), unit, scale)
    share_ref[...] = (start_grad - 2.0 * commit_weight * start).astype(jnp.bfloat16)


def leave(codes, middle_grad, dq, dk, dv, weight, gain, step=256):
    tokens, features = codes.shape
    block = by_rows(step, features)
    total = pl.BlockSpec((1, features), lambda i: (0, 0))
    return pl.pallas_call(
        leave_kernel,
        grid=(tokens // step,),
        in_specs=[block] * 5 + [held(weight.shape), held((1, features))],
        out_specs=[block] + [total] * 4,
        out_shape=[jax.ShapeDtypeStruct((tokens, features), jnp.bfloat16)]
        + [jax.ShapeDtypeStruct((1, features), jnp.float32)] * 4,
        compiler_params=pltpu.CompilerParams(vmem_limit_bytes=48 * 2**20),
        cost_estimate=pl.CostEstimate(
            flops=6 * tokens * features * features,
            bytes_accessed=6 * features * features + 14 * tokens * features,
            transcendentals=0,
        ),
        name="leave",
    )(codes, middle_grad, dq, dk, dv, weight, gain)


def sum_kernel(*refs, layout, homes, count, lead):
    ins = refs[: max(item[0] for item in layout) + 1]
    outs = refs[len(ins) : 2 * len(ins)]
    (own, got0, got1, got2, got3, got4, whole) = refs[2 * len(ins) : 2 * len(ins) + 7]
    (own_sem, s0, r0, s1, r1, s2, r2, s3, r3, s4, r4, s5, r5, s6, r6, out_sem) = refs[2 * len(ins) + 7 :]
    gr, ty, tx = lax.axis_index("gr"), lax.axis_index("ty"), lax.axis_index("tx")
    x, core, half, par = gr // 2, gr % 2, tx // 2, tx % 2
    mate = (2 * x + 1 - core, ty, tx)
    over_x = (2 * (1 - x) + core, ty, tx)
    over_y = (gr, 1 - ty, tx)
    near = (gr, ty, half * 2 + (1 - par))
    away = (gr, ty, (1 - half) * 2 + par)
    barrier = pltpu.get_barrier_semaphore()
    for device in (mate, over_x, over_y, near, away):
        pl.semaphore_signal(barrier, inc=1, device_id=device, device_id_type=pl.DeviceIdType.MESH)
    pl.semaphore_wait(barrier, 5)
    width = own.shape[-1]
    own_columns = pl.ds(pl.multiple_of(core * width, 128), width)

    def part(block, which):
        source, prefix, column = layout[block]
        columns = pl.ds(pl.multiple_of(column + which * width, 128), width)
        if prefix is None:
            return ins[source].at[:, :, :, :, :, columns]
        return ins[source].at[:, :, :, prefix, :, :, columns]

    def put(source, target, sent, received, device):
        return pltpu.make_async_remote_copy(
            src_ref=source,
            dst_ref=target,
            send_sem=sent,
            recv_sem=received,
            device_id=device,
            device_id_type=pl.DeviceIdType.MESH,
        )

    for block in range(2 * count):
        put(part(block, 1 - core), got0.at[block], s0.at[block], r0.at[block], mate).start()
        pltpu.make_async_copy(part(block, core), own.at[block], own_sem.at[block]).start()

    def level0(b):
        return put(got0.at[b], got0.at[b], s0.at[b], r0.at[b], mate)

    def level1x(c):
        return put(own.at[2 * c, :, :, :, 1 - x], got1.at[c, 0], s1.at[c, 0], r1.at[c, 0], over_x)

    def level1y(c):
        return put(own.at[2 * c + 1, 1 - ty], got1.at[c, 1], s1.at[c, 1], r1.at[c, 1], over_y)

    def level2y(c):
        return put(got1.at[c, 0, 1 - ty], got2.at[c, 0], s2.at[c, 0], r2.at[c, 0], over_y)

    def level2x(c):
        return put(got1.at[c, 1, :, :, 1 - x], got2.at[c, 1], s2.at[c, 1], r2.at[c, 1], over_x)

    def level3(c):
        return put(got2.at[c, :, :, 1 - par], got3.at[c], s3.at[c], r3.at[c], near)

    def level4(c):
        return put(got3.at[c, :, 1 - half], got4.at[c], s4.at[c], r4.at[c], away)

    def level5(c):
        place = whole.at[pl.ds(2 * c, 2), x, :, own_columns]
        return put(place, place, s5.at[c], r5.at[c], over_x)

    def level6(c):
        place = whole.at[pl.ds(2 * c, 2), :, :, own_columns]
        return put(place, place, s6.at[c], r6.at[c], mate)

    def stage1(c):
        for b in (2 * c, 2 * c + 1):
            level0(b).wait_recv()
            pltpu.make_async_copy(own.at[b], own.at[b], own_sem.at[b]).wait()

            def add(i, _):
                y, h, p = i // 4, (i // 2) % 2, i % 2
                own[b, y, h, p] = own[b, y, h, p] + got0[b, y, h, p]
                return 0

            lax.fori_loop(0, 8, add, 0)
        level1x(c).start()
        level1y(c).start()

    def stage2(c):
        level1x(c).wait_recv()
        got1[c, 0] = got1[c, 0] + own[2 * c, :, :, :, x]
        level2y(c).start()
        level1y(c).wait_recv()
        got1[c, 1] = got1[c, 1] + own[2 * c + 1, ty]
        level2x(c).start()

    def stage3(c):
        level2y(c).wait_recv()
        level2x(c).wait_recv()
        got2[c, 0] = got2[c, 0] + got1[c, 0, ty]
        got2[c, 1] = got2[c, 1] + got1[c, 1, :, :, x]
        level3(c).start()

    def stage4(c):
        level3(c).wait_recv()
        got3[c] = got3[c] + got2[c, :, :, par]
        level4(c).start()

    def stage5(c):
        level4(c).wait_recv()
        whole[pl.ds(2 * c, 2), x, :, own_columns] = got4[c] + got3[c, :, half]
        level5(c).start()

    def stage6(c):
        level5(c).wait_recv()
        level6(c).start()

    stages = (stage1, stage2, stage3, stage4, stage5, stage6)

    def turn(t, _):
        for stage, behind in zip(stages, lead):
            c = t - behind
            pl.when((c >= 0) & (c < count))(partial(stage, c))
        return 0

    lax.fori_loop(0, count + lead[-1], turn, 0)

    def finish(c, _):
        level6(c).wait_recv()
        level0(2 * c).wait_send()
        level0(2 * c + 1).wait_send()
        for level in (level1x, level1y, level2x, level2y, level3, level4, level5, level6):
            level(c).wait_send()
        return 0

    lax.fori_loop(0, count, finish, 0)
    copies = []
    for block, (home, prefix, column) in enumerate(homes):
        out = outs[home] if prefix is None else outs[home].at[prefix]
        target = out.at[:, :, pl.ds(column, 2 * width)]
        copies.append(pltpu.make_async_copy(whole.at[block], target, out_sem.at[block]))
        copies[-1].start()
    for copy in copies:
        copy.wait()


def sum_blocks(ins, layout, homes, shapes, collective_id):
    blocks = len(layout)
    count = blocks // 2
    rows, width = ins[0].shape[-2], 384
    dma = pltpu.SemaphoreType.DMA
    half_block = pltpu.VMEM((blocks, 2, 2, 2, 2, rows, width), jnp.bfloat16)
    return pl.pallas_call(
        partial(sum_kernel, layout=layout, homes=homes, count=count, lead=(0, 2, 4, 6, 8, 10)),
        in_specs=[pl.BlockSpec(memory_space=pl.ANY)] * len(ins),
        out_specs=[pl.BlockSpec(memory_space=pl.ANY)] * len(ins),
        out_shape=[jax.ShapeDtypeStruct(shape, jnp.bfloat16) for shape in shapes],
        scratch_shapes=[
            half_block,
            half_block,
            pltpu.VMEM((count, 2, 2, 2, 2, rows, width), jnp.bfloat16),
            pltpu.VMEM((count, 2, 2, 2, rows, width), jnp.bfloat16),
            pltpu.VMEM((count, 2, 2, rows, width), jnp.bfloat16),
            pltpu.VMEM((count, 2, rows, width), jnp.bfloat16),
            pltpu.VMEM((blocks, 2, rows, 2 * width), jnp.bfloat16),
        ]
        + [dma((blocks,))] * 3
        + [dma((count, 2))] * 4
        + [dma((count,))] * 8
        + [dma((blocks,))],
        compiler_params=pltpu.CompilerParams(
            collective_id=collective_id, has_side_effects=True, vmem_limit_bytes=56 * 2**20
        ),
        name="sum_blocks",
    )(*ins)


def on_device_grids(
    encoder_out,
    code_ids,
    segments,
    embed_table,
    recon_grad,
    qkv_weight,
    query_bias,
    value_bias,
    out_weight,
    out_bias,
    first_gain,
    first_shift,
    second_gain,
    second_shift,
    up_weight,
    up_bias,
    down_weight,
    down_bias,
    pixel_weight,
    pixel_bias,
):
    features = encoder_out.shape[-1]
    wide = jnp.float32
    height = encoder_out.shape[1] * lax.axis_size("ty")
    width = encoder_out.shape[2] * lax.axis_size("tx")
    tokens = height * width
    down, across = lax.axis_size("ty"), lax.axis_size("tx")
    axes = ("ty", "tx")

    def line(vector):
        return vector.reshape(1, -1)

    cotangent_grid = to_grid(recon_grad)
    marks = segments.reshape(segments.shape[0], 1, -1)
    marks = lax.all_to_all(marks, axes, split_axis=0, concat_axis=0, tiled=True)
    moved, query_marks, key_marks = spread_marks(
        marks.reshape(down * across, -1), down, across, encoder_out.shape[1], encoder_out.shape[2]
    )
    slot_index, fetched = fetch_codes(code_ids, embed_table)
    fetched, cotangent_grid = lax.optimization_barrier((fetched, cotangent_grid))
    returned = lax.all_to_all(fetched, axes, split_axis=0, concat_axis=0, tiled=True)
    returned = returned.reshape(-1, features)

    cotangent = cotangent_grid.reshape(tokens, features)
    pixel_taps = jnp.swapaxes(pixel_weight, 0, 1)
    final_grad, lower_grad, behind = conv(
        cotangent, moved, pixel_taps, line(pixel_bias), width, -1
    )
    returned, lower_grad = lax.optimization_barrier((returned, lower_grad))
    codes_tile = returned.at[slot_index].get(mode="promise_in_bounds").reshape(encoder_out.shape)
    codes = to_grid(codes_tile).reshape(tokens, features)
    hidden_grad = right_product(lower_grad, down_weight).astype(jnp.bfloat16)
    pixel_bias_grad = jnp.sum(cotangent.astype(wide), axis=0)
    down_bias_grad = jnp.sum(lower_grad.astype(wide), axis=0)

    normed, queries, key_rows, values = enter(
        codes, line(first_gain), line(first_shift), qkv_weight, line(query_bias), line(value_bias)
    )
    attended, columns = attend(queries, key_rows, values, query_marks, key_marks)
    (
        features_low,
        normed_two,
        hidden_low,
        pre_grad,
        middle_grad,
        branch_grad,
        attended_grad,
        out_bias_grad,
        second_gain_grad,
        second_shift_grad,
        up_bias_grad,
    ) = middle_block(
        codes,
        attended,
        final_grad,
        hidden_grad,
        out_weight,
        up_weight,
        down_weight,
        line(out_bias),
        line(second_gain),
        line(second_shift),
        line(up_bias),
        line(down_bias),
    )

    recon_rows = conv(features_low, moved, pixel_taps, line(pixel_bias), width, 1)
    recon_tiles = to_tiles(recon_rows.reshape(height, width, features))

    query_grad, key_grad, value_grad = attend_back_grid(
        queries, key_rows, values, columns, key_marks, attended, attended_grad
    )
    share, first_gain_grad, first_shift_grad, query_bias_grad, value_bias_grad = leave(
        codes, middle_grad, query_grad, key_grad, value_grad, qkv_weight, line(first_gain)
    )
    share_tiles = to_tiles(share.reshape(height, width, features))
    input_tiles = (
        share_tiles.astype(wide) + 2.0 * commit_weight * encoder_out.astype(wide)
    ).astype(jnp.bfloat16)

    pixel_weight_grad = left_product(features_low, behind)
    down_weight_grad = left_product(hidden_low, lower_grad)
    up_weight_grad = left_product(normed_two, pre_grad)
    out_weight_grad = left_product(attended, branch_grad)
    projected_grad = jnp.concatenate([query_grad, key_grad, value_grad], axis=1)
    qkv_weight_grad = left_product(normed, projected_grad)

    vectors = [
        query_bias_grad,
        value_bias_grad,
        out_bias_grad,
        first_gain_grad,
        first_shift_grad,
        second_gain_grad,
        second_shift_grad,
        up_bias_grad,
        down_bias_grad,
        pixel_bias_grad,
    ]
    shards = down * across
    rows = features // shards
    packed = jnp.concatenate([v.reshape(shards, -1) for v in vectors], axis=1)
    packed = jnp.pad(packed, ((0, 0), (0, rows * features - packed.shape[1])))
    spread = (2, 2, 2)

    def cut(grad):
        split = spread + ((grad.shape[0] // features,) if grad.shape[0] > features else ())
        return grad.astype(jnp.bfloat16).reshape(split + (2, rows // 2, grad.shape[1]))

    ins = [
        cut(pixel_weight_grad),
        cut(up_weight_grad),
        cut(down_weight_grad),
        cut(out_weight_grad),
        cut(qkv_weight_grad),
        cut(packed.reshape(features, features)),
    ]
    layout = [(0, None, features * k) for k in range(9)]
    layout += [(1, None, features * k) for k in range(4)]
    layout += [(2, k, 0) for k in range(4)]
    layout += [(3, None, 0)]
    layout += [(4, None, features * k) for k in range(3)]
    layout += [(5, None, 0)]
    homes = [(0, k, 0) for k in range(9)] + layout[9:]
    shapes = [(9, 2, rows // 2, features)] + [grad.shape[3:] for grad in ins[1:]]
    pixel_sum, up_sum, down_sum, out_sum, qkv_sum, packed = [
        summed.reshape(-1, summed.shape[-1]).astype(wide)
        for summed in sum_blocks(ins, layout, homes, shapes, 1)
    ]
    packed = packed[:8].reshape(-1)
    sums = []
    at = 0
    for vector in vectors:
        size = vector.size // shards
        sums.append(packed[at : at + size])
        at += size
    (query_bias_sum, value_bias_sum, out_bias_sum, first_gain_sum, first_shift_sum) = sums[:5]
    (second_gain_sum, second_shift_sum, up_bias_sum, down_bias_sum, pixel_bias_sum) = sums[5:]
    return (
        recon_tiles,
        input_tiles,
        qkv_sum,
        query_bias_sum,
        value_bias_sum,
        out_sum,
        out_bias_sum,
        first_gain_sum,
        first_shift_sum,
        second_gain_sum,
        second_shift_sum,
        up_sum,
        up_bias_sum,
        down_sum,
        down_bias_sum,
        jnp.swapaxes(pixel_sum.reshape(9, rows, features), 0, 1),
        pixel_bias_sum,
    )


def solution(mesh):
    in_specs = (
        P("gr", "ty", "tx", None),
        P("gr", "ty", "tx"),
        P("gr", "ty", "tx"),
        P(("ty", "tx"), None),
        P("gr", "ty", "tx", None),
        P(),
        P(),
        P(),
        P(),
        P(),
        P(),
        P(),
        P(),
        P(),
        P(),
        P(),
        P(),
        P(),
        P(),
        P(),
    )
    out_specs = (
        P("gr", "ty", "tx", None),
        P("gr", "ty", "tx", None),
        P(("ty", "tx"), None),
        P(("ty", "tx")),
        P(("ty", "tx")),
        P(("ty", "tx"), None),
        P(("ty", "tx")),
        P(("ty", "tx")),
        P(("ty", "tx")),
        P(("ty", "tx")),
        P(("ty", "tx")),
        P(("ty", "tx"), None),
        P(("ty", "tx")),
        P(("ty", "tx"), None),
        P(("ty", "tx")),
        P(("ty", "tx"), None, None),
        P(("ty", "tx")),
    )
    def on_device(encoder_out, *rest):
        members = mesh.shape["ty"] * mesh.shape["tx"]
        whole_grids = encoder_out.shape[0] == members and tuple(mesh.devices.shape) == (4, 2, 4)
        body = on_device_grids if whole_grids else on_device_bands
        return body(encoder_out, *rest)

    return jax.shard_map(
        on_device, mesh=mesh, in_specs=in_specs, out_specs=out_specs, check_vma=False
    )
```

```python
from functools import partial

import jax
import jax.numpy as jnp
from jax import lax
from jax.experimental import pallas as pl
from jax.experimental.pallas import tpu as pltpu
from jax.sharding import PartitionSpec as P

HEADS = 12
HEAD_DIM = 64


epsilon = 1e-06
commit_weight = 0.25


def with_halo(block, sides, width):
    for axis, dim in sides:
        count = lax.axis_size(axis)
        forward = [(i, i + 1) for i in range(count - 1)]
        backward = [(target, source) for source, target in forward]
        low = lax.ppermute(
            lax.slice_in_dim(block, block.shape[dim] - width, None, axis=dim), axis, forward
        )
        high = lax.ppermute(lax.slice_in_dim(block, 0, width, axis=dim), axis, backward)
        block = jnp.concatenate([low, block, high], axis=dim)
    return block


def layer_norm(values, gain, shift):
    center = values - jnp.mean(values, axis=-1, keepdims=True)
    spread = jnp.mean(center * center, axis=-1, keepdims=True)
    return center * lax.rsqrt(spread + epsilon) * gain + shift


def exact_gelu(values):
    return jax.nn.gelu(values, approximate=False)


def matmul(left_side, right_side):
    return jnp.dot(left_side, right_side, preferred_element_type=jnp.float32)


def left_product(left_side, right_side):
    return lax.dot_general(
        left_side, right_side, (((0,), (0,)), ((), ())), preferred_element_type=jnp.float32
    )


def right_product(left_side, right_side):
    return lax.dot_general(
        left_side, right_side, (((1,), (1,)), ((), ())), preferred_element_type=jnp.float32
    )


def pad_side(array, axis_index):
    widths = [(0, 0)] * array.ndim
    widths[axis_index] = (1, 1)
    return jnp.pad(array, widths)


def blocked(array, block_size):
    return array.reshape((array.shape[0] // block_size, block_size) + array.shape[1:])


def unblock(array):
    return array.reshape((-1,) + array.shape[2:])


def head_scores(queries, key_rows, marks_query, marks_key, head_count, score_scale):
    grid_count, query_rows, features = queries.shape
    query_heads = queries.reshape(grid_count, query_rows, head_count, features // head_count)
    key_heads = key_rows.reshape(grid_count, key_rows.shape[1], head_count, features // head_count)
    scores = (
        jnp.einsum("bqhd,bkhd->bhqk", query_heads, key_heads, preferred_element_type=jnp.float32)
        * score_scale
    )
    same_image = (marks_query[:, :, None] == marks_key[:, None, :])[:, None]
    return jnp.where(same_image, scores, -1000000000.0)


def attend_block(bundle, head_count, score_scale):
    queries, key_rows, values, marks_query, marks_key = bundle
    grid_count, query_rows, features = queries.shape
    scores = head_scores(queries, key_rows, marks_query, marks_key, head_count, score_scale)
    running_max = jnp.max(scores, axis=-1, keepdims=True)
    exponent = jnp.exp(scores - running_max)
    denominator = jnp.sum(exponent, axis=-1, keepdims=True)
    probability = (exponent / denominator).astype(jnp.bfloat16)
    value_heads = values.reshape(grid_count, values.shape[1], head_count, features // head_count)
    attended = jnp.einsum(
        "bhqk,bkhd->bqhd", probability, value_heads, preferred_element_type=jnp.float32
    )
    return (
        attended.reshape(grid_count, query_rows, features).astype(jnp.bfloat16),
        running_max + jnp.log(denominator),
    )


def attend_back(bundle, head_count, score_scale):
    queries, key_rows, values, marks_query, marks_key, log_total, out_grad = bundle
    grid_count, query_rows, features = queries.shape
    head_size = features // head_count
    scores = head_scores(queries, key_rows, marks_query, marks_key, head_count, score_scale)
    probability = jnp.exp(scores - log_total)
    query_heads = queries.reshape(grid_count, query_rows, head_count, head_size)
    key_heads = key_rows.reshape(grid_count, key_rows.shape[1], head_count, head_size)
    value_heads = values.reshape(grid_count, values.shape[1], head_count, head_size)
    grad_heads = out_grad.reshape(grid_count, query_rows, head_count, head_size)
    prob_grad = jnp.einsum(
        "bqhd,bkhd->bhqk", grad_heads, value_heads, preferred_element_type=jnp.float32
    )
    inner_sum = jnp.sum(probability * prob_grad, axis=-1, keepdims=True)
    score_grad = (probability * (prob_grad - inner_sum)).astype(jnp.bfloat16)
    query_grad = (
        jnp.einsum("bhqk,bkhd->bqhd", score_grad, key_heads, preferred_element_type=jnp.float32)
        * score_scale
    )
    key_grad = (
        jnp.einsum("bhqk,bqhd->bkhd", score_grad, query_heads, preferred_element_type=jnp.float32)
        * score_scale
    )
    value_grad = jnp.einsum(
        "bhqk,bqhd->bkhd",
        probability.astype(jnp.bfloat16),
        grad_heads,
        preferred_element_type=jnp.float32,
    )
    key_count = key_rows.shape[1]
    return (
        query_grad.reshape(grid_count, query_rows, features).astype(jnp.bfloat16),
        key_grad.reshape(grid_count, key_count, features),
        value_grad.reshape(grid_count, key_count, features),
    )


def on_device_bands(
    encoder_out,
    code_ids,
    segments,
    embed_table,
    recon_grad,
    qkv_weight,
    query_bias,
    value_bias,
    out_weight,
    out_bias,
    first_gain,
    first_shift,
    second_gain,
    second_shift,
    up_weight,
    up_bias,
    down_weight,
    down_bias,
    pixel_weight,
    pixel_bias,
):
    features = encoder_out.shape[-1]
    head_count = HEADS
    score_scale = float(HEAD_DIM) ** (-0.5)
    holder_count = lax.axis_size(("ty", "tx"))
    share_rows = embed_table.shape[0]
    flat_ids = code_ids.reshape(-1)
    row_count = flat_ids.shape[0]
    slot_count = 3 * row_count // (2 * holder_count)
    holder = flat_ids // share_rows
    offsets = flat_ids - holder * share_rows
    belongs = (holder[:, None] == jnp.arange(holder_count, dtype=jnp.int32)[None, :]).astype(
        jnp.int32
    )
    slot_rank = jnp.sum((jnp.cumsum(belongs, axis=0) - 1) * belongs, axis=1)
    slot_index = holder * slot_count + slot_rank
    requests = jnp.zeros((holder_count * slot_count,), jnp.int32).at[slot_index].set(offsets)
    requests = requests.reshape(holder_count, slot_count)
    fetched = jnp.take(
        embed_table,
        lax.all_to_all(requests, ("ty", "tx"), split_axis=0, concat_axis=0, tiled=True),
        axis=0,
    )
    returned = lax.all_to_all(fetched, ("ty", "tx"), split_axis=0, concat_axis=0, tiled=True)
    codes = returned.reshape(holder_count * slot_count, features)[slot_index].reshape(
        encoder_out.shape
    )
    marks_tile = (segments + 1).astype(jnp.bfloat16)
    arrived = (
        lax.all_to_all(encoder_out, "tx", split_axis=0, concat_axis=2, tiled=True),
        lax.all_to_all(codes, "tx", split_axis=0, concat_axis=2, tiled=True),
        lax.all_to_all(recon_grad, "tx", split_axis=0, concat_axis=2, tiled=True),
        lax.all_to_all(marks_tile, "tx", split_axis=0, concat_axis=2, tiled=True),
    )
    inputs_band, codes_band, cotangent_band, marks_band = arrived
    grid_count, band_rows, band_cols = marks_band.shape
    tokens = band_rows * band_cols
    all_rows = grid_count * tokens
    block_size = max(1, 512 // tokens)
    while grid_count % block_size:
        block_size -= 1
    start_rows = codes_band.reshape(all_rows, features).astype(jnp.float32)
    marks_query = marks_band.reshape(grid_count, tokens)
    normed, first_pull = jax.vjp(
        layer_norm, start_rows, first_gain.astype(jnp.float32), first_shift.astype(jnp.float32)
    )
    normed_low = normed.astype(jnp.bfloat16)
    projected = matmul(normed_low, qkv_weight)
    queries = (
        (projected[:, :features] + query_bias.astype(jnp.float32))
        .astype(jnp.bfloat16)
        .reshape(grid_count, tokens, features)
    )
    key_rows = (
        projected[:, features : 2 * features]
        .astype(jnp.bfloat16)
        .reshape(grid_count, tokens, features)
    )
    values = (
        (projected[:, 2 * features :] + value_bias.astype(jnp.float32))
        .astype(jnp.bfloat16)
        .reshape(grid_count, tokens, features)
    )
    bundle = (key_rows, values, marks_query)
    keys_all = lax.all_gather(bundle[0], "ty", axis=1, tiled=True)
    values_all = lax.all_gather(bundle[1], "ty", axis=1, tiled=True)
    marks_key = lax.all_gather(bundle[2], "ty", axis=1, tiled=True)
    attended_blocks, log_total = lax.map(
        partial(attend_block, head_count=head_count, score_scale=score_scale),
        (
            blocked(queries, block_size),
            blocked(keys_all, block_size),
            blocked(values_all, block_size),
            blocked(marks_query, block_size),
            blocked(marks_key, block_size),
        ),
    )
    attended = unblock(attended_blocks).reshape(all_rows, features)
    branch = matmul(attended, out_weight) + out_bias.astype(jnp.float32)
    middle = start_rows + branch
    normed_two, second_pull = jax.vjp(
        layer_norm, middle, second_gain.astype(jnp.float32), second_shift.astype(jnp.float32)
    )
    normed_two_low = normed_two.astype(jnp.bfloat16)
    hidden_pre = matmul(normed_two_low, up_weight) + up_bias.astype(jnp.float32)
    hidden_act, gelu_pull = jax.vjp(exact_gelu, hidden_pre)
    hidden_low = hidden_act.astype(jnp.bfloat16)
    output_rows = middle + (matmul(hidden_low, down_weight) + down_bias.astype(jnp.float32))
    features_low = output_rows.astype(jnp.bfloat16).reshape(
        grid_count, band_rows, band_cols, features
    )
    bundle = (features_low, marks_band, cotangent_band)
    grown = (
        with_halo(bundle[0], (("ty", 1),), 1),
        with_halo(bundle[1], (("ty", 1),), 1),
        with_halo(bundle[2], (("ty", 1),), 1),
    )
    features_pad, marks_pad, cotangent_pad = tuple((pad_side(member, 2) for member in grown))
    ahead_list = []
    behind_list = []
    for vertical in range(3):
        for lateral in range(3):
            inside = (
                marks_pad[:, vertical : vertical + band_rows, lateral : lateral + band_cols]
                == marks_band
            )
            ahead_list.append(
                jnp.where(
                    inside[..., None],
                    features_pad[:, vertical : vertical + band_rows, lateral : lateral + band_cols],
                    0,
                )
            )
            mirror_row = 2 - vertical
            mirror_col = 2 - lateral
            facing = (
                marks_pad[
                    :, mirror_row : mirror_row + band_rows, mirror_col : mirror_col + band_cols
                ]
                == marks_band
            )
            behind_list.append(
                jnp.where(
                    facing[..., None],
                    cotangent_pad[
                        :, mirror_row : mirror_row + band_rows, mirror_col : mirror_col + band_cols
                    ],
                    0,
                )
            )
    ahead = jnp.stack(ahead_list, axis=3)
    behind = jnp.stack(behind_list, axis=3)
    recon_band = jnp.einsum(
        "nhwkd,dkp->nhwp", ahead, pixel_weight, preferred_element_type=jnp.float32
    ) + pixel_bias.astype(jnp.float32)
    pixel_weight_grad = jnp.einsum(
        "nhwkd,nhwp->dkp", ahead, cotangent_band, preferred_element_type=jnp.float32
    )
    pixel_bias_grad = jnp.sum(cotangent_band.astype(jnp.float32), axis=(0, 1, 2))
    final_grad = jnp.einsum(
        "nhwkp,dkp->nhwd", behind, pixel_weight, preferred_element_type=jnp.float32
    ).reshape(all_rows, features)
    lower_grad = final_grad.astype(jnp.bfloat16)
    down_weight_grad = left_product(hidden_low, lower_grad)
    down_bias_grad = jnp.sum(lower_grad.astype(jnp.float32), axis=0)
    pre_grad = gelu_pull(right_product(lower_grad, down_weight))[0].astype(jnp.bfloat16)
    up_weight_grad = left_product(normed_two_low, pre_grad)
    up_bias_grad = jnp.sum(pre_grad.astype(jnp.float32), axis=0)
    middle_part, second_gain_grad, second_shift_grad = second_pull(
        right_product(pre_grad, up_weight)
    )
    middle_grad = final_grad + middle_part
    branch_grad = middle_grad.astype(jnp.bfloat16)
    out_weight_grad = left_product(attended, branch_grad)
    out_bias_grad = jnp.sum(branch_grad.astype(jnp.float32), axis=0)
    attended_grad = (
        right_product(branch_grad, out_weight)
        .astype(jnp.bfloat16)
        .reshape(grid_count, tokens, features)
    )
    query_blocks, key_blocks, value_blocks = lax.map(
        partial(attend_back, head_count=head_count, score_scale=score_scale),
        (
            blocked(queries, block_size),
            blocked(keys_all, block_size),
            blocked(values_all, block_size),
            blocked(marks_query, block_size),
            blocked(marks_key, block_size),
            log_total,
            blocked(attended_grad, block_size),
        ),
    )
    query_grad = unblock(query_blocks)
    bundle = (unblock(key_blocks), unblock(value_blocks))
    key_sum = lax.psum_scatter(
        bundle[0].astype(jnp.bfloat16), "ty", scatter_dimension=1, tiled=True
    )
    value_sum = lax.psum_scatter(
        bundle[1].astype(jnp.bfloat16), "ty", scatter_dimension=1, tiled=True
    )
    projected_grad = jnp.concatenate([query_grad, key_sum, value_sum], axis=-1).reshape(
        all_rows, 3 * features
    )
    qkv_weight_grad = left_product(normed_low, projected_grad)
    query_bias_grad = jnp.sum(query_grad.astype(jnp.float32), axis=(0, 1))
    value_bias_grad = jnp.sum(value_sum.astype(jnp.float32), axis=(0, 1))
    start_part, first_gain_grad, first_shift_grad = first_pull(
        right_product(projected_grad, qkv_weight)
    )
    start_grad = middle_grad + start_part
    inputs_rows = inputs_band.reshape(all_rows, features).astype(jnp.float32)
    input_band = (start_grad + 2.0 * commit_weight * (inputs_rows - start_rows)).astype(
        jnp.bfloat16
    )
    bundle = (
        recon_band.astype(jnp.bfloat16),
        input_band.reshape(grid_count, band_rows, band_cols, features),
    )
    recon_tiles = lax.all_to_all(bundle[0], "tx", split_axis=2, concat_axis=0, tiled=True)
    input_tiles = lax.all_to_all(bundle[1], "tx", split_axis=2, concat_axis=0, tiled=True)
    local_grads = (
        qkv_weight_grad,
        query_bias_grad,
        value_bias_grad,
        out_weight_grad,
        out_bias_grad,
        first_gain_grad,
        first_shift_grad,
        second_gain_grad,
        second_shift_grad,
        up_weight_grad,
        up_bias_grad,
        down_weight_grad,
        down_bias_grad,
        pixel_weight_grad,
        pixel_bias_grad,
    )
    tile_shares = (
        lax.psum_scatter(
            local_grads[0].astype(jnp.bfloat16), ("ty", "tx"), scatter_dimension=0, tiled=True
        ).astype(jnp.float32),
        lax.psum_scatter(
            local_grads[1].astype(jnp.bfloat16), ("ty", "tx"), scatter_dimension=0, tiled=True
        ).astype(jnp.float32),
        lax.psum_scatter(
            local_grads[2].astype(jnp.bfloat16), ("ty", "tx"), scatter_dimension=0, tiled=True
        ).astype(jnp.float32),
        lax.psum_scatter(
            local_grads[3].astype(jnp.bfloat16), ("ty", "tx"), scatter_dimension=0, tiled=True
        ).astype(jnp.float32),
        lax.psum_scatter(
            local_grads[4].astype(jnp.bfloat16), ("ty", "tx"), scatter_dimension=0, tiled=True
        ).astype(jnp.float32),
        lax.psum_scatter(
            local_grads[5].astype(jnp.bfloat16), ("ty", "tx"), scatter_dimension=0, tiled=True
        ).astype(jnp.float32),
        lax.psum_scatter(
            local_grads[6].astype(jnp.bfloat16), ("ty", "tx"), scatter_dimension=0, tiled=True
        ).astype(jnp.float32),
        lax.psum_scatter(
            local_grads[7].astype(jnp.bfloat16), ("ty", "tx"), scatter_dimension=0, tiled=True
        ).astype(jnp.float32),
        lax.psum_scatter(
            local_grads[8].astype(jnp.bfloat16), ("ty", "tx"), scatter_dimension=0, tiled=True
        ).astype(jnp.float32),
        lax.psum_scatter(
            local_grads[9].astype(jnp.bfloat16), ("ty", "tx"), scatter_dimension=0, tiled=True
        ).astype(jnp.float32),
        lax.psum_scatter(
            local_grads[10].astype(jnp.bfloat16), ("ty", "tx"), scatter_dimension=0, tiled=True
        ).astype(jnp.float32),
        lax.psum_scatter(
            local_grads[11].astype(jnp.bfloat16), ("ty", "tx"), scatter_dimension=0, tiled=True
        ).astype(jnp.float32),
        lax.psum_scatter(
            local_grads[12].astype(jnp.bfloat16), ("ty", "tx"), scatter_dimension=0, tiled=True
        ).astype(jnp.float32),
        lax.psum_scatter(
            local_grads[13].astype(jnp.bfloat16), ("ty", "tx"), scatter_dimension=0, tiled=True
        ).astype(jnp.float32),
        lax.psum_scatter(
            local_grads[14].astype(jnp.bfloat16), ("ty", "tx"), scatter_dimension=0, tiled=True
        ).astype(jnp.float32),
    )
    summed = (
        lax.psum(tile_shares[0].astype(jnp.bfloat16), "gr").astype(jnp.float32),
        lax.psum(tile_shares[1].astype(jnp.bfloat16), "gr").astype(jnp.float32),
        lax.psum(tile_shares[2].astype(jnp.bfloat16), "gr").astype(jnp.float32),
        lax.psum(tile_shares[3].astype(jnp.bfloat16), "gr").astype(jnp.float32),
        lax.psum(tile_shares[4].astype(jnp.bfloat16), "gr").astype(jnp.float32),
        lax.psum(tile_shares[5].astype(jnp.bfloat16), "gr").astype(jnp.float32),
        lax.psum(tile_shares[6].astype(jnp.bfloat16), "gr").astype(jnp.float32),
        lax.psum(tile_shares[7].astype(jnp.bfloat16), "gr").astype(jnp.float32),
        lax.psum(tile_shares[8].astype(jnp.bfloat16), "gr").astype(jnp.float32),
        lax.psum(tile_shares[9].astype(jnp.bfloat16), "gr").astype(jnp.float32),
        lax.psum(tile_shares[10].astype(jnp.bfloat16), "gr").astype(jnp.float32),
        lax.psum(tile_shares[11].astype(jnp.bfloat16), "gr").astype(jnp.float32),
        lax.psum(tile_shares[12].astype(jnp.bfloat16), "gr").astype(jnp.float32),
        lax.psum(tile_shares[13].astype(jnp.bfloat16), "gr").astype(jnp.float32),
        lax.psum(tile_shares[14].astype(jnp.bfloat16), "gr").astype(jnp.float32),
    )
    return (
        recon_tiles,
        input_tiles,
        summed[0],
        summed[1],
        summed[2],
        summed[3],
        summed[4],
        summed[5],
        summed[6],
        summed[7],
        summed[8],
        summed[9],
        summed[10],
        summed[11],
        summed[12],
        summed[13],
        summed[14],
    )


far = float(2.0**30)


def nt(left_side, right_side):
    return lax.dot_general(
        left_side, right_side, (((1,), (1,)), ((), ())), preferred_element_type=jnp.float32
    )


def nn(left_side, right_side):
    return lax.dot_general(
        left_side, right_side, (((1,), (0,)), ((), ())), preferred_element_type=jnp.float32
    )


def tn(left_side, right_side):
    return lax.dot_general(
        left_side, right_side, (((0,), (0,)), ((), ())), preferred_element_type=jnp.float32
    )


def attend_kernel(q_ref, k_ref, v_ref, qa_ref, ka_ref, o_ref, col_ref):
    lane = lax.broadcasted_iota(jnp.int32, (1, 128), 1)
    low = lane < 64
    local = lane % 64
    one = jnp.ones((), jnp.bfloat16)
    queries, key_rows, values = q_ref[...], k_ref[...], v_ref[...]
    query_marks, key_marks = qa_ref[...], ka_ref[...]
    outs = []
    logs = []
    for head in range(2):
        own = low if head == 0 else ~low
        scores = nt(jnp.where(own, queries, query_marks), jnp.where(own, key_rows, key_marks))
        top = jnp.max(scores, axis=1, keepdims=True)
        weights = jnp.exp(scores - top).astype(jnp.bfloat16)
        sums = nn(weights, jnp.where(own, values, one))
        outs.append(sums / pltpu.roll(sums, 64, 1))
        logs.append(top + jnp.log(sums))
    o_ref[...] = jnp.where(low, outs[0], outs[1]).astype(jnp.bfloat16)
    minus = -jnp.where(low, logs[1], logs[0])
    first = minus.astype(jnp.bfloat16).astype(jnp.float32)
    second = (minus - first).astype(jnp.bfloat16).astype(jnp.float32)
    third = minus - first - second
    columns = jnp.where(
        local == 3,
        first,
        jnp.where(local == 4, second, jnp.where(local == 5, third, query_marks.astype(jnp.float32))),
    )
    col_ref[...] = columns.astype(jnp.bfloat16)


def attend(queries, key_rows, values, query_marks, key_marks):
    tokens, features = queries.shape
    pair = pl.BlockSpec((tokens, 128), lambda i: (0, i))
    shared = pl.BlockSpec((tokens, 128), lambda i: (0, 0))
    shape = pltpu.HBM((tokens, features), jnp.bfloat16)
    return pl.pallas_call(
        attend_kernel,
        grid=(features // 128,),
        in_specs=[pair, pair, pair, shared, shared],
        out_specs=[pair, pair],
        out_shape=[shape, shape],
        compiler_params=pltpu.CompilerParams(vmem_limit_bytes=60 * 2**20),
        cost_estimate=pl.CostEstimate(
            flops=16 * tokens * tokens * features,
            bytes_accessed=10 * tokens * features,
            transcendentals=tokens * tokens * features // 64,
        ),
        name="attend",
    )(queries, key_rows, values, query_marks, key_marks)


def groups(down, across, rows, cols):
    for part in range(down * across):
        for r in range(rows):
            grid_row = (part // across) * rows + r
            yield (part * rows + r) * cols, (grid_row * across + part % across) * cols


def conv_kernel(rows_ref, mask_ref, weight_ref, bias_ref, out_ref, plain_ref, shifted, total, other, *, tiling):
    width, cols = tiling[1] * tiling[3], tiling[3]
    tap = pl.program_id(0)
    tokens, features = rows_ref.shape

    @pl.when(tap == 0)
    def _():
        other[...] = rows_ref[...].astype(jnp.float32)
        for tiled, plain in groups(*tiling):
            total[plain : plain + cols, :] = other[tiled : tiled + cols, :]
        rows = total[...]
        plain_ref[...] = rows.astype(jnp.bfloat16)
        for j in range(3):
            moved = rows if j == 1 else pltpu.roll(rows, (1 - j) % tokens, 0)
            shifted[j, 0:width, :] = jnp.zeros((width, features), jnp.bfloat16)
            shifted[j, width + tokens :, :] = jnp.zeros((width, features), jnp.bfloat16)
            shifted[j, width : width + tokens, :] = moved.astype(jnp.bfloat16)
        total[...] = jnp.zeros_like(total)

    below, right = tap // 3, tap % 3
    step = tokens // 4
    for i in range(4):
        rows = slice(i * step, (i + 1) * step)
        first = pl.multiple_of(below * width + i * step, width)
        marks = mask_ref[1, width + i * step : width + (i + 1) * step, :]
        same = mask_ref[right, pl.ds(first, step), :] == marks
        mask = jnp.where(same, 1.0, 0.0).astype(jnp.bfloat16)
        mask = jnp.concatenate([mask] * (features // 128), axis=1)
        total[rows, :] += nn(shifted[right, pl.ds(first, step), :] * mask, weight_ref[0])

    @pl.when(tap == 8)
    def _():
        for tiled, plain in groups(*tiling):
            other[tiled : tiled + cols, :] = total[plain : plain + cols, :]
        out_ref[...] = (other[...] + bias_ref[...].astype(jnp.float32)).astype(jnp.bfloat16)


def in_hbm(shape, dtype=jnp.bfloat16):
    return pltpu.HBM(shape, dtype)


def conv(rows, masks, weight, bias, tiling):
    tokens, features = rows.shape
    width = tiling[1] * tiling[3]

    def whole(shape):
        return pl.BlockSpec(shape, lambda k: (0,) * len(shape), pipeline_mode=pl.Buffered(1))

    return pl.pallas_call(
        partial(conv_kernel, tiling=tiling),
        grid=(9,),
        in_specs=[
            whole((tokens, features)),
            whole(masks.shape),
            pl.BlockSpec((1, features, features), lambda k: (k, 0, 0)),
            whole((1, features)),
        ],
        out_specs=[whole((tokens, features))] * 2,
        out_shape=[in_hbm((tokens, features))] * 2,
        scratch_shapes=[
            pltpu.VMEM((3, tokens + 2 * width, features), jnp.bfloat16),
            pltpu.VMEM((tokens, features), jnp.float32),
            pltpu.VMEM((tokens, features), jnp.float32),
        ],
        compiler_params=pltpu.CompilerParams(vmem_limit_bytes=60 * 2**20),
        cost_estimate=pl.CostEstimate(
            flops=18 * tokens * features * features,
            bytes_accessed=18 * features * features + 4 * tokens * features,
            transcendentals=0,
        ),
        name="conv",
    )(rows, masks, weight, bias)


def marks_kernel(parts_ref, moved_ref, query_ref, key_ref, *, down, across, rows, cols):
    width = across * cols
    tokens = down * rows * width
    turned = parts_ref[...].astype(jnp.float32).T
    lane = lax.broadcasted_iota(jnp.int32, (rows * cols, 128), 1) % 64
    nowhere = jnp.full((width, 128), -1.0, jnp.float32)
    for j in range(3):
        moved_ref[j, 0:width, :] = nowhere
        moved_ref[j, width + tokens :, :] = nowhere
    for part in range(down * across):
        spread = jnp.broadcast_to(turned[:, part : part + 1], (rows * cols, 128))
        hot = spread == lane.astype(jnp.float32)
        here = slice(part * rows * cols, (part + 1) * rows * cols)
        query_ref[here, :] = jnp.where(hot, 1.0, 0.0).astype(jnp.bfloat16)
        key_ref[here, :] = jnp.where((lane < 3) & ~hot, -far, 0.0).astype(jnp.bfloat16)
        for r in range(rows):
            first = ((part // across) * rows + r) * width + (part % across) * cols + width
            moved_ref[1, first : first + cols, :] = spread[r * cols : (r + 1) * cols]
    marks = moved_ref[1, width : width + tokens, :]
    column = lax.broadcasted_iota(jnp.int32, (tokens, 128), 0) % width
    left = jnp.where(column == 0, -1.0, pltpu.roll(marks, 1, 0))
    right = jnp.where(column == width - 1, -1.0, pltpu.roll(marks, tokens - 1, 0))
    moved_ref[0, width : width + tokens, :] = left
    moved_ref[2, width : width + tokens, :] = right


def spread_marks(parts, down, across, rows, cols):
    tokens = down * across * rows * cols
    low = in_hbm((tokens, 128))
    return pl.pallas_call(
        partial(marks_kernel, down=down, across=across, rows=rows, cols=cols),
        out_shape=[
            in_hbm((3, tokens + 2 * across * cols, 128), jnp.float32),
            low,
            low,
        ],
        compiler_params=pltpu.CompilerParams(vmem_limit_bytes=60 * 2**20),
        name="spread_marks",
    )(parts)


def normalize(values):
    center = values - jnp.mean(values, axis=-1, keepdims=True)
    scale = lax.rsqrt(jnp.mean(center * center, axis=-1, keepdims=True) + epsilon)
    return center * scale, scale


def norm_back(grad, gain, unit, scale):
    scaled = grad * gain
    mean = jnp.mean(scaled, axis=-1, keepdims=True)
    along = jnp.mean(scaled * unit, axis=-1, keepdims=True)
    return scale * (scaled - mean - unit * along)


def row(ref):
    return ref[...].astype(jnp.float32)


def add_rows(ref, values):
    ref[...] += jnp.sum(values, axis=0, keepdims=True)


def enter_kernel(
    codes_ref, gain_ref, shift_ref, weight_ref, qb_ref, vb_ref, normed_ref, q_ref, k_ref, v_ref
):
    features = codes_ref.shape[1]
    unit, _ = normalize(row(codes_ref))
    normed = (unit * row(gain_ref) + row(shift_ref)).astype(jnp.bfloat16)
    normed_ref[...] = normed
    queries = nn(normed, weight_ref[:, 0:features]) + row(qb_ref)
    q_ref[...] = queries.astype(jnp.bfloat16) * jnp.asarray(HEAD_DIM**-0.5, jnp.bfloat16)
    k_ref[...] = nn(normed, weight_ref[:, features : 2 * features]).astype(jnp.bfloat16)
    values = nn(normed, weight_ref[:, 2 * features :]) + row(vb_ref)
    v_ref[...] = values.astype(jnp.bfloat16)


def held(shape):
    return pl.BlockSpec(shape, lambda i: (0,) * len(shape), pipeline_mode=pl.Buffered(1))


def by_rows(step, columns):
    return pl.BlockSpec((step, columns), lambda i: (i, 0))


def ask_kernel(ids_ref, marks_ref, got_ref, slot_ref, sends, got, sent, received, *, share, slots):
    gr, ty, tx = lax.axis_index("gr"), lax.axis_index("ty"), lax.axis_index("tx")
    across = lax.axis_size("tx")
    members = lax.axis_size("ty") * across
    me = ty * across + tx
    others = [lax.rem(me + step, members) for step in range(1, members)]

    def place(member):
        return (gr, member // across, lax.rem(member, across))

    barrier = pltpu.get_barrier_semaphore()
    for member in others:
        pl.semaphore_signal(
            barrier, inc=1, device_id=place(member), device_id_type=pl.DeviceIdType.MESH
        )
    grids, each = ids_ref.shape
    turned = ids_ref[...].astype(jnp.float32).T
    lane = lax.broadcasted_iota(jnp.int32, (each, 128), 1)
    earlier = lax.broadcasted_iota(jnp.int32, (each, each), 1)
    earlier = earlier < lax.broadcasted_iota(jnp.int32, (each, each), 0)
    earlier = jnp.where(earlier, 1.0, 0.0).astype(jnp.bfloat16)
    counts = jnp.zeros((1, 128), jnp.float32)
    high = jnp.zeros((128, 128), jnp.float32)
    low = jnp.zeros((128, 128), jnp.float32)
    for grid in range(grids):
        ids = jnp.broadcast_to(turned[:, grid : grid + 1], (each, 128)).astype(jnp.int32)
        holder = jnp.zeros_like(ids)
        for member in range(1, members):
            holder = holder + jnp.where(ids >= member * share, 1, 0)
        offset = ids - holder * share
        belongs = jnp.where(holder == lane, 1.0, 0.0)
        ranks = nn(earlier, belongs.astype(jnp.bfloat16)) + counts
        counts = counts + jnp.sum(belongs, axis=0, keepdims=True)
        rank = jnp.sum(belongs * ranks, axis=1, keepdims=True)
        rank = jnp.broadcast_to(rank, (each, 128)).astype(jnp.int32)
        slot_ref[grid * each : (grid + 1) * each, :] = holder * slots + rank
        second = jnp.where(rank >= 128, 1, 0)
        of_row = 2 * holder + second == lane
        of_lane = jnp.where(rank - 128 * second == lane, 1.0, 0.0).astype(jnp.bfloat16)
        upper = jnp.floor(offset.astype(jnp.float32) * (1.0 / 64.0))
        lower = offset.astype(jnp.float32) - 64.0 * upper
        high = high + tn(jnp.where(of_row, upper, 0.0).astype(jnp.bfloat16), of_lane)
        low = low + tn(jnp.where(of_row, lower, 0.0).astype(jnp.bfloat16), of_lane)
    wanted = (high * 64.0 + low).astype(jnp.int32)
    sends[...] = jnp.zeros_like(sends)
    for member in range(members):
        sends[member, 0:2, :] = wanted[2 * member : 2 * member + 2, :]
        sends[member, 2:3, :] = marks_ref[member : member + 1, :]

    def put(i):
        return pltpu.make_async_remote_copy(
            src_ref=sends.at[others[i]],
            dst_ref=got.at[me],
            send_sem=sent.at[i],
            recv_sem=received.at[i],
            device_id=place(others[i]),
            device_id_type=pl.DeviceIdType.MESH,
        )

    pl.semaphore_wait(barrier, members - 1)
    for i in range(members - 1):
        put(i).start()
    got[me] = sends[me]
    for i in range(members - 1):
        put(i).wait_send()
        put(i).wait_recv()
    got_ref[...] = got[...]


def ask(ids, marks, share, slots):
    members, each = ids.shape
    inside = pl.BlockSpec(memory_space=pltpu.VMEM)
    box = (members, 8, each)
    return pl.pallas_call(
        partial(ask_kernel, share=share, slots=slots),
        in_specs=[inside, inside],
        out_specs=[inside, inside],
        out_shape=[
            jax.ShapeDtypeStruct(box, jnp.int32),
            jax.ShapeDtypeStruct((members * each, 128), jnp.int32),
        ],
        scratch_shapes=[pltpu.VMEM(box, jnp.int32)] * 2
        + [pltpu.SemaphoreType.DMA((members - 1,))] * 2,
        compiler_params=pltpu.CompilerParams(
            collective_id=2, has_side_effects=True, vmem_limit_bytes=60 * 2**20
        ),
        cost_estimate=pl.CostEstimate(
            flops=20 * 10**9, bytes_accessed=40 * 10**6, transcendentals=0
        ),
        name="ask",
    )(ids, marks)


def enter(codes, gain, shift, weight, query_bias, value_bias, step=256):
    tokens, features = codes.shape
    block = by_rows(step, features)
    vector = held((1, features))
    return pl.pallas_call(
        enter_kernel,
        grid=(tokens // step,),
        in_specs=[block, vector, vector, held(weight.shape), vector, vector],
        out_specs=[block] * 4,
        out_shape=[in_hbm((tokens, features))] * 4,
        compiler_params=pltpu.CompilerParams(vmem_limit_bytes=60 * 2**20),
        cost_estimate=pl.CostEstimate(
            flops=6 * tokens * features * features,
            bytes_accessed=6 * features * features + 10 * tokens * features,
            transcendentals=0,
        ),
        name="enter",
    )(codes, gain, shift, weight, query_bias, value_bias)


def gelu_parts(values):
    spread = jnp.exp(-0.5 * values * values)
    t = 1.0 / (1.0 + (0.3275911 * 0.5**0.5) * jnp.abs(values))
    series = 0.5 * 1.061405429
    for factor in (-1.453152027, 1.421413741, -0.284496736, 0.254829592):
        series = series * t + 0.5 * factor
    tail = series * t * spread
    upto = jnp.where(values < 0.0, tail, 1.0 - tail)
    return values * upto, upto + values * spread * 0.3989422804014327


def middle_kernel(
    codes_ref,
    attended_ref,
    final_ref,
    hidden_grad_ref,
    out_weight_ref,
    up_ref,
    down_ref,
    out_bias_ref,
    gain_ref,
    shift_ref,
    up_bias_ref,
    down_bias_ref,
    features_ref,
    normed_ref,
    hidden_ref,
    pre_ref,
    middle_grad_ref,
    branch_ref,
    attended_grad_ref,
    out_bias_sum,
    gain_sum,
    shift_sum,
    up_bias_sum,
):
    @pl.when(pl.program_id(0) == 0)
    def _():
        for ref in (out_bias_sum, gain_sum, shift_sum, up_bias_sum):
            ref[...] = jnp.zeros_like(ref)

    features = codes_ref.shape[1]
    middle = row(codes_ref) + (nn(attended_ref[...], out_weight_ref[...]) + row(out_bias_ref))
    unit, scale = normalize(middle)
    normed = (unit * row(gain_ref) + row(shift_ref)).astype(jnp.bfloat16)
    normed_ref[...] = normed
    total = middle + row(down_bias_ref)
    grad = jnp.zeros_like(middle)
    for first in range(0, up_ref.shape[1], features):
        columns = slice(first, first + features)
        weight = up_ref[:, columns]
        hidden_pre = nn(normed, weight) + up_bias_ref[:, columns].astype(jnp.float32)
        act, slope = gelu_parts(hidden_pre)
        hidden = act.astype(jnp.bfloat16)
        hidden_ref[columns, :] = hidden.T
        pre = (hidden_grad_ref[:, columns].astype(jnp.float32) * slope).astype(jnp.bfloat16)
        pre_ref[:, columns] = pre
        up_bias_sum[:, columns] += jnp.sum(pre.astype(jnp.float32), axis=0, keepdims=True)
        total = total + nn(hidden, down_ref[columns, :])
        grad = grad + nt(pre, weight)
    features_ref[...] = total.astype(jnp.bfloat16)
    add_rows(gain_sum, grad * unit)
    add_rows(shift_sum, grad)
    middle_grad = final_ref[...] + norm_back(grad, row(gain_ref), unit, scale)
    middle_grad_ref[...] = middle_grad
    branch = middle_grad.astype(jnp.bfloat16)
    branch_ref[...] = branch
    add_rows(out_bias_sum, branch.astype(jnp.float32))
    attended_grad_ref[...] = nt(branch, out_weight_ref[...]).astype(jnp.bfloat16)


def middle_block(
    codes,
    attended,
    final_grad,
    hidden_grad,
    out_weight,
    up_weight,
    down_weight,
    out_bias,
    gain,
    shift,
    up_bias,
    down_bias,
    step=256,
):
    tokens, features = codes.shape
    wide = up_weight.shape[1]
    block = by_rows(step, features)
    broad = by_rows(step, wide)
    vector = held((1, features))

    def like(columns, dtype=jnp.bfloat16, rows=tokens):
        return in_hbm((rows, columns), dtype)

    def total(columns):
        return pl.BlockSpec((1, columns), lambda i: (0, 0))

    return pl.pallas_call(
        middle_kernel,
        grid=(tokens // step,),
        in_specs=[
            block,
            block,
            block,
            broad,
            held(out_weight.shape),
            held(up_weight.shape),
            held(down_weight.shape),
            vector,
            vector,
            vector,
            held((1, wide)),
            vector,
        ],
        out_specs=[block, block, pl.BlockSpec((wide, step), lambda i: (0, i)), broad, block, block, block]
        + [total(features)] * 3
        + [total(wide)],
        out_shape=[
            like(features),
            like(features),
            like(tokens, rows=wide),
            like(wide),
            like(features, jnp.float32),
            like(features),
            like(features),
        ]
        + [like(features, jnp.float32, 1)] * 3
        + [like(wide, jnp.float32, 1)],
        compiler_params=pltpu.CompilerParams(vmem_limit_bytes=60 * 2**20),
        cost_estimate=pl.CostEstimate(
            flops=2 * tokens * features * (2 * features + 3 * wide),
            bytes_accessed=4 * features * wide + 6 * tokens * wide + 16 * tokens * features,
            transcendentals=2 * tokens * wide,
        ),
        name="middle",
    )(
        codes,
        attended,
        final_grad,
        hidden_grad,
        out_weight,
        up_weight,
        down_weight,
        out_bias,
        gain,
        shift,
        up_bias,
        down_bias,
    )


def fetch_kernel(
    fetched_ref,
    slot_ref,
    cotangent_ref,
    moved_ref,
    taps_ref,
    down_ref,
    codes_out,
    final_out,
    low_out,
    behind_out,
    hidden_out,
    pixel_bias_sum,
    down_bias_sum,
    got,
    sends,
    shifted,
    total,
    other,
    low,
    taken,
    weight,
    down,
    hidden,
    hop_sent,
    hop_got,
    code_sent,
    code_got,
    own_sem,
    weight_sem,
    taken_sem,
    down_sem,
    hidden_sem,
    out_sem,
    *,
    tiling,
):
    gr, ty, tx = lax.axis_index("gr"), lax.axis_index("ty"), lax.axis_index("tx")
    across = lax.axis_size("tx")
    members = lax.axis_size("ty") * across
    me = ty * across + tx
    others = [lax.rem(me + step, members) for step in range(1, members)]
    tokens, features = cotangent_ref.shape
    each = tokens // members
    wide = tiling[1] * tiling[3]

    def place(member):
        return (gr, member // across, lax.rem(member, across))

    barrier = pltpu.get_barrier_semaphore()
    for member in others:
        pl.semaphore_signal(
            barrier, inc=1, device_id=place(member), device_id_type=pl.DeviceIdType.MESH
        )
    pl.semaphore_wait(barrier, members - 1)

    def hop_put(i):
        return pltpu.make_async_remote_copy(
            src_ref=fetched_ref.at[others[i]],
            dst_ref=got.at[me],
            send_sem=hop_sent.at[i],
            recv_sem=hop_got.at[i],
            device_id=place(others[i]),
            device_id_type=pl.DeviceIdType.MESH,
        )

    def code_put(i):
        return pltpu.make_async_remote_copy(
            src_ref=sends.at[others[i]],
            dst_ref=codes_out.at[me],
            send_sem=code_sent.at[i],
            recv_sem=code_got.at[i],
            device_id=place(others[i]),
            device_id_type=pl.DeviceIdType.MESH,
        )

    own_rows = pltpu.make_async_copy(fetched_ref.at[me], got.at[me], own_sem.at[0])
    own_codes = pltpu.make_async_copy(sends.at[me], codes_out.at[me], own_sem.at[1])
    for i in range(members - 1):
        hop_put(i).start()
    own_rows.start()

    def weight_copy(tap):
        slot = lax.rem(tap, 2)
        return pltpu.make_async_copy(taps_ref.at[tap], weight.at[slot], weight_sem.at[slot])

    def taken_copy(tap):
        slot = lax.rem(tap, 2)
        columns = pl.ds(pl.multiple_of(tap * features, 128), features)
        return pltpu.make_async_copy(taken.at[slot], behind_out.at[:, columns], taken_sem.at[slot])

    def down_copy(j):
        slot = lax.rem(j, 2)
        rows = pl.ds(pl.multiple_of(j * features, 128), features)
        return pltpu.make_async_copy(down_ref.at[rows], down.at[slot], down_sem.at[slot])

    def hidden_copy(j):
        slot = lax.rem(j, 2)
        columns = pl.ds(pl.multiple_of(j * features, 128), features)
        return pltpu.make_async_copy(hidden.at[slot], hidden_out.at[:, columns], hidden_sem.at[slot])

    weight_copy(0).start()
    down_copy(0).start()
    other[...] = cotangent_ref[...].astype(jnp.float32)
    pixel_bias_sum[...] = jnp.sum(other[...], axis=0, keepdims=True)
    for tiled, plain in groups(*tiling):
        total[plain : plain + tiling[3], :] = other[tiled : tiled + tiling[3], :]
    rows_plain = total[...]
    for j in range(3):
        moved_rows = rows_plain if j == 1 else pltpu.roll(rows_plain, (1 - j) % tokens, 0)
        shifted[j, 0:wide, :] = jnp.zeros((wide, features), jnp.bfloat16)
        shifted[j, wide + tokens :, :] = jnp.zeros((wide, features), jnp.bfloat16)
        shifted[j, wide : wide + tokens, :] = moved_rows.astype(jnp.bfloat16)
    total[...] = jnp.zeros_like(total)

    def one_tap(tap, _):
        slot = lax.rem(tap, 2)
        weight_copy(tap).wait()
        pl.when(tap < 8)(lambda: weight_copy(tap + 1).start())
        pl.when(tap >= 2)(lambda: taken_copy(tap - 2).wait())
        below, right = 2 - tap // 3, 2 - lax.rem(tap, 3)
        step = tokens // 4
        for i in range(4):
            rows = slice(i * step, (i + 1) * step)
            first = pl.multiple_of(below * wide + i * step, wide)
            here = moved_ref[1, wide + i * step : wide + (i + 1) * step, :]
            same = moved_ref[right, pl.ds(first, step), :] == here
            mask = jnp.where(same, 1.0, 0.0).astype(jnp.bfloat16)
            mask = jnp.concatenate([mask] * (features // 128), axis=1)
            piece = shifted[right, pl.ds(first, step), :] * mask
            taken[slot, rows, :] = piece
            total[rows, :] += nt(piece, weight[slot])
        taken_copy(tap).start()
        return 0

    lax.fori_loop(0, 9, one_tap, 0)
    for tiled, plain in groups(*tiling):
        other[tiled : tiled + tiling[3], :] = total[plain : plain + tiling[3], :]
    low[...] = other[...].astype(jnp.bfloat16)
    results = [
        pltpu.make_async_copy(other, final_out, out_sem.at[0]),
        pltpu.make_async_copy(low, low_out, out_sem.at[1]),
    ]
    for result in results:
        result.start()
    down_bias_sum[...] = jnp.sum(low[...].astype(jnp.float32), axis=0, keepdims=True)

    own_rows.wait()
    for i in range(members - 1):
        hop_put(i).wait_recv()
    arrived = got[...].reshape(got.shape[0] * got.shape[1], features)
    lane = lax.broadcasted_iota(jnp.int32, (each, 128), 1)
    for member in range(members):
        slots = slot_ref[member * each : (member + 1) * each, :]
        hot = [
            jnp.where(slots == lane + first, 1.0, 0.0).astype(jnp.bfloat16)
            for first in range(0, arrived.shape[0], 128)
        ]
        rows = nn(jnp.concatenate(hot, axis=1), arrived)
        sends[member] = rows.astype(jnp.bfloat16)
    for i in range(members - 1):
        code_put(i).start()
    own_codes.start()

    def one_block(j, _):
        slot = lax.rem(j, 2)
        down_copy(j).wait()
        pl.when(j < 3)(lambda: down_copy(j + 1).start())
        pl.when(j >= 2)(lambda: hidden_copy(j - 2).wait())
        hidden[slot] = nt(low[...], down[slot]).astype(jnp.bfloat16)
        hidden_copy(j).start()
        return 0

    lax.fori_loop(0, 4, one_block, 0)
    for copy in (taken_copy(7), taken_copy(8), hidden_copy(2), hidden_copy(3), own_codes, *results):
        copy.wait()
    for i in range(members - 1):
        hop_put(i).wait_send()
        code_put(i).wait_send()
        code_put(i).wait_recv()


def fetch(fetched, slots, cotangent, moved, taps, down_weight, tiling):
    tokens, features = cotangent.shape
    members = tiling[0] * tiling[1]
    blocks = down_weight.shape[0] // features
    anywhere = pl.BlockSpec(memory_space=pl.ANY)
    inside = pl.BlockSpec(memory_space=pltpu.VMEM)
    dma = pltpu.SemaphoreType.DMA
    low, wide = jnp.bfloat16, jnp.float32
    padded = tokens + 2 * tiling[1] * tiling[3]
    return pl.pallas_call(
        partial(fetch_kernel, tiling=tiling),
        in_specs=[anywhere, inside, inside, inside, anywhere, anywhere],
        out_specs=[anywhere] * 5 + [inside] * 2,
        out_shape=[
            jax.ShapeDtypeStruct((members, tokens // members, features), low),
            jax.ShapeDtypeStruct((tokens, features), wide),
            jax.ShapeDtypeStruct((tokens, features), low),
            jax.ShapeDtypeStruct((tokens, 9 * features), low),
            jax.ShapeDtypeStruct((tokens, blocks * features), low),
            jax.ShapeDtypeStruct((1, features), wide),
            jax.ShapeDtypeStruct((1, features), wide),
        ],
        scratch_shapes=[
            pltpu.VMEM(fetched.shape, low),
            pltpu.VMEM((members, tokens // members, features), low),
            pltpu.VMEM((3, padded, features), low),
            pltpu.VMEM((tokens, features), wide),
            pltpu.VMEM((tokens, features), wide),
            pltpu.VMEM((tokens, features), low),
            pltpu.VMEM((2, tokens, features), low),
            pltpu.VMEM((2, features, features), low),
            pltpu.VMEM((2, features, features), low),
            pltpu.VMEM((2, tokens, features), low),
        ]
        + [dma((members - 1,))] * 4
        + [dma((2,))] * 6,
        compiler_params=pltpu.CompilerParams(
            collective_id=3, has_side_effects=True, vmem_limit_bytes=60 * 2**20
        ),
        cost_estimate=pl.CostEstimate(
            flops=26 * tokens * features * features,
            bytes_accessed=40 * tokens * features,
            transcendentals=0,
        ),
        name="fetch",
    )(fetched, slots, cotangent, moved, taps, down_weight)


def finish_kernel(*refs, blocks, homes, lead, slots, got_slots, tiling):
    (
        q_ref,
        k_ref,
        v_ref,
        col_ref,
        ka_ref,
        o_ref,
        g_ref,
        codes_ref,
        middle_ref,
        features_ref,
        behind_ref,
        normed_two_ref,
        pre_ref,
        hidden_ref,
        lower_ref,
        branch_ref,
        normed_ref,
        weight_ref,
        recon_ref,
        gain_ref,
        out_bias_sum,
        second_gain_sum,
        second_shift_sum,
        up_bias_sum,
        down_bias_sum,
        pixel_bias_sum,
    ) = refs[:26]
    outs = refs[26:31]
    vector_out, recon_out, share_out = refs[31:34]
    refs = refs[34:]
    (parts, got0, got1, got2, got3, got4, whole) = refs[:7]
    (operands, turned, heads, marks, sums, sums_got, middle, share, k_sum, v_sum, dqkv) = refs[7:18]
    (s0, r0, s1, r1, s2, r2, s3, r3, s4, r4, s5, r5, s6, r6) = refs[18:32]
    (out_sem, operand_sem, turned_sem, head_sem, once_sem, free, own_sem) = refs[32:39]
    (recon_sent, recon_got, share_sent, share_got, sums_sent, sums_recv) = refs[39:45]
    count = (blocks + 1) // 2
    tokens, features = normed_ref.shape
    each = tokens // (tiling[0] * tiling[1])
    gr, ty, tx = lax.axis_index("gr"), lax.axis_index("ty"), lax.axis_index("tx")
    x, core, half, par = gr // 2, gr % 2, tx // 2, tx % 2
    across = lax.axis_size("tx")
    members = lax.axis_size("ty") * across
    me = ty * across + tx
    mate = (2 * x + 1 - core, ty, tx)
    over_x = (2 * (1 - x) + core, ty, tx)
    over_y = (gr, 1 - ty, tx)
    near = (gr, ty, half * 2 + (1 - par))
    away = (gr, ty, (1 - half) * 2 + par)
    others = [lax.rem(me + step, members) for step in range(1, members)]

    def place(member):
        return (gr, member // across, lax.rem(member, across))

    barrier = pltpu.get_barrier_semaphore()
    greeted = [mate, over_x] + [place(member) for member in others]
    for device in greeted:
        pl.semaphore_signal(barrier, inc=1, device_id=device, device_id_type=pl.DeviceIdType.MESH)
    pl.semaphore_wait(barrier, len(greeted))
    width = features // 2
    own_columns = pl.ds(pl.multiple_of(core * width, 128), width)

    def put(source, target, sent, received, device):
        return pltpu.make_async_remote_copy(
            src_ref=source,
            dst_ref=target,
            send_sem=sent,
            recv_sem=received,
            device_id=device,
            device_id_type=pl.DeviceIdType.MESH,
        )

    def recon_put(i):
        member = others[i]
        return put(
            recon_ref.at[member], recon_out.at[me], recon_sent.at[i], recon_got.at[i], place(member)
        )

    def share_put(i, member=None):
        member = others[i] if member is None else member
        rows = pl.ds(pl.multiple_of(member * each, 128), each)
        return put(share.at[rows], share_out.at[me], share_sent.at[i], share_got.at[i], place(member))

    def columns(ref, index):
        return ref.at[:, pl.ds(pl.multiple_of(index * features, 128), features)]

    def operand(i, source):
        return pltpu.make_async_copy(source, operands.at[i], operand_sem.at[i])

    def load(sources):
        for i, source in enumerate(sources):
            operand(i, source).start()

    def load_operands(c):
        @pl.when(c < 4)
        def _():
            load([features_ref, columns(behind_ref, 2 * c), features_ref, columns(behind_ref, 2 * c + 1)])

        @pl.when((c == 4) | (c == 5))
        def _():
            load([lower_ref] * 4)
            for b in range(2):
                turned_copy(b, 2 * (c - 4) + b).start()

        @pl.when(c == 6)
        def _():
            load([normed_ref, gradient(0), normed_ref, gradient(1)])

        @pl.when(c == 7)
        def _():
            load([normed_ref, gradient(2), features_ref, columns(behind_ref, 8)])

        @pl.when(c == 8)
        def _():
            load([o_ref, branch_ref, normed_two_ref, columns(pre_ref, 0)])

        @pl.when(c == 9)
        def _():
            load([normed_two_ref, columns(pre_ref, 1), normed_two_ref, columns(pre_ref, 2)])

        @pl.when(c == 10)
        def _():
            load([normed_two_ref, columns(pre_ref, 3), lower_ref, lower_ref])

    def gradient(i):
        return dqkv.at[i, pl.ds(0, tokens)]

    def turned_copy(b, index):
        return pltpu.make_async_copy(hidden_ref.at[:, index], turned.at[b], turned_sem.at[b])

    def wait_operands():
        for i in range(4):
            operand(i, normed_ref).wait()

    def level0(c, b):
        slot = lax.rem(c, slots)
        return put(
            parts.at[slot, b, 1 - core], got0.at[lax.rem(c, got_slots), b], s0.at[c, b], r0.at[c, b], mate
        )

    def both_x(c):
        return (c == 2) | (c == 7)

    def only_y(c):
        return (c < count - 1) & (c != 2) & (c != 7)

    def level1x(c, b=0):
        slot = lax.rem(c, slots)
        return put(
            parts.at[slot, b, core, :, :, :, 1 - x], got1.at[c, b], s1.at[c, b], r1.at[c, b], over_x
        )

    def level1y(c):
        slot = lax.rem(c, slots)
        return put(parts.at[slot, 1, core, 1 - ty], got1.at[c, 1], s1.at[c, 1], r1.at[c, 1], over_y)

    def level2y(c, b=0):
        return put(got1.at[c, b, 1 - ty], got2.at[c, b], s2.at[c, b], r2.at[c, b], over_y)

    def level2x(c):
        return put(got1.at[c, 1, :, :, 1 - x], got2.at[c, 1], s2.at[c, 1], r2.at[c, 1], over_x)

    def level3(c):
        return put(got2.at[c, :, :, 1 - par], got3.at[c], s3.at[c], r3.at[c], near)

    def level4(c):
        return put(got3.at[c, :, 1 - half], got4.at[c], s4.at[c], r4.at[c], away)

    def level5(c):
        where = whole.at[pl.ds(2 * c, 2), x, :, own_columns]
        return put(where, where, s5.at[c], r5.at[c], over_x)

    def level6(c):
        where = whole.at[pl.ds(2 * c, 2), :, :, own_columns]
        return put(where, where, s6.at[c], r6.at[c], mate)

    def stage1(c):
        slot, got_slot = lax.rem(c, slots), lax.rem(c, got_slots)
        for b in range(2):

            @pl.when((b == 0) | (c < count - 1))
            def _():
                level0(c, b).wait_recv()

                def add(i, _):
                    y, h, p = i // 4, lax.rem(i // 2, 2), lax.rem(i, 2)
                    sum_of = parts[slot, b, core, y, h, p] + got0[got_slot, b, y, h, p]
                    parts[slot, b, core, y, h, p] = sum_of
                    return 0

                lax.fori_loop(0, 8, add, 0)

        @pl.when(c < count - got_slots)
        def _():
            pl.semaphore_signal(free, inc=1, device_id=mate, device_id_type=pl.DeviceIdType.MESH)

        level1x(c).start()
        pl.when(only_y(c))(lambda: level1y(c).start())
        pl.when(both_x(c))(lambda: level1x(c, 1).start())

    def stage2(c):
        slot = lax.rem(c, slots)
        level1x(c).wait_recv()
        got1[c, 0] = got1[c, 0] + parts[slot, 0, core, :, :, :, x]
        level2y(c).start()

        @pl.when(only_y(c))
        def _():
            level1y(c).wait_recv()
            got1[c, 1] = got1[c, 1] + parts[slot, 1, core, ty]
            level2x(c).start()
            level1y(c).wait_send()

        @pl.when(both_x(c))
        def _():
            level1x(c, 1).wait_recv()
            got1[c, 1] = got1[c, 1] + parts[slot, 1, core, :, :, :, x]
            level2y(c, 1).start()
            level1x(c, 1).wait_send()

        level1x(c).wait_send()

    def stage3(c):
        level2y(c).wait_recv()
        got2[c, 0] = got2[c, 0] + got1[c, 0, ty]

        @pl.when(only_y(c))
        def _():
            level2x(c).wait_recv()
            got2[c, 1] = got2[c, 1] + got1[c, 1, :, :, x]

        @pl.when(both_x(c))
        def _():
            level2y(c, 1).wait_recv()
            got2[c, 1] = got2[c, 1] + got1[c, 1, ty]

        @pl.when(c == count - 1)
        def _():
            got2[c, 1] = jnp.zeros(got2.shape[2:], jnp.bfloat16)

        level3(c).start()

    def stage4(c):
        level3(c).wait_recv()
        got3[c] = got3[c] + got2[c, :, :, par]
        level4(c).start()

    def stage5(c):
        level4(c).wait_recv()
        whole[pl.ds(2 * c, 2), x, :, own_columns] = got4[c] + got3[c, :, half]
        level5(c).start()

    def stage6(c):
        level5(c).wait_recv()
        level6(c).start()

    def weight_block(slot, b, of_hidden):
        for y in range(2):
            if of_hidden:
                left = turned[b, y * 4 : (y + 1) * 4].reshape(width, tokens)
                block = nn(left, operands[2 * b + 1])
            else:
                left = operands[2 * b, :, y * width : (y + 1) * width]
                block = tn(left, operands[2 * b + 1])
            block = block.astype(jnp.bfloat16)
            for h in range(2):
                piece = block[:, h * width : (h + 1) * width]
                parts[slot, b, h, y] = piece.reshape(parts.shape[4:])

    def make_blocks(c):
        slot = lax.rem(c, slots)

        @pl.when(c >= slots)
        def _():
            for b in range(2):
                level0(c - slots, b).wait_send()

        wait_operands()
        of_hidden = (c == 4) | (c == 5)

        @pl.when(of_hidden)
        def _():
            for b in range(2):
                turned_copy(b, 0).wait()
                weight_block(slot, b, True)

        @pl.when(jnp.logical_not(of_hidden))
        def _():
            weight_block(slot, 0, False)

        @pl.when(jnp.logical_not(of_hidden) & (c < count - 1))
        def _():
            weight_block(slot, 1, False)

        @pl.when(c >= got_slots)
        def _():
            pl.semaphore_wait(free, 1)

        level0(c, 0).start()
        pl.when(c < count - 1)(lambda: level0(c, 1).start())

    lane = lax.broadcasted_iota(jnp.int32, (1, 128), 1)
    low = lane < 64
    local = lane % 64

    def head_copies(pair):
        slot = lax.rem(pair, 2)
        lanes = pl.ds(pl.multiple_of(pair * 128, 128), 128)
        return [
            pltpu.make_async_copy(ref.at[:, lanes], heads.at[slot, i], head_sem.at[slot, i])
            for i, ref in enumerate((q_ref, k_ref, v_ref, col_ref, o_ref, g_ref))
        ]

    pairs = features // 128
    step = tokens // 2

    def attend_part(u, _):
        pair, part = u // 2, lax.rem(u, 2)
        slot = lax.rem(pair, 2)

        @pl.when(part == 0)
        def _():
            for copy in head_copies(pair):
                copy.wait()

            @pl.when(pair < pairs - 1)
            def _():
                for copy in head_copies(pair + 1):
                    copy.start()

            k_sum[...] = jnp.zeros_like(k_sum)
            v_sum[...] = jnp.zeros_like(v_sum)

        rows = pl.ds(pl.multiple_of(part * step, step), step)
        zero, one = jnp.zeros((), jnp.bfloat16), jnp.ones((), jnp.bfloat16)
        queries, columns_ = heads[slot, 0, rows, :], heads[slot, 3, rows, :]
        key_rows, values = heads[slot, 1], heads[slot, 2]
        out, grad = heads[slot, 4, rows, :], heads[slot, 5, rows, :]
        key_columns = jnp.where((local >= 3) & (local < 6), one, marks[...])
        value_columns = jnp.where(local < 2, one, zero)
        keys_across = key_rows.T
        both = grad.astype(jnp.float32) * out.astype(jnp.float32)
        of_low = -jnp.sum(jnp.where(low, both, 0.0), axis=1, keepdims=True)
        of_high = -jnp.sum(jnp.where(low, 0.0, both), axis=1, keepdims=True)
        inner = jnp.where(low, of_high, of_low)
        first = inner.astype(jnp.bfloat16).astype(jnp.float32)
        grad_columns = jnp.where(
            local == 0, first, jnp.where(local == 1, inner - first, 0.0)
        ).astype(jnp.bfloat16)
        query_parts, key_parts, value_parts = [], [], []
        for head in range(2):
            own = low if head == 0 else ~low
            scores = nt(jnp.where(own, key_rows, key_columns), jnp.where(own, queries, columns_))
            weights = jnp.exp(scores)
            change = nt(jnp.where(own, values, value_columns), jnp.where(own, grad, grad_columns))
            score_grad = (weights * change).astype(jnp.bfloat16)
            value_parts.append(nn(weights.astype(jnp.bfloat16), grad))
            key_parts.append(nn(score_grad, queries))
            query_parts.append(nn(keys_across, score_grad))
        k_sum[...] += jnp.where(low, key_parts[0], key_parts[1])
        v_sum[...] += jnp.where(low, value_parts[0], value_parts[1])
        upper = lax.broadcasted_iota(jnp.int32, (128, 1), 0) < 64
        query_grad = jnp.where(upper, query_parts[0], query_parts[1]).T
        lanes = pl.ds(pl.multiple_of(pair * 128, 128), 128)
        dqkv[0, rows, lanes] = (query_grad * HEAD_DIM**-0.5).astype(jnp.bfloat16)

        @pl.when(part == 1)
        def _():
            dqkv[1, 0:tokens, lanes] = k_sum[...].astype(jnp.bfloat16)
            dqkv[2, 0:tokens, lanes] = v_sum[...].astype(jnp.bfloat16)

        return 0

    def back_copies():
        copies = [
            pltpu.make_async_copy(
                weight_ref.at[:, pl.ds(features * i, features)],
                operands.at[i, pl.ds(0, features)],
                operand_sem.at[i],
            )
            for i in range(3)
        ]
        return copies + [operand(3, codes_ref)]

    def back():
        for copy in back_copies():
            copy.wait()
        middle_copy().wait()

        def rows_back(i, _):
            rows = pl.ds(pl.multiple_of(i * 256, 256), 256)
            grad = nt(dqkv[0, rows, :], operands[0, 0:features, :])
            grad = grad + nt(dqkv[1, rows, :], operands[1, 0:features, :])
            grad = grad + nt(dqkv[2, rows, :], operands[2, 0:features, :])
            start = operands[3, rows, :].astype(jnp.float32)
            unit, scale = normalize(start)
            for at, addend in enumerate(
                (dqkv[0, rows, :].astype(jnp.float32), dqkv[2, rows, :].astype(jnp.float32), grad * unit, grad)
            ):
                sums[0, at : at + 1, :] += jnp.sum(addend, axis=0, keepdims=True)
            start_grad = middle[rows, :] + norm_back(grad, row(gain_ref), unit, scale)
            share[rows, :] = (start_grad - 2.0 * commit_weight * start).astype(jnp.bfloat16)
            for member in range(members):

                @pl.when((i == member * each // 256) & (member != me))
                def _():
                    share_put(lax.rem(member - me - 1 + members, members), member).start()

            return 0

        lax.fori_loop(0, tokens // 256, rows_back, 0)
        own_share().start()
        sums_put(0).start()

    partners = (mate, over_x, over_y, near, away)

    def sums_put(i):
        return put(sums.at[i], sums_got.at[i], sums_sent.at[i], sums_recv.at[i], partners[i])

    def sums_step(i):
        sums_put(i).wait_recv()
        sums[i + 1] = sums[i] + sums_got[i]
        if i + 1 < len(partners):
            sums_put(i + 1).start()

    def own_share():
        rows = pl.ds(pl.multiple_of(me * each, 128), each)
        return pltpu.make_async_copy(share.at[rows], share_out.at[me], own_sem.at[0])

    def own_recon():
        return pltpu.make_async_copy(recon_ref.at[me], recon_out.at[me], own_sem.at[1])

    def middle_copy():
        return pltpu.make_async_copy(middle_ref, middle, once_sem.at[0])

    def marks_copy():
        return pltpu.make_async_copy(ka_ref, marks, once_sem.at[1])

    load_operands(0)
    marks_copy().start()
    middle_copy().start()
    for copy in head_copies(0):
        copy.start()
    for i in range(members - 1):
        recon_put(i).start()
    own_recon().start()
    sums[0] = jnp.zeros(sums.shape[1:], jnp.float32)
    for at, ref in ((4, out_bias_sum), (5, second_gain_sum), (6, second_shift_sum)):
        sums[0, at : at + 1, :] = ref[...]
    for k in range(4):
        sums[0, 7 + k : 8 + k, :] = up_bias_sum[:, k * features : (k + 1) * features]
    sums[0, 11:12, :] = down_bias_sum[...]
    sums[0, 12:13, :] = pixel_bias_sum[...]
    marks_copy().wait()
    stages = (stage1, stage2, stage3, stage4, stage5, stage6)
    last = 6

    def turn(t, _):
        @pl.when(t == last)
        def _():
            back()
            load_operands(last)

        @pl.when(t < count)
        def _():
            make_blocks(t)

        @pl.when((t < count - 1) & (t != last - 1))
        def _():
            load_operands(t + 1)

        @pl.when(t == last - 1)
        def _():
            for copy in back_copies():
                copy.start()

        def upto(s):
            return jnp.clip(2 * s, 0, 2 * pairs)

        lax.fori_loop(upto(t), upto(t + 1), attend_part, 0)
        for i in range(len(partners)):
            pl.when(t == last + 1 + i)(partial(sums_step, i))
        for stage, behind in zip(stages, lead):
            c = t - behind
            pl.when((c >= 0) & (c < count))(partial(stage, c))
        return 0

    lax.fori_loop(0, count + lead[-1], turn, 0)

    def finish(c, _):
        level6(c).wait_recv()
        for level in (level2y, level3, level4, level5, level6):
            level(c).wait_send()
        pl.when(only_y(c))(lambda: level2x(c).wait_send())
        pl.when(both_x(c))(lambda: level2y(c, 1).wait_send())
        return 0

    lax.fori_loop(0, count, finish, 0)
    for c in range(count - slots, count):
        for b in range(2 if c < count - 1 else 1):
            level0(c, b).wait_send()
    for i in range(len(partners)):
        sums_put(i).wait_send()
    vector_out[...] = sums[len(partners)]
    copies = []
    for block, (home, prefix, column) in enumerate(homes):
        out = outs[home] if prefix is None else outs[home].at[prefix]
        target = out.at[:, :, pl.ds(column, features)]
        copies.append(pltpu.make_async_copy(whole.at[block], target, out_sem.at[block]))
        copies[-1].start()
    for i in range(members - 1):
        recon_put(i).wait_recv()
        share_put(i).wait_recv()
        recon_put(i).wait_send()
        share_put(i).wait_send()
    own_recon().wait()
    own_share().wait()
    for copy in copies:
        copy.wait()


def finish(inputs, tiling):
    tokens, features = inputs[0].shape
    members = tiling[0] * tiling[1]
    blocks, slots, got_slots = 21, 3, 3
    count = (blocks + 1) // 2
    rows, width = features // members // 2, features // 2
    lead = (0, 2, 4, 6, 8, 10)
    homes = [(0, k, 0) for k in range(8)] + [(2, k, 0) for k in range(4)]
    homes += [(4, None, features * k) for k in range(3)] + [(0, 8, 0), (3, None, 0)]
    homes += [(1, None, features * k) for k in range(4)]
    shapes = [
        (9, 2, rows, features),
        (2, rows, 4 * features),
        (4, 2, rows, features),
        (2, rows, features),
        (2, rows, 3 * features),
        (members, tokens // members, features),
        (members, tokens // members, features),
    ]
    anywhere = pl.BlockSpec(memory_space=pl.ANY)
    inside = pl.BlockSpec(memory_space=pltpu.VMEM)
    dma = pltpu.SemaphoreType.DMA
    low, wide = jnp.bfloat16, jnp.float32
    cut = (2, 2, 2, 2, rows, width)
    scratch = [
        pltpu.VMEM((slots, 2, 2) + cut, low),
        pltpu.VMEM((got_slots, 2) + cut, low),
        pltpu.VMEM((count, 2) + cut[1:], low),
        pltpu.VMEM((count, 2) + cut[2:], low),
        pltpu.VMEM((count, 2) + cut[3:], low),
        pltpu.VMEM((count, 2) + cut[4:], low),
        pltpu.VMEM((2 * count, 2, rows, features), low),
        pltpu.VMEM((4, tokens, features), low),
        pltpu.VMEM((2, members, 2 * rows, tokens), low),
        pltpu.VMEM((2, 6, tokens, 128), low),
        pltpu.VMEM((tokens, 128), low),
        pltpu.VMEM((6, 16, features), wide),
        pltpu.VMEM((5, 16, features), wide),
        pltpu.VMEM((tokens, features), wide),
        pltpu.VMEM((tokens, features), low),
        pltpu.VMEM((tokens, 128), wide),
        pltpu.VMEM((tokens, 128), wide),
        pltpu.VMEM((3, tokens, features), low),
    ]
    scratch += [dma((count, 2))] * 6 + [dma((count,))] * 8
    scratch += [dma((blocks,)), dma((4,)), dma((2,)), dma((2, 6)), dma((2,))]
    scratch += [pltpu.SemaphoreType.REGULAR, dma((2,))]
    scratch += [dma((members - 1,))] * 4 + [dma((5,))] * 2
    return pl.pallas_call(
        partial(
            finish_kernel,
            blocks=blocks,
            homes=homes,
            lead=lead,
            slots=slots,
            got_slots=got_slots,
            tiling=tiling,
        ),
        in_specs=[anywhere] * 19 + [inside] * 7,
        out_specs=[anywhere] * 5 + [inside] + [anywhere] * 2,
        out_shape=[jax.ShapeDtypeStruct(shape, low) for shape in shapes[:5]]
        + [jax.ShapeDtypeStruct((16, features), wide)]
        + [jax.ShapeDtypeStruct(shape, low) for shape in shapes[5:]],
        scratch_shapes=scratch,
        compiler_params=pltpu.CompilerParams(
            collective_id=1, has_side_effects=True, vmem_limit_bytes=60 * 2**20
        ),
        cost_estimate=pl.CostEstimate(
            flops=2 * tokens * features * (24 * features) + 24 * tokens * tokens * features,
            bytes_accessed=100 * tokens * features,
            transcendentals=tokens * tokens * features // 64,
        ),
        name="finish",
    )(*inputs)


def on_device_grids(
    encoder_out,
    code_ids,
    segments,
    embed_table,
    recon_grad,
    qkv_weight,
    query_bias,
    value_bias,
    out_weight,
    out_bias,
    first_gain,
    first_shift,
    second_gain,
    second_shift,
    up_weight,
    up_bias,
    down_weight,
    down_bias,
    pixel_weight,
    pixel_bias,
):
    features = encoder_out.shape[-1]
    wide = jnp.float32
    down, across = lax.axis_size("ty"), lax.axis_size("tx")
    members = down * across
    axes = ("ty", "tx")
    tiling = (down, across) + encoder_out.shape[1:3]
    each = encoder_out.shape[1] * encoder_out.shape[2]
    tokens = members * each

    def line(vector):
        return vector.reshape(1, -1)

    def exchange(tiles):
        return lax.all_to_all(tiles, axes, split_axis=0, concat_axis=0, tiled=True)

    slots = 3 * each // 2
    asked, slot_index = ask(
        code_ids.reshape(members, each), segments.reshape(members, each), embed_table.shape[0], slots
    )
    asked, recon_grad = lax.optimization_barrier((asked, recon_grad))
    cotangent = exchange(recon_grad).reshape(tokens, features)
    moved, query_marks, key_marks = spread_marks(asked[:, 2], *tiling)
    asked = asked[:, :2].reshape(members, -1)[:, :slots].reshape(-1)
    fetched = embed_table.at[asked].get(mode="promise_in_bounds")
    pixel_taps = jnp.swapaxes(pixel_weight, 0, 1)
    codes, final_grad, lower_grad, behind, hidden_grad, pixel_bias_grad, down_bias_grad = fetch(
        fetched.reshape(members, slots, features),
        slot_index,
        cotangent,
        moved,
        pixel_taps,
        down_weight,
        tiling,
    )
    codes = codes.reshape(tokens, features)

    normed, queries, key_rows, values = enter(
        codes, line(first_gain), line(first_shift), qkv_weight, line(query_bias), line(value_bias)
    )
    attended, columns = attend(queries, key_rows, values, query_marks, key_marks)
    (
        features_low,
        normed_two,
        hidden_turned,
        pre_grad,
        middle_grad,
        branch_grad,
        attended_grad,
        out_bias_grad,
        second_gain_grad,
        second_shift_grad,
        up_bias_grad,
    ) = middle_block(
        codes,
        attended,
        final_grad,
        hidden_grad,
        out_weight,
        up_weight,
        down_weight,
        line(out_bias),
        line(second_gain),
        line(second_shift),
        line(up_bias),
        line(down_bias),
    )
    recon_rows, features_plain = conv(features_low, moved, pixel_taps, line(pixel_bias), tiling)
    pixel_sum, up_sum, down_sum, out_sum, qkv_sum, vectors, recon_tiles, share_tiles = finish(
        [
            queries,
            key_rows,
            values,
            columns,
            key_marks,
            attended,
            attended_grad,
            codes,
            middle_grad,
            features_plain,
            behind,
            normed_two,
            pre_grad,
            hidden_turned.reshape(members, 4, features // members, tokens),
            lower_grad,
            branch_grad,
            normed,
            qkv_weight,
            recon_rows.reshape(members, each, features),
            line(first_gain),
            out_bias_grad,
            second_gain_grad,
            second_shift_grad,
            up_bias_grad,
            down_bias_grad,
            pixel_bias_grad,
        ],
        tiling,
    )
    input_tiles = (
        share_tiles.reshape(encoder_out.shape).astype(wide)
        + 2.0 * commit_weight * encoder_out.astype(wide)
    ).astype(jnp.bfloat16)
    rows = features // members
    member = lax.axis_index(axes)

    def mine(first, count=1):
        line_of = vectors[first : first + count].reshape(-1)
        return lax.dynamic_slice(line_of, (member * rows * count,), (rows * count,))

    def whole_sum(summed):
        return summed.reshape(-1, summed.shape[-1]).astype(wide)

    return (
        recon_tiles.reshape(encoder_out.shape),
        input_tiles,
        whole_sum(qkv_sum),
        mine(0),
        mine(1),
        whole_sum(out_sum),
        mine(4),
        mine(2),
        mine(3),
        mine(5),
        mine(6),
        whole_sum(up_sum),
        mine(7, 4),
        whole_sum(down_sum),
        mine(11),
        jnp.swapaxes(whole_sum(pixel_sum).reshape(9, rows, features), 0, 1),
        mine(12),
    )


def solution(mesh):
    in_specs = (
        P("gr", "ty", "tx", None),
        P("gr", "ty", "tx"),
        P("gr", "ty", "tx"),
        P(("ty", "tx"), None),
        P("gr", "ty", "tx", None),
        P(),
        P(),
        P(),
        P(),
        P(),
        P(),
        P(),
        P(),
        P(),
        P(),
        P(),
        P(),
        P(),
        P(),
        P(),
    )
    out_specs = (
        P("gr", "ty", "tx", None),
        P("gr", "ty", "tx", None),
        P(("ty", "tx"), None),
        P(("ty", "tx")),
        P(("ty", "tx")),
        P(("ty", "tx"), None),
        P(("ty", "tx")),
        P(("ty", "tx")),
        P(("ty", "tx")),
        P(("ty", "tx")),
        P(("ty", "tx")),
        P(("ty", "tx"), None),
        P(("ty", "tx")),
        P(("ty", "tx"), None),
        P(("ty", "tx")),
        P(("ty", "tx"), None, None),
        P(("ty", "tx")),
    )
    def on_device(encoder_out, *rest):
        members = mesh.shape["ty"] * mesh.shape["tx"]
        whole_grids = encoder_out.shape[0] == members and tuple(mesh.devices.shape) == (4, 2, 4)
        body = on_device_grids if whole_grids else on_device_bands
        return body(encoder_out, *rest)

    return jax.shard_map(
        on_device, mesh=mesh, in_specs=in_specs, out_specs=out_specs, check_vma=False
    )
```

```python
from functools import partial

import jax
import jax.numpy as jnp
from jax import lax
from jax.experimental import pallas as pl
from jax.experimental.pallas import tpu as pltpu
from jax.sharding import PartitionSpec as P

HEADS = 12
HEAD_DIM = 64


epsilon = 1e-06
commit_weight = 0.25


def with_halo(block, sides, width):
    for axis, dim in sides:
        count = lax.axis_size(axis)
        forward = [(i, i + 1) for i in range(count - 1)]
        backward = [(target, source) for source, target in forward]
        low = lax.ppermute(
            lax.slice_in_dim(block, block.shape[dim] - width, None, axis=dim), axis, forward
        )
        high = lax.ppermute(lax.slice_in_dim(block, 0, width, axis=dim), axis, backward)
        block = jnp.concatenate([low, block, high], axis=dim)
    return block


def layer_norm(values, gain, shift):
    center = values - jnp.mean(values, axis=-1, keepdims=True)
    spread = jnp.mean(center * center, axis=-1, keepdims=True)
    return center * lax.rsqrt(spread + epsilon) * gain + shift


def exact_gelu(values):
    return jax.nn.gelu(values, approximate=False)


def matmul(left_side, right_side):
    return jnp.dot(left_side, right_side, preferred_element_type=jnp.float32)


def left_product(left_side, right_side):
    return lax.dot_general(
        left_side, right_side, (((0,), (0,)), ((), ())), preferred_element_type=jnp.float32
    )


def right_product(left_side, right_side):
    return lax.dot_general(
        left_side, right_side, (((1,), (1,)), ((), ())), preferred_element_type=jnp.float32
    )


def pad_side(array, axis_index):
    widths = [(0, 0)] * array.ndim
    widths[axis_index] = (1, 1)
    return jnp.pad(array, widths)


def blocked(array, block_size):
    return array.reshape((array.shape[0] // block_size, block_size) + array.shape[1:])


def unblock(array):
    return array.reshape((-1,) + array.shape[2:])


def head_scores(queries, key_rows, marks_query, marks_key, head_count, score_scale):
    grid_count, query_rows, features = queries.shape
    query_heads = queries.reshape(grid_count, query_rows, head_count, features // head_count)
    key_heads = key_rows.reshape(grid_count, key_rows.shape[1], head_count, features // head_count)
    scores = (
        jnp.einsum("bqhd,bkhd->bhqk", query_heads, key_heads, preferred_element_type=jnp.float32)
        * score_scale
    )
    same_image = (marks_query[:, :, None] == marks_key[:, None, :])[:, None]
    return jnp.where(same_image, scores, -1000000000.0)


def attend_block(bundle, head_count, score_scale):
    queries, key_rows, values, marks_query, marks_key = bundle
    grid_count, query_rows, features = queries.shape
    scores = head_scores(queries, key_rows, marks_query, marks_key, head_count, score_scale)
    running_max = jnp.max(scores, axis=-1, keepdims=True)
    exponent = jnp.exp(scores - running_max)
    denominator = jnp.sum(exponent, axis=-1, keepdims=True)
    probability = (exponent / denominator).astype(jnp.bfloat16)
    value_heads = values.reshape(grid_count, values.shape[1], head_count, features // head_count)
    attended = jnp.einsum(
        "bhqk,bkhd->bqhd", probability, value_heads, preferred_element_type=jnp.float32
    )
    return (
        attended.reshape(grid_count, query_rows, features).astype(jnp.bfloat16),
        running_max + jnp.log(denominator),
    )


def attend_back(bundle, head_count, score_scale):
    queries, key_rows, values, marks_query, marks_key, log_total, out_grad = bundle
    grid_count, query_rows, features = queries.shape
    head_size = features // head_count
    scores = head_scores(queries, key_rows, marks_query, marks_key, head_count, score_scale)
    probability = jnp.exp(scores - log_total)
    query_heads = queries.reshape(grid_count, query_rows, head_count, head_size)
    key_heads = key_rows.reshape(grid_count, key_rows.shape[1], head_count, head_size)
    value_heads = values.reshape(grid_count, values.shape[1], head_count, head_size)
    grad_heads = out_grad.reshape(grid_count, query_rows, head_count, head_size)
    prob_grad = jnp.einsum(
        "bqhd,bkhd->bhqk", grad_heads, value_heads, preferred_element_type=jnp.float32
    )
    inner_sum = jnp.sum(probability * prob_grad, axis=-1, keepdims=True)
    score_grad = (probability * (prob_grad - inner_sum)).astype(jnp.bfloat16)
    query_grad = (
        jnp.einsum("bhqk,bkhd->bqhd", score_grad, key_heads, preferred_element_type=jnp.float32)
        * score_scale
    )
    key_grad = (
        jnp.einsum("bhqk,bqhd->bkhd", score_grad, query_heads, preferred_element_type=jnp.float32)
        * score_scale
    )
    value_grad = jnp.einsum(
        "bhqk,bqhd->bkhd",
        probability.astype(jnp.bfloat16),
        grad_heads,
        preferred_element_type=jnp.float32,
    )
    key_count = key_rows.shape[1]
    return (
        query_grad.reshape(grid_count, query_rows, features).astype(jnp.bfloat16),
        key_grad.reshape(grid_count, key_count, features),
        value_grad.reshape(grid_count, key_count, features),
    )


def on_device_bands(
    encoder_out,
    code_ids,
    segments,
    embed_table,
    recon_grad,
    qkv_weight,
    query_bias,
    value_bias,
    out_weight,
    out_bias,
    first_gain,
    first_shift,
    second_gain,
    second_shift,
    up_weight,
    up_bias,
    down_weight,
    down_bias,
    pixel_weight,
    pixel_bias,
):
    features = encoder_out.shape[-1]
    head_count = HEADS
    score_scale = float(HEAD_DIM) ** (-0.5)
    holder_count = lax.axis_size(("ty", "tx"))
    share_rows = embed_table.shape[0]
    flat_ids = code_ids.reshape(-1)
    row_count = flat_ids.shape[0]
    slot_count = 3 * row_count // (2 * holder_count)
    holder = flat_ids // share_rows
    offsets = flat_ids - holder * share_rows
    belongs = (holder[:, None] == jnp.arange(holder_count, dtype=jnp.int32)[None, :]).astype(
        jnp.int32
    )
    slot_rank = jnp.sum((jnp.cumsum(belongs, axis=0) - 1) * belongs, axis=1)
    slot_index = holder * slot_count + slot_rank
    requests = jnp.zeros((holder_count * slot_count,), jnp.int32).at[slot_index].set(offsets)
    requests = requests.reshape(holder_count, slot_count)
    fetched = jnp.take(
        embed_table,
        lax.all_to_all(requests, ("ty", "tx"), split_axis=0, concat_axis=0, tiled=True),
        axis=0,
    )
    returned = lax.all_to_all(fetched, ("ty", "tx"), split_axis=0, concat_axis=0, tiled=True)
    codes = returned.reshape(holder_count * slot_count, features)[slot_index].reshape(
        encoder_out.shape
    )
    marks_tile = (segments + 1).astype(jnp.bfloat16)
    arrived = (
        lax.all_to_all(encoder_out, "tx", split_axis=0, concat_axis=2, tiled=True),
        lax.all_to_all(codes, "tx", split_axis=0, concat_axis=2, tiled=True),
        lax.all_to_all(recon_grad, "tx", split_axis=0, concat_axis=2, tiled=True),
        lax.all_to_all(marks_tile, "tx", split_axis=0, concat_axis=2, tiled=True),
    )
    inputs_band, codes_band, cotangent_band, marks_band = arrived
    grid_count, band_rows, band_cols = marks_band.shape
    tokens = band_rows * band_cols
    all_rows = grid_count * tokens
    block_size = max(1, 512 // tokens)
    while grid_count % block_size:
        block_size -= 1
    start_rows = codes_band.reshape(all_rows, features).astype(jnp.float32)
    marks_query = marks_band.reshape(grid_count, tokens)
    normed, first_pull = jax.vjp(
        layer_norm, start_rows, first_gain.astype(jnp.float32), first_shift.astype(jnp.float32)
    )
    normed_low = normed.astype(jnp.bfloat16)
    projected = matmul(normed_low, qkv_weight)
    queries = (
        (projected[:, :features] + query_bias.astype(jnp.float32))
        .astype(jnp.bfloat16)
        .reshape(grid_count, tokens, features)
    )
    key_rows = (
        projected[:, features : 2 * features]
        .astype(jnp.bfloat16)
        .reshape(grid_count, tokens, features)
    )
    values = (
        (projected[:, 2 * features :] + value_bias.astype(jnp.float32))
        .astype(jnp.bfloat16)
        .reshape(grid_count, tokens, features)
    )
    bundle = (key_rows, values, marks_query)
    keys_all = lax.all_gather(bundle[0], "ty", axis=1, tiled=True)
    values_all = lax.all_gather(bundle[1], "ty", axis=1, tiled=True)
    marks_key = lax.all_gather(bundle[2], "ty", axis=1, tiled=True)
    attended_blocks, log_total = lax.map(
        partial(attend_block, head_count=head_count, score_scale=score_scale),
        (
            blocked(queries, block_size),
            blocked(keys_all, block_size),
            blocked(values_all, block_size),
            blocked(marks_query, block_size),
            blocked(marks_key, block_size),
        ),
    )
    attended = unblock(attended_blocks).reshape(all_rows, features)
    branch = matmul(attended, out_weight) + out_bias.astype(jnp.float32)
    middle = start_rows + branch
    normed_two, second_pull = jax.vjp(
        layer_norm, middle, second_gain.astype(jnp.float32), second_shift.astype(jnp.float32)
    )
    normed_two_low = normed_two.astype(jnp.bfloat16)
    hidden_pre = matmul(normed_two_low, up_weight) + up_bias.astype(jnp.float32)
    hidden_act, gelu_pull = jax.vjp(exact_gelu, hidden_pre)
    hidden_low = hidden_act.astype(jnp.bfloat16)
    output_rows = middle + (matmul(hidden_low, down_weight) + down_bias.astype(jnp.float32))
    features_low = output_rows.astype(jnp.bfloat16).reshape(
        grid_count, band_rows, band_cols, features
    )
    bundle = (features_low, marks_band, cotangent_band)
    grown = (
        with_halo(bundle[0], (("ty", 1),), 1),
        with_halo(bundle[1], (("ty", 1),), 1),
        with_halo(bundle[2], (("ty", 1),), 1),
    )
    features_pad, marks_pad, cotangent_pad = tuple((pad_side(member, 2) for member in grown))
    ahead_list = []
    behind_list = []
    for vertical in range(3):
        for lateral in range(3):
            inside = (
                marks_pad[:, vertical : vertical + band_rows, lateral : lateral + band_cols]
                == marks_band
            )
            ahead_list.append(
                jnp.where(
                    inside[..., None],
                    features_pad[:, vertical : vertical + band_rows, lateral : lateral + band_cols],
                    0,
                )
            )
            mirror_row = 2 - vertical
            mirror_col = 2 - lateral
            facing = (
                marks_pad[
                    :, mirror_row : mirror_row + band_rows, mirror_col : mirror_col + band_cols
                ]
                == marks_band
            )
            behind_list.append(
                jnp.where(
                    facing[..., None],
                    cotangent_pad[
                        :, mirror_row : mirror_row + band_rows, mirror_col : mirror_col + band_cols
                    ],
                    0,
                )
            )
    ahead = jnp.stack(ahead_list, axis=3)
    behind = jnp.stack(behind_list, axis=3)
    recon_band = jnp.einsum(
        "nhwkd,dkp->nhwp", ahead, pixel_weight, preferred_element_type=jnp.float32
    ) + pixel_bias.astype(jnp.float32)
    pixel_weight_grad = jnp.einsum(
        "nhwkd,nhwp->dkp", ahead, cotangent_band, preferred_element_type=jnp.float32
    )
    pixel_bias_grad = jnp.sum(cotangent_band.astype(jnp.float32), axis=(0, 1, 2))
    final_grad = jnp.einsum(
        "nhwkp,dkp->nhwd", behind, pixel_weight, preferred_element_type=jnp.float32
    ).reshape(all_rows, features)
    lower_grad = final_grad.astype(jnp.bfloat16)
    down_weight_grad = left_product(hidden_low, lower_grad)
    down_bias_grad = jnp.sum(lower_grad.astype(jnp.float32), axis=0)
    pre_grad = gelu_pull(right_product(lower_grad, down_weight))[0].astype(jnp.bfloat16)
    up_weight_grad = left_product(normed_two_low, pre_grad)
    up_bias_grad = jnp.sum(pre_grad.astype(jnp.float32), axis=0)
    middle_part, second_gain_grad, second_shift_grad = second_pull(
        right_product(pre_grad, up_weight)
    )
    middle_grad = final_grad + middle_part
    branch_grad = middle_grad.astype(jnp.bfloat16)
    out_weight_grad = left_product(attended, branch_grad)
    out_bias_grad = jnp.sum(branch_grad.astype(jnp.float32), axis=0)
    attended_grad = (
        right_product(branch_grad, out_weight)
        .astype(jnp.bfloat16)
        .reshape(grid_count, tokens, features)
    )
    query_blocks, key_blocks, value_blocks = lax.map(
        partial(attend_back, head_count=head_count, score_scale=score_scale),
        (
            blocked(queries, block_size),
            blocked(keys_all, block_size),
            blocked(values_all, block_size),
            blocked(marks_query, block_size),
            blocked(marks_key, block_size),
            log_total,
            blocked(attended_grad, block_size),
        ),
    )
    query_grad = unblock(query_blocks)
    bundle = (unblock(key_blocks), unblock(value_blocks))
    key_sum = lax.psum_scatter(
        bundle[0].astype(jnp.bfloat16), "ty", scatter_dimension=1, tiled=True
    )
    value_sum = lax.psum_scatter(
        bundle[1].astype(jnp.bfloat16), "ty", scatter_dimension=1, tiled=True
    )
    projected_grad = jnp.concatenate([query_grad, key_sum, value_sum], axis=-1).reshape(
        all_rows, 3 * features
    )
    qkv_weight_grad = left_product(normed_low, projected_grad)
    query_bias_grad = jnp.sum(query_grad.astype(jnp.float32), axis=(0, 1))
    value_bias_grad = jnp.sum(value_sum.astype(jnp.float32), axis=(0, 1))
    start_part, first_gain_grad, first_shift_grad = first_pull(
        right_product(projected_grad, qkv_weight)
    )
    start_grad = middle_grad + start_part
    inputs_rows = inputs_band.reshape(all_rows, features).astype(jnp.float32)
    input_band = (start_grad + 2.0 * commit_weight * (inputs_rows - start_rows)).astype(
        jnp.bfloat16
    )
    bundle = (
        recon_band.astype(jnp.bfloat16),
        input_band.reshape(grid_count, band_rows, band_cols, features),
    )
    recon_tiles = lax.all_to_all(bundle[0], "tx", split_axis=2, concat_axis=0, tiled=True)
    input_tiles = lax.all_to_all(bundle[1], "tx", split_axis=2, concat_axis=0, tiled=True)
    local_grads = (
        qkv_weight_grad,
        query_bias_grad,
        value_bias_grad,
        out_weight_grad,
        out_bias_grad,
        first_gain_grad,
        first_shift_grad,
        second_gain_grad,
        second_shift_grad,
        up_weight_grad,
        up_bias_grad,
        down_weight_grad,
        down_bias_grad,
        pixel_weight_grad,
        pixel_bias_grad,
    )
    tile_shares = (
        lax.psum_scatter(
            local_grads[0].astype(jnp.bfloat16), ("ty", "tx"), scatter_dimension=0, tiled=True
        ).astype(jnp.float32),
        lax.psum_scatter(
            local_grads[1].astype(jnp.bfloat16), ("ty", "tx"), scatter_dimension=0, tiled=True
        ).astype(jnp.float32),
        lax.psum_scatter(
            local_grads[2].astype(jnp.bfloat16), ("ty", "tx"), scatter_dimension=0, tiled=True
        ).astype(jnp.float32),
        lax.psum_scatter(
            local_grads[3].astype(jnp.bfloat16), ("ty", "tx"), scatter_dimension=0, tiled=True
        ).astype(jnp.float32),
        lax.psum_scatter(
            local_grads[4].astype(jnp.bfloat16), ("ty", "tx"), scatter_dimension=0, tiled=True
        ).astype(jnp.float32),
        lax.psum_scatter(
            local_grads[5].astype(jnp.bfloat16), ("ty", "tx"), scatter_dimension=0, tiled=True
        ).astype(jnp.float32),
        lax.psum_scatter(
            local_grads[6].astype(jnp.bfloat16), ("ty", "tx"), scatter_dimension=0, tiled=True
        ).astype(jnp.float32),
        lax.psum_scatter(
            local_grads[7].astype(jnp.bfloat16), ("ty", "tx"), scatter_dimension=0, tiled=True
        ).astype(jnp.float32),
        lax.psum_scatter(
            local_grads[8].astype(jnp.bfloat16), ("ty", "tx"), scatter_dimension=0, tiled=True
        ).astype(jnp.float32),
        lax.psum_scatter(
            local_grads[9].astype(jnp.bfloat16), ("ty", "tx"), scatter_dimension=0, tiled=True
        ).astype(jnp.float32),
        lax.psum_scatter(
            local_grads[10].astype(jnp.bfloat16), ("ty", "tx"), scatter_dimension=0, tiled=True
        ).astype(jnp.float32),
        lax.psum_scatter(
            local_grads[11].astype(jnp.bfloat16), ("ty", "tx"), scatter_dimension=0, tiled=True
        ).astype(jnp.float32),
        lax.psum_scatter(
            local_grads[12].astype(jnp.bfloat16), ("ty", "tx"), scatter_dimension=0, tiled=True
        ).astype(jnp.float32),
        lax.psum_scatter(
            local_grads[13].astype(jnp.bfloat16), ("ty", "tx"), scatter_dimension=0, tiled=True
        ).astype(jnp.float32),
        lax.psum_scatter(
            local_grads[14].astype(jnp.bfloat16), ("ty", "tx"), scatter_dimension=0, tiled=True
        ).astype(jnp.float32),
    )
    summed = (
        lax.psum(tile_shares[0].astype(jnp.bfloat16), "gr").astype(jnp.float32),
        lax.psum(tile_shares[1].astype(jnp.bfloat16), "gr").astype(jnp.float32),
        lax.psum(tile_shares[2].astype(jnp.bfloat16), "gr").astype(jnp.float32),
        lax.psum(tile_shares[3].astype(jnp.bfloat16), "gr").astype(jnp.float32),
        lax.psum(tile_shares[4].astype(jnp.bfloat16), "gr").astype(jnp.float32),
        lax.psum(tile_shares[5].astype(jnp.bfloat16), "gr").astype(jnp.float32),
        lax.psum(tile_shares[6].astype(jnp.bfloat16), "gr").astype(jnp.float32),
        lax.psum(tile_shares[7].astype(jnp.bfloat16), "gr").astype(jnp.float32),
        lax.psum(tile_shares[8].astype(jnp.bfloat16), "gr").astype(jnp.float32),
        lax.psum(tile_shares[9].astype(jnp.bfloat16), "gr").astype(jnp.float32),
        lax.psum(tile_shares[10].astype(jnp.bfloat16), "gr").astype(jnp.float32),
        lax.psum(tile_shares[11].astype(jnp.bfloat16), "gr").astype(jnp.float32),
        lax.psum(tile_shares[12].astype(jnp.bfloat16), "gr").astype(jnp.float32),
        lax.psum(tile_shares[13].astype(jnp.bfloat16), "gr").astype(jnp.float32),
        lax.psum(tile_shares[14].astype(jnp.bfloat16), "gr").astype(jnp.float32),
    )
    return (
        recon_tiles,
        input_tiles,
        summed[0],
        summed[1],
        summed[2],
        summed[3],
        summed[4],
        summed[5],
        summed[6],
        summed[7],
        summed[8],
        summed[9],
        summed[10],
        summed[11],
        summed[12],
        summed[13],
        summed[14],
    )


far = float(2.0**30)


def nt(left_side, right_side):
    return lax.dot_general(
        left_side, right_side, (((1,), (1,)), ((), ())), preferred_element_type=jnp.float32
    )


def nn(left_side, right_side):
    return lax.dot_general(
        left_side, right_side, (((1,), (0,)), ((), ())), preferred_element_type=jnp.float32
    )


def tn(left_side, right_side):
    return lax.dot_general(
        left_side, right_side, (((0,), (0,)), ((), ())), preferred_element_type=jnp.float32
    )


def groups(down, across, rows, cols):
    for part in range(down * across):
        for r in range(rows):
            grid_row = (part // across) * rows + r
            yield (part * rows + r) * cols, (grid_row * across + part % across) * cols


def conv_kernel(rows_ref, mask_ref, weight_ref, bias_ref, out_ref, plain_ref, shifted, total, other, *, tiling):
    width, cols = tiling[1] * tiling[3], tiling[3]
    tap = pl.program_id(0)
    tokens, features = rows_ref.shape

    @pl.when(tap == 0)
    def _():
        other[...] = rows_ref[...].astype(jnp.float32)
        for tiled, plain in groups(*tiling):
            total[plain : plain + cols, :] = other[tiled : tiled + cols, :]
        rows = total[...]
        plain_ref[...] = rows.astype(jnp.bfloat16)
        for j in range(3):
            moved = rows if j == 1 else pltpu.roll(rows, (1 - j) % tokens, 0)
            shifted[j, 0:width, :] = jnp.zeros((width, features), jnp.bfloat16)
            shifted[j, width + tokens :, :] = jnp.zeros((width, features), jnp.bfloat16)
            shifted[j, width : width + tokens, :] = moved.astype(jnp.bfloat16)
        total[...] = jnp.zeros_like(total)

    below, right = tap // 3, tap % 3
    step = tokens // 4
    for i in range(4):
        rows = slice(i * step, (i + 1) * step)
        first = pl.multiple_of(below * width + i * step, width)
        marks = mask_ref[1, width + i * step : width + (i + 1) * step, :]
        same = mask_ref[right, pl.ds(first, step), :] == marks
        mask = jnp.where(same, 1.0, 0.0).astype(jnp.bfloat16)
        mask = jnp.concatenate([mask] * (features // 128), axis=1)
        total[rows, :] += nn(shifted[right, pl.ds(first, step), :] * mask, weight_ref[0])

    @pl.when(tap == 8)
    def _():
        for tiled, plain in groups(*tiling):
            other[tiled : tiled + cols, :] = total[plain : plain + cols, :]
        out_ref[...] = (other[...] + bias_ref[...].astype(jnp.float32)).astype(jnp.bfloat16)


def in_hbm(shape, dtype=jnp.bfloat16):
    return pltpu.HBM(shape, dtype)


def conv(rows, masks, weight, bias, tiling):
    tokens, features = rows.shape
    width = tiling[1] * tiling[3]

    def whole(shape):
        return pl.BlockSpec(shape, lambda k: (0,) * len(shape), pipeline_mode=pl.Buffered(1))

    return pl.pallas_call(
        partial(conv_kernel, tiling=tiling),
        grid=(9,),
        in_specs=[
            whole((tokens, features)),
            whole(masks.shape),
            pl.BlockSpec((1, features, features), lambda k: (k, 0, 0)),
            whole((1, features)),
        ],
        out_specs=[whole((tokens, features))] * 2,
        out_shape=[in_hbm((tokens, features))] * 2,
        scratch_shapes=[
            pltpu.VMEM((3, tokens + 2 * width, features), jnp.bfloat16),
            pltpu.VMEM((tokens, features), jnp.float32),
            pltpu.VMEM((tokens, features), jnp.float32),
        ],
        compiler_params=pltpu.CompilerParams(vmem_limit_bytes=60 * 2**20),
        cost_estimate=pl.CostEstimate(
            flops=18 * tokens * features * features,
            bytes_accessed=18 * features * features + 4 * tokens * features,
            transcendentals=0,
        ),
        name="conv",
    )(rows, masks, weight, bias)


def marks_kernel(parts_ref, moved_ref, query_ref, key_ref, *, down, across, rows, cols):
    width = across * cols
    tokens = down * rows * width
    turned = parts_ref[...].astype(jnp.float32).T
    lane = lax.broadcasted_iota(jnp.int32, (rows * cols, 128), 1) % 64
    nowhere = jnp.full((width, 128), -1.0, jnp.float32)
    for j in range(3):
        moved_ref[j, 0:width, :] = nowhere
        moved_ref[j, width + tokens :, :] = nowhere
    for part in range(down * across):
        spread = jnp.broadcast_to(turned[:, part : part + 1], (rows * cols, 128))
        hot = spread == lane.astype(jnp.float32)
        here = slice(part * rows * cols, (part + 1) * rows * cols)
        query_ref[here, :] = jnp.where(hot, 1.0, 0.0).astype(jnp.bfloat16)
        key_ref[here, :] = jnp.where((lane < 3) & ~hot, -far, 0.0).astype(jnp.bfloat16)
        for r in range(rows):
            first = ((part // across) * rows + r) * width + (part % across) * cols + width
            moved_ref[1, first : first + cols, :] = spread[r * cols : (r + 1) * cols]
    marks = moved_ref[1, width : width + tokens, :]
    column = lax.broadcasted_iota(jnp.int32, (tokens, 128), 0) % width
    left = jnp.where(column == 0, -1.0, pltpu.roll(marks, 1, 0))
    right = jnp.where(column == width - 1, -1.0, pltpu.roll(marks, tokens - 1, 0))
    moved_ref[0, width : width + tokens, :] = left
    moved_ref[2, width : width + tokens, :] = right


def spread_marks(parts, down, across, rows, cols):
    tokens = down * across * rows * cols
    low = in_hbm((tokens, 128))
    return pl.pallas_call(
        partial(marks_kernel, down=down, across=across, rows=rows, cols=cols),
        out_shape=[
            in_hbm((3, tokens + 2 * across * cols, 128), jnp.float32),
            low,
            low,
        ],
        compiler_params=pltpu.CompilerParams(vmem_limit_bytes=60 * 2**20),
        name="spread_marks",
    )(parts)


def normalize(values):
    center = values - jnp.mean(values, axis=-1, keepdims=True)
    scale = lax.rsqrt(jnp.mean(center * center, axis=-1, keepdims=True) + epsilon)
    return center * scale, scale


def norm_back(grad, gain, unit, scale):
    scaled = grad * gain
    mean = jnp.mean(scaled, axis=-1, keepdims=True)
    along = jnp.mean(scaled * unit, axis=-1, keepdims=True)
    return scale * (scaled - mean - unit * along)


def row(ref):
    return ref[...].astype(jnp.float32)


def add_rows(ref, values):
    ref[...] += jnp.sum(values, axis=0, keepdims=True)


def ask_kernel(ids_ref, marks_ref, got_ref, slot_ref, sends, got, sent, received, *, share, slots):
    gr, ty, tx = lax.axis_index("gr"), lax.axis_index("ty"), lax.axis_index("tx")
    across = lax.axis_size("tx")
    members = lax.axis_size("ty") * across
    me = ty * across + tx
    others = [lax.rem(me + step, members) for step in range(1, members)]

    def place(member):
        return (gr, member // across, lax.rem(member, across))

    barrier = pltpu.get_barrier_semaphore()
    for member in others:
        pl.semaphore_signal(
            barrier, inc=1, device_id=place(member), device_id_type=pl.DeviceIdType.MESH
        )
    grids, each = ids_ref.shape
    turned = ids_ref[...].astype(jnp.float32).T
    lane = lax.broadcasted_iota(jnp.int32, (each, 128), 1)
    earlier = lax.broadcasted_iota(jnp.int32, (each, each), 1)
    earlier = earlier < lax.broadcasted_iota(jnp.int32, (each, each), 0)
    earlier = jnp.where(earlier, 1.0, 0.0).astype(jnp.bfloat16)
    counts = jnp.zeros((1, 128), jnp.float32)
    high = jnp.zeros((128, 128), jnp.float32)
    low = jnp.zeros((128, 128), jnp.float32)
    for grid in range(grids):
        ids = jnp.broadcast_to(turned[:, grid : grid + 1], (each, 128)).astype(jnp.int32)
        holder = jnp.zeros_like(ids)
        for member in range(1, members):
            holder = holder + jnp.where(ids >= member * share, 1, 0)
        offset = ids - holder * share
        belongs = jnp.where(holder == lane, 1.0, 0.0)
        ranks = nn(earlier, belongs.astype(jnp.bfloat16)) + counts
        counts = counts + jnp.sum(belongs, axis=0, keepdims=True)
        rank = jnp.sum(belongs * ranks, axis=1, keepdims=True)
        rank = jnp.broadcast_to(rank, (each, 128)).astype(jnp.int32)
        slot_ref[grid * each : (grid + 1) * each, :] = holder * slots + rank
        second = jnp.where(rank >= 128, 1, 0)
        of_row = 2 * holder + second == lane
        of_lane = jnp.where(rank - 128 * second == lane, 1.0, 0.0).astype(jnp.bfloat16)
        upper = jnp.floor(offset.astype(jnp.float32) * (1.0 / 64.0))
        lower = offset.astype(jnp.float32) - 64.0 * upper
        high = high + tn(jnp.where(of_row, upper, 0.0).astype(jnp.bfloat16), of_lane)
        low = low + tn(jnp.where(of_row, lower, 0.0).astype(jnp.bfloat16), of_lane)
    wanted = (high * 64.0 + low).astype(jnp.int32)
    sends[...] = jnp.zeros_like(sends)
    for member in range(members):
        sends[member, 0:2, :] = wanted[2 * member : 2 * member + 2, :]
        sends[member, 2:3, :] = marks_ref[member : member + 1, :]

    def put(i):
        return pltpu.make_async_remote_copy(
            src_ref=sends.at[others[i]],
            dst_ref=got.at[me],
            send_sem=sent.at[i],
            recv_sem=received.at[i],
            device_id=place(others[i]),
            device_id_type=pl.DeviceIdType.MESH,
        )

    pl.semaphore_wait(barrier, members - 1)
    for i in range(members - 1):
        put(i).start()
    got[me] = sends[me]
    for i in range(members - 1):
        put(i).wait_send()
        put(i).wait_recv()
    got_ref[...] = got[...]


def ask(ids, marks, share, slots):
    members, each = ids.shape
    inside = pl.BlockSpec(memory_space=pltpu.VMEM)
    box = (members, 8, each)
    return pl.pallas_call(
        partial(ask_kernel, share=share, slots=slots),
        in_specs=[inside, inside],
        out_specs=[inside, inside],
        out_shape=[
            jax.ShapeDtypeStruct(box, jnp.int32),
            jax.ShapeDtypeStruct((members * each, 128), jnp.int32),
        ],
        scratch_shapes=[pltpu.VMEM(box, jnp.int32)] * 2
        + [pltpu.SemaphoreType.DMA((members - 1,))] * 2,
        compiler_params=pltpu.CompilerParams(
            collective_id=2, has_side_effects=True, vmem_limit_bytes=60 * 2**20
        ),
        cost_estimate=pl.CostEstimate(
            flops=20 * 10**9, bytes_accessed=40 * 10**6, transcendentals=0
        ),
        name="ask",
    )(ids, marks)


def gelu_parts(values):
    spread = jnp.exp(-0.5 * values * values)
    t = 1.0 / (1.0 + (0.3275911 * 0.5**0.5) * jnp.abs(values))
    series = 0.5 * 1.061405429
    for factor in (-1.453152027, 1.421413741, -0.284496736, 0.254829592):
        series = series * t + 0.5 * factor
    tail = series * t * spread
    upto = jnp.where(values < 0.0, tail, 1.0 - tail)
    return values * upto, upto + values * spread * 0.3989422804014327


def forward_kernel(
    codes_ref,
    final_ref,
    hidden_grad_ref,
    query_marks_ref,
    key_marks_ref,
    qkv_ref,
    out_weight_ref,
    up_ref,
    down_ref,
    first_gain_ref,
    first_shift_ref,
    qb_ref,
    vb_ref,
    out_bias_ref,
    gain_ref,
    shift_ref,
    up_bias_ref,
    down_bias_ref,
    normed_out,
    q_out,
    k_out,
    v_out,
    attended_out,
    columns_out,
    features_out,
    normed_two_out,
    hidden_out,
    pre_out,
    middle_grad_out,
    branch_out,
    attended_grad_out,
    out_bias_sum,
    gain_sum,
    shift_sum,
    up_bias_sum,
    codes,
    query_marks,
    key_marks,
    qkv_weight,
    out_weight,
    up_weight,
    down_weight,
    normed,
    queries,
    keys,
    values,
    attended,
    columns,
    final,
    hidden_grad,
    features_stage,
    normed_two_stage,
    hidden_stage,
    pre_stage,
    middle_grad_stage,
    branch_stage,
    attended_grad_stage,
    in_sem,
    once_sem,
    block_sem,
    stage_sem,
    *,
    step,
):
    tokens, features = codes.shape
    pairs = queries.shape[0]
    blocks = tokens // step
    loads = [
        pltpu.make_async_copy(source, target, in_sem.at[i])
        for i, (source, target) in enumerate(
            (
                (codes_ref, codes),
                (qkv_ref, qkv_weight),
                (query_marks_ref, query_marks),
                (key_marks_ref, key_marks),
                (out_weight_ref, out_weight),
                (up_ref, up_weight),
                (down_ref, down_weight),
            )
        )
    ]
    for copy in loads:
        copy.start()

    def block_copies(i):
        rows = pl.ds(pl.multiple_of(i * step, step), step)
        slot = lax.rem(i, 2)
        return [
            pltpu.make_async_copy(final_ref.at[rows], final.at[slot], block_sem.at[slot, 0]),
            pltpu.make_async_copy(
                hidden_grad_ref.at[rows], hidden_grad.at[slot], block_sem.at[slot, 1]
            ),
        ]

    for copy in block_copies(0):
        copy.start()
    for ref in (out_bias_sum, gain_sum, shift_sum, up_bias_sum):
        ref[...] = jnp.zeros_like(ref)

    for copy in loads[:2]:
        copy.wait()

    def enter_rows(i, _):
        rows = pl.ds(pl.multiple_of(i * step, step), step)
        unit, _ = normalize(codes[rows, :].astype(jnp.float32))
        low = (unit * row(first_gain_ref) + row(first_shift_ref)).astype(jnp.bfloat16)
        normed[rows, :] = low
        query_rows = nn(low, qkv_weight[:, 0:features]) + row(qb_ref)
        query_rows = query_rows.astype(jnp.bfloat16) * jnp.asarray(HEAD_DIM**-0.5, jnp.bfloat16)
        key_rows = nn(low, qkv_weight[:, features : 2 * features]).astype(jnp.bfloat16)
        value_rows = (nn(low, qkv_weight[:, 2 * features :]) + row(vb_ref)).astype(jnp.bfloat16)
        for pair in range(pairs):
            lanes = slice(pair * 128, (pair + 1) * 128)
            queries[pair, rows, :] = query_rows[:, lanes]
            keys[pair, rows, :] = key_rows[:, lanes]
            values[pair, rows, :] = value_rows[:, lanes]
        return 0

    lax.fori_loop(0, blocks, enter_rows, 0)
    onces = [
        pltpu.make_async_copy(source, target, once_sem.at[i])
        for i, (source, target) in enumerate(
            (
                (normed, normed_out),
                (queries, q_out),
                (keys, k_out),
                (values, v_out),
                (attended, attended_out),
                (columns, columns_out),
            )
        )
    ]
    for copy in onces[:4]:
        copy.start()

    for copy in loads[2:4]:
        copy.wait()
    lane = lax.broadcasted_iota(jnp.int32, (1, 128), 1)
    low_lanes = lane < 64
    local = lane % 64
    one = jnp.ones((), jnp.bfloat16)

    def attend_pair(pair, _):
        key_rows, value_rows, marks = keys[pair], values[pair], key_marks[...]
        keys_of = [jnp.where(low_lanes, key_rows, marks), jnp.where(low_lanes, marks, key_rows)]
        values_of = [jnp.where(low_lanes, value_rows, one), jnp.where(low_lanes, one, value_rows)]
        parts = [(first, head) for first in range(0, tokens, step) for head in range(2)]

        def scores_of(part):
            first, head = part
            rows = slice(first, first + step)
            rows_q, rows_m = queries[pair, rows, :], query_marks[rows, :]
            if head == 0:
                return nt(jnp.where(low_lanes, rows_q, rows_m), keys_of[0])
            return nt(jnp.where(low_lanes, rows_m, rows_q), keys_of[1])

        waiting = [scores_of(part) for part in parts[:2]]
        outs, logs = [None, None], [None, None]
        for i, (first, head) in enumerate(parts):
            scores = waiting.pop(0)
            if i + 2 < len(parts):
                waiting.append(scores_of(parts[i + 2]))
            top = jnp.max(scores, axis=1, keepdims=True)
            weights = jnp.exp(scores - top).astype(jnp.bfloat16)
            sums = nn(weights, values_of[head])
            outs[head] = sums / pltpu.roll(sums, 64, 1)
            logs[head] = top + jnp.log(sums)
            if head == 1:
                rows = slice(first, first + step)
                attended[pair, rows, :] = jnp.where(low_lanes, outs[0], outs[1]).astype(jnp.bfloat16)
                minus = -jnp.where(low_lanes, logs[1], logs[0])
                part1 = minus.astype(jnp.bfloat16).astype(jnp.float32)
                part2 = (minus - part1).astype(jnp.bfloat16).astype(jnp.float32)
                part3 = minus - part1 - part2
                column = jnp.where(local == 5, part3, query_marks[rows, :].astype(jnp.float32))
                column = jnp.where(local == 4, part2, column)
                column = jnp.where(local == 3, part1, column)
                columns[pair, rows, :] = column.astype(jnp.bfloat16)
        return 0

    lax.fori_loop(0, pairs, attend_pair, 0)
    for copy in onces[4:]:
        copy.start()

    for copy in loads[4:]:
        copy.wait()

    def stage_copies(i):
        rows = pl.ds(pl.multiple_of(i * step, step), step)
        slot = lax.rem(i, 2)
        moves = (
            (features_stage, features_out.at[rows]),
            (normed_two_stage, normed_two_out.at[rows]),
            (hidden_stage, hidden_out.at[:, rows]),
            (pre_stage, pre_out.at[rows]),
            (middle_grad_stage, middle_grad_out.at[rows]),
            (branch_stage, branch_out.at[rows]),
            (attended_grad_stage, attended_grad_out.at[:, rows]),
        )
        return [
            pltpu.make_async_copy(source.at[slot], target, stage_sem.at[slot, k])
            for k, (source, target) in enumerate(moves)
        ]

    def middle_rows(i, _):
        rows = pl.ds(pl.multiple_of(i * step, step), step)
        slot = lax.rem(i, 2)
        for copy in block_copies(i):
            copy.wait()

        @pl.when(i + 1 < blocks)
        def _():
            for copy in block_copies(i + 1):
                copy.start()

        @pl.when(i >= 2)
        def _():
            for copy in stage_copies(i - 2):
                copy.wait()

        attended_rows = jnp.concatenate([attended[p, rows, :] for p in range(pairs)], axis=1)
        branch = nn(attended_rows, out_weight[...]) + row(out_bias_ref)
        middle = codes[rows, :].astype(jnp.float32) + branch
        unit, scale = normalize(middle)
        low = (unit * row(gain_ref) + row(shift_ref)).astype(jnp.bfloat16)
        normed_two_stage[slot] = low
        total = middle + row(down_bias_ref)
        grad = jnp.zeros_like(middle)
        for first in range(0, up_weight.shape[1], features):
            block = slice(first, first + features)
            weight = up_weight[:, block]
            hidden_pre = nn(low, weight) + up_bias_ref[:, block].astype(jnp.float32)
            act, slope = gelu_parts(hidden_pre)
            hidden = act.astype(jnp.bfloat16)
            hidden_stage[slot, block, :] = hidden.T
            pre = hidden_grad[slot, :, block].astype(jnp.float32) * slope
            pre = pre.astype(jnp.bfloat16)
            pre_stage[slot, :, block] = pre
            up_bias_sum[:, block] += jnp.sum(pre.astype(jnp.float32), axis=0, keepdims=True)
            total = total + nn(hidden, down_weight[block, :])
            grad = grad + nt(pre, weight)
        features_stage[slot] = total.astype(jnp.bfloat16)
        add_rows(gain_sum, grad * unit)
        add_rows(shift_sum, grad)
        middle_grad = final[slot] + norm_back(grad, row(gain_ref), unit, scale)
        middle_grad_stage[slot] = middle_grad
        branch_grad = middle_grad.astype(jnp.bfloat16)
        branch_stage[slot] = branch_grad
        add_rows(out_bias_sum, branch_grad.astype(jnp.float32))
        attended_grad = nt(branch_grad, out_weight[...]).astype(jnp.bfloat16)
        for pair in range(pairs):
            attended_grad_stage[slot, pair] = attended_grad[:, pair * 128 : (pair + 1) * 128]
        for copy in stage_copies(i):
            copy.start()
        return 0

    lax.fori_loop(0, blocks, middle_rows, 0)
    for copy in onces:
        copy.wait()
    for i in (blocks - 2, blocks - 1):
        for copy in stage_copies(i):
            copy.wait()


def forward(inputs, vectors, step=256):
    codes, qkv_weight, up_weight = inputs[0], inputs[5], inputs[7]
    tokens, features = codes.shape
    wide = up_weight.shape[1]
    pairs = features // 128
    anywhere = pl.BlockSpec(memory_space=pl.ANY)
    inside = pl.BlockSpec(memory_space=pltpu.VMEM)
    dma = pltpu.SemaphoreType.DMA
    low, full = jnp.bfloat16, jnp.float32
    paired = (pairs, tokens, 128)
    shapes = [
        ((tokens, features), low),
        (paired, low),
        (paired, low),
        (paired, low),
        (paired, low),
        (paired, low),
        ((tokens, features), low),
        ((tokens, features), low),
        ((wide, tokens), low),
        ((tokens, wide), low),
        ((tokens, features), full),
        ((tokens, features), low),
        (paired, low),
    ]
    sums = [(1, features)] * 3 + [(1, wide)]
    return pl.pallas_call(
        partial(forward_kernel, step=step),
        in_specs=[anywhere] * 9 + [inside] * 9,
        out_specs=[anywhere] * len(shapes) + [inside] * 4,
        out_shape=[pltpu.HBM(shape, dtype) for shape, dtype in shapes]
        + [jax.ShapeDtypeStruct(shape, full) for shape in sums],
        scratch_shapes=[
            pltpu.VMEM((tokens, features), low),
            pltpu.VMEM((tokens, 128), low),
            pltpu.VMEM((tokens, 128), low),
            pltpu.VMEM(qkv_weight.shape, low),
            pltpu.VMEM((features, features), low),
            pltpu.VMEM((features, wide), low),
            pltpu.VMEM((wide, features), low),
            pltpu.VMEM((tokens, features), low),
        ]
        + [pltpu.VMEM(paired, low)] * 5
        + [
            pltpu.VMEM((2, step, features), full),
            pltpu.VMEM((2, step, wide), low),
            pltpu.VMEM((2, step, features), low),
            pltpu.VMEM((2, step, features), low),
            pltpu.VMEM((2, wide, step), low),
            pltpu.VMEM((2, step, wide), low),
            pltpu.VMEM((2, step, features), full),
            pltpu.VMEM((2, step, features), low),
            pltpu.VMEM((2, pairs, step, 128), low),
            dma((7,)),
            dma((6,)),
            dma((2, 2)),
            dma((2, 7)),
        ],
        compiler_params=pltpu.CompilerParams(vmem_limit_bytes=60 * 2**20),
        cost_estimate=pl.CostEstimate(
            flops=2 * tokens * features * (5 * features + 3 * wide) + 16 * tokens**2 * features,
            bytes_accessed=4 * features * wide + 6 * tokens * wide + 30 * tokens * features,
            transcendentals=2 * tokens * wide + 2 * tokens**2 * pairs,
        ),
        name="forward",
    )(*inputs, *vectors)


def fetch_kernel(
    fetched_ref,
    slot_ref,
    cotangent_ref,
    moved_ref,
    taps_ref,
    down_ref,
    codes_out,
    final_out,
    low_out,
    behind_out,
    hidden_out,
    pixel_bias_sum,
    down_bias_sum,
    got,
    sends,
    shifted,
    total,
    other,
    low,
    taken,
    weight,
    down,
    hidden,
    hop_sent,
    hop_got,
    code_sent,
    code_got,
    own_sem,
    weight_sem,
    taken_sem,
    down_sem,
    hidden_sem,
    out_sem,
    *,
    tiling,
):
    gr, ty, tx = lax.axis_index("gr"), lax.axis_index("ty"), lax.axis_index("tx")
    across = lax.axis_size("tx")
    members = lax.axis_size("ty") * across
    me = ty * across + tx
    others = [lax.rem(me + step, members) for step in range(1, members)]
    tokens, features = cotangent_ref.shape
    each = tokens // members
    wide = tiling[1] * tiling[3]

    def place(member):
        return (gr, member // across, lax.rem(member, across))

    barrier = pltpu.get_barrier_semaphore()
    for member in others:
        pl.semaphore_signal(
            barrier, inc=1, device_id=place(member), device_id_type=pl.DeviceIdType.MESH
        )
    pl.semaphore_wait(barrier, members - 1)

    def hop_put(i):
        return pltpu.make_async_remote_copy(
            src_ref=fetched_ref.at[others[i]],
            dst_ref=got.at[me],
            send_sem=hop_sent.at[i],
            recv_sem=hop_got.at[i],
            device_id=place(others[i]),
            device_id_type=pl.DeviceIdType.MESH,
        )

    def code_put(i):
        return pltpu.make_async_remote_copy(
            src_ref=sends.at[others[i]],
            dst_ref=codes_out.at[me],
            send_sem=code_sent.at[i],
            recv_sem=code_got.at[i],
            device_id=place(others[i]),
            device_id_type=pl.DeviceIdType.MESH,
        )

    own_rows = pltpu.make_async_copy(fetched_ref.at[me], got.at[me], own_sem.at[0])
    own_codes = pltpu.make_async_copy(sends.at[me], codes_out.at[me], own_sem.at[1])
    for i in range(members - 1):
        hop_put(i).start()
    own_rows.start()

    def weight_copy(tap):
        slot = lax.rem(tap, 2)
        return pltpu.make_async_copy(taps_ref.at[tap], weight.at[slot], weight_sem.at[slot])

    def taken_copy(tap):
        slot = lax.rem(tap, 2)
        columns = pl.ds(pl.multiple_of(tap * features, 128), features)
        return pltpu.make_async_copy(taken.at[slot], behind_out.at[:, columns], taken_sem.at[slot])

    def down_copy(j):
        slot = lax.rem(j, 2)
        rows = pl.ds(pl.multiple_of(j * features, 128), features)
        return pltpu.make_async_copy(down_ref.at[rows], down.at[slot], down_sem.at[slot])

    def hidden_copy(j):
        slot = lax.rem(j, 2)
        columns = pl.ds(pl.multiple_of(j * features, 128), features)
        return pltpu.make_async_copy(hidden.at[slot], hidden_out.at[:, columns], hidden_sem.at[slot])

    weight_copy(0).start()
    down_copy(0).start()
    other[...] = cotangent_ref[...].astype(jnp.float32)
    pixel_bias_sum[...] = jnp.sum(other[...], axis=0, keepdims=True)
    for tiled, plain in groups(*tiling):
        total[plain : plain + tiling[3], :] = other[tiled : tiled + tiling[3], :]
    rows_plain = total[...]
    for j in range(3):
        moved_rows = rows_plain if j == 1 else pltpu.roll(rows_plain, (1 - j) % tokens, 0)
        shifted[j, 0:wide, :] = jnp.zeros((wide, features), jnp.bfloat16)
        shifted[j, wide + tokens :, :] = jnp.zeros((wide, features), jnp.bfloat16)
        shifted[j, wide : wide + tokens, :] = moved_rows.astype(jnp.bfloat16)
    total[...] = jnp.zeros_like(total)

    def one_tap(tap, _):
        slot = lax.rem(tap, 2)
        weight_copy(tap).wait()
        pl.when(tap < 8)(lambda: weight_copy(tap + 1).start())
        pl.when(tap >= 2)(lambda: taken_copy(tap - 2).wait())
        below, right = 2 - tap // 3, 2 - lax.rem(tap, 3)
        step = tokens // 4
        for i in range(4):
            rows = slice(i * step, (i + 1) * step)
            first = pl.multiple_of(below * wide + i * step, wide)
            here = moved_ref[1, wide + i * step : wide + (i + 1) * step, :]
            same = moved_ref[right, pl.ds(first, step), :] == here
            mask = jnp.where(same, 1.0, 0.0).astype(jnp.bfloat16)
            mask = jnp.concatenate([mask] * (features // 128), axis=1)
            piece = shifted[right, pl.ds(first, step), :] * mask
            taken[slot, rows, :] = piece
            total[rows, :] += nt(piece, weight[slot])
        taken_copy(tap).start()
        return 0

    lax.fori_loop(0, 9, one_tap, 0)
    for tiled, plain in groups(*tiling):
        other[tiled : tiled + tiling[3], :] = total[plain : plain + tiling[3], :]
    low[...] = other[...].astype(jnp.bfloat16)
    results = [
        pltpu.make_async_copy(other, final_out, out_sem.at[0]),
        pltpu.make_async_copy(low, low_out, out_sem.at[1]),
    ]
    for result in results:
        result.start()
    down_bias_sum[...] = jnp.sum(low[...].astype(jnp.float32), axis=0, keepdims=True)

    own_rows.wait()
    for i in range(members - 1):
        hop_put(i).wait_recv()
    arrived = got[...].reshape(got.shape[0] * got.shape[1], features)
    lane = lax.broadcasted_iota(jnp.int32, (each, 128), 1)
    for member in range(members):
        slots = slot_ref[member * each : (member + 1) * each, :]
        hot = [
            jnp.where(slots == lane + first, 1.0, 0.0).astype(jnp.bfloat16)
            for first in range(0, arrived.shape[0], 128)
        ]
        rows = nn(jnp.concatenate(hot, axis=1), arrived)
        sends[member] = rows.astype(jnp.bfloat16)
    for i in range(members - 1):
        code_put(i).start()
    own_codes.start()

    def one_block(j, _):
        slot = lax.rem(j, 2)
        down_copy(j).wait()
        pl.when(j < 3)(lambda: down_copy(j + 1).start())
        pl.when(j >= 2)(lambda: hidden_copy(j - 2).wait())
        hidden[slot] = nt(low[...], down[slot]).astype(jnp.bfloat16)
        hidden_copy(j).start()
        return 0

    lax.fori_loop(0, 4, one_block, 0)
    for copy in (taken_copy(7), taken_copy(8), hidden_copy(2), hidden_copy(3), own_codes, *results):
        copy.wait()
    for i in range(members - 1):
        hop_put(i).wait_send()
        code_put(i).wait_send()
        code_put(i).wait_recv()


def fetch(fetched, slots, cotangent, moved, taps, down_weight, tiling):
    tokens, features = cotangent.shape
    members = tiling[0] * tiling[1]
    blocks = down_weight.shape[0] // features
    anywhere = pl.BlockSpec(memory_space=pl.ANY)
    inside = pl.BlockSpec(memory_space=pltpu.VMEM)
    dma = pltpu.SemaphoreType.DMA
    low, wide = jnp.bfloat16, jnp.float32
    padded = tokens + 2 * tiling[1] * tiling[3]
    return pl.pallas_call(
        partial(fetch_kernel, tiling=tiling),
        in_specs=[anywhere, inside, inside, inside, anywhere, anywhere],
        out_specs=[anywhere] * 5 + [inside] * 2,
        out_shape=[
            jax.ShapeDtypeStruct((members, tokens // members, features), low),
            jax.ShapeDtypeStruct((tokens, features), wide),
            jax.ShapeDtypeStruct((tokens, features), low),
            jax.ShapeDtypeStruct((tokens, 9 * features), low),
            jax.ShapeDtypeStruct((tokens, blocks * features), low),
            jax.ShapeDtypeStruct((1, features), wide),
            jax.ShapeDtypeStruct((1, features), wide),
        ],
        scratch_shapes=[
            pltpu.VMEM(fetched.shape, low),
            pltpu.VMEM((members, tokens // members, features), low),
            pltpu.VMEM((3, padded, features), low),
            pltpu.VMEM((tokens, features), wide),
            pltpu.VMEM((tokens, features), wide),
            pltpu.VMEM((tokens, features), low),
            pltpu.VMEM((2, tokens, features), low),
            pltpu.VMEM((2, features, features), low),
            pltpu.VMEM((2, features, features), low),
            pltpu.VMEM((2, tokens, features), low),
        ]
        + [dma((members - 1,))] * 4
        + [dma((2,))] * 6,
        compiler_params=pltpu.CompilerParams(
            collective_id=3, has_side_effects=True, vmem_limit_bytes=60 * 2**20
        ),
        cost_estimate=pl.CostEstimate(
            flops=26 * tokens * features * features,
            bytes_accessed=40 * tokens * features,
            transcendentals=0,
        ),
        name="fetch",
    )(fetched, slots, cotangent, moved, taps, down_weight)


def finish_kernel(*refs, blocks, homes, lead, slots, got_slots, tiling):
    (
        q_ref,
        k_ref,
        v_ref,
        col_ref,
        ka_ref,
        o_ref,
        g_ref,
        codes_ref,
        middle_ref,
        features_ref,
        behind_ref,
        normed_two_ref,
        pre_ref,
        hidden_ref,
        lower_ref,
        branch_ref,
        normed_ref,
        weight_ref,
        recon_ref,
        gain_ref,
        out_bias_sum,
        second_gain_sum,
        second_shift_sum,
        up_bias_sum,
        down_bias_sum,
        pixel_bias_sum,
    ) = refs[:26]
    outs = refs[26:31]
    vector_out, recon_out, share_out = refs[31:34]
    refs = refs[34:]
    (parts, got0, got1, got2, got3, got4, whole) = refs[:7]
    (operands, turned, heads, marks, sums, sums_got, middle, share, k_sum, v_sum, dqkv) = refs[7:18]
    (s0, r0, s1, r1, s2, r2, s3, r3, s4, r4, s5, r5, s6, r6) = refs[18:32]
    (out_sem, operand_sem, turned_sem, head_sem, once_sem, free, own_sem) = refs[32:39]
    (recon_sent, recon_got, share_sent, share_got, sums_sent, sums_recv) = refs[39:45]
    count = (blocks + 1) // 2
    tokens, features = normed_ref.shape
    each = tokens // (tiling[0] * tiling[1])
    gr, ty, tx = lax.axis_index("gr"), lax.axis_index("ty"), lax.axis_index("tx")
    x, core, half, par = gr // 2, gr % 2, tx // 2, tx % 2
    across = lax.axis_size("tx")
    members = lax.axis_size("ty") * across
    me = ty * across + tx
    mate = (2 * x + 1 - core, ty, tx)
    over_x = (2 * (1 - x) + core, ty, tx)
    over_y = (gr, 1 - ty, tx)
    near = (gr, ty, half * 2 + (1 - par))
    away = (gr, ty, (1 - half) * 2 + par)
    others = [lax.rem(me + step, members) for step in range(1, members)]

    def place(member):
        return (gr, member // across, lax.rem(member, across))

    barrier = pltpu.get_barrier_semaphore()
    greeted = [mate, over_x] + [place(member) for member in others]
    for device in greeted:
        pl.semaphore_signal(barrier, inc=1, device_id=device, device_id_type=pl.DeviceIdType.MESH)
    pl.semaphore_wait(barrier, len(greeted))
    width = features // 2
    own_columns = pl.ds(pl.multiple_of(core * width, 128), width)

    def put(source, target, sent, received, device):
        return pltpu.make_async_remote_copy(
            src_ref=source,
            dst_ref=target,
            send_sem=sent,
            recv_sem=received,
            device_id=device,
            device_id_type=pl.DeviceIdType.MESH,
        )

    def recon_put(i):
        member = others[i]
        return put(
            recon_ref.at[member], recon_out.at[me], recon_sent.at[i], recon_got.at[i], place(member)
        )

    def share_put(i, member=None):
        member = others[i] if member is None else member
        rows = pl.ds(pl.multiple_of(member * each, 128), each)
        return put(share.at[rows], share_out.at[me], share_sent.at[i], share_got.at[i], place(member))

    def columns(ref, index):
        return ref.at[:, pl.ds(pl.multiple_of(index * features, 128), features)]

    def operand(i, source):
        return pltpu.make_async_copy(source, operands.at[i], operand_sem.at[i])

    def load(sources):
        for i, source in enumerate(sources):
            operand(i, source).start()

    def load_operands(c):
        @pl.when(c < 4)
        def _():
            load([features_ref, columns(behind_ref, 2 * c), features_ref, columns(behind_ref, 2 * c + 1)])

        @pl.when((c == 4) | (c == 5))
        def _():
            load([lower_ref] * 4)
            for b in range(2):
                turned_copy(b, 2 * (c - 4) + b).start()

        @pl.when(c == 6)
        def _():
            load([normed_ref, gradient(0), normed_ref, gradient(1)])

        @pl.when(c == 7)
        def _():
            load([normed_ref, gradient(2), features_ref, columns(behind_ref, 8)])

        @pl.when(c == 8)
        def _():
            for pair in range(o_ref.shape[0]):
                target = operands.at[0, :, pl.ds(pair * 128, 128)]
                pltpu.make_async_copy(o_ref.at[pair], target, operand_sem.at[0]).start()
            for i, source in ((1, branch_ref), (2, normed_two_ref), (3, columns(pre_ref, 0))):
                operand(i, source).start()

        @pl.when(c == 9)
        def _():
            load([normed_two_ref, columns(pre_ref, 1), normed_two_ref, columns(pre_ref, 2)])

        @pl.when(c == 10)
        def _():
            load([normed_two_ref, columns(pre_ref, 3), lower_ref, lower_ref])

    def gradient(i):
        return dqkv.at[i, pl.ds(0, tokens)]

    def turned_copy(b, index):
        return pltpu.make_async_copy(hidden_ref.at[:, index], turned.at[b], turned_sem.at[b])

    def wait_operands():
        for i in range(4):
            operand(i, normed_ref).wait()

    def level0(c, b):
        slot = lax.rem(c, slots)
        return put(
            parts.at[slot, b, 1 - core], got0.at[lax.rem(c, got_slots), b], s0.at[c, b], r0.at[c, b], mate
        )

    def both_x(c):
        return (c == 2) | (c == 7)

    def only_y(c):
        return (c < count - 1) & (c != 2) & (c != 7)

    def level1x(c, b=0):
        slot = lax.rem(c, slots)
        return put(
            parts.at[slot, b, core, :, :, :, 1 - x], got1.at[c, b], s1.at[c, b], r1.at[c, b], over_x
        )

    def level1y(c):
        slot = lax.rem(c, slots)
        return put(parts.at[slot, 1, core, 1 - ty], got1.at[c, 1], s1.at[c, 1], r1.at[c, 1], over_y)

    def level2y(c, b=0):
        return put(got1.at[c, b, 1 - ty], got2.at[c, b], s2.at[c, b], r2.at[c, b], over_y)

    def level2x(c):
        return put(got1.at[c, 1, :, :, 1 - x], got2.at[c, 1], s2.at[c, 1], r2.at[c, 1], over_x)

    def level3(c):
        return put(got2.at[c, :, :, 1 - par], got3.at[c], s3.at[c], r3.at[c], near)

    def level4(c):
        return put(got3.at[c, :, 1 - half], got4.at[c], s4.at[c], r4.at[c], away)

    def level5(c):
        where = whole.at[pl.ds(2 * c, 2), x, :, own_columns]
        return put(where, where, s5.at[c], r5.at[c], over_x)

    def level6(c):
        where = whole.at[pl.ds(2 * c, 2), :, :, own_columns]
        return put(where, where, s6.at[c], r6.at[c], mate)

    def stage1(c):
        slot, got_slot = lax.rem(c, slots), lax.rem(c, got_slots)
        for b in range(2):

            @pl.when((b == 0) | (c < count - 1))
            def _():
                level0(c, b).wait_recv()

                def add(i, _):
                    y, h, p = i // 4, lax.rem(i // 2, 2), lax.rem(i, 2)
                    sum_of = parts[slot, b, core, y, h, p] + got0[got_slot, b, y, h, p]
                    parts[slot, b, core, y, h, p] = sum_of
                    return 0

                lax.fori_loop(0, 8, add, 0)

        @pl.when(c < count - got_slots)
        def _():
            pl.semaphore_signal(free, inc=1, device_id=mate, device_id_type=pl.DeviceIdType.MESH)

        level1x(c).start()
        pl.when(only_y(c))(lambda: level1y(c).start())
        pl.when(both_x(c))(lambda: level1x(c, 1).start())

    def stage2(c):
        slot = lax.rem(c, slots)
        level1x(c).wait_recv()
        got1[c, 0] = got1[c, 0] + parts[slot, 0, core, :, :, :, x]
        level2y(c).start()

        @pl.when(only_y(c))
        def _():
            level1y(c).wait_recv()
            got1[c, 1] = got1[c, 1] + parts[slot, 1, core, ty]
            level2x(c).start()
            level1y(c).wait_send()

        @pl.when(both_x(c))
        def _():
            level1x(c, 1).wait_recv()
            got1[c, 1] = got1[c, 1] + parts[slot, 1, core, :, :, :, x]
            level2y(c, 1).start()
            level1x(c, 1).wait_send()

        level1x(c).wait_send()

    def stage3(c):
        level2y(c).wait_recv()
        got2[c, 0] = got2[c, 0] + got1[c, 0, ty]

        @pl.when(only_y(c))
        def _():
            level2x(c).wait_recv()
            got2[c, 1] = got2[c, 1] + got1[c, 1, :, :, x]

        @pl.when(both_x(c))
        def _():
            level2y(c, 1).wait_recv()
            got2[c, 1] = got2[c, 1] + got1[c, 1, ty]

        @pl.when(c == count - 1)
        def _():
            got2[c, 1] = jnp.zeros(got2.shape[2:], jnp.bfloat16)

        level3(c).start()

    def stage4(c):
        level3(c).wait_recv()
        got3[c] = got3[c] + got2[c, :, :, par]
        level4(c).start()

    def stage5(c):
        level4(c).wait_recv()
        whole[pl.ds(2 * c, 2), x, :, own_columns] = got4[c] + got3[c, :, half]
        level5(c).start()

    def stage6(c):
        level5(c).wait_recv()
        level6(c).start()

    def weight_block(slot, b, of_hidden):
        for y in range(2):
            if of_hidden:
                left = turned[b, y * 4 : (y + 1) * 4].reshape(width, tokens)
                block = nn(left, operands[2 * b + 1])
            else:
                left = operands[2 * b, :, y * width : (y + 1) * width]
                block = tn(left, operands[2 * b + 1])
            block = block.astype(jnp.bfloat16)
            for h in range(2):
                piece = block[:, h * width : (h + 1) * width]
                parts[slot, b, h, y] = piece.reshape(parts.shape[4:])

    def make_blocks(c):
        slot = lax.rem(c, slots)

        @pl.when(c >= slots)
        def _():
            for b in range(2):
                level0(c - slots, b).wait_send()

        wait_operands()
        of_hidden = (c == 4) | (c == 5)

        @pl.when(of_hidden)
        def _():
            for b in range(2):
                turned_copy(b, 0).wait()
                weight_block(slot, b, True)

        @pl.when(jnp.logical_not(of_hidden))
        def _():
            weight_block(slot, 0, False)

        @pl.when(jnp.logical_not(of_hidden) & (c < count - 1))
        def _():
            weight_block(slot, 1, False)

        @pl.when(c >= got_slots)
        def _():
            pl.semaphore_wait(free, 1)

        level0(c, 0).start()
        pl.when(c < count - 1)(lambda: level0(c, 1).start())

    lane = lax.broadcasted_iota(jnp.int32, (1, 128), 1)
    low = lane < 64
    local = lane % 64

    def head_copies(pair):
        slot = lax.rem(pair, 2)
        return [
            pltpu.make_async_copy(ref.at[pair], heads.at[slot, i], head_sem.at[slot, i])
            for i, ref in enumerate((q_ref, k_ref, v_ref, col_ref, o_ref, g_ref))
        ]

    pairs = features // 128
    step = tokens // 2

    def attend_part(u, _):
        pair, part = u // 2, lax.rem(u, 2)
        slot = lax.rem(pair, 2)

        @pl.when(part == 0)
        def _():
            for copy in head_copies(pair):
                copy.wait()

            @pl.when(pair < pairs - 1)
            def _():
                for copy in head_copies(pair + 1):
                    copy.start()

            k_sum[...] = jnp.zeros_like(k_sum)
            v_sum[...] = jnp.zeros_like(v_sum)

        rows = pl.ds(pl.multiple_of(part * step, step), step)
        zero, one = jnp.zeros((), jnp.bfloat16), jnp.ones((), jnp.bfloat16)
        queries, columns_ = heads[slot, 0, rows, :], heads[slot, 3, rows, :]
        key_rows, values = heads[slot, 1], heads[slot, 2]
        out, grad = heads[slot, 4, rows, :], heads[slot, 5, rows, :]
        key_columns = jnp.where((local >= 3) & (local < 6), one, marks[...])
        value_columns = jnp.where(local < 2, one, zero)
        keys_across = key_rows.T
        both = grad.astype(jnp.float32) * out.astype(jnp.float32)
        of_low = -jnp.sum(jnp.where(low, both, 0.0), axis=1, keepdims=True)
        of_high = -jnp.sum(jnp.where(low, 0.0, both), axis=1, keepdims=True)
        inner = jnp.where(low, of_high, of_low)
        first = inner.astype(jnp.bfloat16).astype(jnp.float32)
        grad_columns = jnp.where(
            local == 0, first, jnp.where(local == 1, inner - first, 0.0)
        ).astype(jnp.bfloat16)
        query_parts, key_parts, value_parts = [], [], []
        for head in range(2):
            own = low if head == 0 else ~low
            scores = nt(jnp.where(own, key_rows, key_columns), jnp.where(own, queries, columns_))
            weights = jnp.exp(scores)
            change = nt(jnp.where(own, values, value_columns), jnp.where(own, grad, grad_columns))
            score_grad = (weights * change).astype(jnp.bfloat16)
            value_parts.append(nn(weights.astype(jnp.bfloat16), grad))
            key_parts.append(nn(score_grad, queries))
            query_parts.append(nn(keys_across, score_grad))
        k_sum[...] += jnp.where(low, key_parts[0], key_parts[1])
        v_sum[...] += jnp.where(low, value_parts[0], value_parts[1])
        upper = lax.broadcasted_iota(jnp.int32, (128, 1), 0) < 64
        query_grad = jnp.where(upper, query_parts[0], query_parts[1]).T
        lanes = pl.ds(pl.multiple_of(pair * 128, 128), 128)
        dqkv[0, rows, lanes] = (query_grad * HEAD_DIM**-0.5).astype(jnp.bfloat16)

        @pl.when(part == 1)
        def _():
            dqkv[1, 0:tokens, lanes] = k_sum[...].astype(jnp.bfloat16)
            dqkv[2, 0:tokens, lanes] = v_sum[...].astype(jnp.bfloat16)

        return 0

    def back_copies():
        copies = [
            pltpu.make_async_copy(
                weight_ref.at[:, pl.ds(features * i, features)],
                operands.at[i, pl.ds(0, features)],
                operand_sem.at[i],
            )
            for i in range(3)
        ]
        return copies + [operand(3, codes_ref)]

    def back():
        for copy in back_copies():
            copy.wait()
        middle_copy().wait()

        def rows_back(i, _):
            rows = pl.ds(pl.multiple_of(i * 256, 256), 256)
            grad = nt(dqkv[0, rows, :], operands[0, 0:features, :])
            grad = grad + nt(dqkv[1, rows, :], operands[1, 0:features, :])
            grad = grad + nt(dqkv[2, rows, :], operands[2, 0:features, :])
            start = operands[3, rows, :].astype(jnp.float32)
            unit, scale = normalize(start)
            for at, addend in enumerate(
                (dqkv[0, rows, :].astype(jnp.float32), dqkv[2, rows, :].astype(jnp.float32), grad * unit, grad)
            ):
                sums[0, at : at + 1, :] += jnp.sum(addend, axis=0, keepdims=True)
            start_grad = middle[rows, :] + norm_back(grad, row(gain_ref), unit, scale)
            share[rows, :] = (start_grad - 2.0 * commit_weight * start).astype(jnp.bfloat16)
            for member in range(members):

                @pl.when((i == member * each // 256) & (member != me))
                def _():
                    share_put(lax.rem(member - me - 1 + members, members), member).start()

            return 0

        lax.fori_loop(0, tokens // 256, rows_back, 0)
        own_share().start()
        sums_put(0).start()

    partners = (mate, over_x, over_y, near, away)

    def sums_put(i):
        return put(sums.at[i], sums_got.at[i], sums_sent.at[i], sums_recv.at[i], partners[i])

    def sums_step(i):
        sums_put(i).wait_recv()
        sums[i + 1] = sums[i] + sums_got[i]
        if i + 1 < len(partners):
            sums_put(i + 1).start()

    def own_share():
        rows = pl.ds(pl.multiple_of(me * each, 128), each)
        return pltpu.make_async_copy(share.at[rows], share_out.at[me], own_sem.at[0])

    def own_recon():
        return pltpu.make_async_copy(recon_ref.at[me], recon_out.at[me], own_sem.at[1])

    def middle_copy():
        return pltpu.make_async_copy(middle_ref, middle, once_sem.at[0])

    def marks_copy():
        return pltpu.make_async_copy(ka_ref, marks, once_sem.at[1])

    load_operands(0)
    marks_copy().start()
    middle_copy().start()
    for copy in head_copies(0):
        copy.start()
    for i in range(members - 1):
        recon_put(i).start()
    own_recon().start()
    sums[0] = jnp.zeros(sums.shape[1:], jnp.float32)
    for at, ref in ((4, out_bias_sum), (5, second_gain_sum), (6, second_shift_sum)):
        sums[0, at : at + 1, :] = ref[...]
    for k in range(4):
        sums[0, 7 + k : 8 + k, :] = up_bias_sum[:, k * features : (k + 1) * features]
    sums[0, 11:12, :] = down_bias_sum[...]
    sums[0, 12:13, :] = pixel_bias_sum[...]
    marks_copy().wait()
    stages = (stage1, stage2, stage3, stage4, stage5, stage6)
    last = 6

    def turn(t, _):
        @pl.when(t == last)
        def _():
            back()
            load_operands(last)

        @pl.when(t < count)
        def _():
            make_blocks(t)

        @pl.when((t < count - 1) & (t != last - 1))
        def _():
            load_operands(t + 1)

        @pl.when(t == last - 1)
        def _():
            for copy in back_copies():
                copy.start()

        def upto(s):
            return jnp.clip(2 * s, 0, 2 * pairs)

        lax.fori_loop(upto(t), upto(t + 1), attend_part, 0)
        for i in range(len(partners)):
            pl.when(t == last + 1 + i)(partial(sums_step, i))
        for stage, behind in zip(stages, lead):
            c = t - behind
            pl.when((c >= 0) & (c < count))(partial(stage, c))
        return 0

    lax.fori_loop(0, count + lead[-1], turn, 0)

    def finish(c, _):
        level6(c).wait_recv()
        for level in (level2y, level3, level4, level5, level6):
            level(c).wait_send()
        pl.when(only_y(c))(lambda: level2x(c).wait_send())
        pl.when(both_x(c))(lambda: level2y(c, 1).wait_send())
        return 0

    lax.fori_loop(0, count, finish, 0)
    for c in range(count - slots, count):
        for b in range(2 if c < count - 1 else 1):
            level0(c, b).wait_send()
    for i in range(len(partners)):
        sums_put(i).wait_send()
    vector_out[...] = sums[len(partners)]
    copies = []
    for block, (home, prefix, column) in enumerate(homes):
        out = outs[home] if prefix is None else outs[home].at[prefix]
        target = out.at[:, :, pl.ds(column, features)]
        copies.append(pltpu.make_async_copy(whole.at[block], target, out_sem.at[block]))
        copies[-1].start()
    for i in range(members - 1):
        recon_put(i).wait_recv()
        share_put(i).wait_recv()
        recon_put(i).wait_send()
        share_put(i).wait_send()
    own_recon().wait()
    own_share().wait()
    for copy in copies:
        copy.wait()


def finish(inputs, tiling):
    tokens, features = inputs[7].shape
    members = tiling[0] * tiling[1]
    blocks, slots, got_slots = 21, 3, 3
    count = (blocks + 1) // 2
    rows, width = features // members // 2, features // 2
    lead = (0, 2, 4, 6, 8, 10)
    homes = [(0, k, 0) for k in range(8)] + [(2, k, 0) for k in range(4)]
    homes += [(4, None, features * k) for k in range(3)] + [(0, 8, 0), (3, None, 0)]
    homes += [(1, None, features * k) for k in range(4)]
    shapes = [
        (9, 2, rows, features),
        (2, rows, 4 * features),
        (4, 2, rows, features),
        (2, rows, features),
        (2, rows, 3 * features),
        (members, tokens // members, features),
        (members, tokens // members, features),
    ]
    anywhere = pl.BlockSpec(memory_space=pl.ANY)
    inside = pl.BlockSpec(memory_space=pltpu.VMEM)
    dma = pltpu.SemaphoreType.DMA
    low, wide = jnp.bfloat16, jnp.float32
    cut = (2, 2, 2, 2, rows, width)
    scratch = [
        pltpu.VMEM((slots, 2, 2) + cut, low),
        pltpu.VMEM((got_slots, 2) + cut, low),
        pltpu.VMEM((count, 2) + cut[1:], low),
        pltpu.VMEM((count, 2) + cut[2:], low),
        pltpu.VMEM((count, 2) + cut[3:], low),
        pltpu.VMEM((count, 2) + cut[4:], low),
        pltpu.VMEM((2 * count, 2, rows, features), low),
        pltpu.VMEM((4, tokens, features), low),
        pltpu.VMEM((2, members, 2 * rows, tokens), low),
        pltpu.VMEM((2, 6, tokens, 128), low),
        pltpu.VMEM((tokens, 128), low),
        pltpu.VMEM((6, 16, features), wide),
        pltpu.VMEM((5, 16, features), wide),
        pltpu.VMEM((tokens, features), wide),
        pltpu.VMEM((tokens, features), low),
        pltpu.VMEM((tokens, 128), wide),
        pltpu.VMEM((tokens, 128), wide),
        pltpu.VMEM((3, tokens, features), low),
    ]
    scratch += [dma((count, 2))] * 6 + [dma((count,))] * 8
    scratch += [dma((blocks,)), dma((4,)), dma((2,)), dma((2, 6)), dma((2,))]
    scratch += [pltpu.SemaphoreType.REGULAR, dma((2,))]
    scratch += [dma((members - 1,))] * 4 + [dma((5,))] * 2
    return pl.pallas_call(
        partial(
            finish_kernel,
            blocks=blocks,
            homes=homes,
            lead=lead,
            slots=slots,
            got_slots=got_slots,
            tiling=tiling,
        ),
        in_specs=[anywhere] * 19 + [inside] * 7,
        out_specs=[anywhere] * 5 + [inside] + [anywhere] * 2,
        out_shape=[jax.ShapeDtypeStruct(shape, low) for shape in shapes[:5]]
        + [jax.ShapeDtypeStruct((16, features), wide)]
        + [jax.ShapeDtypeStruct(shape, low) for shape in shapes[5:]],
        scratch_shapes=scratch,
        compiler_params=pltpu.CompilerParams(
            collective_id=1, has_side_effects=True, vmem_limit_bytes=60 * 2**20
        ),
        cost_estimate=pl.CostEstimate(
            flops=2 * tokens * features * (24 * features) + 24 * tokens * tokens * features,
            bytes_accessed=100 * tokens * features,
            transcendentals=tokens * tokens * features // 64,
        ),
        name="finish",
    )(*inputs)


def on_device_grids(
    encoder_out,
    code_ids,
    segments,
    embed_table,
    recon_grad,
    qkv_weight,
    query_bias,
    value_bias,
    out_weight,
    out_bias,
    first_gain,
    first_shift,
    second_gain,
    second_shift,
    up_weight,
    up_bias,
    down_weight,
    down_bias,
    pixel_weight,
    pixel_bias,
):
    features = encoder_out.shape[-1]
    wide = jnp.float32
    down, across = lax.axis_size("ty"), lax.axis_size("tx")
    members = down * across
    axes = ("ty", "tx")
    tiling = (down, across) + encoder_out.shape[1:3]
    each = encoder_out.shape[1] * encoder_out.shape[2]
    tokens = members * each

    def line(vector):
        return vector.reshape(1, -1)

    def exchange(tiles):
        return lax.all_to_all(tiles, axes, split_axis=0, concat_axis=0, tiled=True)

    slots = 3 * each // 2
    asked, slot_index = ask(
        code_ids.reshape(members, each), segments.reshape(members, each), embed_table.shape[0], slots
    )
    asked, recon_grad = lax.optimization_barrier((asked, recon_grad))
    cotangent = exchange(recon_grad).reshape(tokens, features)
    moved, query_marks, key_marks = spread_marks(asked[:, 2], *tiling)
    asked = asked[:, :2].reshape(members, -1)[:, :slots].reshape(-1)
    fetched = embed_table.at[asked].get(mode="promise_in_bounds")
    pixel_taps = jnp.swapaxes(pixel_weight, 0, 1)
    codes, final_grad, lower_grad, behind, hidden_grad, pixel_bias_grad, down_bias_grad = fetch(
        fetched.reshape(members, slots, features),
        slot_index,
        cotangent,
        moved,
        pixel_taps,
        down_weight,
        tiling,
    )
    codes = codes.reshape(tokens, features)

    (
        normed,
        queries,
        key_rows,
        values,
        attended,
        columns,
        features_low,
        normed_two,
        hidden_turned,
        pre_grad,
        middle_grad,
        branch_grad,
        attended_grad,
        out_bias_grad,
        second_gain_grad,
        second_shift_grad,
        up_bias_grad,
    ) = forward(
        [
            codes,
            final_grad,
            hidden_grad,
            query_marks,
            key_marks,
            qkv_weight,
            out_weight,
            up_weight,
            down_weight,
        ],
        [
            line(first_gain),
            line(first_shift),
            line(query_bias),
            line(value_bias),
            line(out_bias),
            line(second_gain),
            line(second_shift),
            line(up_bias),
            line(down_bias),
        ],
    )
    recon_rows, features_plain = conv(features_low, moved, pixel_taps, line(pixel_bias), tiling)
    pixel_sum, up_sum, down_sum, out_sum, qkv_sum, vectors, recon_tiles, share_tiles = finish(
        [
            queries,
            key_rows,
            values,
            columns,
            key_marks,
            attended,
            attended_grad,
            codes,
            middle_grad,
            features_plain,
            behind,
            normed_two,
            pre_grad,
            hidden_turned.reshape(members, 4, features // members, tokens),
            lower_grad,
            branch_grad,
            normed,
            qkv_weight,
            recon_rows.reshape(members, each, features),
            line(first_gain),
            out_bias_grad,
            second_gain_grad,
            second_shift_grad,
            up_bias_grad,
            down_bias_grad,
            pixel_bias_grad,
        ],
        tiling,
    )
    input_tiles = (
        share_tiles.reshape(encoder_out.shape).astype(wide)
        + 2.0 * commit_weight * encoder_out.astype(wide)
    ).astype(jnp.bfloat16)
    rows = features // members
    member = lax.axis_index(axes)

    def mine(first, count=1):
        line_of = vectors[first : first + count].reshape(-1)
        return lax.dynamic_slice(line_of, (member * rows * count,), (rows * count,))

    def whole_sum(summed):
        return summed.reshape(-1, summed.shape[-1]).astype(wide)

    return (
        recon_tiles.reshape(encoder_out.shape),
        input_tiles,
        whole_sum(qkv_sum),
        mine(0),
        mine(1),
        whole_sum(out_sum),
        mine(4),
        mine(2),
        mine(3),
        mine(5),
        mine(6),
        whole_sum(up_sum),
        mine(7, 4),
        whole_sum(down_sum),
        mine(11),
        jnp.swapaxes(whole_sum(pixel_sum).reshape(9, rows, features), 0, 1),
        mine(12),
    )


def solution(mesh):
    in_specs = (
        P("gr", "ty", "tx", None),
        P("gr", "ty", "tx"),
        P("gr", "ty", "tx"),
        P(("ty", "tx"), None),
        P("gr", "ty", "tx", None),
        P(),
        P(),
        P(),
        P(),
        P(),
        P(),
        P(),
        P(),
        P(),
        P(),
        P(),
        P(),
        P(),
        P(),
        P(),
    )
    out_specs = (
        P("gr", "ty", "tx", None),
        P("gr", "ty", "tx", None),
        P(("ty", "tx"), None),
        P(("ty", "tx")),
        P(("ty", "tx")),
        P(("ty", "tx"), None),
        P(("ty", "tx")),
        P(("ty", "tx")),
        P(("ty", "tx")),
        P(("ty", "tx")),
        P(("ty", "tx")),
        P(("ty", "tx"), None),
        P(("ty", "tx")),
        P(("ty", "tx"), None),
        P(("ty", "tx")),
        P(("ty", "tx"), None, None),
        P(("ty", "tx")),
    )
    def on_device(encoder_out, *rest):
        members = mesh.shape["ty"] * mesh.shape["tx"]
        whole_grids = encoder_out.shape[0] == members and tuple(mesh.devices.shape) == (4, 2, 4)
        body = on_device_grids if whole_grids else on_device_bands
        return body(encoder_out, *rest)

    return jax.shard_map(
        on_device, mesh=mesh, in_specs=in_specs, out_specs=out_specs, check_vma=False
    )
```

```python
from functools import partial

import jax
import jax.numpy as jnp
from jax import lax
from jax.experimental import pallas as pl
from jax.experimental.pallas import tpu as pltpu
from jax.sharding import PartitionSpec as P

HEADS = 12
HEAD_DIM = 64


epsilon = 1e-06
commit_weight = 0.25


def with_halo(block, sides, width):
    for axis, dim in sides:
        count = lax.axis_size(axis)
        forward = [(i, i + 1) for i in range(count - 1)]
        backward = [(target, source) for source, target in forward]
        low = lax.ppermute(
            lax.slice_in_dim(block, block.shape[dim] - width, None, axis=dim), axis, forward
        )
        high = lax.ppermute(lax.slice_in_dim(block, 0, width, axis=dim), axis, backward)
        block = jnp.concatenate([low, block, high], axis=dim)
    return block


def layer_norm(values, gain, shift):
    center = values - jnp.mean(values, axis=-1, keepdims=True)
    spread = jnp.mean(center * center, axis=-1, keepdims=True)
    return center * lax.rsqrt(spread + epsilon) * gain + shift


def exact_gelu(values):
    return jax.nn.gelu(values, approximate=False)


def matmul(left_side, right_side):
    return jnp.dot(left_side, right_side, preferred_element_type=jnp.float32)


def left_product(left_side, right_side):
    return lax.dot_general(
        left_side, right_side, (((0,), (0,)), ((), ())), preferred_element_type=jnp.float32
    )


def right_product(left_side, right_side):
    return lax.dot_general(
        left_side, right_side, (((1,), (1,)), ((), ())), preferred_element_type=jnp.float32
    )


def pad_side(array, axis_index):
    widths = [(0, 0)] * array.ndim
    widths[axis_index] = (1, 1)
    return jnp.pad(array, widths)


def blocked(array, block_size):
    return array.reshape((array.shape[0] // block_size, block_size) + array.shape[1:])


def unblock(array):
    return array.reshape((-1,) + array.shape[2:])


def head_scores(queries, key_rows, marks_query, marks_key, head_count, score_scale):
    grid_count, query_rows, features = queries.shape
    query_heads = queries.reshape(grid_count, query_rows, head_count, features // head_count)
    key_heads = key_rows.reshape(grid_count, key_rows.shape[1], head_count, features // head_count)
    scores = (
        jnp.einsum("bqhd,bkhd->bhqk", query_heads, key_heads, preferred_element_type=jnp.float32)
        * score_scale
    )
    same_image = (marks_query[:, :, None] == marks_key[:, None, :])[:, None]
    return jnp.where(same_image, scores, -1000000000.0)


def attend_block(bundle, head_count, score_scale):
    queries, key_rows, values, marks_query, marks_key = bundle
    grid_count, query_rows, features = queries.shape
    scores = head_scores(queries, key_rows, marks_query, marks_key, head_count, score_scale)
    running_max = jnp.max(scores, axis=-1, keepdims=True)
    exponent = jnp.exp(scores - running_max)
    denominator = jnp.sum(exponent, axis=-1, keepdims=True)
    probability = (exponent / denominator).astype(jnp.bfloat16)
    value_heads = values.reshape(grid_count, values.shape[1], head_count, features // head_count)
    attended = jnp.einsum(
        "bhqk,bkhd->bqhd", probability, value_heads, preferred_element_type=jnp.float32
    )
    return (
        attended.reshape(grid_count, query_rows, features).astype(jnp.bfloat16),
        running_max + jnp.log(denominator),
    )


def attend_back(bundle, head_count, score_scale):
    queries, key_rows, values, marks_query, marks_key, log_total, out_grad = bundle
    grid_count, query_rows, features = queries.shape
    head_size = features // head_count
    scores = head_scores(queries, key_rows, marks_query, marks_key, head_count, score_scale)
    probability = jnp.exp(scores - log_total)
    query_heads = queries.reshape(grid_count, query_rows, head_count, head_size)
    key_heads = key_rows.reshape(grid_count, key_rows.shape[1], head_count, head_size)
    value_heads = values.reshape(grid_count, values.shape[1], head_count, head_size)
    grad_heads = out_grad.reshape(grid_count, query_rows, head_count, head_size)
    prob_grad = jnp.einsum(
        "bqhd,bkhd->bhqk", grad_heads, value_heads, preferred_element_type=jnp.float32
    )
    inner_sum = jnp.sum(probability * prob_grad, axis=-1, keepdims=True)
    score_grad = (probability * (prob_grad - inner_sum)).astype(jnp.bfloat16)
    query_grad = (
        jnp.einsum("bhqk,bkhd->bqhd", score_grad, key_heads, preferred_element_type=jnp.float32)
        * score_scale
    )
    key_grad = (
        jnp.einsum("bhqk,bqhd->bkhd", score_grad, query_heads, preferred_element_type=jnp.float32)
        * score_scale
    )
    value_grad = jnp.einsum(
        "bhqk,bqhd->bkhd",
        probability.astype(jnp.bfloat16),
        grad_heads,
        preferred_element_type=jnp.float32,
    )
    key_count = key_rows.shape[1]
    return (
        query_grad.reshape(grid_count, query_rows, features).astype(jnp.bfloat16),
        key_grad.reshape(grid_count, key_count, features),
        value_grad.reshape(grid_count, key_count, features),
    )


def on_device_bands(
    encoder_out,
    code_ids,
    segments,
    embed_table,
    recon_grad,
    qkv_weight,
    query_bias,
    value_bias,
    out_weight,
    out_bias,
    first_gain,
    first_shift,
    second_gain,
    second_shift,
    up_weight,
    up_bias,
    down_weight,
    down_bias,
    pixel_weight,
    pixel_bias,
):
    features = encoder_out.shape[-1]
    head_count = HEADS
    score_scale = float(HEAD_DIM) ** (-0.5)
    holder_count = lax.axis_size(("ty", "tx"))
    share_rows = embed_table.shape[0]
    flat_ids = code_ids.reshape(-1)
    row_count = flat_ids.shape[0]
    slot_count = 3 * row_count // (2 * holder_count)
    holder = flat_ids // share_rows
    offsets = flat_ids - holder * share_rows
    belongs = (holder[:, None] == jnp.arange(holder_count, dtype=jnp.int32)[None, :]).astype(
        jnp.int32
    )
    slot_rank = jnp.sum((jnp.cumsum(belongs, axis=0) - 1) * belongs, axis=1)
    slot_index = holder * slot_count + slot_rank
    requests = jnp.zeros((holder_count * slot_count,), jnp.int32).at[slot_index].set(offsets)
    requests = requests.reshape(holder_count, slot_count)
    fetched = jnp.take(
        embed_table,
        lax.all_to_all(requests, ("ty", "tx"), split_axis=0, concat_axis=0, tiled=True),
        axis=0,
    )
    returned = lax.all_to_all(fetched, ("ty", "tx"), split_axis=0, concat_axis=0, tiled=True)
    codes = returned.reshape(holder_count * slot_count, features)[slot_index].reshape(
        encoder_out.shape
    )
    marks_tile = (segments + 1).astype(jnp.bfloat16)
    arrived = (
        lax.all_to_all(encoder_out, "tx", split_axis=0, concat_axis=2, tiled=True),
        lax.all_to_all(codes, "tx", split_axis=0, concat_axis=2, tiled=True),
        lax.all_to_all(recon_grad, "tx", split_axis=0, concat_axis=2, tiled=True),
        lax.all_to_all(marks_tile, "tx", split_axis=0, concat_axis=2, tiled=True),
    )
    inputs_band, codes_band, cotangent_band, marks_band = arrived
    grid_count, band_rows, band_cols = marks_band.shape
    tokens = band_rows * band_cols
    all_rows = grid_count * tokens
    block_size = max(1, 512 // tokens)
    while grid_count % block_size:
        block_size -= 1
    start_rows = codes_band.reshape(all_rows, features).astype(jnp.float32)
    marks_query = marks_band.reshape(grid_count, tokens)
    normed, first_pull = jax.vjp(
        layer_norm, start_rows, first_gain.astype(jnp.float32), first_shift.astype(jnp.float32)
    )
    normed_low = normed.astype(jnp.bfloat16)
    projected = matmul(normed_low, qkv_weight)
    queries = (
        (projected[:, :features] + query_bias.astype(jnp.float32))
        .astype(jnp.bfloat16)
        .reshape(grid_count, tokens, features)
    )
    key_rows = (
        projected[:, features : 2 * features]
        .astype(jnp.bfloat16)
        .reshape(grid_count, tokens, features)
    )
    values = (
        (projected[:, 2 * features :] + value_bias.astype(jnp.float32))
        .astype(jnp.bfloat16)
        .reshape(grid_count, tokens, features)
    )
    bundle = (key_rows, values, marks_query)
    keys_all = lax.all_gather(bundle[0], "ty", axis=1, tiled=True)
    values_all = lax.all_gather(bundle[1], "ty", axis=1, tiled=True)
    marks_key = lax.all_gather(bundle[2], "ty", axis=1, tiled=True)
    attended_blocks, log_total = lax.map(
        partial(attend_block, head_count=head_count, score_scale=score_scale),
        (
            blocked(queries, block_size),
            blocked(keys_all, block_size),
            blocked(values_all, block_size),
            blocked(marks_query, block_size),
            blocked(marks_key, block_size),
        ),
    )
    attended = unblock(attended_blocks).reshape(all_rows, features)
    branch = matmul(attended, out_weight) + out_bias.astype(jnp.float32)
    middle = start_rows + branch
    normed_two, second_pull = jax.vjp(
        layer_norm, middle, second_gain.astype(jnp.float32), second_shift.astype(jnp.float32)
    )
    normed_two_low = normed_two.astype(jnp.bfloat16)
    hidden_pre = matmul(normed_two_low, up_weight) + up_bias.astype(jnp.float32)
    hidden_act, gelu_pull = jax.vjp(exact_gelu, hidden_pre)
    hidden_low = hidden_act.astype(jnp.bfloat16)
    output_rows = middle + (matmul(hidden_low, down_weight) + down_bias.astype(jnp.float32))
    features_low = output_rows.astype(jnp.bfloat16).reshape(
        grid_count, band_rows, band_cols, features
    )
    bundle = (features_low, marks_band, cotangent_band)
    grown = (
        with_halo(bundle[0], (("ty", 1),), 1),
        with_halo(bundle[1], (("ty", 1),), 1),
        with_halo(bundle[2], (("ty", 1),), 1),
    )
    features_pad, marks_pad, cotangent_pad = tuple((pad_side(member, 2) for member in grown))
    ahead_list = []
    behind_list = []
    for vertical in range(3):
        for lateral in range(3):
            inside = (
                marks_pad[:, vertical : vertical + band_rows, lateral : lateral + band_cols]
                == marks_band
            )
            ahead_list.append(
                jnp.where(
                    inside[..., None],
                    features_pad[:, vertical : vertical + band_rows, lateral : lateral + band_cols],
                    0,
                )
            )
            mirror_row = 2 - vertical
            mirror_col = 2 - lateral
            facing = (
                marks_pad[
                    :, mirror_row : mirror_row + band_rows, mirror_col : mirror_col + band_cols
                ]
                == marks_band
            )
            behind_list.append(
                jnp.where(
                    facing[..., None],
                    cotangent_pad[
                        :, mirror_row : mirror_row + band_rows, mirror_col : mirror_col + band_cols
                    ],
                    0,
                )
            )
    ahead = jnp.stack(ahead_list, axis=3)
    behind = jnp.stack(behind_list, axis=3)
    recon_band = jnp.einsum(
        "nhwkd,dkp->nhwp", ahead, pixel_weight, preferred_element_type=jnp.float32
    ) + pixel_bias.astype(jnp.float32)
    pixel_weight_grad = jnp.einsum(
        "nhwkd,nhwp->dkp", ahead, cotangent_band, preferred_element_type=jnp.float32
    )
    pixel_bias_grad = jnp.sum(cotangent_band.astype(jnp.float32), axis=(0, 1, 2))
    final_grad = jnp.einsum(
        "nhwkp,dkp->nhwd", behind, pixel_weight, preferred_element_type=jnp.float32
    ).reshape(all_rows, features)
    lower_grad = final_grad.astype(jnp.bfloat16)
    down_weight_grad = left_product(hidden_low, lower_grad)
    down_bias_grad = jnp.sum(lower_grad.astype(jnp.float32), axis=0)
    pre_grad = gelu_pull(right_product(lower_grad, down_weight))[0].astype(jnp.bfloat16)
    up_weight_grad = left_product(normed_two_low, pre_grad)
    up_bias_grad = jnp.sum(pre_grad.astype(jnp.float32), axis=0)
    middle_part, second_gain_grad, second_shift_grad = second_pull(
        right_product(pre_grad, up_weight)
    )
    middle_grad = final_grad + middle_part
    branch_grad = middle_grad.astype(jnp.bfloat16)
    out_weight_grad = left_product(attended, branch_grad)
    out_bias_grad = jnp.sum(branch_grad.astype(jnp.float32), axis=0)
    attended_grad = (
        right_product(branch_grad, out_weight)
        .astype(jnp.bfloat16)
        .reshape(grid_count, tokens, features)
    )
    query_blocks, key_blocks, value_blocks = lax.map(
        partial(attend_back, head_count=head_count, score_scale=score_scale),
        (
            blocked(queries, block_size),
            blocked(keys_all, block_size),
            blocked(values_all, block_size),
            blocked(marks_query, block_size),
            blocked(marks_key, block_size),
            log_total,
            blocked(attended_grad, block_size),
        ),
    )
    query_grad = unblock(query_blocks)
    bundle = (unblock(key_blocks), unblock(value_blocks))
    key_sum = lax.psum_scatter(
        bundle[0].astype(jnp.bfloat16), "ty", scatter_dimension=1, tiled=True
    )
    value_sum = lax.psum_scatter(
        bundle[1].astype(jnp.bfloat16), "ty", scatter_dimension=1, tiled=True
    )
    projected_grad = jnp.concatenate([query_grad, key_sum, value_sum], axis=-1).reshape(
        all_rows, 3 * features
    )
    qkv_weight_grad = left_product(normed_low, projected_grad)
    query_bias_grad = jnp.sum(query_grad.astype(jnp.float32), axis=(0, 1))
    value_bias_grad = jnp.sum(value_sum.astype(jnp.float32), axis=(0, 1))
    start_part, first_gain_grad, first_shift_grad = first_pull(
        right_product(projected_grad, qkv_weight)
    )
    start_grad = middle_grad + start_part
    inputs_rows = inputs_band.reshape(all_rows, features).astype(jnp.float32)
    input_band = (start_grad + 2.0 * commit_weight * (inputs_rows - start_rows)).astype(
        jnp.bfloat16
    )
    bundle = (
        recon_band.astype(jnp.bfloat16),
        input_band.reshape(grid_count, band_rows, band_cols, features),
    )
    recon_tiles = lax.all_to_all(bundle[0], "tx", split_axis=2, concat_axis=0, tiled=True)
    input_tiles = lax.all_to_all(bundle[1], "tx", split_axis=2, concat_axis=0, tiled=True)
    local_grads = (
        qkv_weight_grad,
        query_bias_grad,
        value_bias_grad,
        out_weight_grad,
        out_bias_grad,
        first_gain_grad,
        first_shift_grad,
        second_gain_grad,
        second_shift_grad,
        up_weight_grad,
        up_bias_grad,
        down_weight_grad,
        down_bias_grad,
        pixel_weight_grad,
        pixel_bias_grad,
    )
    tile_shares = (
        lax.psum_scatter(
            local_grads[0].astype(jnp.bfloat16), ("ty", "tx"), scatter_dimension=0, tiled=True
        ).astype(jnp.float32),
        lax.psum_scatter(
            local_grads[1].astype(jnp.bfloat16), ("ty", "tx"), scatter_dimension=0, tiled=True
        ).astype(jnp.float32),
        lax.psum_scatter(
            local_grads[2].astype(jnp.bfloat16), ("ty", "tx"), scatter_dimension=0, tiled=True
        ).astype(jnp.float32),
        lax.psum_scatter(
            local_grads[3].astype(jnp.bfloat16), ("ty", "tx"), scatter_dimension=0, tiled=True
        ).astype(jnp.float32),
        lax.psum_scatter(
            local_grads[4].astype(jnp.bfloat16), ("ty", "tx"), scatter_dimension=0, tiled=True
        ).astype(jnp.float32),
        lax.psum_scatter(
            local_grads[5].astype(jnp.bfloat16), ("ty", "tx"), scatter_dimension=0, tiled=True
        ).astype(jnp.float32),
        lax.psum_scatter(
            local_grads[6].astype(jnp.bfloat16), ("ty", "tx"), scatter_dimension=0, tiled=True
        ).astype(jnp.float32),
        lax.psum_scatter(
            local_grads[7].astype(jnp.bfloat16), ("ty", "tx"), scatter_dimension=0, tiled=True
        ).astype(jnp.float32),
        lax.psum_scatter(
            local_grads[8].astype(jnp.bfloat16), ("ty", "tx"), scatter_dimension=0, tiled=True
        ).astype(jnp.float32),
        lax.psum_scatter(
            local_grads[9].astype(jnp.bfloat16), ("ty", "tx"), scatter_dimension=0, tiled=True
        ).astype(jnp.float32),
        lax.psum_scatter(
            local_grads[10].astype(jnp.bfloat16), ("ty", "tx"), scatter_dimension=0, tiled=True
        ).astype(jnp.float32),
        lax.psum_scatter(
            local_grads[11].astype(jnp.bfloat16), ("ty", "tx"), scatter_dimension=0, tiled=True
        ).astype(jnp.float32),
        lax.psum_scatter(
            local_grads[12].astype(jnp.bfloat16), ("ty", "tx"), scatter_dimension=0, tiled=True
        ).astype(jnp.float32),
        lax.psum_scatter(
            local_grads[13].astype(jnp.bfloat16), ("ty", "tx"), scatter_dimension=0, tiled=True
        ).astype(jnp.float32),
        lax.psum_scatter(
            local_grads[14].astype(jnp.bfloat16), ("ty", "tx"), scatter_dimension=0, tiled=True
        ).astype(jnp.float32),
    )
    summed = (
        lax.psum(tile_shares[0].astype(jnp.bfloat16), "gr").astype(jnp.float32),
        lax.psum(tile_shares[1].astype(jnp.bfloat16), "gr").astype(jnp.float32),
        lax.psum(tile_shares[2].astype(jnp.bfloat16), "gr").astype(jnp.float32),
        lax.psum(tile_shares[3].astype(jnp.bfloat16), "gr").astype(jnp.float32),
        lax.psum(tile_shares[4].astype(jnp.bfloat16), "gr").astype(jnp.float32),
        lax.psum(tile_shares[5].astype(jnp.bfloat16), "gr").astype(jnp.float32),
        lax.psum(tile_shares[6].astype(jnp.bfloat16), "gr").astype(jnp.float32),
        lax.psum(tile_shares[7].astype(jnp.bfloat16), "gr").astype(jnp.float32),
        lax.psum(tile_shares[8].astype(jnp.bfloat16), "gr").astype(jnp.float32),
        lax.psum(tile_shares[9].astype(jnp.bfloat16), "gr").astype(jnp.float32),
        lax.psum(tile_shares[10].astype(jnp.bfloat16), "gr").astype(jnp.float32),
        lax.psum(tile_shares[11].astype(jnp.bfloat16), "gr").astype(jnp.float32),
        lax.psum(tile_shares[12].astype(jnp.bfloat16), "gr").astype(jnp.float32),
        lax.psum(tile_shares[13].astype(jnp.bfloat16), "gr").astype(jnp.float32),
        lax.psum(tile_shares[14].astype(jnp.bfloat16), "gr").astype(jnp.float32),
    )
    return (
        recon_tiles,
        input_tiles,
        summed[0],
        summed[1],
        summed[2],
        summed[3],
        summed[4],
        summed[5],
        summed[6],
        summed[7],
        summed[8],
        summed[9],
        summed[10],
        summed[11],
        summed[12],
        summed[13],
        summed[14],
    )


far = float(2.0**30)


def nt(left_side, right_side):
    return lax.dot_general(
        left_side, right_side, (((1,), (1,)), ((), ())), preferred_element_type=jnp.float32
    )


def nn(left_side, right_side):
    return lax.dot_general(
        left_side, right_side, (((1,), (0,)), ((), ())), preferred_element_type=jnp.float32
    )


def tn(left_side, right_side):
    return lax.dot_general(
        left_side, right_side, (((0,), (0,)), ((), ())), preferred_element_type=jnp.float32
    )


def groups(down, across, rows, cols):
    for part in range(down * across):
        for r in range(rows):
            grid_row = (part // across) * rows + r
            yield (part * rows + r) * cols, (grid_row * across + part % across) * cols


def conv_kernel(rows_ref, mask_ref, weight_ref, bias_ref, out_ref, plain_ref, shifted, total, other, *, tiling):
    width, cols = tiling[1] * tiling[3], tiling[3]
    tap = pl.program_id(0)
    tokens, features = rows_ref.shape

    @pl.when(tap == 0)
    def _():
        other[...] = rows_ref[...].astype(jnp.float32)
        for tiled, plain in groups(*tiling):
            total[plain : plain + cols, :] = other[tiled : tiled + cols, :]
        rows = total[...]
        plain_ref[...] = rows.astype(jnp.bfloat16)
        for j in range(3):
            moved = rows if j == 1 else pltpu.roll(rows, (1 - j) % tokens, 0)
            shifted[j, 0:width, :] = jnp.zeros((width, features), jnp.bfloat16)
            shifted[j, width + tokens :, :] = jnp.zeros((width, features), jnp.bfloat16)
            shifted[j, width : width + tokens, :] = moved.astype(jnp.bfloat16)
        total[...] = jnp.zeros_like(total)

    below, right = tap // 3, tap % 3
    step = tokens // 4
    for i in range(4):
        rows = slice(i * step, (i + 1) * step)
        first = pl.multiple_of(below * width + i * step, width)
        marks = mask_ref[1, width + i * step : width + (i + 1) * step, :]
        same = mask_ref[right, pl.ds(first, step), :] == marks
        mask = jnp.where(same, 1.0, 0.0).astype(jnp.bfloat16)
        mask = jnp.concatenate([mask] * (features // 128), axis=1)
        total[rows, :] += nn(shifted[right, pl.ds(first, step), :] * mask, weight_ref[0])

    @pl.when(tap == 8)
    def _():
        for tiled, plain in groups(*tiling):
            other[tiled : tiled + cols, :] = total[plain : plain + cols, :]
        out_ref[...] = (other[...] + bias_ref[...].astype(jnp.float32)).astype(jnp.bfloat16)


def in_hbm(shape, dtype=jnp.bfloat16):
    return pltpu.HBM(shape, dtype)


def conv(rows, masks, weight, bias, tiling):
    tokens, features = rows.shape
    width = tiling[1] * tiling[3]

    def whole(shape):
        return pl.BlockSpec(shape, lambda k: (0,) * len(shape), pipeline_mode=pl.Buffered(1))

    return pl.pallas_call(
        partial(conv_kernel, tiling=tiling),
        grid=(9,),
        in_specs=[
            whole((tokens, features)),
            whole(masks.shape),
            pl.BlockSpec((1, features, features), lambda k: (k, 0, 0)),
            whole((1, features)),
        ],
        out_specs=[whole((tokens, features))] * 2,
        out_shape=[in_hbm((tokens, features))] * 2,
        scratch_shapes=[
            pltpu.VMEM((3, tokens + 2 * width, features), jnp.bfloat16),
            pltpu.VMEM((tokens, features), jnp.float32),
            pltpu.VMEM((tokens, features), jnp.float32),
        ],
        compiler_params=pltpu.CompilerParams(vmem_limit_bytes=60 * 2**20),
        cost_estimate=pl.CostEstimate(
            flops=18 * tokens * features * features,
            bytes_accessed=18 * features * features + 4 * tokens * features,
            transcendentals=0,
        ),
        name="conv",
    )(rows, masks, weight, bias)


def marks_kernel(parts_ref, moved_ref, query_ref, key_ref, *, down, across, rows, cols):
    width = across * cols
    tokens = down * rows * width
    turned = parts_ref[...].astype(jnp.float32).T
    lane = lax.broadcasted_iota(jnp.int32, (rows * cols, 128), 1) % 64
    nowhere = jnp.full((width, 128), -1.0, jnp.float32)
    for j in range(3):
        moved_ref[j, 0:width, :] = nowhere
        moved_ref[j, width + tokens :, :] = nowhere
    for part in range(down * across):
        spread = jnp.broadcast_to(turned[:, part : part + 1], (rows * cols, 128))
        hot = spread == lane.astype(jnp.float32)
        here = slice(part * rows * cols, (part + 1) * rows * cols)
        query_ref[here, :] = jnp.where(hot, 1.0, 0.0).astype(jnp.bfloat16)
        key_ref[here, :] = jnp.where((lane < 3) & ~hot, -far, 0.0).astype(jnp.bfloat16)
        for r in range(rows):
            first = ((part // across) * rows + r) * width + (part % across) * cols + width
            moved_ref[1, first : first + cols, :] = spread[r * cols : (r + 1) * cols]
    marks = moved_ref[1, width : width + tokens, :]
    column = lax.broadcasted_iota(jnp.int32, (tokens, 128), 0) % width
    left = jnp.where(column == 0, -1.0, pltpu.roll(marks, 1, 0))
    right = jnp.where(column == width - 1, -1.0, pltpu.roll(marks, tokens - 1, 0))
    moved_ref[0, width : width + tokens, :] = left
    moved_ref[2, width : width + tokens, :] = right


def spread_marks(parts, down, across, rows, cols):
    tokens = down * across * rows * cols
    low = in_hbm((tokens, 128))
    return pl.pallas_call(
        partial(marks_kernel, down=down, across=across, rows=rows, cols=cols),
        out_shape=[
            in_hbm((3, tokens + 2 * across * cols, 128), jnp.float32),
            low,
            low,
        ],
        compiler_params=pltpu.CompilerParams(vmem_limit_bytes=60 * 2**20),
        name="spread_marks",
    )(parts)


def normalize(values):
    center = values - jnp.mean(values, axis=-1, keepdims=True)
    scale = lax.rsqrt(jnp.mean(center * center, axis=-1, keepdims=True) + epsilon)
    return center * scale, scale


def norm_back(grad, gain, unit, scale):
    scaled = grad * gain
    mean = jnp.mean(scaled, axis=-1, keepdims=True)
    along = jnp.mean(scaled * unit, axis=-1, keepdims=True)
    return scale * (scaled - mean - unit * along)


def row(ref):
    return ref[...].astype(jnp.float32)


def add_rows(ref, values):
    ref[...] += jnp.sum(values, axis=0, keepdims=True)


def ask_kernel(ids_ref, marks_ref, got_ref, slot_ref, sends, got, sent, received, *, share, slots):
    gr, ty, tx = lax.axis_index("gr"), lax.axis_index("ty"), lax.axis_index("tx")
    across = lax.axis_size("tx")
    members = lax.axis_size("ty") * across
    me = ty * across + tx
    others = [lax.rem(me + step, members) for step in range(1, members)]

    def place(member):
        return (gr, member // across, lax.rem(member, across))

    barrier = pltpu.get_barrier_semaphore()
    for member in others:
        pl.semaphore_signal(
            barrier, inc=1, device_id=place(member), device_id_type=pl.DeviceIdType.MESH
        )
    grids, tile_cols, tile_rows = ids_ref.shape
    each = tile_cols * tile_rows

    def spread(tile):
        return jnp.concatenate(
            [jnp.broadcast_to(tile[:, r : r + 1], (tile_cols, 128)) for r in range(tile_rows)], axis=0
        )

    lane = lax.broadcasted_iota(jnp.int32, (each, 128), 1)
    earlier = lax.broadcasted_iota(jnp.int32, (each, each), 1)
    earlier = earlier < lax.broadcasted_iota(jnp.int32, (each, each), 0)
    earlier = jnp.where(earlier, 1.0, 0.0).astype(jnp.bfloat16)
    counts = jnp.zeros((1, 128), jnp.float32)
    high = jnp.zeros((128, 128), jnp.float32)
    low = jnp.zeros((128, 128), jnp.float32)
    for grid in range(grids):
        ids = spread(ids_ref[grid])
        holder = jnp.zeros_like(ids)
        for member in range(1, members):
            holder = holder + jnp.where(ids >= member * share, 1, 0)
        offset = ids - holder * share
        belongs = jnp.where(holder == lane, 1.0, 0.0)
        ranks = nn(earlier, belongs.astype(jnp.bfloat16)) + counts
        counts = counts + jnp.sum(belongs, axis=0, keepdims=True)
        rank = jnp.sum(belongs * ranks, axis=1, keepdims=True)
        rank = jnp.broadcast_to(rank, (each, 128)).astype(jnp.int32)
        slot_ref[grid * each : (grid + 1) * each, :] = holder * slots + rank
        second = jnp.where(rank >= 128, 1, 0)
        of_row = 2 * holder + second == lane
        of_lane = jnp.where(rank - 128 * second == lane, 1.0, 0.0).astype(jnp.bfloat16)
        upper = jnp.floor(offset.astype(jnp.float32) * (1.0 / 64.0))
        lower = offset.astype(jnp.float32) - 64.0 * upper
        high = high + tn(jnp.where(of_row, upper, 0.0).astype(jnp.bfloat16), of_lane)
        low = low + tn(jnp.where(of_row, lower, 0.0).astype(jnp.bfloat16), of_lane)
    wanted = (high * 64.0 + low).astype(jnp.int32)
    sends[...] = jnp.zeros_like(sends)
    for member in range(members):
        sends[member, 0:2, :] = wanted[2 * member : 2 * member + 2, :]
        marks = spread(marks_ref[member]).astype(jnp.float32)
        sends[member, 2:3, :] = marks.T[0:1, :].astype(jnp.int32)

    def put(i):
        return pltpu.make_async_remote_copy(
            src_ref=sends.at[others[i]],
            dst_ref=got.at[me],
            send_sem=sent.at[i],
            recv_sem=received.at[i],
            device_id=place(others[i]),
            device_id_type=pl.DeviceIdType.MESH,
        )

    pl.semaphore_wait(barrier, members - 1)
    for i in range(members - 1):
        put(i).start()
    got[me] = sends[me]
    for i in range(members - 1):
        put(i).wait_send()
        put(i).wait_recv()
    got_ref[...] = got[...]


def ask(ids, marks, share, slots):
    members, each = ids.shape[0], ids.shape[1] * ids.shape[2]
    inside = pl.BlockSpec(memory_space=pltpu.VMEM)
    box = (members, 8, each)
    return pl.pallas_call(
        partial(ask_kernel, share=share, slots=slots),
        in_specs=[inside, inside],
        out_specs=[inside, inside],
        out_shape=[
            jax.ShapeDtypeStruct(box, jnp.int32),
            jax.ShapeDtypeStruct((members * each, 128), jnp.int32),
        ],
        scratch_shapes=[pltpu.VMEM(box, jnp.int32)] * 2
        + [pltpu.SemaphoreType.DMA((members - 1,))] * 2,
        compiler_params=pltpu.CompilerParams(
            collective_id=2, has_side_effects=True, vmem_limit_bytes=60 * 2**20
        ),
        cost_estimate=pl.CostEstimate(
            flops=20 * 10**9, bytes_accessed=40 * 10**6, transcendentals=0
        ),
        name="ask",
    )(ids, marks)


def gelu_parts(values):
    spread = jnp.exp(-0.5 * values * values)
    t = 1.0 / (1.0 + (0.3275911 * 0.5**0.5) * jnp.abs(values))
    series = 0.5 * 1.061405429
    for factor in (-1.453152027, 1.421413741, -0.284496736, 0.254829592):
        series = series * t + 0.5 * factor
    tail = series * t * spread
    upto = jnp.where(values < 0.0, tail, 1.0 - tail)
    return values * upto, upto + values * spread * 0.3989422804014327


def forward_kernel(
    codes_ref,
    final_ref,
    hidden_grad_ref,
    query_marks_ref,
    key_marks_ref,
    qkv_ref,
    out_weight_ref,
    up_ref,
    down_ref,
    first_gain_ref,
    first_shift_ref,
    qb_ref,
    vb_ref,
    out_bias_ref,
    gain_ref,
    shift_ref,
    up_bias_ref,
    down_bias_ref,
    normed_out,
    q_out,
    k_out,
    v_out,
    attended_out,
    columns_out,
    features_out,
    normed_two_out,
    hidden_out,
    pre_out,
    middle_grad_out,
    branch_out,
    attended_grad_out,
    out_bias_sum,
    gain_sum,
    shift_sum,
    up_bias_sum,
    codes,
    query_marks,
    key_marks,
    qkv_weight,
    out_weight,
    up_weight,
    down_weight,
    normed,
    queries,
    keys,
    values,
    attended,
    columns,
    final,
    hidden_grad,
    features_stage,
    normed_two_stage,
    hidden_stage,
    pre_stage,
    middle_grad_stage,
    branch_stage,
    attended_grad_stage,
    in_sem,
    once_sem,
    block_sem,
    stage_sem,
    *,
    step,
):
    tokens, features = codes.shape
    pairs = queries.shape[0]
    blocks = tokens // step
    loads = [
        pltpu.make_async_copy(source, target, in_sem.at[i])
        for i, (source, target) in enumerate(
            (
                (codes_ref, codes),
                (qkv_ref, qkv_weight),
                (query_marks_ref, query_marks),
                (key_marks_ref, key_marks),
                (out_weight_ref, out_weight),
                (up_ref, up_weight),
                (down_ref, down_weight),
            )
        )
    ]
    for copy in loads:
        copy.start()

    def block_copies(i):
        rows = pl.ds(pl.multiple_of(i * step, step), step)
        slot = lax.rem(i, 2)
        return [
            pltpu.make_async_copy(final_ref.at[rows], final.at[slot], block_sem.at[slot, 0]),
            pltpu.make_async_copy(
                hidden_grad_ref.at[rows], hidden_grad.at[slot], block_sem.at[slot, 1]
            ),
        ]

    for copy in block_copies(0):
        copy.start()
    for ref in (out_bias_sum, gain_sum, shift_sum, up_bias_sum):
        ref[...] = jnp.zeros_like(ref)

    for copy in loads[:2]:
        copy.wait()

    def enter_rows(i, _):
        rows = pl.ds(pl.multiple_of(i * step, step), step)
        unit, _ = normalize(codes[rows, :].astype(jnp.float32))
        low = (unit * row(first_gain_ref) + row(first_shift_ref)).astype(jnp.bfloat16)
        normed[rows, :] = low
        query_rows = nn(low, qkv_weight[:, 0:features]) + row(qb_ref)
        query_rows = query_rows.astype(jnp.bfloat16) * jnp.asarray(HEAD_DIM**-0.5, jnp.bfloat16)
        key_rows = nn(low, qkv_weight[:, features : 2 * features]).astype(jnp.bfloat16)
        value_rows = (nn(low, qkv_weight[:, 2 * features :]) + row(vb_ref)).astype(jnp.bfloat16)
        for pair in range(pairs):
            lanes = slice(pair * 128, (pair + 1) * 128)
            queries[pair, rows, :] = query_rows[:, lanes]
            keys[pair, rows, :] = key_rows[:, lanes]
            values[pair, rows, :] = value_rows[:, lanes]
        return 0

    lax.fori_loop(0, blocks, enter_rows, 0)
    onces = [
        pltpu.make_async_copy(source, target, once_sem.at[i])
        for i, (source, target) in enumerate(
            (
                (normed, normed_out),
                (queries, q_out),
                (keys, k_out),
                (values, v_out),
                (attended, attended_out),
                (columns, columns_out),
            )
        )
    ]
    for copy in onces[:4]:
        copy.start()

    for copy in loads[2:4]:
        copy.wait()
    lane = lax.broadcasted_iota(jnp.int32, (1, 128), 1)
    low_lanes = lane < 64
    local = lane % 64
    one = jnp.ones((), jnp.bfloat16)

    def attend_pair(pair, _):
        key_rows, value_rows, marks = keys[pair], values[pair], key_marks[...]
        keys_of = [jnp.where(low_lanes, key_rows, marks), jnp.where(low_lanes, marks, key_rows)]
        values_of = [jnp.where(low_lanes, value_rows, one), jnp.where(low_lanes, one, value_rows)]
        parts = [(first, head) for first in range(0, tokens, step) for head in range(2)]

        def scores_of(part):
            first, head = part
            rows = slice(first, first + step)
            rows_q, rows_m = queries[pair, rows, :], query_marks[rows, :]
            if head == 0:
                return nt(jnp.where(low_lanes, rows_q, rows_m), keys_of[0])
            return nt(jnp.where(low_lanes, rows_m, rows_q), keys_of[1])

        waiting = [scores_of(part) for part in parts[:2]]
        outs, logs = [None, None], [None, None]
        for i, (first, head) in enumerate(parts):
            scores = waiting.pop(0)
            if i + 2 < len(parts):
                waiting.append(scores_of(parts[i + 2]))
            top = jnp.max(scores, axis=1, keepdims=True)
            weights = jnp.exp(scores - top).astype(jnp.bfloat16)
            sums = nn(weights, values_of[head])
            outs[head] = sums / pltpu.roll(sums, 64, 1)
            logs[head] = top + jnp.log(sums)
            if head == 1:
                rows = slice(first, first + step)
                attended[pair, rows, :] = jnp.where(low_lanes, outs[0], outs[1]).astype(jnp.bfloat16)
                minus = -jnp.where(low_lanes, logs[1], logs[0])
                part1 = minus.astype(jnp.bfloat16).astype(jnp.float32)
                part2 = (minus - part1).astype(jnp.bfloat16).astype(jnp.float32)
                part3 = minus - part1 - part2
                column = jnp.where(local == 5, part3, query_marks[rows, :].astype(jnp.float32))
                column = jnp.where(local == 4, part2, column)
                column = jnp.where(local == 3, part1, column)
                columns[pair, rows, :] = column.astype(jnp.bfloat16)
        return 0

    lax.fori_loop(0, pairs, attend_pair, 0)
    for copy in onces[4:]:
        copy.start()

    for copy in loads[4:]:
        copy.wait()

    def stage_copies(i):
        rows = pl.ds(pl.multiple_of(i * step, step), step)
        slot = lax.rem(i, 2)
        moves = (
            (features_stage, features_out.at[rows]),
            (normed_two_stage, normed_two_out.at[rows]),
            (hidden_stage, hidden_out.at[:, rows]),
            (pre_stage, pre_out.at[rows]),
            (middle_grad_stage, middle_grad_out.at[rows]),
            (branch_stage, branch_out.at[rows]),
            (attended_grad_stage, attended_grad_out.at[:, rows]),
        )
        return [
            pltpu.make_async_copy(source.at[slot], target, stage_sem.at[slot, k])
            for k, (source, target) in enumerate(moves)
        ]

    def middle_rows(i, _):
        rows = pl.ds(pl.multiple_of(i * step, step), step)
        slot = lax.rem(i, 2)
        for copy in block_copies(i):
            copy.wait()

        @pl.when(i + 1 < blocks)
        def _():
            for copy in block_copies(i + 1):
                copy.start()

        @pl.when(i >= 2)
        def _():
            for copy in stage_copies(i - 2):
                copy.wait()

        attended_rows = jnp.concatenate([attended[p, rows, :] for p in range(pairs)], axis=1)
        branch = nn(attended_rows, out_weight[...]) + row(out_bias_ref)
        middle = codes[rows, :].astype(jnp.float32) + branch
        unit, scale = normalize(middle)
        low = (unit * row(gain_ref) + row(shift_ref)).astype(jnp.bfloat16)
        normed_two_stage[slot] = low
        total = middle + row(down_bias_ref)
        grad = jnp.zeros_like(middle)
        for first in range(0, up_weight.shape[1], features):
            block = slice(first, first + features)
            weight = up_weight[:, block]
            hidden_pre = nn(low, weight) + up_bias_ref[:, block].astype(jnp.float32)
            act, slope = gelu_parts(hidden_pre)
            hidden = act.astype(jnp.bfloat16)
            hidden_stage[slot, block, :] = hidden.T
            pre = hidden_grad[slot, :, block].astype(jnp.float32) * slope
            pre = pre.astype(jnp.bfloat16)
            pre_stage[slot, :, block] = pre
            up_bias_sum[:, block] += jnp.sum(pre.astype(jnp.float32), axis=0, keepdims=True)
            total = total + nn(hidden, down_weight[block, :])
            grad = grad + nt(pre, weight)
        features_stage[slot] = total.astype(jnp.bfloat16)
        add_rows(gain_sum, grad * unit)
        add_rows(shift_sum, grad)
        middle_grad = final[slot] + norm_back(grad, row(gain_ref), unit, scale)
        middle_grad_stage[slot] = middle_grad
        branch_grad = middle_grad.astype(jnp.bfloat16)
        branch_stage[slot] = branch_grad
        add_rows(out_bias_sum, branch_grad.astype(jnp.float32))
        attended_grad = nt(branch_grad, out_weight[...]).astype(jnp.bfloat16)
        for pair in range(pairs):
            attended_grad_stage[slot, pair] = attended_grad[:, pair * 128 : (pair + 1) * 128]
        for copy in stage_copies(i):
            copy.start()
        return 0

    lax.fori_loop(0, blocks, middle_rows, 0)
    for copy in onces:
        copy.wait()
    for i in (blocks - 2, blocks - 1):
        for copy in stage_copies(i):
            copy.wait()


def forward(inputs, vectors, step=256):
    codes, qkv_weight, up_weight = inputs[0], inputs[5], inputs[7]
    tokens, features = codes.shape
    wide = up_weight.shape[1]
    pairs = features // 128
    anywhere = pl.BlockSpec(memory_space=pl.ANY)
    inside = pl.BlockSpec(memory_space=pltpu.VMEM)
    dma = pltpu.SemaphoreType.DMA
    low, full = jnp.bfloat16, jnp.float32
    paired = (pairs, tokens, 128)
    shapes = [
        ((tokens, features), low),
        (paired, low),
        (paired, low),
        (paired, low),
        (paired, low),
        (paired, low),
        ((tokens, features), low),
        ((tokens, features), low),
        ((wide, tokens), low),
        ((tokens, wide), low),
        ((tokens, features), full),
        ((tokens, features), low),
        (paired, low),
    ]
    sums = [(1, features)] * 3 + [(1, wide)]
    return pl.pallas_call(
        partial(forward_kernel, step=step),
        in_specs=[anywhere] * 9 + [inside] * 9,
        out_specs=[anywhere] * len(shapes) + [inside] * 4,
        out_shape=[pltpu.HBM(shape, dtype) for shape, dtype in shapes]
        + [jax.ShapeDtypeStruct(shape, full) for shape in sums],
        scratch_shapes=[
            pltpu.VMEM((tokens, features), low),
            pltpu.VMEM((tokens, 128), low),
            pltpu.VMEM((tokens, 128), low),
            pltpu.VMEM(qkv_weight.shape, low),
            pltpu.VMEM((features, features), low),
            pltpu.VMEM((features, wide), low),
            pltpu.VMEM((wide, features), low),
            pltpu.VMEM((tokens, features), low),
        ]
        + [pltpu.VMEM(paired, low)] * 5
        + [
            pltpu.VMEM((2, step, features), full),
            pltpu.VMEM((2, step, wide), low),
            pltpu.VMEM((2, step, features), low),
            pltpu.VMEM((2, step, features), low),
            pltpu.VMEM((2, wide, step), low),
            pltpu.VMEM((2, step, wide), low),
            pltpu.VMEM((2, step, features), full),
            pltpu.VMEM((2, step, features), low),
            pltpu.VMEM((2, pairs, step, 128), low),
            dma((7,)),
            dma((6,)),
            dma((2, 2)),
            dma((2, 7)),
        ],
        compiler_params=pltpu.CompilerParams(vmem_limit_bytes=60 * 2**20),
        cost_estimate=pl.CostEstimate(
            flops=2 * tokens * features * (5 * features + 3 * wide) + 16 * tokens**2 * features,
            bytes_accessed=4 * features * wide + 6 * tokens * wide + 30 * tokens * features,
            transcendentals=2 * tokens * wide + 2 * tokens**2 * pairs,
        ),
        name="forward",
    )(*inputs, *vectors)


def fetch_kernel(
    fetched_ref,
    slot_ref,
    cotangent_ref,
    moved_ref,
    taps_ref,
    down_ref,
    codes_out,
    final_out,
    low_out,
    behind_out,
    hidden_out,
    pixel_bias_sum,
    down_bias_sum,
    cotangent,
    got,
    sends,
    shifted,
    total,
    other,
    low,
    taken,
    weight,
    down,
    hidden,
    hop_sent,
    hop_got,
    code_sent,
    code_got,
    own_sem,
    weight_sem,
    taken_sem,
    down_sem,
    hidden_sem,
    out_sem,
    *,
    tiling,
):
    gr, ty, tx = lax.axis_index("gr"), lax.axis_index("ty"), lax.axis_index("tx")
    across = lax.axis_size("tx")
    members = lax.axis_size("ty") * across
    me = ty * across + tx
    others = [lax.rem(me + step, members) for step in range(1, members)]
    tokens, features = cotangent_ref.shape
    each = tokens // members
    wide = tiling[1] * tiling[3]

    def place(member):
        return (gr, member // across, lax.rem(member, across))

    barrier = pltpu.get_barrier_semaphore()
    for member in others:
        pl.semaphore_signal(
            barrier, inc=1, device_id=place(member), device_id_type=pl.DeviceIdType.MESH
        )
    pl.semaphore_wait(barrier, members - 1)

    def hop_put(i):
        return pltpu.make_async_remote_copy(
            src_ref=fetched_ref.at[others[i]],
            dst_ref=got.at[me],
            send_sem=hop_sent.at[i],
            recv_sem=hop_got.at[i],
            device_id=place(others[i]),
            device_id_type=pl.DeviceIdType.MESH,
        )

    def code_put(i):
        return pltpu.make_async_remote_copy(
            src_ref=sends.at[others[i]],
            dst_ref=codes_out.at[me],
            send_sem=code_sent.at[i],
            recv_sem=code_got.at[i],
            device_id=place(others[i]),
            device_id_type=pl.DeviceIdType.MESH,
        )

    own_rows = pltpu.make_async_copy(fetched_ref.at[me], got.at[me], own_sem.at[0])
    own_codes = pltpu.make_async_copy(sends.at[me], codes_out.at[me], own_sem.at[1])
    for i in range(members - 1):
        hop_put(i).start()
    own_rows.start()

    def weight_copy(tap):
        slot = lax.rem(tap, 2)
        return pltpu.make_async_copy(taps_ref.at[tap], weight.at[slot], weight_sem.at[slot])

    def taken_copy(tap):
        slot = lax.rem(tap, 2)
        columns = pl.ds(pl.multiple_of(tap * features, 128), features)
        return pltpu.make_async_copy(taken.at[slot], behind_out.at[:, columns], taken_sem.at[slot])

    def down_copy(j):
        slot = lax.rem(j, 2)
        rows = pl.ds(pl.multiple_of(j * features, 128), features)
        return pltpu.make_async_copy(down_ref.at[rows], down.at[slot], down_sem.at[slot])

    def hidden_copy(j):
        slot = lax.rem(j, 2)
        columns = pl.ds(pl.multiple_of(j * features, 128), features)
        return pltpu.make_async_copy(hidden.at[slot], hidden_out.at[:, columns], hidden_sem.at[slot])

    arriving = pltpu.make_async_copy(cotangent_ref, cotangent, own_sem.at[2])
    arriving.start()
    weight_copy(0).start()
    down_copy(0).start()
    arriving.wait()
    other[...] = cotangent[...].astype(jnp.float32)
    pixel_bias_sum[...] = jnp.sum(other[...], axis=0, keepdims=True)
    for tiled, plain in groups(*tiling):
        total[plain : plain + tiling[3], :] = other[tiled : tiled + tiling[3], :]
    rows_plain = total[...]
    for j in range(3):
        moved_rows = rows_plain if j == 1 else pltpu.roll(rows_plain, (1 - j) % tokens, 0)
        shifted[j, 0:wide, :] = jnp.zeros((wide, features), jnp.bfloat16)
        shifted[j, wide + tokens :, :] = jnp.zeros((wide, features), jnp.bfloat16)
        shifted[j, wide : wide + tokens, :] = moved_rows.astype(jnp.bfloat16)
    total[...] = jnp.zeros_like(total)

    def one_tap(tap, _):
        slot = lax.rem(tap, 2)
        weight_copy(tap).wait()
        pl.when(tap < 8)(lambda: weight_copy(tap + 1).start())
        pl.when(tap >= 2)(lambda: taken_copy(tap - 2).wait())
        below, right = 2 - tap // 3, 2 - lax.rem(tap, 3)
        step = tokens // 4
        for i in range(4):
            rows = slice(i * step, (i + 1) * step)
            first = pl.multiple_of(below * wide + i * step, wide)
            here = moved_ref[1, wide + i * step : wide + (i + 1) * step, :]
            same = moved_ref[right, pl.ds(first, step), :] == here
            mask = jnp.where(same, 1.0, 0.0).astype(jnp.bfloat16)
            mask = jnp.concatenate([mask] * (features // 128), axis=1)
            piece = shifted[right, pl.ds(first, step), :] * mask
            taken[slot, rows, :] = piece
            total[rows, :] += nt(piece, weight[slot])
        taken_copy(tap).start()
        return 0

    lax.fori_loop(0, 9, one_tap, 0)
    for tiled, plain in groups(*tiling):
        other[tiled : tiled + tiling[3], :] = total[plain : plain + tiling[3], :]
    low[...] = other[...].astype(jnp.bfloat16)
    results = [
        pltpu.make_async_copy(other, final_out, out_sem.at[0]),
        pltpu.make_async_copy(low, low_out, out_sem.at[1]),
    ]
    for result in results:
        result.start()
    down_bias_sum[...] = jnp.sum(low[...].astype(jnp.float32), axis=0, keepdims=True)

    own_rows.wait()
    for i in range(members - 1):
        hop_put(i).wait_recv()
    arrived = got[...].reshape(got.shape[0] * got.shape[1], features)
    lane = lax.broadcasted_iota(jnp.int32, (each, 128), 1)
    for member in range(members):
        slots = slot_ref[member * each : (member + 1) * each, :]
        hot = [
            jnp.where(slots == lane + first, 1.0, 0.0).astype(jnp.bfloat16)
            for first in range(0, arrived.shape[0], 128)
        ]
        rows = nn(jnp.concatenate(hot, axis=1), arrived)
        sends[member] = rows.astype(jnp.bfloat16)
    for i in range(members - 1):
        code_put(i).start()
    own_codes.start()

    def one_block(j, _):
        slot = lax.rem(j, 2)
        down_copy(j).wait()
        pl.when(j < 3)(lambda: down_copy(j + 1).start())
        pl.when(j >= 2)(lambda: hidden_copy(j - 2).wait())
        hidden[slot] = nt(low[...], down[slot]).astype(jnp.bfloat16)
        hidden_copy(j).start()
        return 0

    lax.fori_loop(0, 4, one_block, 0)
    for copy in (taken_copy(7), taken_copy(8), hidden_copy(2), hidden_copy(3), own_codes, *results):
        copy.wait()
    for i in range(members - 1):
        hop_put(i).wait_send()
        code_put(i).wait_send()
        code_put(i).wait_recv()


def fetch(fetched, slots, cotangent, moved, taps, down_weight, tiling):
    tokens, features = cotangent.shape
    members = tiling[0] * tiling[1]
    blocks = down_weight.shape[0] // features
    anywhere = pl.BlockSpec(memory_space=pl.ANY)
    inside = pl.BlockSpec(memory_space=pltpu.VMEM)
    dma = pltpu.SemaphoreType.DMA
    low, wide = jnp.bfloat16, jnp.float32
    padded = tokens + 2 * tiling[1] * tiling[3]
    return pl.pallas_call(
        partial(fetch_kernel, tiling=tiling),
        in_specs=[anywhere, inside, anywhere, inside, anywhere, anywhere],
        out_specs=[anywhere] * 5 + [inside] * 2,
        out_shape=[
            jax.ShapeDtypeStruct((members, tokens // members, features), low),
            jax.ShapeDtypeStruct((tokens, features), wide),
            jax.ShapeDtypeStruct((tokens, features), low),
            jax.ShapeDtypeStruct((tokens, 9 * features), low),
            jax.ShapeDtypeStruct((tokens, blocks * features), low),
            jax.ShapeDtypeStruct((1, features), wide),
            jax.ShapeDtypeStruct((1, features), wide),
        ],
        scratch_shapes=[
            pltpu.VMEM((tokens, features), low),
            pltpu.VMEM(fetched.shape, low),
            pltpu.VMEM((members, tokens // members, features), low),
            pltpu.VMEM((3, padded, features), low),
            pltpu.VMEM((tokens, features), wide),
            pltpu.VMEM((tokens, features), wide),
            pltpu.VMEM((tokens, features), low),
            pltpu.VMEM((2, tokens, features), low),
            pltpu.VMEM((2, features, features), low),
            pltpu.VMEM((2, features, features), low),
            pltpu.VMEM((2, tokens, features), low),
        ]
        + [dma((members - 1,))] * 4
        + [dma((3,))]
        + [dma((2,))] * 5,
        compiler_params=pltpu.CompilerParams(
            collective_id=3, has_side_effects=True, vmem_limit_bytes=60 * 2**20
        ),
        cost_estimate=pl.CostEstimate(
            flops=26 * tokens * features * features,
            bytes_accessed=40 * tokens * features,
            transcendentals=0,
        ),
        name="fetch",
    )(fetched, slots, cotangent, moved, taps, down_weight)


def finish_kernel(*refs, blocks, homes, lead, slots, got_slots, tiling):
    (
        q_ref,
        k_ref,
        v_ref,
        col_ref,
        ka_ref,
        o_ref,
        g_ref,
        codes_ref,
        middle_ref,
        features_ref,
        behind_ref,
        normed_two_ref,
        pre_ref,
        hidden_ref,
        lower_ref,
        branch_ref,
        normed_ref,
        weight_ref,
        recon_ref,
        gain_ref,
        out_bias_sum,
        second_gain_sum,
        second_shift_sum,
        up_bias_sum,
        down_bias_sum,
        pixel_bias_sum,
    ) = refs[:26]
    outs = refs[26:31]
    vector_out, recon_out, share_out = refs[31:34]
    refs = refs[34:]
    (parts, got0, got1, got2, got3, got4, whole) = refs[:7]
    (operands, turned, heads, marks, sums, sums_got, middle, share, k_sum, v_sum, dqkv) = refs[7:18]
    (s0, r0, s1, r1, s2, r2, s3, r3, s4, r4, s5, r5, s6, r6) = refs[18:32]
    (out_sem, operand_sem, turned_sem, head_sem, once_sem, free, own_sem) = refs[32:39]
    (recon_sent, recon_got, share_sent, share_got, sums_sent, sums_recv) = refs[39:45]
    count = (blocks + 1) // 2
    tokens, features = normed_ref.shape
    each = tokens // (tiling[0] * tiling[1])
    gr, ty, tx = lax.axis_index("gr"), lax.axis_index("ty"), lax.axis_index("tx")
    x, core, half, par = gr // 2, gr % 2, tx // 2, tx % 2
    across = lax.axis_size("tx")
    members = lax.axis_size("ty") * across
    me = ty * across + tx
    mate = (2 * x + 1 - core, ty, tx)
    over_x = (2 * (1 - x) + core, ty, tx)
    over_y = (gr, 1 - ty, tx)
    near = (gr, ty, half * 2 + (1 - par))
    away = (gr, ty, (1 - half) * 2 + par)
    others = [lax.rem(me + step, members) for step in range(1, members)]

    def place(member):
        return (gr, member // across, lax.rem(member, across))

    barrier = pltpu.get_barrier_semaphore()
    greeted = [mate, over_x] + [place(member) for member in others]
    for device in greeted:
        pl.semaphore_signal(barrier, inc=1, device_id=device, device_id_type=pl.DeviceIdType.MESH)
    pl.semaphore_wait(barrier, len(greeted))
    width = features // 2
    own_columns = pl.ds(pl.multiple_of(core * width, 128), width)

    def put(source, target, sent, received, device):
        return pltpu.make_async_remote_copy(
            src_ref=source,
            dst_ref=target,
            send_sem=sent,
            recv_sem=received,
            device_id=device,
            device_id_type=pl.DeviceIdType.MESH,
        )

    def recon_put(i):
        member = others[i]
        return put(
            recon_ref.at[member], recon_out.at[me], recon_sent.at[i], recon_got.at[i], place(member)
        )

    def share_put(i, member=None):
        member = others[i] if member is None else member
        rows = pl.ds(pl.multiple_of(member * each, 128), each)
        return put(share.at[rows], share_out.at[me], share_sent.at[i], share_got.at[i], place(member))

    def columns(ref, index):
        return ref.at[:, pl.ds(pl.multiple_of(index * features, 128), features)]

    def operand(i, source):
        return pltpu.make_async_copy(source, operands.at[i], operand_sem.at[i])

    def load(sources):
        for i, source in enumerate(sources):
            operand(i, source).start()

    def load_operands(c):
        @pl.when(c < 4)
        def _():
            load([features_ref, columns(behind_ref, 2 * c), features_ref, columns(behind_ref, 2 * c + 1)])

        @pl.when((c == 4) | (c == 5))
        def _():
            load([lower_ref] * 4)
            for b in range(2):
                turned_copy(b, 2 * (c - 4) + b).start()

        @pl.when(c == 6)
        def _():
            load([normed_ref, gradient(0), normed_ref, gradient(1)])

        @pl.when(c == 7)
        def _():
            load([normed_ref, gradient(2), features_ref, columns(behind_ref, 8)])

        @pl.when(c == 8)
        def _():
            for pair in range(o_ref.shape[0]):
                target = operands.at[0, :, pl.ds(pair * 128, 128)]
                pltpu.make_async_copy(o_ref.at[pair], target, operand_sem.at[0]).start()
            for i, source in ((1, branch_ref), (2, normed_two_ref), (3, columns(pre_ref, 0))):
                operand(i, source).start()

        @pl.when(c == 9)
        def _():
            load([normed_two_ref, columns(pre_ref, 1), normed_two_ref, columns(pre_ref, 2)])

        @pl.when(c == 10)
        def _():
            load([normed_two_ref, columns(pre_ref, 3), lower_ref, lower_ref])

    def gradient(i):
        return dqkv.at[i, pl.ds(0, tokens)]

    def turned_copy(b, index):
        return pltpu.make_async_copy(hidden_ref.at[:, index], turned.at[b], turned_sem.at[b])

    def wait_operands():
        for i in range(4):
            operand(i, normed_ref).wait()

    def level0(c, b):
        slot = lax.rem(c, slots)
        return put(
            parts.at[slot, b, 1 - core], got0.at[lax.rem(c, got_slots), b], s0.at[c, b], r0.at[c, b], mate
        )

    def both_x(c):
        return (c == 2) | (c == 7)

    def only_y(c):
        return (c < count - 1) & (c != 2) & (c != 7)

    def level1x(c, b=0):
        slot = lax.rem(c, slots)
        return put(
            parts.at[slot, b, core, :, :, :, 1 - x], got1.at[c, b], s1.at[c, b], r1.at[c, b], over_x
        )

    def level1y(c):
        slot = lax.rem(c, slots)
        return put(parts.at[slot, 1, core, 1 - ty], got1.at[c, 1], s1.at[c, 1], r1.at[c, 1], over_y)

    def level2y(c, b=0):
        return put(got1.at[c, b, 1 - ty], got2.at[c, b], s2.at[c, b], r2.at[c, b], over_y)

    def level2x(c):
        return put(got1.at[c, 1, :, :, 1 - x], got2.at[c, 1], s2.at[c, 1], r2.at[c, 1], over_x)

    def level3(c):
        return put(got2.at[c, :, :, 1 - par], got3.at[c], s3.at[c], r3.at[c], near)

    def level4(c):
        return put(got3.at[c, :, 1 - half], got4.at[c], s4.at[c], r4.at[c], away)

    def level5(c):
        where = whole.at[pl.ds(2 * c, 2), x, :, own_columns]
        return put(where, where, s5.at[c], r5.at[c], over_x)

    def level6(c):
        where = whole.at[pl.ds(2 * c, 2), :, :, own_columns]
        return put(where, where, s6.at[c], r6.at[c], mate)

    def stage1(c):
        slot, got_slot = lax.rem(c, slots), lax.rem(c, got_slots)
        for b in range(2):

            @pl.when((b == 0) | (c < count - 1))
            def _():
                level0(c, b).wait_recv()

                def add(i, _):
                    y, h, p = i // 4, lax.rem(i // 2, 2), lax.rem(i, 2)
                    sum_of = parts[slot, b, core, y, h, p] + got0[got_slot, b, y, h, p]
                    parts[slot, b, core, y, h, p] = sum_of
                    return 0

                lax.fori_loop(0, 8, add, 0)

        @pl.when(c < count - got_slots)
        def _():
            pl.semaphore_signal(free, inc=1, device_id=mate, device_id_type=pl.DeviceIdType.MESH)

        level1x(c).start()
        pl.when(only_y(c))(lambda: level1y(c).start())
        pl.when(both_x(c))(lambda: level1x(c, 1).start())

    def stage2(c):
        slot = lax.rem(c, slots)
        level1x(c).wait_recv()
        got1[c, 0] = got1[c, 0] + parts[slot, 0, core, :, :, :, x]
        level2y(c).start()

        @pl.when(only_y(c))
        def _():
            level1y(c).wait_recv()
            got1[c, 1] = got1[c, 1] + parts[slot, 1, core, ty]
            level2x(c).start()
            level1y(c).wait_send()

        @pl.when(both_x(c))
        def _():
            level1x(c, 1).wait_recv()
            got1[c, 1] = got1[c, 1] + parts[slot, 1, core, :, :, :, x]
            level2y(c, 1).start()
            level1x(c, 1).wait_send()

        level1x(c).wait_send()

    def stage3(c):
        level2y(c).wait_recv()
        got2[c, 0] = got2[c, 0] + got1[c, 0, ty]

        @pl.when(only_y(c))
        def _():
            level2x(c).wait_recv()
            got2[c, 1] = got2[c, 1] + got1[c, 1, :, :, x]

        @pl.when(both_x(c))
        def _():
            level2y(c, 1).wait_recv()
            got2[c, 1] = got2[c, 1] + got1[c, 1, ty]

        @pl.when(c == count - 1)
        def _():
            got2[c, 1] = jnp.zeros(got2.shape[2:], jnp.bfloat16)

        level3(c).start()

    def stage4(c):
        level3(c).wait_recv()
        got3[c] = got3[c] + got2[c, :, :, par]
        level4(c).start()

    def stage5(c):
        level4(c).wait_recv()
        whole[pl.ds(2 * c, 2), x, :, own_columns] = got4[c] + got3[c, :, half]
        level5(c).start()

    def stage6(c):
        level5(c).wait_recv()
        level6(c).start()

    def weight_block(slot, b, of_hidden):
        for y in range(2):
            if of_hidden:
                left = turned[b, y * 4 : (y + 1) * 4].reshape(width, tokens)
                block = nn(left, operands[2 * b + 1])
            else:
                left = operands[2 * b, :, y * width : (y + 1) * width]
                block = tn(left, operands[2 * b + 1])
            block = block.astype(jnp.bfloat16)
            for h in range(2):
                piece = block[:, h * width : (h + 1) * width]
                parts[slot, b, h, y] = piece.reshape(parts.shape[4:])

    def make_blocks(c):
        slot = lax.rem(c, slots)

        @pl.when(c >= slots)
        def _():
            for b in range(2):
                level0(c - slots, b).wait_send()

        @pl.when(c >= got_slots)
        def _():
            pl.semaphore_wait(free, 1)

        wait_operands()
        of_hidden = (c == 4) | (c == 5)

        @pl.when(of_hidden)
        def _():
            for b in range(2):
                turned_copy(b, 0).wait()
                weight_block(slot, b, True)
                level0(c, b).start()

        @pl.when(jnp.logical_not(of_hidden))
        def _():
            weight_block(slot, 0, False)
            level0(c, 0).start()

        @pl.when(jnp.logical_not(of_hidden) & (c < count - 1))
        def _():
            weight_block(slot, 1, False)
            level0(c, 1).start()

    lane = lax.broadcasted_iota(jnp.int32, (1, 128), 1)
    low = lane < 64
    local = lane % 64

    def head_copies(pair):
        slot = lax.rem(pair, 2)
        return [
            pltpu.make_async_copy(ref.at[pair], heads.at[slot, i], head_sem.at[slot, i])
            for i, ref in enumerate((q_ref, k_ref, v_ref, col_ref, o_ref, g_ref))
        ]

    pairs = features // 128
    step = tokens // 2

    def attend_part(u, _):
        pair, part = u // 2, lax.rem(u, 2)
        slot = lax.rem(pair, 2)

        @pl.when(part == 0)
        def _():
            for copy in head_copies(pair):
                copy.wait()

            @pl.when(pair < pairs - 1)
            def _():
                for copy in head_copies(pair + 1):
                    copy.start()

            k_sum[...] = jnp.zeros_like(k_sum)
            v_sum[...] = jnp.zeros_like(v_sum)

        rows = pl.ds(pl.multiple_of(part * step, step), step)
        zero, one = jnp.zeros((), jnp.bfloat16), jnp.ones((), jnp.bfloat16)
        queries, columns_ = heads[slot, 0, rows, :], heads[slot, 3, rows, :]
        key_rows, values = heads[slot, 1], heads[slot, 2]
        out, grad = heads[slot, 4, rows, :], heads[slot, 5, rows, :]
        key_columns = jnp.where((local >= 3) & (local < 6), one, marks[...])
        value_columns = jnp.where(local < 2, one, zero)
        keys_across = key_rows.T
        both = grad.astype(jnp.float32) * out.astype(jnp.float32)
        of_low = -jnp.sum(jnp.where(low, both, 0.0), axis=1, keepdims=True)
        of_high = -jnp.sum(jnp.where(low, 0.0, both), axis=1, keepdims=True)
        inner = jnp.where(low, of_high, of_low)
        first = inner.astype(jnp.bfloat16).astype(jnp.float32)
        grad_columns = jnp.where(
            local == 0, first, jnp.where(local == 1, inner - first, 0.0)
        ).astype(jnp.bfloat16)
        query_parts, key_parts, value_parts = [], [], []
        for head in range(2):
            own = low if head == 0 else ~low
            scores = nt(jnp.where(own, key_rows, key_columns), jnp.where(own, queries, columns_))
            weights = jnp.exp(scores)
            change = nt(jnp.where(own, values, value_columns), jnp.where(own, grad, grad_columns))
            score_grad = (weights * change).astype(jnp.bfloat16)
            value_parts.append(nn(weights.astype(jnp.bfloat16), grad))
            key_parts.append(nn(score_grad, queries))
            query_parts.append(nn(keys_across, score_grad))
        k_sum[...] += jnp.where(low, key_parts[0], key_parts[1])
        v_sum[...] += jnp.where(low, value_parts[0], value_parts[1])
        upper = lax.broadcasted_iota(jnp.int32, (128, 1), 0) < 64
        query_grad = jnp.where(upper, query_parts[0], query_parts[1]).T
        lanes = pl.ds(pl.multiple_of(pair * 128, 128), 128)
        dqkv[0, rows, lanes] = (query_grad * HEAD_DIM**-0.5).astype(jnp.bfloat16)

        @pl.when(part == 1)
        def _():
            dqkv[1, 0:tokens, lanes] = k_sum[...].astype(jnp.bfloat16)
            dqkv[2, 0:tokens, lanes] = v_sum[...].astype(jnp.bfloat16)

        return 0

    def back_copies():
        copies = [
            pltpu.make_async_copy(
                weight_ref.at[:, pl.ds(features * i, features)],
                operands.at[i, pl.ds(0, features)],
                operand_sem.at[i],
            )
            for i in range(3)
        ]
        return copies + [operand(3, codes_ref)]

    def back():
        for copy in back_copies():
            copy.wait()
        middle_copy().wait()

        def rows_back(i, _):
            rows = pl.ds(pl.multiple_of(i * 256, 256), 256)
            grad = nt(dqkv[0, rows, :], operands[0, 0:features, :])
            grad = grad + nt(dqkv[1, rows, :], operands[1, 0:features, :])
            grad = grad + nt(dqkv[2, rows, :], operands[2, 0:features, :])
            start = operands[3, rows, :].astype(jnp.float32)
            unit, scale = normalize(start)
            for at, addend in enumerate(
                (dqkv[0, rows, :].astype(jnp.float32), dqkv[2, rows, :].astype(jnp.float32), grad * unit, grad)
            ):
                sums[0, at : at + 1, :] += jnp.sum(addend, axis=0, keepdims=True)
            start_grad = middle[rows, :] + norm_back(grad, row(gain_ref), unit, scale)
            share[rows, :] = (start_grad - 2.0 * commit_weight * start).astype(jnp.bfloat16)
            for member in range(members):

                @pl.when((i == member * each // 256) & (member != me))
                def _():
                    share_put(lax.rem(member - me - 1 + members, members), member).start()

            return 0

        lax.fori_loop(0, tokens // 256, rows_back, 0)
        own_share().start()
        sums_put(0).start()

    partners = (mate, over_x, over_y, near, away)

    def sums_put(i):
        return put(sums.at[i], sums_got.at[i], sums_sent.at[i], sums_recv.at[i], partners[i])

    def sums_step(i):
        sums_put(i).wait_recv()
        sums[i + 1] = sums[i] + sums_got[i]
        if i + 1 < len(partners):
            sums_put(i + 1).start()

    def own_share():
        rows = pl.ds(pl.multiple_of(me * each, 128), each)
        return pltpu.make_async_copy(share.at[rows], share_out.at[me], own_sem.at[0])

    def own_recon():
        return pltpu.make_async_copy(recon_ref.at[me], recon_out.at[me], own_sem.at[1])

    def middle_copy():
        return pltpu.make_async_copy(middle_ref, middle, once_sem.at[0])

    def marks_copy():
        return pltpu.make_async_copy(ka_ref, marks, once_sem.at[1])

    load_operands(0)
    marks_copy().start()
    middle_copy().start()
    for copy in head_copies(0):
        copy.start()
    for i in range(members - 1):
        recon_put(i).start()
    own_recon().start()
    sums[0] = jnp.zeros(sums.shape[1:], jnp.float32)
    for at, ref in ((4, out_bias_sum), (5, second_gain_sum), (6, second_shift_sum)):
        sums[0, at : at + 1, :] = ref[...]
    for k in range(4):
        sums[0, 7 + k : 8 + k, :] = up_bias_sum[:, k * features : (k + 1) * features]
    sums[0, 11:12, :] = down_bias_sum[...]
    sums[0, 12:13, :] = pixel_bias_sum[...]
    marks_copy().wait()
    stages = (stage1, stage2, stage3, stage4, stage5, stage6)
    last = 6

    def turn(t, _):
        @pl.when(t == last)
        def _():
            back()
            load_operands(last)

        @pl.when(t < count)
        def _():
            make_blocks(t)

        @pl.when((t < count - 1) & (t != last - 1))
        def _():
            load_operands(t + 1)

        @pl.when(t == last - 1)
        def _():
            for copy in back_copies():
                copy.start()

        def upto(s):
            return jnp.clip(2 * (s - 1) + jnp.maximum(s - last + 2, 0), 0, 2 * pairs)

        lax.fori_loop(upto(t), upto(t + 1), attend_part, 0)
        for i in range(len(partners)):
            pl.when(t == last + 1 + i)(partial(sums_step, i))
        for stage, behind in zip(stages, lead):
            c = t - behind
            pl.when((c >= 0) & (c < count))(partial(stage, c))
        return 0

    lax.fori_loop(0, count + lead[-1], turn, 0)

    def finish(c, _):
        level6(c).wait_recv()
        for level in (level2y, level3, level4, level5, level6):
            level(c).wait_send()
        pl.when(only_y(c))(lambda: level2x(c).wait_send())
        pl.when(both_x(c))(lambda: level2y(c, 1).wait_send())
        return 0

    lax.fori_loop(0, count, finish, 0)
    for c in range(count - slots, count):
        for b in range(2 if c < count - 1 else 1):
            level0(c, b).wait_send()
    for i in range(len(partners)):
        sums_put(i).wait_send()
    own = pltpu.roll(sums[len(partners)], lax.rem((members - me) * (features // members), features), 1)
    vector_out[0:16, :] = own
    wide_row = sums[len(partners), pl.ds(7 + me // 2, 1), :]
    vector_out[16:24, :] = jnp.broadcast_to(
        jnp.where(lax.rem(me, 2) == 0, wide_row, pltpu.roll(wide_row, features // 2, 1)), (8, features)
    )
    copies = []
    for block, (home, prefix, column) in enumerate(homes):
        out = outs[home] if prefix is None else outs[home].at[prefix]
        target = out.at[:, :, pl.ds(column, features)]
        copies.append(pltpu.make_async_copy(whole.at[block], target, out_sem.at[block]))
        copies[-1].start()
    for i in range(members - 1):
        recon_put(i).wait_recv()
        share_put(i).wait_recv()
        recon_put(i).wait_send()
        share_put(i).wait_send()
    own_recon().wait()
    own_share().wait()
    for copy in copies:
        copy.wait()


def finish(inputs, tiling):
    tokens, features = inputs[7].shape
    members = tiling[0] * tiling[1]
    blocks, slots, got_slots = 21, 3, 3
    count = (blocks + 1) // 2
    rows, width = features // members // 2, features // 2
    lead = (0, 2, 4, 6, 8, 10)
    homes = [(0, k, 0) for k in range(8)] + [(2, k, 0) for k in range(4)]
    homes += [(4, None, features * k) for k in range(3)] + [(0, 8, 0), (3, None, 0)]
    homes += [(1, None, features * k) for k in range(4)]
    shapes = [
        (9, 2, rows, features),
        (2, rows, 4 * features),
        (4, 2, rows, features),
        (2, rows, features),
        (2, rows, 3 * features),
        (members, tokens // members, features),
        (members, tokens // members, features),
    ]
    anywhere = pl.BlockSpec(memory_space=pl.ANY)
    inside = pl.BlockSpec(memory_space=pltpu.VMEM)
    dma = pltpu.SemaphoreType.DMA
    low, wide = jnp.bfloat16, jnp.float32
    cut = (2, 2, 2, 2, rows, width)
    scratch = [
        pltpu.VMEM((slots, 2, 2) + cut, low),
        pltpu.VMEM((got_slots, 2) + cut, low),
        pltpu.VMEM((count, 2) + cut[1:], low),
        pltpu.VMEM((count, 2) + cut[2:], low),
        pltpu.VMEM((count, 2) + cut[3:], low),
        pltpu.VMEM((count, 2) + cut[4:], low),
        pltpu.VMEM((2 * count, 2, rows, features), low),
        pltpu.VMEM((4, tokens, features), low),
        pltpu.VMEM((2, members, 2 * rows, tokens), low),
        pltpu.VMEM((2, 6, tokens, 128), low),
        pltpu.VMEM((tokens, 128), low),
        pltpu.VMEM((6, 16, features), wide),
        pltpu.VMEM((5, 16, features), wide),
        pltpu.VMEM((tokens, features), wide),
        pltpu.VMEM((tokens, features), low),
        pltpu.VMEM((tokens, 128), wide),
        pltpu.VMEM((tokens, 128), wide),
        pltpu.VMEM((3, tokens, features), low),
    ]
    scratch += [dma((count, 2))] * 6 + [dma((count,))] * 8
    scratch += [dma((blocks,)), dma((4,)), dma((2,)), dma((2, 6)), dma((2,))]
    scratch += [pltpu.SemaphoreType.REGULAR, dma((2,))]
    scratch += [dma((members - 1,))] * 4 + [dma((5,))] * 2
    return pl.pallas_call(
        partial(
            finish_kernel,
            blocks=blocks,
            homes=homes,
            lead=lead,
            slots=slots,
            got_slots=got_slots,
            tiling=tiling,
        ),
        in_specs=[anywhere] * 19 + [inside] * 7,
        out_specs=[anywhere] * 5 + [inside] + [anywhere] * 2,
        out_shape=[jax.ShapeDtypeStruct(shape, low) for shape in shapes[:5]]
        + [jax.ShapeDtypeStruct((24, features), wide)]
        + [jax.ShapeDtypeStruct(shape, low) for shape in shapes[5:]],
        scratch_shapes=scratch,
        compiler_params=pltpu.CompilerParams(
            collective_id=1, has_side_effects=True, vmem_limit_bytes=60 * 2**20
        ),
        cost_estimate=pl.CostEstimate(
            flops=2 * tokens * features * (24 * features) + 24 * tokens * tokens * features,
            bytes_accessed=100 * tokens * features,
            transcendentals=tokens * tokens * features // 64,
        ),
        name="finish",
    )(*inputs)


def on_device_grids(
    encoder_out,
    code_ids,
    segments,
    embed_table,
    recon_grad,
    qkv_weight,
    query_bias,
    value_bias,
    out_weight,
    out_bias,
    first_gain,
    first_shift,
    second_gain,
    second_shift,
    up_weight,
    up_bias,
    down_weight,
    down_bias,
    pixel_weight,
    pixel_bias,
):
    features = encoder_out.shape[-1]
    wide = jnp.float32
    down, across = lax.axis_size("ty"), lax.axis_size("tx")
    members = down * across
    axes = ("ty", "tx")
    tiling = (down, across) + encoder_out.shape[1:3]
    each = encoder_out.shape[1] * encoder_out.shape[2]
    tokens = members * each

    def line(vector):
        return vector.reshape(1, -1)

    def exchange(tiles):
        return lax.all_to_all(tiles, axes, split_axis=0, concat_axis=0, tiled=True)

    slots = 3 * each // 2
    asked, slot_index = ask(
        jnp.swapaxes(code_ids, 1, 2), jnp.swapaxes(segments, 1, 2), embed_table.shape[0], slots
    )
    asked, recon_grad = lax.optimization_barrier((asked, recon_grad))
    cotangent = exchange(recon_grad).reshape(tokens, features)
    moved, query_marks, key_marks = spread_marks(asked[:, 2], *tiling)
    asked = asked[:, :2].reshape(members, -1)[:, :slots].reshape(-1)
    fetched = embed_table.at[asked].get(mode="promise_in_bounds")
    pixel_taps = jnp.swapaxes(pixel_weight, 0, 1)
    codes, final_grad, lower_grad, behind, hidden_grad, pixel_bias_grad, down_bias_grad = fetch(
        fetched.reshape(members, slots, features),
        slot_index,
        cotangent,
        moved,
        pixel_taps,
        down_weight,
        tiling,
    )
    codes = codes.reshape(tokens, features)

    (
        normed,
        queries,
        key_rows,
        values,
        attended,
        columns,
        features_low,
        normed_two,
        hidden_turned,
        pre_grad,
        middle_grad,
        branch_grad,
        attended_grad,
        out_bias_grad,
        second_gain_grad,
        second_shift_grad,
        up_bias_grad,
    ) = forward(
        [
            codes,
            final_grad,
            hidden_grad,
            query_marks,
            key_marks,
            qkv_weight,
            out_weight,
            up_weight,
            down_weight,
        ],
        [
            line(first_gain),
            line(first_shift),
            line(query_bias),
            line(value_bias),
            line(out_bias),
            line(second_gain),
            line(second_shift),
            line(up_bias),
            line(down_bias),
        ],
    )
    recon_rows, features_plain = conv(features_low, moved, pixel_taps, line(pixel_bias), tiling)
    pixel_sum, up_sum, down_sum, out_sum, qkv_sum, vectors, recon_tiles, share_tiles = finish(
        [
            queries,
            key_rows,
            values,
            columns,
            key_marks,
            attended,
            attended_grad,
            codes,
            middle_grad,
            features_plain,
            behind,
            normed_two,
            pre_grad,
            hidden_turned.reshape(members, 4, features // members, tokens),
            lower_grad,
            branch_grad,
            normed,
            qkv_weight,
            recon_rows.reshape(members, each, features),
            line(first_gain),
            out_bias_grad,
            second_gain_grad,
            second_shift_grad,
            up_bias_grad,
            down_bias_grad,
            pixel_bias_grad,
        ],
        tiling,
    )
    input_tiles = (
        share_tiles.reshape(encoder_out.shape).astype(wide)
        + 2.0 * commit_weight * encoder_out.astype(wide)
    ).astype(jnp.bfloat16)
    rows = features // members

    def mine(at, count=1):
        return vectors[at, : rows * count]

    def whole_sum(summed):
        return summed.reshape(-1, summed.shape[-1]).astype(wide)

    return (
        recon_tiles.reshape(encoder_out.shape),
        input_tiles,
        whole_sum(qkv_sum),
        mine(0),
        mine(1),
        whole_sum(out_sum),
        mine(4),
        mine(2),
        mine(3),
        mine(5),
        mine(6),
        whole_sum(up_sum),
        mine(16, 4),
        whole_sum(down_sum),
        mine(11),
        jnp.swapaxes(whole_sum(pixel_sum).reshape(9, rows, features), 0, 1),
        mine(12),
    )


def solution(mesh):
    in_specs = (
        P("gr", "ty", "tx", None),
        P("gr", "ty", "tx"),
        P("gr", "ty", "tx"),
        P(("ty", "tx"), None),
        P("gr", "ty", "tx", None),
        P(),
        P(),
        P(),
        P(),
        P(),
        P(),
        P(),
        P(),
        P(),
        P(),
        P(),
        P(),
        P(),
        P(),
        P(),
    )
    out_specs = (
        P("gr", "ty", "tx", None),
        P("gr", "ty", "tx", None),
        P(("ty", "tx"), None),
        P(("ty", "tx")),
        P(("ty", "tx")),
        P(("ty", "tx"), None),
        P(("ty", "tx")),
        P(("ty", "tx")),
        P(("ty", "tx")),
        P(("ty", "tx")),
        P(("ty", "tx")),
        P(("ty", "tx"), None),
        P(("ty", "tx")),
        P(("ty", "tx"), None),
        P(("ty", "tx")),
        P(("ty", "tx"), None, None),
        P(("ty", "tx")),
    )
    def on_device(encoder_out, *rest):
        members = mesh.shape["ty"] * mesh.shape["tx"]
        whole_grids = encoder_out.shape[0] == members and tuple(mesh.devices.shape) == (4, 2, 4)
        body = on_device_grids if whole_grids else on_device_bands
        return body(encoder_out, *rest)

    return jax.shard_map(
        on_device, mesh=mesh, in_specs=in_specs, out_specs=out_specs, check_vma=False
    )
```

```python
from functools import partial

import jax
import jax.numpy as jnp
from jax import lax
from jax.experimental import pallas as pl
from jax.experimental.pallas import tpu as pltpu
from jax.sharding import PartitionSpec as P

HEADS = 12
HEAD_DIM = 64


epsilon = 1e-06
commit_weight = 0.25


def with_halo(block, sides, width):
    for axis, dim in sides:
        count = lax.axis_size(axis)
        forward = [(i, i + 1) for i in range(count - 1)]
        backward = [(target, source) for source, target in forward]
        low = lax.ppermute(
            lax.slice_in_dim(block, block.shape[dim] - width, None, axis=dim), axis, forward
        )
        high = lax.ppermute(lax.slice_in_dim(block, 0, width, axis=dim), axis, backward)
        block = jnp.concatenate([low, block, high], axis=dim)
    return block


def layer_norm(values, gain, shift):
    center = values - jnp.mean(values, axis=-1, keepdims=True)
    spread = jnp.mean(center * center, axis=-1, keepdims=True)
    return center * lax.rsqrt(spread + epsilon) * gain + shift


def exact_gelu(values):
    return jax.nn.gelu(values, approximate=False)


def matmul(left_side, right_side):
    return jnp.dot(left_side, right_side, preferred_element_type=jnp.float32)


def left_product(left_side, right_side):
    return lax.dot_general(
        left_side, right_side, (((0,), (0,)), ((), ())), preferred_element_type=jnp.float32
    )


def right_product(left_side, right_side):
    return lax.dot_general(
        left_side, right_side, (((1,), (1,)), ((), ())), preferred_element_type=jnp.float32
    )


def pad_side(array, axis_index):
    widths = [(0, 0)] * array.ndim
    widths[axis_index] = (1, 1)
    return jnp.pad(array, widths)


def blocked(array, block_size):
    return array.reshape((array.shape[0] // block_size, block_size) + array.shape[1:])


def unblock(array):
    return array.reshape((-1,) + array.shape[2:])


def head_scores(queries, key_rows, marks_query, marks_key, head_count, score_scale):
    grid_count, query_rows, features = queries.shape
    query_heads = queries.reshape(grid_count, query_rows, head_count, features // head_count)
    key_heads = key_rows.reshape(grid_count, key_rows.shape[1], head_count, features // head_count)
    scores = (
        jnp.einsum("bqhd,bkhd->bhqk", query_heads, key_heads, preferred_element_type=jnp.float32)
        * score_scale
    )
    same_image = (marks_query[:, :, None] == marks_key[:, None, :])[:, None]
    return jnp.where(same_image, scores, -1000000000.0)


def attend_block(bundle, head_count, score_scale):
    queries, key_rows, values, marks_query, marks_key = bundle
    grid_count, query_rows, features = queries.shape
    scores = head_scores(queries, key_rows, marks_query, marks_key, head_count, score_scale)
    running_max = jnp.max(scores, axis=-1, keepdims=True)
    exponent = jnp.exp(scores - running_max)
    denominator = jnp.sum(exponent, axis=-1, keepdims=True)
    probability = (exponent / denominator).astype(jnp.bfloat16)
    value_heads = values.reshape(grid_count, values.shape[1], head_count, features // head_count)
    attended = jnp.einsum(
        "bhqk,bkhd->bqhd", probability, value_heads, preferred_element_type=jnp.float32
    )
    return (
        attended.reshape(grid_count, query_rows, features).astype(jnp.bfloat16),
        running_max + jnp.log(denominator),
    )


def attend_back(bundle, head_count, score_scale):
    queries, key_rows, values, marks_query, marks_key, log_total, out_grad = bundle
    grid_count, query_rows, features = queries.shape
    head_size = features // head_count
    scores = head_scores(queries, key_rows, marks_query, marks_key, head_count, score_scale)
    probability = jnp.exp(scores - log_total)
    query_heads = queries.reshape(grid_count, query_rows, head_count, head_size)
    key_heads = key_rows.reshape(grid_count, key_rows.shape[1], head_count, head_size)
    value_heads = values.reshape(grid_count, values.shape[1], head_count, head_size)
    grad_heads = out_grad.reshape(grid_count, query_rows, head_count, head_size)
    prob_grad = jnp.einsum(
        "bqhd,bkhd->bhqk", grad_heads, value_heads, preferred_element_type=jnp.float32
    )
    inner_sum = jnp.sum(probability * prob_grad, axis=-1, keepdims=True)
    score_grad = (probability * (prob_grad - inner_sum)).astype(jnp.bfloat16)
    query_grad = (
        jnp.einsum("bhqk,bkhd->bqhd", score_grad, key_heads, preferred_element_type=jnp.float32)
        * score_scale
    )
    key_grad = (
        jnp.einsum("bhqk,bqhd->bkhd", score_grad, query_heads, preferred_element_type=jnp.float32)
        * score_scale
    )
    value_grad = jnp.einsum(
        "bhqk,bqhd->bkhd",
        probability.astype(jnp.bfloat16),
        grad_heads,
        preferred_element_type=jnp.float32,
    )
    key_count = key_rows.shape[1]
    return (
        query_grad.reshape(grid_count, query_rows, features).astype(jnp.bfloat16),
        key_grad.reshape(grid_count, key_count, features),
        value_grad.reshape(grid_count, key_count, features),
    )


def on_device_bands(
    encoder_out,
    code_ids,
    segments,
    embed_table,
    recon_grad,
    qkv_weight,
    query_bias,
    value_bias,
    out_weight,
    out_bias,
    first_gain,
    first_shift,
    second_gain,
    second_shift,
    up_weight,
    up_bias,
    down_weight,
    down_bias,
    pixel_weight,
    pixel_bias,
):
    features = encoder_out.shape[-1]
    head_count = HEADS
    score_scale = float(HEAD_DIM) ** (-0.5)
    holder_count = lax.axis_size(("ty", "tx"))
    share_rows = embed_table.shape[0]
    flat_ids = code_ids.reshape(-1)
    row_count = flat_ids.shape[0]
    slot_count = 3 * row_count // (2 * holder_count)
    holder = flat_ids // share_rows
    offsets = flat_ids - holder * share_rows
    belongs = (holder[:, None] == jnp.arange(holder_count, dtype=jnp.int32)[None, :]).astype(
        jnp.int32
    )
    slot_rank = jnp.sum((jnp.cumsum(belongs, axis=0) - 1) * belongs, axis=1)
    slot_index = holder * slot_count + slot_rank
    requests = jnp.zeros((holder_count * slot_count,), jnp.int32).at[slot_index].set(offsets)
    requests = requests.reshape(holder_count, slot_count)
    fetched = jnp.take(
        embed_table,
        lax.all_to_all(requests, ("ty", "tx"), split_axis=0, concat_axis=0, tiled=True),
        axis=0,
    )
    returned = lax.all_to_all(fetched, ("ty", "tx"), split_axis=0, concat_axis=0, tiled=True)
    codes = returned.reshape(holder_count * slot_count, features)[slot_index].reshape(
        encoder_out.shape
    )
    marks_tile = (segments + 1).astype(jnp.bfloat16)
    arrived = (
        lax.all_to_all(encoder_out, "tx", split_axis=0, concat_axis=2, tiled=True),
        lax.all_to_all(codes, "tx", split_axis=0, concat_axis=2, tiled=True),
        lax.all_to_all(recon_grad, "tx", split_axis=0, concat_axis=2, tiled=True),
        lax.all_to_all(marks_tile, "tx", split_axis=0, concat_axis=2, tiled=True),
    )
    inputs_band, codes_band, cotangent_band, marks_band = arrived
    grid_count, band_rows, band_cols = marks_band.shape
    tokens = band_rows * band_cols
    all_rows = grid_count * tokens
    block_size = max(1, 512 // tokens)
    while grid_count % block_size:
        block_size -= 1
    start_rows = codes_band.reshape(all_rows, features).astype(jnp.float32)
    marks_query = marks_band.reshape(grid_count, tokens)
    normed, first_pull = jax.vjp(
        layer_norm, start_rows, first_gain.astype(jnp.float32), first_shift.astype(jnp.float32)
    )
    normed_low = normed.astype(jnp.bfloat16)
    projected = matmul(normed_low, qkv_weight)
    queries = (
        (projected[:, :features] + query_bias.astype(jnp.float32))
        .astype(jnp.bfloat16)
        .reshape(grid_count, tokens, features)
    )
    key_rows = (
        projected[:, features : 2 * features]
        .astype(jnp.bfloat16)
        .reshape(grid_count, tokens, features)
    )
    values = (
        (projected[:, 2 * features :] + value_bias.astype(jnp.float32))
        .astype(jnp.bfloat16)
        .reshape(grid_count, tokens, features)
    )
    bundle = (key_rows, values, marks_query)
    keys_all = lax.all_gather(bundle[0], "ty", axis=1, tiled=True)
    values_all = lax.all_gather(bundle[1], "ty", axis=1, tiled=True)
    marks_key = lax.all_gather(bundle[2], "ty", axis=1, tiled=True)
    attended_blocks, log_total = lax.map(
        partial(attend_block, head_count=head_count, score_scale=score_scale),
        (
            blocked(queries, block_size),
            blocked(keys_all, block_size),
            blocked(values_all, block_size),
            blocked(marks_query, block_size),
            blocked(marks_key, block_size),
        ),
    )
    attended = unblock(attended_blocks).reshape(all_rows, features)
    branch = matmul(attended, out_weight) + out_bias.astype(jnp.float32)
    middle = start_rows + branch
    normed_two, second_pull = jax.vjp(
        layer_norm, middle, second_gain.astype(jnp.float32), second_shift.astype(jnp.float32)
    )
    normed_two_low = normed_two.astype(jnp.bfloat16)
    hidden_pre = matmul(normed_two_low, up_weight) + up_bias.astype(jnp.float32)
    hidden_act, gelu_pull = jax.vjp(exact_gelu, hidden_pre)
    hidden_low = hidden_act.astype(jnp.bfloat16)
    output_rows = middle + (matmul(hidden_low, down_weight) + down_bias.astype(jnp.float32))
    features_low = output_rows.astype(jnp.bfloat16).reshape(
        grid_count, band_rows, band_cols, features
    )
    bundle = (features_low, marks_band, cotangent_band)
    grown = (
        with_halo(bundle[0], (("ty", 1),), 1),
        with_halo(bundle[1], (("ty", 1),), 1),
        with_halo(bundle[2], (("ty", 1),), 1),
    )
    features_pad, marks_pad, cotangent_pad = tuple((pad_side(member, 2) for member in grown))
    ahead_list = []
    behind_list = []
    for vertical in range(3):
        for lateral in range(3):
            inside = (
                marks_pad[:, vertical : vertical + band_rows, lateral : lateral + band_cols]
                == marks_band
            )
            ahead_list.append(
                jnp.where(
                    inside[..., None],
                    features_pad[:, vertical : vertical + band_rows, lateral : lateral + band_cols],
                    0,
                )
            )
            mirror_row = 2 - vertical
            mirror_col = 2 - lateral
            facing = (
                marks_pad[
                    :, mirror_row : mirror_row + band_rows, mirror_col : mirror_col + band_cols
                ]
                == marks_band
            )
            behind_list.append(
                jnp.where(
                    facing[..., None],
                    cotangent_pad[
                        :, mirror_row : mirror_row + band_rows, mirror_col : mirror_col + band_cols
                    ],
                    0,
                )
            )
    ahead = jnp.stack(ahead_list, axis=3)
    behind = jnp.stack(behind_list, axis=3)
    recon_band = jnp.einsum(
        "nhwkd,dkp->nhwp", ahead, pixel_weight, preferred_element_type=jnp.float32
    ) + pixel_bias.astype(jnp.float32)
    pixel_weight_grad = jnp.einsum(
        "nhwkd,nhwp->dkp", ahead, cotangent_band, preferred_element_type=jnp.float32
    )
    pixel_bias_grad = jnp.sum(cotangent_band.astype(jnp.float32), axis=(0, 1, 2))
    final_grad = jnp.einsum(
        "nhwkp,dkp->nhwd", behind, pixel_weight, preferred_element_type=jnp.float32
    ).reshape(all_rows, features)
    lower_grad = final_grad.astype(jnp.bfloat16)
    down_weight_grad = left_product(hidden_low, lower_grad)
    down_bias_grad = jnp.sum(lower_grad.astype(jnp.float32), axis=0)
    pre_grad = gelu_pull(right_product(lower_grad, down_weight))[0].astype(jnp.bfloat16)
    up_weight_grad = left_product(normed_two_low, pre_grad)
    up_bias_grad = jnp.sum(pre_grad.astype(jnp.float32), axis=0)
    middle_part, second_gain_grad, second_shift_grad = second_pull(
        right_product(pre_grad, up_weight)
    )
    middle_grad = final_grad + middle_part
    branch_grad = middle_grad.astype(jnp.bfloat16)
    out_weight_grad = left_product(attended, branch_grad)
    out_bias_grad = jnp.sum(branch_grad.astype(jnp.float32), axis=0)
    attended_grad = (
        right_product(branch_grad, out_weight)
        .astype(jnp.bfloat16)
        .reshape(grid_count, tokens, features)
    )
    query_blocks, key_blocks, value_blocks = lax.map(
        partial(attend_back, head_count=head_count, score_scale=score_scale),
        (
            blocked(queries, block_size),
            blocked(keys_all, block_size),
            blocked(values_all, block_size),
            blocked(marks_query, block_size),
            blocked(marks_key, block_size),
            log_total,
            blocked(attended_grad, block_size),
        ),
    )
    query_grad = unblock(query_blocks)
    bundle = (unblock(key_blocks), unblock(value_blocks))
    key_sum = lax.psum_scatter(
        bundle[0].astype(jnp.bfloat16), "ty", scatter_dimension=1, tiled=True
    )
    value_sum = lax.psum_scatter(
        bundle[1].astype(jnp.bfloat16), "ty", scatter_dimension=1, tiled=True
    )
    projected_grad = jnp.concatenate([query_grad, key_sum, value_sum], axis=-1).reshape(
        all_rows, 3 * features
    )
    qkv_weight_grad = left_product(normed_low, projected_grad)
    query_bias_grad = jnp.sum(query_grad.astype(jnp.float32), axis=(0, 1))
    value_bias_grad = jnp.sum(value_sum.astype(jnp.float32), axis=(0, 1))
    start_part, first_gain_grad, first_shift_grad = first_pull(
        right_product(projected_grad, qkv_weight)
    )
    start_grad = middle_grad + start_part
    inputs_rows = inputs_band.reshape(all_rows, features).astype(jnp.float32)
    input_band = (start_grad + 2.0 * commit_weight * (inputs_rows - start_rows)).astype(
        jnp.bfloat16
    )
    bundle = (
        recon_band.astype(jnp.bfloat16),
        input_band.reshape(grid_count, band_rows, band_cols, features),
    )
    recon_tiles = lax.all_to_all(bundle[0], "tx", split_axis=2, concat_axis=0, tiled=True)
    input_tiles = lax.all_to_all(bundle[1], "tx", split_axis=2, concat_axis=0, tiled=True)
    local_grads = (
        qkv_weight_grad,
        query_bias_grad,
        value_bias_grad,
        out_weight_grad,
        out_bias_grad,
        first_gain_grad,
        first_shift_grad,
        second_gain_grad,
        second_shift_grad,
        up_weight_grad,
        up_bias_grad,
        down_weight_grad,
        down_bias_grad,
        pixel_weight_grad,
        pixel_bias_grad,
    )
    tile_shares = (
        lax.psum_scatter(
            local_grads[0].astype(jnp.bfloat16), ("ty", "tx"), scatter_dimension=0, tiled=True
        ).astype(jnp.float32),
        lax.psum_scatter(
            local_grads[1].astype(jnp.bfloat16), ("ty", "tx"), scatter_dimension=0, tiled=True
        ).astype(jnp.float32),
        lax.psum_scatter(
            local_grads[2].astype(jnp.bfloat16), ("ty", "tx"), scatter_dimension=0, tiled=True
        ).astype(jnp.float32),
        lax.psum_scatter(
            local_grads[3].astype(jnp.bfloat16), ("ty", "tx"), scatter_dimension=0, tiled=True
        ).astype(jnp.float32),
        lax.psum_scatter(
            local_grads[4].astype(jnp.bfloat16), ("ty", "tx"), scatter_dimension=0, tiled=True
        ).astype(jnp.float32),
        lax.psum_scatter(
            local_grads[5].astype(jnp.bfloat16), ("ty", "tx"), scatter_dimension=0, tiled=True
        ).astype(jnp.float32),
        lax.psum_scatter(
            local_grads[6].astype(jnp.bfloat16), ("ty", "tx"), scatter_dimension=0, tiled=True
        ).astype(jnp.float32),
        lax.psum_scatter(
            local_grads[7].astype(jnp.bfloat16), ("ty", "tx"), scatter_dimension=0, tiled=True
        ).astype(jnp.float32),
        lax.psum_scatter(
            local_grads[8].astype(jnp.bfloat16), ("ty", "tx"), scatter_dimension=0, tiled=True
        ).astype(jnp.float32),
        lax.psum_scatter(
            local_grads[9].astype(jnp.bfloat16), ("ty", "tx"), scatter_dimension=0, tiled=True
        ).astype(jnp.float32),
        lax.psum_scatter(
            local_grads[10].astype(jnp.bfloat16), ("ty", "tx"), scatter_dimension=0, tiled=True
        ).astype(jnp.float32),
        lax.psum_scatter(
            local_grads[11].astype(jnp.bfloat16), ("ty", "tx"), scatter_dimension=0, tiled=True
        ).astype(jnp.float32),
        lax.psum_scatter(
            local_grads[12].astype(jnp.bfloat16), ("ty", "tx"), scatter_dimension=0, tiled=True
        ).astype(jnp.float32),
        lax.psum_scatter(
            local_grads[13].astype(jnp.bfloat16), ("ty", "tx"), scatter_dimension=0, tiled=True
        ).astype(jnp.float32),
        lax.psum_scatter(
            local_grads[14].astype(jnp.bfloat16), ("ty", "tx"), scatter_dimension=0, tiled=True
        ).astype(jnp.float32),
    )
    summed = (
        lax.psum(tile_shares[0].astype(jnp.bfloat16), "gr").astype(jnp.float32),
        lax.psum(tile_shares[1].astype(jnp.bfloat16), "gr").astype(jnp.float32),
        lax.psum(tile_shares[2].astype(jnp.bfloat16), "gr").astype(jnp.float32),
        lax.psum(tile_shares[3].astype(jnp.bfloat16), "gr").astype(jnp.float32),
        lax.psum(tile_shares[4].astype(jnp.bfloat16), "gr").astype(jnp.float32),
        lax.psum(tile_shares[5].astype(jnp.bfloat16), "gr").astype(jnp.float32),
        lax.psum(tile_shares[6].astype(jnp.bfloat16), "gr").astype(jnp.float32),
        lax.psum(tile_shares[7].astype(jnp.bfloat16), "gr").astype(jnp.float32),
        lax.psum(tile_shares[8].astype(jnp.bfloat16), "gr").astype(jnp.float32),
        lax.psum(tile_shares[9].astype(jnp.bfloat16), "gr").astype(jnp.float32),
        lax.psum(tile_shares[10].astype(jnp.bfloat16), "gr").astype(jnp.float32),
        lax.psum(tile_shares[11].astype(jnp.bfloat16), "gr").astype(jnp.float32),
        lax.psum(tile_shares[12].astype(jnp.bfloat16), "gr").astype(jnp.float32),
        lax.psum(tile_shares[13].astype(jnp.bfloat16), "gr").astype(jnp.float32),
        lax.psum(tile_shares[14].astype(jnp.bfloat16), "gr").astype(jnp.float32),
    )
    return (
        recon_tiles,
        input_tiles,
        summed[0],
        summed[1],
        summed[2],
        summed[3],
        summed[4],
        summed[5],
        summed[6],
        summed[7],
        summed[8],
        summed[9],
        summed[10],
        summed[11],
        summed[12],
        summed[13],
        summed[14],
    )


far = float(2.0**30)


def nt(left_side, right_side):
    return lax.dot_general(
        left_side, right_side, (((1,), (1,)), ((), ())), preferred_element_type=jnp.float32
    )


def nn(left_side, right_side):
    return lax.dot_general(
        left_side, right_side, (((1,), (0,)), ((), ())), preferred_element_type=jnp.float32
    )


def tn(left_side, right_side):
    return lax.dot_general(
        left_side, right_side, (((0,), (0,)), ((), ())), preferred_element_type=jnp.float32
    )


def groups(down, across, rows, cols):
    for part in range(down * across):
        for r in range(rows):
            grid_row = (part // across) * rows + r
            yield (part * rows + r) * cols, (grid_row * across + part % across) * cols


def conv_kernel(rows_ref, mask_ref, weight_ref, bias_ref, out_ref, plain_ref, shifted, total, other, *, tiling):
    width, cols = tiling[1] * tiling[3], tiling[3]
    tap = pl.program_id(0)
    tokens, features = rows_ref.shape

    @pl.when(tap == 0)
    def _():
        other[...] = rows_ref[...].astype(jnp.float32)
        for tiled, plain in groups(*tiling):
            total[plain : plain + cols, :] = other[tiled : tiled + cols, :]
        rows = total[...]
        plain_ref[...] = rows.astype(jnp.bfloat16)
        for j in range(3):
            moved = rows if j == 1 else pltpu.roll(rows, (1 - j) % tokens, 0)
            shifted[j, 0:width, :] = jnp.zeros((width, features), jnp.bfloat16)
            shifted[j, width + tokens :, :] = jnp.zeros((width, features), jnp.bfloat16)
            shifted[j, width : width + tokens, :] = moved.astype(jnp.bfloat16)
        total[...] = jnp.zeros_like(total)

    below, right = tap // 3, tap % 3
    step = tokens // 4
    for i in range(4):
        rows = slice(i * step, (i + 1) * step)
        first = pl.multiple_of(below * width + i * step, width)
        marks = mask_ref[1, width + i * step : width + (i + 1) * step, :]
        same = mask_ref[right, pl.ds(first, step), :] == marks
        mask = jnp.where(same, 1.0, 0.0).astype(jnp.bfloat16)
        mask = jnp.concatenate([mask] * (features // 128), axis=1)
        total[rows, :] += nn(shifted[right, pl.ds(first, step), :] * mask, weight_ref[0])

    @pl.when(tap == 8)
    def _():
        for tiled, plain in groups(*tiling):
            other[tiled : tiled + cols, :] = total[plain : plain + cols, :]
        out_ref[...] = (other[...] + bias_ref[...].astype(jnp.float32)).astype(jnp.bfloat16)


def in_hbm(shape, dtype=jnp.bfloat16):
    return pltpu.HBM(shape, dtype)


def conv(rows, masks, weight, bias, tiling):
    tokens, features = rows.shape
    width = tiling[1] * tiling[3]

    def whole(shape):
        return pl.BlockSpec(shape, lambda k: (0,) * len(shape), pipeline_mode=pl.Buffered(1))

    return pl.pallas_call(
        partial(conv_kernel, tiling=tiling),
        grid=(9,),
        in_specs=[
            whole((tokens, features)),
            whole(masks.shape),
            pl.BlockSpec((1, features, features), lambda k: (k, 0, 0)),
            whole((1, features)),
        ],
        out_specs=[whole((tokens, features))] * 2,
        out_shape=[in_hbm((tokens, features))] * 2,
        scratch_shapes=[
            pltpu.VMEM((3, tokens + 2 * width, features), jnp.bfloat16),
            pltpu.VMEM((tokens, features), jnp.float32),
            pltpu.VMEM((tokens, features), jnp.float32),
        ],
        compiler_params=pltpu.CompilerParams(vmem_limit_bytes=60 * 2**20),
        cost_estimate=pl.CostEstimate(
            flops=18 * tokens * features * features,
            bytes_accessed=18 * features * features + 4 * tokens * features,
            transcendentals=0,
        ),
        name="conv",
    )(rows, masks, weight, bias)


def marks_kernel(parts_ref, moved_ref, query_ref, key_ref, *, down, across, rows, cols):
    width = across * cols
    tokens = down * rows * width
    turned = parts_ref[...].astype(jnp.float32).T
    lane = lax.broadcasted_iota(jnp.int32, (rows * cols, 128), 1) % 64
    nowhere = jnp.full((width, 128), -1.0, jnp.float32)
    for j in range(3):
        moved_ref[j, 0:width, :] = nowhere
        moved_ref[j, width + tokens :, :] = nowhere
    for part in range(down * across):
        spread = jnp.broadcast_to(turned[:, part : part + 1], (rows * cols, 128))
        hot = spread == lane.astype(jnp.float32)
        here = slice(part * rows * cols, (part + 1) * rows * cols)
        query_ref[here, :] = jnp.where(hot, 1.0, 0.0).astype(jnp.bfloat16)
        key_ref[here, :] = jnp.where((lane < 3) & ~hot, -far, 0.0).astype(jnp.bfloat16)
        for r in range(rows):
            first = ((part // across) * rows + r) * width + (part % across) * cols + width
            moved_ref[1, first : first + cols, :] = spread[r * cols : (r + 1) * cols]
    marks = moved_ref[1, width : width + tokens, :]
    column = lax.broadcasted_iota(jnp.int32, (tokens, 128), 0) % width
    left = jnp.where(column == 0, -1.0, pltpu.roll(marks, 1, 0))
    right = jnp.where(column == width - 1, -1.0, pltpu.roll(marks, tokens - 1, 0))
    moved_ref[0, width : width + tokens, :] = left
    moved_ref[2, width : width + tokens, :] = right


def spread_marks(parts, down, across, rows, cols):
    tokens = down * across * rows * cols
    low = in_hbm((tokens, 128))
    return pl.pallas_call(
        partial(marks_kernel, down=down, across=across, rows=rows, cols=cols),
        out_shape=[
            in_hbm((3, tokens + 2 * across * cols, 128), jnp.float32),
            low,
            low,
        ],
        compiler_params=pltpu.CompilerParams(vmem_limit_bytes=60 * 2**20),
        name="spread_marks",
    )(parts)


def normalize(values):
    center = values - jnp.mean(values, axis=-1, keepdims=True)
    scale = lax.rsqrt(jnp.mean(center * center, axis=-1, keepdims=True) + epsilon)
    return center * scale, scale


def norm_back(grad, gain, unit, scale):
    scaled = grad * gain
    mean = jnp.mean(scaled, axis=-1, keepdims=True)
    along = jnp.mean(scaled * unit, axis=-1, keepdims=True)
    return scale * (scaled - mean - unit * along)


def row(ref):
    return ref[...].astype(jnp.float32)


def add_rows(ref, values):
    ref[...] += jnp.sum(values, axis=0, keepdims=True)


def ask_kernel(ids_ref, marks_ref, got_ref, slot_ref, sends, got, sent, received, *, share, slots):
    gr, ty, tx = lax.axis_index("gr"), lax.axis_index("ty"), lax.axis_index("tx")
    across = lax.axis_size("tx")
    members = lax.axis_size("ty") * across
    me = ty * across + tx
    others = [lax.rem(me + step, members) for step in range(1, members)]

    def place(member):
        return (gr, member // across, lax.rem(member, across))

    barrier = pltpu.get_barrier_semaphore()
    for member in others:
        pl.semaphore_signal(
            barrier, inc=1, device_id=place(member), device_id_type=pl.DeviceIdType.MESH
        )
    grids, tile_cols, tile_rows = ids_ref.shape
    each = tile_cols * tile_rows

    def spread(tile):
        return jnp.concatenate(
            [jnp.broadcast_to(tile[:, r : r + 1], (tile_cols, 128)) for r in range(tile_rows)], axis=0
        )

    lane = lax.broadcasted_iota(jnp.int32, (each, 128), 1)
    earlier = lax.broadcasted_iota(jnp.int32, (each, each), 1)
    earlier = earlier < lax.broadcasted_iota(jnp.int32, (each, each), 0)
    earlier = jnp.where(earlier, 1.0, 0.0).astype(jnp.bfloat16)
    counts = jnp.zeros((1, 128), jnp.float32)
    high = jnp.zeros((128, 128), jnp.float32)
    low = jnp.zeros((128, 128), jnp.float32)
    for grid in range(grids):
        ids = spread(ids_ref[grid])
        holder = jnp.zeros_like(ids)
        for member in range(1, members):
            holder = holder + jnp.where(ids >= member * share, 1, 0)
        offset = ids - holder * share
        belongs = jnp.where(holder == lane, 1.0, 0.0)
        ranks = nn(earlier, belongs.astype(jnp.bfloat16)) + counts
        counts = counts + jnp.sum(belongs, axis=0, keepdims=True)
        rank = jnp.sum(belongs * ranks, axis=1, keepdims=True)
        rank = jnp.broadcast_to(rank, (each, 128)).astype(jnp.int32)
        slot_ref[grid * each : (grid + 1) * each, :] = holder * slots + rank
        second = jnp.where(rank >= 128, 1, 0)
        of_row = 2 * holder + second == lane
        of_lane = jnp.where(rank - 128 * second == lane, 1.0, 0.0).astype(jnp.bfloat16)
        upper = jnp.floor(offset.astype(jnp.float32) * (1.0 / 64.0))
        lower = offset.astype(jnp.float32) - 64.0 * upper
        high = high + tn(jnp.where(of_row, upper, 0.0).astype(jnp.bfloat16), of_lane)
        low = low + tn(jnp.where(of_row, lower, 0.0).astype(jnp.bfloat16), of_lane)
    wanted = (high * 64.0 + low).astype(jnp.int32)
    sends[...] = jnp.zeros_like(sends)
    for member in range(members):
        sends[member, 0:2, :] = wanted[2 * member : 2 * member + 2, :]
        marks = spread(marks_ref[member]).astype(jnp.float32)
        sends[member, 2:3, :] = marks.T[0:1, :].astype(jnp.int32)

    def put(i):
        return pltpu.make_async_remote_copy(
            src_ref=sends.at[others[i]],
            dst_ref=got.at[me],
            send_sem=sent.at[i],
            recv_sem=received.at[i],
            device_id=place(others[i]),
            device_id_type=pl.DeviceIdType.MESH,
        )

    pl.semaphore_wait(barrier, members - 1)
    for i in range(members - 1):
        put(i).start()
    got[me] = sends[me]
    for i in range(members - 1):
        put(i).wait_send()
        put(i).wait_recv()
    got_ref[...] = got[...]


def ask(ids, marks, share, slots):
    members, each = ids.shape[0], ids.shape[1] * ids.shape[2]
    inside = pl.BlockSpec(memory_space=pltpu.VMEM)
    box = (members, 8, each)
    return pl.pallas_call(
        partial(ask_kernel, share=share, slots=slots),
        in_specs=[inside, inside],
        out_specs=[inside, inside],
        out_shape=[
            jax.ShapeDtypeStruct(box, jnp.int32),
            jax.ShapeDtypeStruct((members * each, 128), jnp.int32),
        ],
        scratch_shapes=[pltpu.VMEM(box, jnp.int32)] * 2
        + [pltpu.SemaphoreType.DMA((members - 1,))] * 2,
        compiler_params=pltpu.CompilerParams(
            collective_id=2, has_side_effects=True, vmem_limit_bytes=60 * 2**20
        ),
        cost_estimate=pl.CostEstimate(
            flops=20 * 10**9, bytes_accessed=40 * 10**6, transcendentals=0
        ),
        name="ask",
    )(ids, marks)


def gelu_parts(values):
    spread = jnp.exp(-0.5 * values * values)
    t = 1.0 / (1.0 + (0.3275911 * 0.5**0.5) * jnp.abs(values))
    series = 0.5 * 1.061405429
    for factor in (-1.453152027, 1.421413741, -0.284496736, 0.254829592):
        series = series * t + 0.5 * factor
    tail = series * t * spread
    upto = jnp.where(values < 0.0, tail, 1.0 - tail)
    return values * upto, upto + values * spread * 0.3989422804014327


def forward_kernel(
    codes_ref,
    final_ref,
    hidden_grad_ref,
    query_marks_ref,
    key_marks_ref,
    qkv_ref,
    out_weight_ref,
    up_ref,
    down_ref,
    first_gain_ref,
    first_shift_ref,
    qb_ref,
    vb_ref,
    out_bias_ref,
    gain_ref,
    shift_ref,
    up_bias_ref,
    down_bias_ref,
    normed_out,
    q_out,
    k_out,
    v_out,
    attended_out,
    columns_out,
    features_out,
    normed_two_out,
    hidden_out,
    pre_out,
    middle_grad_out,
    branch_out,
    attended_grad_out,
    out_bias_sum,
    gain_sum,
    shift_sum,
    up_bias_sum,
    codes,
    query_marks,
    key_marks,
    qkv_weight,
    out_weight,
    up_weight,
    down_weight,
    normed,
    queries,
    keys,
    values,
    attended,
    columns,
    final,
    hidden_grad,
    features_stage,
    normed_two_stage,
    hidden_stage,
    pre_stage,
    middle_grad_stage,
    branch_stage,
    attended_grad_stage,
    in_sem,
    once_sem,
    block_sem,
    stage_sem,
    *,
    step,
):
    tokens, features = codes.shape
    pairs = queries.shape[0]
    blocks = tokens // step
    loads = [
        pltpu.make_async_copy(source, target, in_sem.at[i])
        for i, (source, target) in enumerate(
            (
                (codes_ref, codes),
                (qkv_ref, qkv_weight),
                (query_marks_ref, query_marks),
                (key_marks_ref, key_marks),
                (out_weight_ref, out_weight),
                (up_ref, up_weight),
                (down_ref, down_weight),
            )
        )
    ]
    for copy in loads:
        copy.start()

    def block_copies(i):
        rows = pl.ds(pl.multiple_of(i * step, step), step)
        slot = lax.rem(i, 2)
        return [
            pltpu.make_async_copy(final_ref.at[rows], final.at[slot], block_sem.at[slot, 0]),
            pltpu.make_async_copy(
                hidden_grad_ref.at[rows], hidden_grad.at[slot], block_sem.at[slot, 1]
            ),
        ]

    for copy in block_copies(0):
        copy.start()
    for ref in (out_bias_sum, gain_sum, shift_sum, up_bias_sum):
        ref[...] = jnp.zeros_like(ref)

    for copy in loads[:2]:
        copy.wait()

    def enter_rows(i, _):
        rows = pl.ds(pl.multiple_of(i * step, step), step)
        unit, _ = normalize(codes[rows, :].astype(jnp.float32))
        low = (unit * row(first_gain_ref) + row(first_shift_ref)).astype(jnp.bfloat16)
        normed[rows, :] = low
        query_rows = nn(low, qkv_weight[:, 0:features]) + row(qb_ref)
        query_rows = query_rows.astype(jnp.bfloat16) * jnp.asarray(HEAD_DIM**-0.5, jnp.bfloat16)
        key_rows = nn(low, qkv_weight[:, features : 2 * features]).astype(jnp.bfloat16)
        value_rows = (nn(low, qkv_weight[:, 2 * features :]) + row(vb_ref)).astype(jnp.bfloat16)
        for pair in range(pairs):
            lanes = slice(pair * 128, (pair + 1) * 128)
            queries[pair, rows, :] = query_rows[:, lanes]
            keys[pair, rows, :] = key_rows[:, lanes]
            values[pair, rows, :] = value_rows[:, lanes]
        return 0

    lax.fori_loop(0, blocks, enter_rows, 0)
    onces = [
        pltpu.make_async_copy(source, target, once_sem.at[i])
        for i, (source, target) in enumerate(
            (
                (normed, normed_out),
                (queries, q_out),
                (keys, k_out),
                (values, v_out),
                (attended, attended_out),
                (columns, columns_out),
            )
        )
    ]
    for copy in onces[:4]:
        copy.start()

    for copy in loads[2:4]:
        copy.wait()
    lane = lax.broadcasted_iota(jnp.int32, (1, 128), 1)
    low_lanes = lane < 64
    local = lane % 64
    one = jnp.ones((), jnp.bfloat16)

    def attend_pair(pair, _):
        key_rows, value_rows, marks = keys[pair], values[pair], key_marks[...]
        keys_of = [jnp.where(low_lanes, key_rows, marks), jnp.where(low_lanes, marks, key_rows)]
        values_of = [jnp.where(low_lanes, value_rows, one), jnp.where(low_lanes, one, value_rows)]
        parts = [(first, head) for first in range(0, tokens, step) for head in range(2)]

        def scores_of(part):
            first, head = part
            rows = slice(first, first + step)
            rows_q, rows_m = queries[pair, rows, :], query_marks[rows, :]
            if head == 0:
                return nt(jnp.where(low_lanes, rows_q, rows_m), keys_of[0])
            return nt(jnp.where(low_lanes, rows_m, rows_q), keys_of[1])

        waiting = [scores_of(part) for part in parts[:2]]
        outs, logs = [None, None], [None, None]
        for i, (first, head) in enumerate(parts):
            scores = waiting.pop(0)
            if i + 2 < len(parts):
                waiting.append(scores_of(parts[i + 2]))
            top = jnp.max(scores, axis=1, keepdims=True)
            weights = jnp.exp(scores - top).astype(jnp.bfloat16)
            sums = nn(weights, values_of[head])
            outs[head] = sums / pltpu.roll(sums, 64, 1)
            logs[head] = top + jnp.log(sums)
            if head == 1:
                rows = slice(first, first + step)
                attended[pair, rows, :] = jnp.where(low_lanes, outs[0], outs[1]).astype(jnp.bfloat16)
                minus = -jnp.where(low_lanes, logs[1], logs[0])
                part1 = minus.astype(jnp.bfloat16).astype(jnp.float32)
                part2 = (minus - part1).astype(jnp.bfloat16).astype(jnp.float32)
                part3 = minus - part1 - part2
                column = jnp.where(local == 5, part3, query_marks[rows, :].astype(jnp.float32))
                column = jnp.where(local == 4, part2, column)
                column = jnp.where(local == 3, part1, column)
                columns[pair, rows, :] = column.astype(jnp.bfloat16)
        return 0

    lax.fori_loop(0, pairs, attend_pair, 0)
    for copy in onces[4:]:
        copy.start()

    for copy in loads[4:]:
        copy.wait()

    def stage_copies(i):
        rows = pl.ds(pl.multiple_of(i * step, step), step)
        slot = lax.rem(i, 2)
        moves = (
            (features_stage, features_out.at[rows]),
            (normed_two_stage, normed_two_out.at[rows]),
            (hidden_stage, hidden_out.at[:, rows]),
            (pre_stage, pre_out.at[rows]),
            (middle_grad_stage, middle_grad_out.at[rows]),
            (branch_stage, branch_out.at[rows]),
            (attended_grad_stage, attended_grad_out.at[:, rows]),
        )
        return [
            pltpu.make_async_copy(source.at[slot], target, stage_sem.at[slot, k])
            for k, (source, target) in enumerate(moves)
        ]

    def middle_rows(i, _):
        rows = pl.ds(pl.multiple_of(i * step, step), step)
        slot = lax.rem(i, 2)
        for copy in block_copies(i):
            copy.wait()

        @pl.when(i + 1 < blocks)
        def _():
            for copy in block_copies(i + 1):
                copy.start()

        @pl.when(i >= 2)
        def _():
            for copy in stage_copies(i - 2):
                copy.wait()

        attended_rows = jnp.concatenate([attended[p, rows, :] for p in range(pairs)], axis=1)
        branch = nn(attended_rows, out_weight[...]) + row(out_bias_ref)
        middle = codes[rows, :].astype(jnp.float32) + branch
        unit, scale = normalize(middle)
        low = (unit * row(gain_ref) + row(shift_ref)).astype(jnp.bfloat16)
        normed_two_stage[slot] = low
        total = middle + row(down_bias_ref)
        grad = jnp.zeros_like(middle)
        for first in range(0, up_weight.shape[1], features):
            block = slice(first, first + features)
            weight = up_weight[:, block]
            hidden_pre = nn(low, weight) + up_bias_ref[:, block].astype(jnp.float32)
            act, slope = gelu_parts(hidden_pre)
            hidden = act.astype(jnp.bfloat16)
            hidden_stage[slot, block, :] = hidden.T
            pre = hidden_grad[slot, :, block].astype(jnp.float32) * slope
            pre = pre.astype(jnp.bfloat16)
            pre_stage[slot, :, block] = pre
            up_bias_sum[:, block] += jnp.sum(pre.astype(jnp.float32), axis=0, keepdims=True)
            total = total + nn(hidden, down_weight[block, :])
            grad = grad + nt(pre, weight)
        features_stage[slot] = total.astype(jnp.bfloat16)
        add_rows(gain_sum, grad * unit)
        add_rows(shift_sum, grad)
        middle_grad = final[slot] + norm_back(grad, row(gain_ref), unit, scale)
        middle_grad_stage[slot] = middle_grad
        branch_grad = middle_grad.astype(jnp.bfloat16)
        branch_stage[slot] = branch_grad
        add_rows(out_bias_sum, branch_grad.astype(jnp.float32))
        attended_grad = nt(branch_grad, out_weight[...]).astype(jnp.bfloat16)
        for pair in range(pairs):
            attended_grad_stage[slot, pair] = attended_grad[:, pair * 128 : (pair + 1) * 128]
        for copy in stage_copies(i):
            copy.start()
        return 0

    lax.fori_loop(0, blocks, middle_rows, 0)
    for copy in onces:
        copy.wait()
    for i in (blocks - 2, blocks - 1):
        for copy in stage_copies(i):
            copy.wait()


def forward(inputs, vectors, step=256):
    codes, qkv_weight, up_weight = inputs[0], inputs[5], inputs[7]
    tokens, features = codes.shape
    wide = up_weight.shape[1]
    pairs = features // 128
    anywhere = pl.BlockSpec(memory_space=pl.ANY)
    inside = pl.BlockSpec(memory_space=pltpu.VMEM)
    dma = pltpu.SemaphoreType.DMA
    low, full = jnp.bfloat16, jnp.float32
    paired = (pairs, tokens, 128)
    shapes = [
        ((tokens, features), low),
        (paired, low),
        (paired, low),
        (paired, low),
        (paired, low),
        (paired, low),
        ((tokens, features), low),
        ((tokens, features), low),
        ((wide, tokens), low),
        ((tokens, wide), low),
        ((tokens, features), full),
        ((tokens, features), low),
        (paired, low),
    ]
    sums = [(1, features)] * 3 + [(1, wide)]
    return pl.pallas_call(
        partial(forward_kernel, step=step),
        in_specs=[anywhere] * 9 + [inside] * 9,
        out_specs=[anywhere] * len(shapes) + [inside] * 4,
        out_shape=[pltpu.HBM(shape, dtype) for shape, dtype in shapes]
        + [jax.ShapeDtypeStruct(shape, full) for shape in sums],
        scratch_shapes=[
            pltpu.VMEM((tokens, features), low),
            pltpu.VMEM((tokens, 128), low),
            pltpu.VMEM((tokens, 128), low),
            pltpu.VMEM(qkv_weight.shape, low),
            pltpu.VMEM((features, features), low),
            pltpu.VMEM((features, wide), low),
            pltpu.VMEM((wide, features), low),
            pltpu.VMEM((tokens, features), low),
        ]
        + [pltpu.VMEM(paired, low)] * 5
        + [
            pltpu.VMEM((2, step, features), full),
            pltpu.VMEM((2, step, wide), low),
            pltpu.VMEM((2, step, features), low),
            pltpu.VMEM((2, step, features), low),
            pltpu.VMEM((2, wide, step), low),
            pltpu.VMEM((2, step, wide), low),
            pltpu.VMEM((2, step, features), full),
            pltpu.VMEM((2, step, features), low),
            pltpu.VMEM((2, pairs, step, 128), low),
            dma((7,)),
            dma((6,)),
            dma((2, 2)),
            dma((2, 7)),
        ],
        compiler_params=pltpu.CompilerParams(vmem_limit_bytes=60 * 2**20),
        cost_estimate=pl.CostEstimate(
            flops=2 * tokens * features * (5 * features + 3 * wide) + 16 * tokens**2 * features,
            bytes_accessed=4 * features * wide + 6 * tokens * wide + 30 * tokens * features,
            transcendentals=2 * tokens * wide + 2 * tokens**2 * pairs,
        ),
        name="forward",
    )(*inputs, *vectors)


def fetch_kernel(
    fetched_ref,
    slot_ref,
    cotangent_ref,
    moved_ref,
    taps_ref,
    down_ref,
    codes_out,
    final_out,
    low_out,
    behind_out,
    hidden_out,
    pixel_bias_sum,
    down_bias_sum,
    cotangent,
    got,
    sends,
    shifted,
    total,
    other,
    low,
    taken,
    weight,
    down,
    hidden,
    hop_sent,
    hop_got,
    code_sent,
    code_got,
    own_sem,
    weight_sem,
    taken_sem,
    down_sem,
    hidden_sem,
    out_sem,
    *,
    tiling,
):
    gr, ty, tx = lax.axis_index("gr"), lax.axis_index("ty"), lax.axis_index("tx")
    across = lax.axis_size("tx")
    members = lax.axis_size("ty") * across
    me = ty * across + tx
    others = [lax.rem(me + step, members) for step in range(1, members)]
    tokens, features = cotangent_ref.shape
    each = tokens // members
    wide = tiling[1] * tiling[3]

    def place(member):
        return (gr, member // across, lax.rem(member, across))

    barrier = pltpu.get_barrier_semaphore()
    for member in others:
        pl.semaphore_signal(
            barrier, inc=1, device_id=place(member), device_id_type=pl.DeviceIdType.MESH
        )
    pl.semaphore_wait(barrier, members - 1)

    def hop_put(i):
        return pltpu.make_async_remote_copy(
            src_ref=fetched_ref.at[others[i]],
            dst_ref=got.at[me],
            send_sem=hop_sent.at[i],
            recv_sem=hop_got.at[i],
            device_id=place(others[i]),
            device_id_type=pl.DeviceIdType.MESH,
        )

    def code_put(i):
        return pltpu.make_async_remote_copy(
            src_ref=sends.at[others[i]],
            dst_ref=codes_out.at[me],
            send_sem=code_sent.at[i],
            recv_sem=code_got.at[i],
            device_id=place(others[i]),
            device_id_type=pl.DeviceIdType.MESH,
        )

    own_rows = pltpu.make_async_copy(fetched_ref.at[me], got.at[me], own_sem.at[0])
    own_codes = pltpu.make_async_copy(sends.at[me], codes_out.at[me], own_sem.at[1])
    for i in range(members - 1):
        hop_put(i).start()
    own_rows.start()

    def weight_copy(tap):
        slot = lax.rem(tap, 2)
        return pltpu.make_async_copy(taps_ref.at[tap], weight.at[slot], weight_sem.at[slot])

    def taken_copy(tap):
        slot = lax.rem(tap, 2)
        columns = pl.ds(pl.multiple_of(tap * features, 128), features)
        return pltpu.make_async_copy(taken.at[slot], behind_out.at[:, columns], taken_sem.at[slot])

    def down_copy(j):
        slot = lax.rem(j, 2)
        rows = pl.ds(pl.multiple_of(j * features, 128), features)
        return pltpu.make_async_copy(down_ref.at[rows], down.at[slot], down_sem.at[slot])

    def hidden_copy(j):
        slot = lax.rem(j, 2)
        columns = pl.ds(pl.multiple_of(j * features, 128), features)
        return pltpu.make_async_copy(hidden.at[slot], hidden_out.at[:, columns], hidden_sem.at[slot])

    arriving = pltpu.make_async_copy(cotangent_ref, cotangent, own_sem.at[2])
    arriving.start()
    weight_copy(0).start()
    down_copy(0).start()
    arriving.wait()
    other[...] = cotangent[...].astype(jnp.float32)
    pixel_bias_sum[...] = jnp.sum(other[...], axis=0, keepdims=True)
    for tiled, plain in groups(*tiling):
        total[plain : plain + tiling[3], :] = other[tiled : tiled + tiling[3], :]
    rows_plain = total[...]
    for j in range(3):
        moved_rows = rows_plain if j == 1 else pltpu.roll(rows_plain, (1 - j) % tokens, 0)
        shifted[j, 0:wide, :] = jnp.zeros((wide, features), jnp.bfloat16)
        shifted[j, wide + tokens :, :] = jnp.zeros((wide, features), jnp.bfloat16)
        shifted[j, wide : wide + tokens, :] = moved_rows.astype(jnp.bfloat16)
    total[...] = jnp.zeros_like(total)

    def one_tap(tap, _):
        slot = lax.rem(tap, 2)
        weight_copy(tap).wait()
        pl.when(tap < 8)(lambda: weight_copy(tap + 1).start())
        pl.when(tap >= 2)(lambda: taken_copy(tap - 2).wait())
        below, right = 2 - tap // 3, 2 - lax.rem(tap, 3)
        step = tokens // 4
        for i in range(4):
            rows = slice(i * step, (i + 1) * step)
            first = pl.multiple_of(below * wide + i * step, wide)
            here = moved_ref[1, wide + i * step : wide + (i + 1) * step, :]
            same = moved_ref[right, pl.ds(first, step), :] == here
            mask = jnp.where(same, 1.0, 0.0).astype(jnp.bfloat16)
            mask = jnp.concatenate([mask] * (features // 128), axis=1)
            piece = shifted[right, pl.ds(first, step), :] * mask
            taken[slot, rows, :] = piece
            total[rows, :] += nt(piece, weight[slot])
        taken_copy(tap).start()
        return 0

    lax.fori_loop(0, 9, one_tap, 0)
    for tiled, plain in groups(*tiling):
        other[tiled : tiled + tiling[3], :] = total[plain : plain + tiling[3], :]
    low[...] = other[...].astype(jnp.bfloat16)
    results = [
        pltpu.make_async_copy(other, final_out, out_sem.at[0]),
        pltpu.make_async_copy(low, low_out, out_sem.at[1]),
    ]
    for result in results:
        result.start()
    down_bias_sum[...] = jnp.sum(low[...].astype(jnp.float32), axis=0, keepdims=True)

    own_rows.wait()
    for i in range(members - 1):
        hop_put(i).wait_recv()
    arrived = got[...].reshape(got.shape[0] * got.shape[1], features)
    lane = lax.broadcasted_iota(jnp.int32, (each, 128), 1)
    for i, member in enumerate(others + [me]):
        slots = slot_ref[pl.ds(pl.multiple_of(member * each, 128), each), :]
        hot = [
            jnp.where(slots == lane + first, 1.0, 0.0).astype(jnp.bfloat16)
            for first in range(0, arrived.shape[0], 128)
        ]
        rows = nn(jnp.concatenate(hot, axis=1), arrived)
        sends[member] = rows.astype(jnp.bfloat16)
        if i < members - 1:
            code_put(i).start()
    own_codes.start()

    def one_block(j, _):
        slot = lax.rem(j, 2)
        down_copy(j).wait()
        pl.when(j < 3)(lambda: down_copy(j + 1).start())
        pl.when(j >= 2)(lambda: hidden_copy(j - 2).wait())
        hidden[slot] = nt(low[...], down[slot]).astype(jnp.bfloat16)
        hidden_copy(j).start()
        return 0

    lax.fori_loop(0, 4, one_block, 0)
    for copy in (taken_copy(7), taken_copy(8), hidden_copy(2), hidden_copy(3), own_codes, *results):
        copy.wait()
    for i in range(members - 1):
        hop_put(i).wait_send()
        code_put(i).wait_send()
        code_put(i).wait_recv()


def fetch(fetched, slots, cotangent, moved, taps, down_weight, tiling):
    tokens, features = cotangent.shape
    members = tiling[0] * tiling[1]
    blocks = down_weight.shape[0] // features
    anywhere = pl.BlockSpec(memory_space=pl.ANY)
    inside = pl.BlockSpec(memory_space=pltpu.VMEM)
    dma = pltpu.SemaphoreType.DMA
    low, wide = jnp.bfloat16, jnp.float32
    padded = tokens + 2 * tiling[1] * tiling[3]
    return pl.pallas_call(
        partial(fetch_kernel, tiling=tiling),
        in_specs=[anywhere, inside, anywhere, inside, anywhere, anywhere],
        out_specs=[anywhere] * 5 + [inside] * 2,
        out_shape=[
            jax.ShapeDtypeStruct((members, tokens // members, features), low),
            jax.ShapeDtypeStruct((tokens, features), wide),
            jax.ShapeDtypeStruct((tokens, features), low),
            jax.ShapeDtypeStruct((tokens, 9 * features), low),
            jax.ShapeDtypeStruct((tokens, blocks * features), low),
            jax.ShapeDtypeStruct((1, features), wide),
            jax.ShapeDtypeStruct((1, features), wide),
        ],
        scratch_shapes=[
            pltpu.VMEM((tokens, features), low),
            pltpu.VMEM(fetched.shape, low),
            pltpu.VMEM((members, tokens // members, features), low),
            pltpu.VMEM((3, padded, features), low),
            pltpu.VMEM((tokens, features), wide),
            pltpu.VMEM((tokens, features), wide),
            pltpu.VMEM((tokens, features), low),
            pltpu.VMEM((2, tokens, features), low),
            pltpu.VMEM((2, features, features), low),
            pltpu.VMEM((2, features, features), low),
            pltpu.VMEM((2, tokens, features), low),
        ]
        + [dma((members - 1,))] * 4
        + [dma((3,))]
        + [dma((2,))] * 5,
        compiler_params=pltpu.CompilerParams(
            collective_id=3, has_side_effects=True, vmem_limit_bytes=60 * 2**20
        ),
        cost_estimate=pl.CostEstimate(
            flops=26 * tokens * features * features,
            bytes_accessed=40 * tokens * features,
            transcendentals=0,
        ),
        name="fetch",
    )(fetched, slots, cotangent, moved, taps, down_weight)


def finish_kernel(*refs, blocks, homes, lead, slots, got_slots, tiling):
    (
        q_ref,
        k_ref,
        v_ref,
        col_ref,
        ka_ref,
        o_ref,
        g_ref,
        codes_ref,
        middle_ref,
        features_ref,
        behind_ref,
        normed_two_ref,
        pre_ref,
        hidden_ref,
        lower_ref,
        branch_ref,
        normed_ref,
        weight_ref,
        recon_ref,
        gain_ref,
        out_bias_sum,
        second_gain_sum,
        second_shift_sum,
        up_bias_sum,
        down_bias_sum,
        pixel_bias_sum,
    ) = refs[:26]
    outs = refs[26:31]
    vector_out, recon_out, share_out = refs[31:34]
    refs = refs[34:]
    (parts, got0, got1, got2, got3, got4, whole) = refs[:7]
    (operands, turned, heads, marks, sums, sums_got, middle, share, k_sum, v_sum, dqkv) = refs[7:18]
    (s0, r0, s1, r1, s2, r2, s3, r3, s4, r4, s5, r5, s6, r6) = refs[18:32]
    (out_sem, operand_sem, turned_sem, head_sem, once_sem, free, own_sem) = refs[32:39]
    (recon_sent, recon_got, share_sent, share_got, sums_sent, sums_recv) = refs[39:45]
    count = (blocks + 1) // 2
    tokens, features = normed_ref.shape
    each = tokens // (tiling[0] * tiling[1])
    gr, ty, tx = lax.axis_index("gr"), lax.axis_index("ty"), lax.axis_index("tx")
    x, core, half, par = gr // 2, gr % 2, tx // 2, tx % 2
    across = lax.axis_size("tx")
    members = lax.axis_size("ty") * across
    me = ty * across + tx
    mate = (2 * x + 1 - core, ty, tx)
    over_x = (2 * (1 - x) + core, ty, tx)
    over_y = (gr, 1 - ty, tx)
    near = (gr, ty, half * 2 + (1 - par))
    away = (gr, ty, (1 - half) * 2 + par)
    others = [lax.rem(me + step, members) for step in range(1, members)]

    def place(member):
        return (gr, member // across, lax.rem(member, across))

    barrier = pltpu.get_barrier_semaphore()
    greeted = [mate, over_x] + [place(member) for member in others]
    for device in greeted:
        pl.semaphore_signal(barrier, inc=1, device_id=device, device_id_type=pl.DeviceIdType.MESH)
    pl.semaphore_wait(barrier, len(greeted))
    width = features // 2
    own_columns = pl.ds(pl.multiple_of(core * width, 128), width)

    def put(source, target, sent, received, device):
        return pltpu.make_async_remote_copy(
            src_ref=source,
            dst_ref=target,
            send_sem=sent,
            recv_sem=received,
            device_id=device,
            device_id_type=pl.DeviceIdType.MESH,
        )

    def recon_put(i):
        member = others[i]
        return put(
            recon_ref.at[member], recon_out.at[me], recon_sent.at[i], recon_got.at[i], place(member)
        )

    def share_put(i, member=None):
        member = others[i] if member is None else member
        rows = pl.ds(pl.multiple_of(member * each, 128), each)
        return put(share.at[rows], share_out.at[me], share_sent.at[i], share_got.at[i], place(member))

    def columns(ref, index):
        return ref.at[:, pl.ds(pl.multiple_of(index * features, 128), features)]

    def operand(i, source):
        return pltpu.make_async_copy(source, operands.at[i], operand_sem.at[i])

    def load(sources):
        for i, source in enumerate(sources):
            operand(i, source).start()

    def load_operands(c):
        @pl.when(c < 4)
        def _():
            load([features_ref, columns(behind_ref, 2 * c), features_ref, columns(behind_ref, 2 * c + 1)])

        @pl.when((c == 4) | (c == 5))
        def _():
            load([lower_ref] * 4)
            for b in range(2):
                turned_copy(b, 2 * (c - 4) + b).start()

        @pl.when(c == 6)
        def _():
            load([normed_ref, gradient(0), normed_ref, gradient(1)])

        @pl.when(c == 7)
        def _():
            load([normed_ref, gradient(2), features_ref, columns(behind_ref, 8)])

        @pl.when(c == 8)
        def _():
            for pair in range(o_ref.shape[0]):
                target = operands.at[0, :, pl.ds(pair * 128, 128)]
                pltpu.make_async_copy(o_ref.at[pair], target, operand_sem.at[0]).start()
            for i, source in ((1, branch_ref), (2, normed_two_ref), (3, columns(pre_ref, 0))):
                operand(i, source).start()

        @pl.when(c == 9)
        def _():
            load([normed_two_ref, columns(pre_ref, 1), normed_two_ref, columns(pre_ref, 2)])

        @pl.when(c == 10)
        def _():
            load([normed_two_ref, columns(pre_ref, 3), lower_ref, lower_ref])

    def gradient(i):
        return dqkv.at[i, pl.ds(0, tokens)]

    def turned_copy(b, index):
        return pltpu.make_async_copy(hidden_ref.at[:, index], turned.at[b], turned_sem.at[b])

    def wait_operands():
        for i in range(4):
            operand(i, normed_ref).wait()

    def level0(c, b):
        slot = lax.rem(c, slots)
        return put(
            parts.at[slot, b, 1 - core], got0.at[lax.rem(c, got_slots), b], s0.at[c, b], r0.at[c, b], mate
        )

    def both_x(c):
        return (c == 2) | (c == 7)

    def only_y(c):
        return (c < count - 1) & (c != 2) & (c != 7)

    def level1x(c, b=0):
        slot = lax.rem(c, slots)
        return put(
            parts.at[slot, b, core, :, :, :, 1 - x], got1.at[c, b], s1.at[c, b], r1.at[c, b], over_x
        )

    def level1y(c):
        slot = lax.rem(c, slots)
        return put(parts.at[slot, 1, core, 1 - ty], got1.at[c, 1], s1.at[c, 1], r1.at[c, 1], over_y)

    def level2y(c, b=0):
        return put(got1.at[c, b, 1 - ty], got2.at[c, b], s2.at[c, b], r2.at[c, b], over_y)

    def level2x(c):
        return put(got1.at[c, 1, :, :, 1 - x], got2.at[c, 1], s2.at[c, 1], r2.at[c, 1], over_x)

    def level3(c):
        return put(got2.at[c, :, :, 1 - par], got3.at[c], s3.at[c], r3.at[c], near)

    def level4(c):
        return put(got3.at[c, :, 1 - half], got4.at[c], s4.at[c], r4.at[c], away)

    def level5(c):
        where = whole.at[pl.ds(2 * c, 2), x, :, own_columns]
        return put(where, where, s5.at[c], r5.at[c], over_x)

    def level6(c):
        where = whole.at[pl.ds(2 * c, 2), :, :, own_columns]
        return put(where, where, s6.at[c], r6.at[c], mate)

    def stage1(c):
        slot, got_slot = lax.rem(c, slots), lax.rem(c, got_slots)
        for b in range(2):

            @pl.when((b == 0) | (c < count - 1))
            def _():
                level0(c, b).wait_recv()

                def add(i, _):
                    y, h, p = i // 4, lax.rem(i // 2, 2), lax.rem(i, 2)
                    sum_of = parts[slot, b, core, y, h, p] + got0[got_slot, b, y, h, p]
                    parts[slot, b, core, y, h, p] = sum_of
                    return 0

                lax.fori_loop(0, 8, add, 0)

        @pl.when(c < count - got_slots)
        def _():
            pl.semaphore_signal(free, inc=1, device_id=mate, device_id_type=pl.DeviceIdType.MESH)

        level1x(c).start()
        pl.when(only_y(c))(lambda: level1y(c).start())
        pl.when(both_x(c))(lambda: level1x(c, 1).start())

    def stage2(c):
        slot = lax.rem(c, slots)
        level1x(c).wait_recv()
        got1[c, 0] = got1[c, 0] + parts[slot, 0, core, :, :, :, x]
        level2y(c).start()

        @pl.when(only_y(c))
        def _():
            level1y(c).wait_recv()
            got1[c, 1] = got1[c, 1] + parts[slot, 1, core, ty]
            level2x(c).start()
            level1y(c).wait_send()

        @pl.when(both_x(c))
        def _():
            level1x(c, 1).wait_recv()
            got1[c, 1] = got1[c, 1] + parts[slot, 1, core, :, :, :, x]
            level2y(c, 1).start()
            level1x(c, 1).wait_send()

        level1x(c).wait_send()

    def stage3(c):
        level2y(c).wait_recv()
        got2[c, 0] = got2[c, 0] + got1[c, 0, ty]

        @pl.when(only_y(c))
        def _():
            level2x(c).wait_recv()
            got2[c, 1] = got2[c, 1] + got1[c, 1, :, :, x]

        @pl.when(both_x(c))
        def _():
            level2y(c, 1).wait_recv()
            got2[c, 1] = got2[c, 1] + got1[c, 1, ty]

        @pl.when(c == count - 1)
        def _():
            got2[c, 1] = jnp.zeros(got2.shape[2:], jnp.bfloat16)

        level3(c).start()

    def stage4(c):
        level3(c).wait_recv()
        got3[c] = got3[c] + got2[c, :, :, par]
        level4(c).start()

    def stage5(c):
        level4(c).wait_recv()
        whole[pl.ds(2 * c, 2), x, :, own_columns] = got4[c] + got3[c, :, half]
        level5(c).start()

    def stage6(c):
        level5(c).wait_recv()
        level6(c).start()

    def weight_block(slot, b, of_hidden):
        for y in range(2):
            if of_hidden:
                left = turned[b, y * 4 : (y + 1) * 4].reshape(width, tokens)
                block = nn(left, operands[2 * b + 1])
            else:
                left = operands[2 * b, :, y * width : (y + 1) * width]
                block = tn(left, operands[2 * b + 1])
            block = block.astype(jnp.bfloat16)
            for h in range(2):
                piece = block[:, h * width : (h + 1) * width]
                parts[slot, b, h, y] = piece.reshape(parts.shape[4:])

    def make_blocks(c):
        slot = lax.rem(c, slots)

        @pl.when(c >= slots)
        def _():
            for b in range(2):
                level0(c - slots, b).wait_send()

        @pl.when(c >= got_slots)
        def _():
            pl.semaphore_wait(free, 1)

        wait_operands()
        of_hidden = (c == 4) | (c == 5)

        @pl.when(of_hidden)
        def _():
            for b in range(2):
                turned_copy(b, 0).wait()
                weight_block(slot, b, True)
                level0(c, b).start()

        @pl.when(jnp.logical_not(of_hidden))
        def _():
            weight_block(slot, 0, False)
            level0(c, 0).start()

        @pl.when(jnp.logical_not(of_hidden) & (c < count - 1))
        def _():
            weight_block(slot, 1, False)
            level0(c, 1).start()

    lane = lax.broadcasted_iota(jnp.int32, (1, 128), 1)
    low = lane < 64
    local = lane % 64

    def head_copies(pair):
        slot = lax.rem(pair, 2)
        return [
            pltpu.make_async_copy(ref.at[pair], heads.at[slot, i], head_sem.at[slot, i])
            for i, ref in enumerate((q_ref, k_ref, v_ref, col_ref, o_ref, g_ref))
        ]

    pairs = features // 128
    step = tokens // 2

    def attend_part(u, _):
        pair, part = u // 2, lax.rem(u, 2)
        slot = lax.rem(pair, 2)

        @pl.when(part == 0)
        def _():
            for copy in head_copies(pair):
                copy.wait()

            @pl.when(pair < pairs - 1)
            def _():
                for copy in head_copies(pair + 1):
                    copy.start()

            k_sum[...] = jnp.zeros_like(k_sum)
            v_sum[...] = jnp.zeros_like(v_sum)

        rows = pl.ds(pl.multiple_of(part * step, step), step)
        zero, one = jnp.zeros((), jnp.bfloat16), jnp.ones((), jnp.bfloat16)
        queries, columns_ = heads[slot, 0, rows, :], heads[slot, 3, rows, :]
        key_rows, values = heads[slot, 1], heads[slot, 2]
        out, grad = heads[slot, 4, rows, :], heads[slot, 5, rows, :]
        key_columns = jnp.where((local >= 3) & (local < 6), one, marks[...])
        value_columns = jnp.where(local < 2, one, zero)
        keys_across = key_rows.T
        both = grad.astype(jnp.float32) * out.astype(jnp.float32)
        of_low = -jnp.sum(jnp.where(low, both, 0.0), axis=1, keepdims=True)
        of_high = -jnp.sum(jnp.where(low, 0.0, both), axis=1, keepdims=True)
        inner = jnp.where(low, of_high, of_low)
        first = inner.astype(jnp.bfloat16).astype(jnp.float32)
        grad_columns = jnp.where(
            local == 0, first, jnp.where(local == 1, inner - first, 0.0)
        ).astype(jnp.bfloat16)
        query_parts, key_parts, value_parts = [], [], []
        for head in range(2):
            own = low if head == 0 else ~low
            scores = nt(jnp.where(own, key_rows, key_columns), jnp.where(own, queries, columns_))
            weights = jnp.exp(scores)
            change = nt(jnp.where(own, values, value_columns), jnp.where(own, grad, grad_columns))
            score_grad = (weights * change).astype(jnp.bfloat16)
            value_parts.append(nn(weights.astype(jnp.bfloat16), grad))
            key_parts.append(nn(score_grad, queries))
            query_parts.append(nn(keys_across, score_grad))
        k_sum[...] += jnp.where(low, key_parts[0], key_parts[1])
        v_sum[...] += jnp.where(low, value_parts[0], value_parts[1])
        upper = lax.broadcasted_iota(jnp.int32, (128, 1), 0) < 64
        query_grad = jnp.where(upper, query_parts[0], query_parts[1]).T
        lanes = pl.ds(pl.multiple_of(pair * 128, 128), 128)
        dqkv[0, rows, lanes] = (query_grad * HEAD_DIM**-0.5).astype(jnp.bfloat16)

        @pl.when(part == 1)
        def _():
            dqkv[1, 0:tokens, lanes] = k_sum[...].astype(jnp.bfloat16)
            dqkv[2, 0:tokens, lanes] = v_sum[...].astype(jnp.bfloat16)

        return 0

    def back_copies():
        copies = [
            pltpu.make_async_copy(
                weight_ref.at[:, pl.ds(features * i, features)],
                operands.at[i, pl.ds(0, features)],
                operand_sem.at[i],
            )
            for i in range(3)
        ]
        return copies + [operand(3, codes_ref)]

    def back():
        for copy in back_copies():
            copy.wait()
        middle_copy().wait()

        def rows_back(i, _):
            rows = pl.ds(pl.multiple_of(i * 256, 256), 256)
            grad = nt(dqkv[0, rows, :], operands[0, 0:features, :])
            grad = grad + nt(dqkv[1, rows, :], operands[1, 0:features, :])
            grad = grad + nt(dqkv[2, rows, :], operands[2, 0:features, :])
            start = operands[3, rows, :].astype(jnp.float32)
            unit, scale = normalize(start)
            for at, addend in enumerate(
                (dqkv[0, rows, :].astype(jnp.float32), dqkv[2, rows, :].astype(jnp.float32), grad * unit, grad)
            ):
                sums[0, at : at + 1, :] += jnp.sum(addend, axis=0, keepdims=True)
            start_grad = middle[rows, :] + norm_back(grad, row(gain_ref), unit, scale)
            share[rows, :] = (start_grad - 2.0 * commit_weight * start).astype(jnp.bfloat16)
            for member in range(members):

                @pl.when((i == member * each // 256) & (member != me))
                def _():
                    share_put(lax.rem(member - me - 1 + members, members), member).start()

            return 0

        lax.fori_loop(0, tokens // 256, rows_back, 0)
        own_share().start()
        sums_put(0).start()

    partners = (mate, over_x, over_y, near, away)

    def sums_put(i):
        return put(sums.at[i], sums_got.at[i], sums_sent.at[i], sums_recv.at[i], partners[i])

    def sums_step(i):
        sums_put(i).wait_recv()
        sums[i + 1] = sums[i] + sums_got[i]
        if i + 1 < len(partners):
            sums_put(i + 1).start()

    def own_share():
        rows = pl.ds(pl.multiple_of(me * each, 128), each)
        return pltpu.make_async_copy(share.at[rows], share_out.at[me], own_sem.at[0])

    def own_recon():
        return pltpu.make_async_copy(recon_ref.at[me], recon_out.at[me], own_sem.at[1])

    def middle_copy():
        return pltpu.make_async_copy(middle_ref, middle, once_sem.at[0])

    def marks_copy():
        return pltpu.make_async_copy(ka_ref, marks, once_sem.at[1])

    load_operands(0)
    marks_copy().start()
    middle_copy().start()
    for copy in head_copies(0):
        copy.start()
    for i in range(members - 1):
        recon_put(i).start()
    own_recon().start()
    sums[0] = jnp.zeros(sums.shape[1:], jnp.float32)
    for at, ref in ((4, out_bias_sum), (5, second_gain_sum), (6, second_shift_sum)):
        sums[0, at : at + 1, :] = ref[...]
    for k in range(4):
        sums[0, 7 + k : 8 + k, :] = up_bias_sum[:, k * features : (k + 1) * features]
    sums[0, 11:12, :] = down_bias_sum[...]
    sums[0, 12:13, :] = pixel_bias_sum[...]
    marks_copy().wait()
    stages = (stage1, stage2, stage3, stage4, stage5, stage6)
    last = 6

    def turn(t, _):
        @pl.when(t == last)
        def _():
            back()
            load_operands(last)

        @pl.when(t < count)
        def _():
            make_blocks(t)

        @pl.when((t < count - 1) & (t != last - 1))
        def _():
            load_operands(t + 1)

        @pl.when(t == last - 1)
        def _():
            for copy in back_copies():
                copy.start()

        def upto(s):
            return jnp.clip(2 * (s - 1) + jnp.maximum(s - last + 2, 0), 0, 2 * pairs)

        lax.fori_loop(upto(t), upto(t + 1), attend_part, 0)
        for i in range(len(partners)):
            pl.when(t == last + 1 + i)(partial(sums_step, i))
        for stage, behind in zip(stages, lead):
            c = t - behind
            pl.when((c >= 0) & (c < count))(partial(stage, c))
        return 0

    lax.fori_loop(0, count + lead[-1], turn, 0)

    copies = []
    for block, (home, prefix, column) in enumerate(homes):
        out = outs[home] if prefix is None else outs[home].at[prefix]
        target = out.at[:, :, pl.ds(column, features)]
        if block % 2 == 0:
            level6(block // 2).wait_recv()
        copies.append(pltpu.make_async_copy(whole.at[block], target, out_sem.at[block]))
        copies[-1].start()

    def finish(c, _):
        for level in (level2y, level3, level4, level5, level6):
            level(c).wait_send()
        pl.when(only_y(c))(lambda: level2x(c).wait_send())
        pl.when(both_x(c))(lambda: level2y(c, 1).wait_send())
        return 0

    lax.fori_loop(0, count, finish, 0)
    for c in range(count - slots, count):
        for b in range(2 if c < count - 1 else 1):
            level0(c, b).wait_send()
    for i in range(len(partners)):
        sums_put(i).wait_send()
    own = pltpu.roll(sums[len(partners)], lax.rem((members - me) * (features // members), features), 1)
    vector_out[0:16, :] = own
    wide_row = sums[len(partners), pl.ds(7 + me // 2, 1), :]
    vector_out[16:24, :] = jnp.broadcast_to(
        jnp.where(lax.rem(me, 2) == 0, wide_row, pltpu.roll(wide_row, features // 2, 1)), (8, features)
    )
    for i in range(members - 1):
        recon_put(i).wait_recv()
        share_put(i).wait_recv()
        recon_put(i).wait_send()
        share_put(i).wait_send()
    own_recon().wait()
    own_share().wait()
    for copy in copies:
        copy.wait()


def finish(inputs, tiling):
    tokens, features = inputs[7].shape
    members = tiling[0] * tiling[1]
    blocks, slots, got_slots = 21, 3, 3
    count = (blocks + 1) // 2
    rows, width = features // members // 2, features // 2
    lead = (0, 2, 4, 6, 8, 10)
    homes = [(0, k, 0) for k in range(8)] + [(2, k, 0) for k in range(4)]
    homes += [(4, None, features * k) for k in range(3)] + [(0, 8, 0), (3, None, 0)]
    homes += [(1, None, features * k) for k in range(4)]
    shapes = [
        (9, 2, rows, features),
        (2, rows, 4 * features),
        (4, 2, rows, features),
        (2, rows, features),
        (2, rows, 3 * features),
        (members, tokens // members, features),
        (members, tokens // members, features),
    ]
    anywhere = pl.BlockSpec(memory_space=pl.ANY)
    inside = pl.BlockSpec(memory_space=pltpu.VMEM)
    dma = pltpu.SemaphoreType.DMA
    low, wide = jnp.bfloat16, jnp.float32
    cut = (2, 2, 2, 2, rows, width)
    scratch = [
        pltpu.VMEM((slots, 2, 2) + cut, low),
        pltpu.VMEM((got_slots, 2) + cut, low),
        pltpu.VMEM((count, 2) + cut[1:], low),
        pltpu.VMEM((count, 2) + cut[2:], low),
        pltpu.VMEM((count, 2) + cut[3:], low),
        pltpu.VMEM((count, 2) + cut[4:], low),
        pltpu.VMEM((2 * count, 2, rows, features), low),
        pltpu.VMEM((4, tokens, features), low),
        pltpu.VMEM((2, members, 2 * rows, tokens), low),
        pltpu.VMEM((2, 6, tokens, 128), low),
        pltpu.VMEM((tokens, 128), low),
        pltpu.VMEM((6, 16, features), wide),
        pltpu.VMEM((5, 16, features), wide),
        pltpu.VMEM((tokens, features), wide),
        pltpu.VMEM((tokens, features), low),
        pltpu.VMEM((tokens, 128), wide),
        pltpu.VMEM((tokens, 128), wide),
        pltpu.VMEM((3, tokens, features), low),
    ]
    scratch += [dma((count, 2))] * 6 + [dma((count,))] * 8
    scratch += [dma((blocks,)), dma((4,)), dma((2,)), dma((2, 6)), dma((2,))]
    scratch += [pltpu.SemaphoreType.REGULAR, dma((2,))]
    scratch += [dma((members - 1,))] * 4 + [dma((5,))] * 2
    return pl.pallas_call(
        partial(
            finish_kernel,
            blocks=blocks,
            homes=homes,
            lead=lead,
            slots=slots,
            got_slots=got_slots,
            tiling=tiling,
        ),
        in_specs=[anywhere] * 19 + [inside] * 7,
        out_specs=[anywhere] * 5 + [inside] + [anywhere] * 2,
        out_shape=[jax.ShapeDtypeStruct(shape, low) for shape in shapes[:5]]
        + [jax.ShapeDtypeStruct((24, features), wide)]
        + [jax.ShapeDtypeStruct(shape, low) for shape in shapes[5:]],
        scratch_shapes=scratch,
        compiler_params=pltpu.CompilerParams(
            collective_id=1, has_side_effects=True, vmem_limit_bytes=60 * 2**20
        ),
        cost_estimate=pl.CostEstimate(
            flops=2 * tokens * features * (24 * features) + 24 * tokens * tokens * features,
            bytes_accessed=100 * tokens * features,
            transcendentals=tokens * tokens * features // 64,
        ),
        name="finish",
    )(*inputs)


def on_device_grids(
    encoder_out,
    code_ids,
    segments,
    embed_table,
    recon_grad,
    qkv_weight,
    query_bias,
    value_bias,
    out_weight,
    out_bias,
    first_gain,
    first_shift,
    second_gain,
    second_shift,
    up_weight,
    up_bias,
    down_weight,
    down_bias,
    pixel_weight,
    pixel_bias,
):
    features = encoder_out.shape[-1]
    wide = jnp.float32
    down, across = lax.axis_size("ty"), lax.axis_size("tx")
    members = down * across
    axes = ("ty", "tx")
    tiling = (down, across) + encoder_out.shape[1:3]
    each = encoder_out.shape[1] * encoder_out.shape[2]
    tokens = members * each

    def line(vector):
        return vector.reshape(1, -1)

    def exchange(tiles):
        return lax.all_to_all(tiles, axes, split_axis=0, concat_axis=0, tiled=True)

    slots = 3 * each // 2
    asked, slot_index = ask(
        jnp.swapaxes(code_ids, 1, 2), jnp.swapaxes(segments, 1, 2), embed_table.shape[0], slots
    )
    asked, recon_grad = lax.optimization_barrier((asked, recon_grad))
    cotangent = exchange(recon_grad).reshape(tokens, features)
    moved, query_marks, key_marks = spread_marks(asked[:, 2], *tiling)
    asked = asked[:, :2].reshape(members, -1)[:, :slots].reshape(-1)
    fetched = embed_table.at[asked].get(mode="promise_in_bounds")
    pixel_taps = jnp.swapaxes(pixel_weight, 0, 1)
    codes, final_grad, lower_grad, behind, hidden_grad, pixel_bias_grad, down_bias_grad = fetch(
        fetched.reshape(members, slots, features),
        slot_index,
        cotangent,
        moved,
        pixel_taps,
        down_weight,
        tiling,
    )
    codes = codes.reshape(tokens, features)

    (
        normed,
        queries,
        key_rows,
        values,
        attended,
        columns,
        features_low,
        normed_two,
        hidden_turned,
        pre_grad,
        middle_grad,
        branch_grad,
        attended_grad,
        out_bias_grad,
        second_gain_grad,
        second_shift_grad,
        up_bias_grad,
    ) = forward(
        [
            codes,
            final_grad,
            hidden_grad,
            query_marks,
            key_marks,
            qkv_weight,
            out_weight,
            up_weight,
            down_weight,
        ],
        [
            line(first_gain),
            line(first_shift),
            line(query_bias),
            line(value_bias),
            line(out_bias),
            line(second_gain),
            line(second_shift),
            line(up_bias),
            line(down_bias),
        ],
    )
    recon_rows, features_plain = conv(features_low, moved, pixel_taps, line(pixel_bias), tiling)
    pixel_sum, up_sum, down_sum, out_sum, qkv_sum, vectors, recon_tiles, share_tiles = finish(
        [
            queries,
            key_rows,
            values,
            columns,
            key_marks,
            attended,
            attended_grad,
            codes,
            middle_grad,
            features_plain,
            behind,
            normed_two,
            pre_grad,
            hidden_turned.reshape(members, 4, features // members, tokens),
            lower_grad,
            branch_grad,
            normed,
            qkv_weight,
            recon_rows.reshape(members, each, features),
            line(first_gain),
            out_bias_grad,
            second_gain_grad,
            second_shift_grad,
            up_bias_grad,
            down_bias_grad,
            pixel_bias_grad,
        ],
        tiling,
    )
    input_tiles = (
        share_tiles.reshape(encoder_out.shape).astype(wide)
        + 2.0 * commit_weight * encoder_out.astype(wide)
    ).astype(jnp.bfloat16)
    rows = features // members

    def mine(at, count=1):
        return vectors[at, : rows * count]

    def whole_sum(summed):
        return summed.reshape(-1, summed.shape[-1]).astype(wide)

    return (
        recon_tiles.reshape(encoder_out.shape),
        input_tiles,
        whole_sum(qkv_sum),
        mine(0),
        mine(1),
        whole_sum(out_sum),
        mine(4),
        mine(2),
        mine(3),
        mine(5),
        mine(6),
        whole_sum(up_sum),
        mine(16, 4),
        whole_sum(down_sum),
        mine(11),
        jnp.swapaxes(whole_sum(pixel_sum).reshape(9, rows, features), 0, 1),
        mine(12),
    )


def solution(mesh):
    in_specs = (
        P("gr", "ty", "tx", None),
        P("gr", "ty", "tx"),
        P("gr", "ty", "tx"),
        P(("ty", "tx"), None),
        P("gr", "ty", "tx", None),
        P(),
        P(),
        P(),
        P(),
        P(),
        P(),
        P(),
        P(),
        P(),
        P(),
        P(),
        P(),
        P(),
        P(),
        P(),
    )
    out_specs = (
        P("gr", "ty", "tx", None),
        P("gr", "ty", "tx", None),
        P(("ty", "tx"), None),
        P(("ty", "tx")),
        P(("ty", "tx")),
        P(("ty", "tx"), None),
        P(("ty", "tx")),
        P(("ty", "tx")),
        P(("ty", "tx")),
        P(("ty", "tx")),
        P(("ty", "tx")),
        P(("ty", "tx"), None),
        P(("ty", "tx")),
        P(("ty", "tx"), None),
        P(("ty", "tx")),
        P(("ty", "tx"), None, None),
        P(("ty", "tx")),
    )
    def on_device(encoder_out, *rest):
        members = mesh.shape["ty"] * mesh.shape["tx"]
        whole_grids = encoder_out.shape[0] == members and tuple(mesh.devices.shape) == (4, 2, 4)
        body = on_device_grids if whole_grids else on_device_bands
        return body(encoder_out, *rest)

    return jax.shard_map(
        on_device, mesh=mesh, in_specs=in_specs, out_specs=out_specs, check_vma=False
    )
```
